32 devices in a mesh: dp: 8 (over y, x, core), narrow: 4 (over z).
Axes of the slice: x: 2, y: 2, z: 4, core: 2. Of those that a mesh axis runs over, the one named last changes fastest.
Arguments:
- tokens: bfloat16 [32768, 512], P(('dp', 'narrow')), may hold values from -6 to 6
- memory: bfloat16 [32, 512, 512], P(('dp', 'narrow')), may hold values from -6 to 6
- neighbour_bank: bfloat16 [32, 512, 512], P(('dp', 'narrow')), may hold values from -6 to 6
- starts: int32 [32768], P(('dp', 'narrow')), may hold values 0 or 1
- neighbours: int32 [32768, 4], P(('dp', 'narrow')), may hold values from 0 to 511
- cotangent: bfloat16 [32768, 512], P(('dp', 'narrow')), may hold values from -6 to 6
- attn_weights: float32 [4, 512, 512], P(None, 'dp', 'narrow'), may hold values from -0.375 to 0.375
- up_weights: float32 [512, 2048], P('dp', 'narrow'), may hold values from -0.25 to 0.25
- down_weights: float32 [2048, 512], P('narrow', 'dp'), may hold values from -0.125 to 0.125
- vectors: float32 [10, 512], replicated, as said below
- attn_moment: float32 [4, 512, 512], P(None, 'dp', 'narrow'), may hold values from -0.75 to 0.75
- up_moment: float32 [512, 2048], P('dp', 'narrow'), may hold values from -0.75 to 0.75
- down_moment: float32 [2048, 512], P('narrow', 'dp'), may hold values from -0.75 to 0.75
- vector_moment: float32 [10, 512], replicated, may hold values from -2 to 2
Outputs:
- out: bfloat16 [32768, 512], P(('dp', 'narrow'))
- grad_in: bfloat16 [32768, 512], P(('dp', 'narrow'))
- attn_new: float32 [4, 512, 512], P(None, 'dp', 'narrow')
- up_new: float32 [512, 2048], P('dp', 'narrow')
- down_new: float32 [2048, 512], P('narrow', 'dp')
- attn_mom_new: float32 [4, 512, 512], P(None, 'dp', 'narrow')
- up_mom_new: float32 [512, 2048], P('dp', 'narrow')
- down_mom_new: float32 [2048, 512], P('narrow', 'dp')
- vectors_new: float32 [10, 512], replicated
- vector_mom_new: float32 [10, 512], replicated
- grad_norm: float32 [], replicated
The draws below stay inside these ranges and needn't reach their ends.
Inputs may be any that keep to these rules, and one draw needn't show every extreme that they name: `neighbours`: each entry names a row of the neighbour bank of the token's own segment. `starts`: 1 marks the first token of a document. `vectors`: rows 0 and 1 are positive norm gains, the other 8 rows the gate's weights.
All inputs are finite; a program needn't handle non-finite values. No bound on the sum of `starts` on one device may be relied on, other than what follows from the above.
Results may differ from the reference program's by a relative error of at most 0.022.
Values may be sent and summed in bfloat16 or wider, within the bound.
No kernel may reach another device: no remote copies, remote signals or barrier semaphores. Data moves between devices by JAX's collectives and lax.ppermute only.
A program may use at most 192 MiB of HBM per device.

```python
import math
import jax
import jax.numpy as jnp
from jax import lax

D = 512
H = 8
FF = 2048
MEM = 512
BANK = 512
KNB = 4
LEN = 1024
NS_ITERS = 5
SEGS = 32
TOKENS = 32768
VROWS = 10
PARAMS = 3150848
N_NARROW = 4


def draw_vectors(key, part):
    key = jax.random.fold_in(key, 7)
    key_gain, key_gate = jax.random.split(key, 2)
    fraction = jnp.arange(D, dtype=jnp.float32) / (D - 1)
    rising = 0.75 * jnp.exp(fraction * 0.5 * jnp.log(3.0))
    jitter = jax.random.uniform(key_gain, (2, D), jnp.float32, 0.85, 1.15)
    gate_rows = jax.random.truncated_normal(key_gate, -3.0, 3.0, (H, D), jnp.float32) / jnp.sqrt(D * 1.0)
    gains = rising[None, :] * jitter
    return jnp.concatenate([gains, gate_rows], axis=0).astype(jnp.float32)


def touch_ends(values, key, low, top_value):
    longest = values.shape.index(max(values.shape))
    spots = []
    for shift in (0, 1):
        where = [jax.random.randint(jax.random.fold_in(key, axis), (), 0, length) for axis, length in enumerate(values.shape)]
        where[longest] = (where[longest] + shift) % values.shape[longest]
        spots.append(tuple(where))
    return values.at[spots[0]].set(low).at[spots[1]].set(top_value)


def level_of(key, shape, cuts, smallest, high):
    factor_of = 1.0
    for dim, shards_of in cuts:
        draws = jax.random.uniform(jax.random.fold_in(jax.random.fold_in(key, 6), dim), (shards_of,), jnp.float32, smallest / len(cuts), high / len(cuts))
        factor_of = factor_of * jnp.repeat(jnp.exp(draws), shape[dim] // shards_of).reshape((-1,) + (1,) * (len(shape) - 1 - dim))
    return factor_of


def normal_values(own_key, dims, scale, most, shards=(), kind=jnp.bfloat16):
    array = scale * jax.random.normal(own_key, dims, jnp.float32)
    if shards:
        array = array * level_of(own_key, dims, shards, -0.22, 0.18)
    return jnp.clip(array, -most, most).astype(kind)


def setup_inputs(seed: int = 0) -> dict:
    seeds = jax.random.split(jax.random.key(seed), 15)
    return {
        "tokens": normal_values(seeds[0], (TOKENS, D), 1.0, 6.0, ((0, 32),)),
        "memory": normal_values(seeds[1], (SEGS, MEM, D), 1.0, 6.0, ((0, 32),)),
        "neighbour_bank": normal_values(seeds[2], (SEGS, BANK, D), 1.0, 6.0, ((0, 32),)),
        "starts": touch_ends((jax.random.randint(seeds[3], (TOKENS,), 0, LEN) < 4).astype(jnp.int32), jax.random.fold_in(seeds[3], 1), 0, 1),
        "neighbours": touch_ends(jax.random.randint(seeds[4], (TOKENS, KNB), 0, BANK), jax.random.fold_in(seeds[4], 1), 0, BANK - 1).astype(jnp.int32),
        "cotangent": normal_values(seeds[5], (TOKENS, D), 1.0, 6.0, ((0, 32),)),
        "attn_weights": normal_values(seeds[6], (4, D, D), (D // 2) ** -0.5, 0.375, ((1, 8), (2, 4)), jnp.float32),
        "up_weights": normal_values(seeds[7], (D, FF), D ** -0.5, 0.25, ((0, 8), (1, 4)), jnp.float32),
        "down_weights": normal_values(seeds[8], (FF, D), FF ** -0.5, 0.125, ((0, 4), (1, 8)), jnp.float32),
        "vectors": draw_vectors(jax.random.fold_in(seeds[14], 71), 0),
        "attn_moment": normal_values(seeds[10], (4, D, D), 0.05, 0.75, ((1, 8), (2, 4)), jnp.float32),
        "up_moment": normal_values(seeds[11], (D, FF), 0.05, 0.75, ((0, 8), (1, 4)), jnp.float32),
        "down_moment": normal_values(seeds[12], (FF, D), 0.05, 0.75, ((0, 4), (1, 8)), jnp.float32),
        "vector_moment": normal_values(seeds[13], (VROWS, D), 0.15, 2.0, (), jnp.float32),
    }


@jax.custom_vjp
def low(v):
    return lax.optimization_barrier(v.astype(jnp.bfloat16)).astype(jnp.float32)

@jax.custom_vjp
def low_back(v):
    return v

def low_keep(v):
    return (low(v), None)

def low_pass(kept, grad):
    return (grad,)

def back_keep(v):
    return (v, None)

def back_low(kept, grad):
    return (low(grad),)
low.defvjp(low_keep, low_pass)
low_back.defvjp(back_keep, back_low)
epsilon = 1e-06
coef_first = 3.4445
coef_second = -4.775
coef_third = 2.0315
clip_fraction = 0.05
muon_rate = 0.5
muon_decay = 0.5
vector_rate = 0.5
vector_decay = 0.9
highest = lax.Precision.HIGHEST

def rms_factor(values):
    return lax.rsqrt(lax.optimization_barrier(jnp.mean(values * values, axis=-1, keepdims=True)) + epsilon)

def product(first_factor, second_factor):
    return jnp.dot(first_factor, second_factor, precision=highest)

def visibility(seg_starts):
    doc_index = jnp.cumsum(seg_starts)
    before_reset = doc_index == 0
    positions = jnp.arange(LEN)
    causal = (positions[None, :] <= positions[:, None]) & (doc_index[None, :] == doc_index[:, None])
    return jnp.concatenate([jnp.broadcast_to(before_reset[:, None], (LEN, MEM)), causal], axis=1)

def segment_forward(params, seg_tokens, seg_memory, seg_bank, seg_starts, seg_near):
    attn_weights, up_weights, down_weights, vectors = params
    head_dim = D // H
    score_scale = 1.0 / math.sqrt(head_dim)
    context = jnp.concatenate([seg_memory, seg_tokens], axis=0)
    normed = low(context * rms_factor(context) * vectors[0])
    queries = low(low_back(product(normed[MEM:], low(attn_weights[0]))))
    key_rows = low(low_back(product(normed, low(attn_weights[1]))))
    value_rows = low(low_back(product(normed, low(attn_weights[2]))))
    bank_keys = low(low_back(product(seg_bank, low(attn_weights[1]))))
    bank_values = low(low_back(product(seg_bank, low(attn_weights[2]))))
    query_heads = queries.reshape(LEN, H, head_dim)
    key_heads = key_rows.reshape(MEM + LEN, H, head_dim)
    value_heads = value_rows.reshape(MEM + LEN, H, head_dim)
    scores = low_back(jnp.einsum('qhd,khd->hqk', query_heads, key_heads, precision=highest) * score_scale)
    scores = jnp.where(visibility(seg_starts)[None], scores, -1e+30)
    row_peak = lax.optimization_barrier(jnp.max(scores, axis=-1, keepdims=True))
    weights = jnp.exp(scores - row_peak)
    probabilities = weights / lax.optimization_barrier(jnp.sum(weights, axis=-1, keepdims=True))
    local_out = low_back(jnp.einsum('hqk,khd->qhd', low(probabilities), value_heads, precision=highest))
    near_keys = jnp.take(bank_keys, seg_near, axis=0).reshape(LEN, KNB, H, head_dim)
    near_values = jnp.take(bank_values, seg_near, axis=0).reshape(LEN, KNB, H, head_dim)
    near_scores = jnp.einsum('qhd,qjhd->qjh', query_heads, near_keys, precision=highest) * score_scale
    near_peak = lax.optimization_barrier(jnp.max(near_scores, axis=1, keepdims=True))
    near_weights = jnp.exp(near_scores - near_peak)
    near_probs = near_weights / lax.optimization_barrier(jnp.sum(near_weights, axis=1, keepdims=True))
    fetched = jnp.einsum('qjh,qjhd->qhd', near_probs, near_values, precision=highest)
    logits = low_back(product(normed[MEM:], low(vectors[2:]).T))
    gate_open = jax.nn.sigmoid(logits)[:, :, None]
    mixed_heads = low(((1.0 - gate_open) * local_out + gate_open * fetched).reshape(LEN, D))
    residual = seg_tokens + low_back(product(mixed_heads, low(attn_weights[3])))
    ffn_in = low(residual * rms_factor(residual) * vectors[1])
    hidden = low_back(product(ffn_in, low(up_weights)))
    activation = low(jax.nn.gelu(hidden, approximate=False))
    return residual + low_back(product(activation, low(down_weights)))

def partial_gram(matrix):
    row_count, col_count = matrix.shape
    pieces = matrix.reshape(row_count, N_NARROW, col_count // N_NARROW)
    block_terms = jnp.einsum('mbk,nbk->bmn', pieces, pieces, precision=highest)
    return lax.optimization_barrier(jnp.sum(low(block_terms), axis=0))

def orthogonalize(moment):
    gram_total = partial_gram(moment)
    norm_scale = 1.0 / (jnp.sqrt(jnp.trace(gram_total)) + 1e-07)
    current = moment * norm_scale
    square = gram_total * (norm_scale * norm_scale)
    for iteration in range(NS_ITERS):
        if iteration > 0:
            square = partial_gram(current)
        applied_once = product(square, current)
        applied_twice = product(square, applied_once)
        current = coef_first * current + coef_second * applied_once + coef_third * applied_twice
    return current

def reference(tokens, memory, neighbour_bank, starts, neighbours, cotangent, attn_weights, up_weights, down_weights, vectors, attn_moment, up_moment, down_moment, vector_moment):
    params = (attn_weights, up_weights, down_weights, vectors)
    segment_items = (tokens.astype(jnp.float32).reshape(SEGS, LEN, D), memory.astype(jnp.float32), neighbour_bank.astype(jnp.float32), starts.reshape(SEGS, LEN), neighbours.reshape(SEGS, LEN, KNB), cotangent.astype(jnp.float32).reshape(SEGS, LEN, D))

    def segment_step(totals, scan_items):
        seg_tokens, seg_memory, seg_bank, seg_starts, seg_near, seg_cot = scan_items

        def forward(param_set, inputs):
            return segment_forward(param_set, inputs, seg_memory, seg_bank, seg_starts, seg_near)
        output, pullback = jax.vjp(forward, params, seg_tokens)
        param_grads, token_grads = pullback(seg_cot)
        return (jax.tree.map(jnp.add, totals, param_grads), (output.astype(jnp.bfloat16), token_grads.astype(jnp.bfloat16)))
    zero_grads = jax.tree.map(jnp.zeros_like, params)
    totals, (outputs, grad_tokens) = lax.scan(segment_step, zero_grads, segment_items)
    grad_attn, grad_up, grad_down, grad_vectors = totals
    squares = jnp.sum(grad_attn * grad_attn) + jnp.sum(grad_up * grad_up) + jnp.sum(grad_down * grad_down) + jnp.sum(grad_vectors * grad_vectors)
    grad_norm = jnp.sqrt(squares)
    clip_limit = clip_fraction * math.sqrt(PARAMS)
    clip_factor = clip_limit / jnp.maximum(grad_norm, clip_limit)
    attn_mom_new = muon_decay * attn_moment + clip_factor * grad_attn
    up_mom_new = muon_decay * up_moment + clip_factor * grad_up
    down_mom_new = muon_decay * down_moment + clip_factor * grad_down
    attn_ortho = jnp.stack([orthogonalize(attn_mom_new[matrix_index]) for matrix_index in range(4)])
    up_ortho = orthogonalize(up_mom_new)
    down_ortho = orthogonalize(down_mom_new.T).T
    shape_factor = math.sqrt(max(1.0, FF / D))
    attn_new = attn_weights - muon_rate * attn_ortho
    up_new = up_weights - muon_rate * up_ortho
    down_new = down_weights - muon_rate * shape_factor * down_ortho
    vector_mom_new = vector_decay * vector_moment + clip_factor * grad_vectors
    vectors_new = vectors - vector_rate * vector_mom_new
    return (outputs.reshape(TOKENS, D), grad_tokens.reshape(TOKENS, D), attn_new, up_new, down_new, attn_mom_new, up_mom_new, down_mom_new, vectors_new, vector_mom_new, grad_norm)
```

```python
import math

import jax
import jax.numpy as jnp
from jax import lax
from jax.experimental import pallas as pl
from jax.experimental.pallas import tpu as pltpu
from jax.sharding import Mesh, PartitionSpec as P

D = 512
H = 8
FF = 2048
MEM = 512
BANK = 512
KNB = 4
LEN = 1024
CTX = MEM + LEN
ROWS = CTX + BANK
HD = D // H
TB = 256
NT = LEN // TB
MC = MEM // TB
BC = BANK // TB
PAIR = 2 * HD
NPAIR = D // PAIR
F32 = jnp.float32
BF16 = jnp.bfloat16
NS_ITERS = 5
PARAMS = 3150848
epsilon = 1e-06
masked_score = -1e30
coef_first = 3.4445
coef_second = -4.775
coef_third = 2.0315
clip_fraction = 0.05
muon_rate = 0.5
muon_decay = 0.5
vector_rate = 0.5
vector_decay = 0.9
highest = lax.Precision.HIGHEST
VMEM_LIMIT = 60 * 1024 * 1024


def nn(a, b):
    return lax.dot_general(a, b, (((1,), (0,)), ((), ())), preferred_element_type=F32)


def nt(a, b):
    return lax.dot_general(a, b, (((1,), (1,)), ((), ())), preferred_element_type=F32)


def tn(a, b):
    return lax.dot_general(a, b, (((0,), (0,)), ((), ())), preferred_element_type=F32)


def rms_factor(values):
    return lax.rsqrt(jnp.mean(values * values, axis=-1, keepdims=True) + epsilon)


def whole(shape):
    return pl.BlockSpec(shape, lambda *_: (0,) * len(shape))


def call(body, grid, in_specs, out_specs, out_shape, flops, nbytes, name, scratch=(), trans=0, prefetch=0):
    return pl.pallas_call(
        body,
        grid_spec=pltpu.PrefetchScalarGridSpec(
            num_scalar_prefetch=prefetch,
            grid=grid,
            in_specs=in_specs,
            out_specs=out_specs,
            scratch_shapes=list(scratch),
        ),
        out_shape=out_shape,
        name=name,
        cost_estimate=pl.CostEstimate(flops=int(flops), bytes_accessed=int(nbytes), transcendentals=int(trans)),
        compiler_params=pltpu.CompilerParams(
            vmem_limit_bytes=VMEM_LIMIT, dimension_semantics=("arbitrary",) * len(grid)
        ),
    )


SMEM = pl.BlockSpec(memory_space=pltpu.SMEM)


def sds(shape, dtype):
    return jax.ShapeDtypeStruct(shape, dtype)


def context_body(tok_ref, mem_ref, bank_ref, cot_ref, vec_ref, x_ref, xt_ref, cott_ref, gate_ref):
    i = pl.program_id(0)
    gain = vec_ref[0:1, :]

    def put(rows):
        x_ref[...] = rows
        xt_ref[...] = rows.T

    def norm(values):
        wide = values.astype(F32)
        return (wide * rms_factor(wide) * gain).astype(BF16)

    @pl.when(i < MC)
    def _():
        put(norm(mem_ref[...]))

    @pl.when((i >= MC) & (i < MC + NT))
    def _():
        rows = norm(tok_ref[...])
        put(rows)
        logits = nt(vec_ref[2:10, :].astype(BF16), rows)
        gate = jax.nn.sigmoid(logits)
        for p in range(NPAIR):
            gate_ref[p] = gate[2 * p : 2 * p + 2, :]
        cott_ref[...] = cot_ref[...].T

    @pl.when(i >= MC + NT)
    def _():
        put(bank_ref[...])


def context_kernel(tokens, memory, bank, cot, vectors):
    steps = MC + NT + BC
    clip_tok = lambda i: jnp.clip(i - MC, 0, NT - 1)
    return call(
        context_body,
        (steps,),
        [
            pl.BlockSpec((TB, D), lambda i: (clip_tok(i), 0)),
            pl.BlockSpec((TB, D), lambda i: (jnp.minimum(i, MC - 1), 0)),
            pl.BlockSpec((TB, D), lambda i: (jnp.clip(i - MC - NT, 0, BC - 1), 0)),
            pl.BlockSpec((TB, D), lambda i: (clip_tok(i), 0)),
            whole((2 + H, D)),
        ],
        [
            pl.BlockSpec((TB, D), lambda i: (i, 0)),
            pl.BlockSpec((D, TB), lambda i: (0, i)),
            pl.BlockSpec((D, TB), lambda i: (0, clip_tok(i))),
            pl.BlockSpec((NPAIR, 2, TB), lambda i: (0, 0, clip_tok(i))),
        ],
        [sds((ROWS, D), BF16), sds((D, ROWS), BF16), sds((D, LEN), BF16), sds((NPAIR, 2, LEN), F32)],
        1e7,
        8e6,
        "context",
    )(tokens, memory, bank, cot, vectors)


def mask_body(doc_row_ref, doc_col_ref, near_ref, tok_ref, bank_ref):
    i = pl.program_id(0)
    doc_row = doc_row_ref[...]

    @pl.when(i < NT)
    def _():
        keys = lax.broadcasted_iota(jnp.int32, (TB, LEN), 0) + i * TB
        rows = lax.broadcasted_iota(jnp.int32, (TB, LEN), 1)
        seen = (keys <= rows) & (doc_col_ref[...] == doc_row)
        tok_ref[...] = jnp.where(seen, 0.0, masked_score)

    @pl.when(i >= NT)
    def _():
        keys = lax.broadcasted_iota(jnp.int32, (TB, LEN), 0) + (i - NT) * TB
        count = jnp.zeros((TB, LEN), F32)
        for j in range(KNB):
            count = count + jnp.where(near_ref[j : j + 1, :] == keys, 1.0, 0.0)
        bias = jnp.where(count > 0.5, 0.0, masked_score)
        for j in range(2, KNB + 1):
            bias = jnp.where(count > j - 0.5, math.log(j), bias)
        bank_ref[...] = bias


def mask_kernel(doc_row, doc_col, near_t):
    return call(
        mask_body,
        (NT + BC,),
        [
            whole((1, LEN)),
            pl.BlockSpec((TB, 1), lambda i: (jnp.minimum(i, NT - 1), 0)),
            whole((KNB, LEN)),
        ],
        [
            pl.BlockSpec((TB, LEN), lambda i: (jnp.minimum(i, NT - 1), 0)),
            pl.BlockSpec((TB, LEN), lambda i: (jnp.clip(i - NT, 0, BC - 1), 0)),
        ],
        [sds((LEN, LEN), F32), sds((BANK, LEN), F32)],
        1e7,
        7e6,
        "masks",
    )(doc_row, doc_col, near_t)


def each_block(place_ref, chips, planes):
    for core in range(2):
        for chip in range(chips):
            row = ((place_ref[0] ^ chip) * 2 + (place_ref[1] ^ core))
            for plane in range(planes):
                yield core, chip, plane, row, place_ref[2] ^ plane


def part(index, size):
    return pl.ds(pl.multiple_of(index * size, size), size)


def project_rows(i, x_ref, w_ref, q_ref, k_ref, v_ref, kt_ref, vt_ref):
    rows = x_ref[...]
    keys = nn(rows, w_ref[1]).astype(BF16)
    values = nn(rows, w_ref[2]).astype(BF16)
    k_ref[...] = keys
    v_ref[...] = values
    kt_ref[...] = keys.T
    vt_ref[...] = values.T

    @pl.when((i >= MC) & (i < MC + NT))
    def _():
        q_ref[...] = (nn(rows, w_ref[0]).astype(BF16).astype(F32) * (1.0 / math.sqrt(HD))).astype(BF16)


def project_kernel(x, w, place=None):
    steps = MC + NT + BC
    fast = place is not None
    if fast:
        chips, planes = len(w) // 2, w[0].shape[0]
        own_rows, own_cols = w[0].shape[2:]

    def body(*refs):
        i = pl.program_id(0)
        if not fast:
            project_rows(i, *refs)
            return
        place_ref, x_ref, *rest = refs
        blocks, (w_ref, *outs) = rest[: len(w)], rest[len(w) :]

        @pl.when(i == 0)
        def _():
            for core, chip, plane, row, col in each_block(place_ref, chips, planes):
                for j in range(3):
                    w_ref[j, part(row, own_rows), part(col, own_cols)] = blocks[core * chips + chip][plane, j]

        project_rows(i, x_ref, w_ref, *outs)

    out_specs = [
        pl.BlockSpec((TB, D), lambda i: (jnp.clip(i - MC, 0, NT - 1), 0)),
        pl.BlockSpec((TB, D), lambda i: (i, 0)),
        pl.BlockSpec((TB, D), lambda i: (i, 0)),
        pl.BlockSpec((D, TB), lambda i: (0, i)),
        pl.BlockSpec((D, TB), lambda i: (0, i)),
    ]
    out_shape = [
        sds((LEN, D), BF16),
        sds((ROWS, D), BF16),
        sds((ROWS, D), BF16),
        sds((D, ROWS), BF16),
        sds((D, ROWS), BF16),
    ]
    in_specs = [pl.BlockSpec((TB, D), lambda i: (i, 0))]
    if fast:
        in_specs = [SMEM] + in_specs + [whole(b.shape) for b in w]
        out_specs = [whole((3, D, D))] + out_specs
        out_shape = [sds((3, D, D), BF16)] + out_shape
        operands = (place, x, *w)
    else:
        in_specs = in_specs + [whole((3, D, D))]
        operands = (x, w)
    result = call(
        body, (steps,), in_specs, out_specs, out_shape, 2 * D * D * (LEN + 2 * ROWS), 14e6, "project"
    )(*operands)
    return result if fast else [w, *result]


def head_lanes(values, h):
    lanes = lax.broadcasted_iota(jnp.int32, values.shape, 1)
    keep = (lanes < HD) if h == 0 else (lanes >= HD)
    return jnp.where(keep, values, jnp.zeros_like(values))


def key_chunks(tb):
    return list(range(MC + tb + 1)), list(range(MC + NT, MC + NT + BC))


def attend_body(
    q_ref, k_ref, vt_ref, tok_ref, bank_ref, doc_ref, gate_ref,
    e_ref, local_ref, fetched_ref, stat_ref, mixed_ref, mixedt_ref, s_ref,
):
    p = pl.program_id(0)
    for tb in range(NT):
        cols = slice(tb * TB, (tb + 1) * TB)
        q_rows = q_ref[cols, :]
        mem_bias = jnp.where(doc_ref[:, cols] == 0.0, 0.0, masked_score)
        mixed_parts = []
        for h in range(2):
            q_head = head_lanes(q_rows, h)
            head_rows = slice(h * HD, (h + 1) * HD)

            def soft(chunks, slot):
                peak = jnp.full((8, TB), -3e38, F32)
                for c in chunks:
                    keys = slice(c * TB, (c + 1) * TB)
                    s = nt(k_ref[keys, :], q_head)
                    if c < MC:
                        s = s + mem_bias
                    elif c < MC + NT:
                        s = s + tok_ref[(c - MC) * TB : (c - MC + 1) * TB, cols]
                    else:
                        s = s + bank_ref[(c - MC - NT) * TB : (c - MC - NT + 1) * TB, cols]
                    s_ref[slot, keys, :] = s
                    peak = jnp.maximum(peak, jnp.max(s.reshape(TB // 8, 8, TB), axis=0))
                top = jnp.max(peak, axis=0, keepdims=True)
                total = jnp.zeros((8, TB), F32)
                result = jnp.zeros((HD, TB), F32)
                for c in chunks:
                    keys = slice(c * TB, (c + 1) * TB)
                    e = jnp.exp(s_ref[slot, keys, :] - top)
                    total = total + jnp.sum(e.reshape(TB // 8, 8, TB), axis=0)
                    low = e.astype(BF16)
                    e_ref[h, keys, cols] = low
                    result = result + nn(vt_ref[head_rows, keys], low)
                inverse = 1.0 / jnp.sum(total, axis=0, keepdims=True)
                return result * inverse, inverse

            near, far = key_chunks(tb)
            local, local_inv = soft(near, h)
            fetched, fetched_inv = soft(far, h)
            local_ref[head_rows, cols] = local
            fetched_ref[head_rows, cols] = fetched
            stat_ref[0, h : h + 1, cols] = local_inv
            stat_ref[0, 2 + h : 3 + h, cols] = fetched_inv
            gate = gate_ref[0, h : h + 1, cols]
            mixed_parts.append((1.0 - gate) * local + gate * fetched)
        mixed = jnp.concatenate(mixed_parts, axis=0)
        mixedt_ref[:, cols] = mixed.astype(BF16)
        mixed_ref[cols, :] = mixed.T.astype(BF16)


def attend_kernel(q, k, vt, bias_tok, bias_bank, doc_row, gate, first, count):
    spec_cols = lambda rows: pl.BlockSpec((rows, PAIR), lambda p: (0, p + first))
    return call(
        attend_body,
        (count,),
        [
            spec_cols(LEN),
            spec_cols(ROWS),
            pl.BlockSpec((PAIR, ROWS), lambda p: (p + first, 0)),
            whole((LEN, LEN)),
            whole((BANK, LEN)),
            whole((1, LEN)),
            pl.BlockSpec((1, 2, LEN), lambda p: (p + first, 0, 0)),
        ],
        [
            pl.BlockSpec((2, ROWS, LEN), lambda p: (p, 0, 0)),
            pl.BlockSpec((PAIR, LEN), lambda p: (p, 0)),
            pl.BlockSpec((PAIR, LEN), lambda p: (p, 0)),
            pl.BlockSpec((1, 8, LEN), lambda p: (p, 0, 0)),
            pl.BlockSpec((LEN, PAIR), lambda p: (0, p)),
            pl.BlockSpec((PAIR, LEN), lambda p: (p, 0)),
        ],
        [
            sds((2 * count, ROWS, LEN), BF16),
            sds((PAIR * count, LEN), F32),
            sds((PAIR * count, LEN), F32),
            sds((count, 8, LEN), F32),
            sds((LEN, PAIR * count), BF16),
            sds((PAIR * count, LEN), BF16),
        ],
        count * 4 * 2 * PAIR * ROWS * LEN,
        count * 14e6 + 6e6,
        "attend",
        scratch=[pltpu.VMEM((2, ROWS, TB), F32)],
        trans=count * 2 * ROWS * LEN,
    )(q, k, vt, bias_tok, bias_bank, doc_row, gate)


def gelu_parts(x):
    square = jnp.exp(x * x * -0.5)
    z = jnp.abs(x) * 0.7071067811865476
    t = 1.0 / (1.0 + 0.3275911 * z)
    poly = t * (
        0.254829592 + t * (-0.284496736 + t * (1.421413741 + t * (-1.453152027 + t * 1.061405429)))
    )
    tail = 0.5 * poly * square
    cdf = jnp.where(x >= 0.0, 1.0 - tail, tail)
    return cdf, square * 0.3989422804014327


FC = 512


def feed_body(
    mixed_ref, tok_ref, cot_ref, wo_ref, up_ref, dt_ref, vec_ref,
    out_ref, act_ref, gh_ref, ffnt_ref, branch_ref, gres_ref, gmt_ref, gain_ref,
):
    i = pl.program_id(0)
    residual = tok_ref[...].astype(F32) + nn(mixed_ref[...], wo_ref[...])
    factor = rms_factor(residual)
    hat = residual * factor
    gain = vec_ref[1:2, :]
    ffn = (hat * gain).astype(BF16)
    ffnt_ref[...] = ffn.T
    cot = cot_ref[...]
    out = residual
    grad_ffn = jnp.zeros(residual.shape, F32)
    for c in range(FF // FC):
        cols = slice(c * FC, (c + 1) * FC)
        hidden = nn(ffn, up_ref[:, cols])
        cdf, pdf = gelu_parts(hidden)
        act = (hidden * cdf).astype(BF16)
        act_ref[:, cols] = act
        grad_act = nn(cot, dt_ref[:, cols])
        gh = (grad_act * (cdf + hidden * pdf)).astype(BF16)
        gh_ref[:, cols] = gh
        out = out + nt(act, dt_ref[:, cols])
        grad_ffn = grad_ffn + nt(gh, up_ref[:, cols])
    out_ref[...] = out.astype(BF16)
    part = jnp.sum(grad_ffn * hat, axis=0, keepdims=True)

    @pl.when(i == 0)
    def _():
        gain_ref[...] = part

    @pl.when(i > 0)
    def _():
        gain_ref[...] += part

    scaled = grad_ffn * gain
    grad_res = cot.astype(F32) + factor * (scaled - hat * jnp.mean(scaled * hat, axis=-1, keepdims=True))
    gres_ref[...] = grad_res
    branch = grad_res.astype(BF16)
    branch_ref[...] = branch
    gmt_ref[...] = nt(wo_ref[...], branch)


def feed_kernel(mixed, tokens, cot, vectors, w, place=None):
    rows = lambda width: pl.BlockSpec((TB, width), lambda i: (i, 0))
    cols = lambda height: pl.BlockSpec((height, TB), lambda i: (0, i))
    fast = place is not None
    if fast:
        chips, planes = len(w) // 2, w[0].shape[0]
        own_rows, own_o, own_ff = w[0].shape[1], D // planes, FF // planes

    def body(*refs):
        if not fast:
            mixed_ref, tok_ref, cot_ref, vec_ref, wo_ref, up_ref, dt_ref, *outs = refs
            feed_body(mixed_ref, tok_ref, cot_ref, wo_ref, up_ref, dt_ref, vec_ref, *outs)
            return
        place_ref, mixed_ref, tok_ref, cot_ref, vec_ref, *rest = refs
        blocks, outs = rest[: len(w)], rest[len(w) : -3]
        wo_ref, up_ref, dt_ref = rest[-3:]

        @pl.when(pl.program_id(0) == 0)
        def _():
            for core, chip, plane, row, col in each_block(place_ref, chips, planes):
                block = blocks[core * chips + chip]
                here = part(row, own_rows)
                wo_ref[here, part(col, own_o)] = block[plane, :, :own_o]
                up_ref[here, part(col, own_ff)] = block[plane, :, own_o : own_o + own_ff]
                dt_ref[here, part(col, own_ff)] = block[plane, :, own_o + own_ff :]

        feed_body(mixed_ref, tok_ref, cot_ref, wo_ref, up_ref, dt_ref, vec_ref, *outs)

    in_specs = [rows(D), rows(D), rows(D), whole((2 + H, D))] + [whole(b.shape) for b in w]
    scratch = []
    operands = (mixed, tokens, cot, vectors, *w)
    if fast:
        in_specs = [SMEM] + in_specs
        operands = (place, *operands)
        scratch = [pltpu.VMEM((D, D), BF16), pltpu.VMEM((D, FF), BF16), pltpu.VMEM((D, FF), BF16)]
    return call(
        body,
        (NT,),
        in_specs,
        [rows(D), rows(FF), rows(FF), cols(D), rows(D), rows(D), cols(D), whole((1, D))],
        [
            sds((LEN, D), BF16),
            sds((LEN, FF), BF16),
            sds((LEN, FF), BF16),
            sds((D, LEN), BF16),
            sds((LEN, D), BF16),
            sds((LEN, D), F32),
            sds((D, LEN), F32),
            sds((1, D), F32),
        ],
        2 * LEN * D * (4 * FF + 2 * D),
        22e6,
        "feed",
        scratch=scratch,
        trans=LEN * FF * 2,
    )(*operands)


def feed_grads_body(cott_ref, act_ref, ffnt_ref, gh_ref, mixedt_ref, branch_ref, gd_ref, gu_ref, go_ref):
    gd_ref[...] = nn(cott_ref[...], act_ref[...]).astype(BF16)
    gu_ref[...] = nn(ffnt_ref[...], gh_ref[...]).astype(BF16)
    go_ref[...] = nn(mixedt_ref[...], branch_ref[...]).astype(BF16)


def feed_grads_kernel(cot_t, act, ffn_t, gh, mixed_t, branch):
    steps = 4
    wide = lambda width: pl.BlockSpec((LEN, width // steps), lambda i: (0, i))
    out = lambda width: pl.BlockSpec((D, width // steps), lambda i: (0, i))
    return call(
        feed_grads_body,
        (steps,),
        [whole((D, LEN)), wide(FF), whole((D, LEN)), wide(FF), whole((D, LEN)), wide(D)],
        [out(FF), out(FF), out(D)],
        [sds((D, FF), BF16), sds((D, FF), BF16), sds((D, D), BF16)],
        2 * LEN * D * (2 * FF + D),
        17e6,
        "feed_grads",
    )(cot_t, act, ffn_t, gh, mixed_t, branch)


def feed_grads_blocks(cot_t, act, ffn_t, gh, mixed_t, branch, place, chips, planes):
    own_rows, own_o, own_ff = D // (2 * chips), D // planes, FF // planes
    width = own_o + 2 * own_ff

    def body(place_ref, cott_ref, act_ref, ffnt_ref, gh_ref, mixedt_ref, branch_ref, keep_ref, send_ref, all_ref):
        all_ref[:, :own_o] = nn(mixedt_ref[...], branch_ref[...]).astype(BF16)
        all_ref[:, own_o : own_o + own_ff] = nn(ffnt_ref[...], gh_ref[...]).astype(BF16)
        all_ref[:, own_o + own_ff :] = nn(cott_ref[...], act_ref[...]).astype(BF16)
        for chip in range(chips):
            slot = place_ref[0] ^ chip
            keep_ref[slot, 0] = all_ref[part(chip * 2 + place_ref[1], own_rows), :]
            send_ref[slot, 0] = all_ref[part(chip * 2 + 1 - place_ref[1], own_rows), :]

    wide = lambda cols: pl.BlockSpec((LEN, cols // planes), lambda i, _: (0, i))
    out = pl.BlockSpec((chips, 1, own_rows, width), lambda i, place_ref: (0, i ^ place_ref[2], 0, 0))
    shape = sds((chips, planes, own_rows, width), BF16)
    return call(
        body,
        (planes,),
        [whole((D, LEN)), wide(FF), whole((D, LEN)), wide(FF), whole((D, LEN)), wide(D)],
        [out, out],
        [shape, shape],
        2 * LEN * D * (2 * FF + D),
        17e6,
        "feed_grads",
        scratch=[pltpu.VMEM((D, width), BF16)],
        prefetch=1,
    )(place, cot_t, act, ffn_t, gh, mixed_t, branch)


def unattend_body(
    q_ref, k_ref, kt_ref, v_ref, e_ref, gmt_ref, local_ref, fetched_ref, stat_ref, gate_ref,
    dq_ref, dk_ref, dv_ref, gl_ref, ds_ref, do_ref, df_ref, dot_ref,
):
    heads = []
    for h in range(2):
        head_rows = slice(h * HD, (h + 1) * HD)
        gm = gmt_ref[head_rows, :]
        local = local_ref[head_rows, :]
        fetched = fetched_ref[head_rows, :]
        gate = gate_ref[0, h : h + 1, :]
        local_inv = stat_ref[0, h : h + 1, :]
        fetched_inv = stat_ref[0, 2 + h : 3 + h, :]
        grad_gate = jnp.sum(gm * (fetched - local), axis=0, keepdims=True)
        gl_ref[0, h : h + 1, :] = grad_gate * gate * (1.0 - gate)
        grad_local = ((1.0 - gate) * gm).astype(BF16).astype(F32)
        grad_fetched = gate * gm
        do_ref[h] = jnp.zeros((PAIR, LEN), BF16)
        df_ref[h] = jnp.zeros((PAIR, LEN), BF16)
        do_ref[h, head_rows, :] = (grad_local * local_inv).astype(BF16)
        df_ref[h, head_rows, :] = (grad_fetched * fetched_inv).astype(BF16)
        dot_ref[h : h + 1, :] = jnp.sum(grad_local * local, axis=0, keepdims=True) * local_inv
        dot_ref[2 + h : 3 + h, :] = jnp.sum(grad_fetched * fetched, axis=0, keepdims=True) * fetched_inv
    for tb in range(NT):
        cols = slice(tb * TB, (tb + 1) * TB)
        near, far = key_chunks(tb)
        dq_parts = []
        for h in range(2):
            head_rows = slice(h * HD, (h + 1) * HD)
            dq = jnp.zeros((HD, TB), F32)
            for c in near + far:
                keys = slice(c * TB, (c + 1) * TB)
                bank = c >= MC + NT
                grad_out = (df_ref if bank else do_ref)[h, :, cols]
                row = 2 + h if bank else h
                gp = nn(v_ref[keys, :], grad_out) - dot_ref[row : row + 1, cols]
                ds = (e_ref[h, keys, cols].astype(F32) * gp).astype(BF16)
                ds_ref[h, keys, cols] = ds
                dq = dq + nn(kt_ref[head_rows, keys], ds)
            dq_parts.append(dq)
        dq_pair = jnp.concatenate(dq_parts, axis=0) * (1.0 / math.sqrt(HD))
        dq_ref[cols, :] = dq_pair.T.astype(BF16)
    for c in range(ROWS // TB):
        keys = slice(c * TB, (c + 1) * TB)
        bank = c >= MC + NT
        start = (c - MC) * TB if MC <= c < MC + NT else 0
        dk = jnp.zeros((TB, PAIR), F32)
        dv = jnp.zeros((TB, PAIR), F32)
        for h in range(2):
            grad_out = (df_ref if bank else do_ref)[h, :, start:]
            dv = dv + nt(e_ref[h, keys, start:], grad_out)
            dk = dk + nn(ds_ref[h, keys, start:], head_lanes(q_ref[start:, :], h))
        dk_ref[keys, :] = dk.astype(BF16)
        dv_ref[keys, :] = dv.astype(BF16)


def unattend_kernel(q, k, kt, v, e, gmt, local, fetched, stat, gate, first, count):
    spec_cols = lambda rows: pl.BlockSpec((rows, PAIR), lambda p: (0, p + first))
    spec_rows = lambda cols: pl.BlockSpec((PAIR, cols), lambda p: (p + first, 0))
    own_rows = lambda cols: pl.BlockSpec((PAIR, cols), lambda p: (p, 0))
    own_cols = lambda rows: pl.BlockSpec((rows, PAIR), lambda p: (0, p))
    return call(
        unattend_body,
        (count,),
        [
            spec_cols(LEN),
            spec_cols(ROWS),
            spec_rows(ROWS),
            spec_cols(ROWS),
            pl.BlockSpec((2, ROWS, LEN), lambda p: (p, 0, 0)),
            spec_rows(LEN),
            own_rows(LEN),
            own_rows(LEN),
            pl.BlockSpec((1, 8, LEN), lambda p: (p, 0, 0)),
            pl.BlockSpec((1, 2, LEN), lambda p: (p + first, 0, 0)),
        ],
        [
            own_cols(LEN),
            own_cols(ROWS),
            own_cols(ROWS),
            pl.BlockSpec((1, 2, LEN), lambda p: (p, 0, 0)),
        ],
        [
            sds((LEN, PAIR * count), BF16),
            sds((ROWS, PAIR * count), BF16),
            sds((ROWS, PAIR * count), BF16),
            sds((count, 2, LEN), F32),
        ],
        count * 4 * 4 * PAIR * ROWS * LEN,
        count * 14e6,
        "unattend",
        scratch=[
            pltpu.VMEM((2, ROWS, LEN), BF16),
            pltpu.VMEM((2, PAIR, LEN), BF16),
            pltpu.VMEM((2, PAIR, LEN), BF16),
            pltpu.VMEM((8, LEN), F32),
        ],
    )(q, k, kt, v, e, gmt, local, fetched, stat, gate)


def all_heads(gl_ref):
    return jnp.concatenate([gl_ref[p] for p in range(NPAIR)], axis=0).astype(BF16)


def proj_grads_body(xt_ref, dq_ref, dk_ref, dv_ref, gl_ref, g_ref, gate_ref):
    g_ref[0] = nn(xt_ref[:, MEM:CTX], dq_ref[...]).astype(BF16)
    g_ref[1] = nn(xt_ref[...], dk_ref[...]).astype(BF16)
    g_ref[2] = nn(xt_ref[...], dv_ref[...]).astype(BF16)

    @pl.when(pl.program_id(0) == 0)
    def _():
        gate_ref[...] = nt(all_heads(gl_ref), xt_ref[:, MEM:CTX])


def proj_grads_kernel(xt, dq, dk, dv, gl, place=None, chips=0, planes=0):
    steps = 2
    fast = place is not None
    wide = lambda rows: pl.BlockSpec((rows, D // steps), lambda i, *_: (0, i))
    in_specs = [whole((D, ROWS)), wide(LEN), wide(ROWS), wide(ROWS), whole((NPAIR, 2, LEN))]
    gate_spec, gate_shape = whole((H, D)), sds((H, D), F32)
    flops, nbytes = 2 * D * D * (LEN + 2 * ROWS), 10e6
    if not fast:
        return call(
            proj_grads_body,
            (steps,),
            in_specs,
            [pl.BlockSpec((3, D, D // steps), lambda i: (0, 0, i)), gate_spec],
            [sds((3, D, D), BF16), gate_shape],
            flops,
            nbytes,
            "proj_grads",
        )(xt, dq, dk, dv, gl)
    own_rows, own_cols, group = D // (2 * chips), D // planes, planes // steps

    def body(place_ref, xt_ref, dq_ref, dk_ref, dv_ref, gl_ref, keep_ref, send_ref, gate_ref, all_ref):
        proj_grads_body(xt_ref, dq_ref, dk_ref, dv_ref, gl_ref, all_ref, gate_ref)
        for b in range(group):
            col = b ^ (place_ref[2] % group)
            cols = slice(b * own_cols, (b + 1) * own_cols)
            for chip in range(chips):
                slot = place_ref[0] ^ chip
                for j in range(3):
                    keep_ref[slot, col, j] = all_ref[j, part(chip * 2 + place_ref[1], own_rows), cols]
                    send_ref[slot, col, j] = all_ref[j, part(chip * 2 + 1 - place_ref[1], own_rows), cols]

    out = pl.BlockSpec(
        (chips, group, 3, own_rows, own_cols), lambda i, place_ref: (0, i ^ (place_ref[2] // group), 0, 0, 0)
    )
    shape = sds((chips, planes, 3, own_rows, own_cols), BF16)
    return call(
        body,
        (steps,),
        in_specs,
        [out, out, gate_spec],
        [shape, shape, gate_shape],
        flops,
        nbytes,
        "proj_grads",
        scratch=[pltpu.VMEM((3, D, D // steps), BF16)],
        prefetch=1,
    )(place, xt, dq, dk, dv, gl)


def input_body(dq_ref, dk_ref, dv_ref, gl_ref, w_ref, tok_ref, mem_ref, vec_ref, gres_ref, gin_ref, gain_ref):
    i = pl.program_id(0)
    gn = nt(dk_ref[...], w_ref[1]) + nt(dv_ref[...], w_ref[2])

    @pl.when(i < MC)
    def _():
        wide = mem_ref[...].astype(F32)
        part = jnp.sum(gn * (wide * rms_factor(wide)), axis=0, keepdims=True)

        @pl.when(i == 0)
        def _():
            gain_ref[...] = part

        @pl.when(i > 0)
        def _():
            gain_ref[...] += part

    @pl.when(i >= MC)
    def _():
        wide = tok_ref[...].astype(F32)
        factor = rms_factor(wide)
        hat = wide * factor
        full = gn + nt(dq_ref[...], w_ref[0]) + tn(all_heads(gl_ref), vec_ref[2:10, :].astype(BF16))
        gain_ref[...] += jnp.sum(full * hat, axis=0, keepdims=True)
        scaled = full * vec_ref[0:1, :]
        gin_ref[...] = (
            gres_ref[...] + factor * (scaled - hat * jnp.mean(scaled * hat, axis=-1, keepdims=True))
        ).astype(BF16)


def input_kernel(dq, dk, dv, gl, w, tokens, memory, vectors, gres):
    tok = lambda i: jnp.clip(i - MC, 0, NT - 1)
    rows = pl.BlockSpec((TB, D), lambda i: (tok(i), 0))
    return call(
        input_body,
        (MC + NT,),
        [
            rows,
            pl.BlockSpec((TB, D), lambda i: (i, 0)),
            pl.BlockSpec((TB, D), lambda i: (i, 0)),
            pl.BlockSpec((NPAIR, 2, TB), lambda i: (0, 0, tok(i))),
            whole((3, D, D)),
            rows,
            pl.BlockSpec((TB, D), lambda i: (jnp.minimum(i, MC - 1), 0)),
            whole((2 + H, D)),
            rows,
        ],
        [rows, whole((1, D))],
        [sds((LEN, D), BF16), sds((1, D), F32)],
        2 * D * D * (LEN + 2 * CTX),
        10e6,
        "input",
    )(dq, dk, dv, gl, w, tokens, memory, vectors, gres)


def exchange(slots, axis):
    size = len(slots)
    return [slots[0]] + [
        lax.ppermute(slots[r], axis, [(i, i ^ r) for i in range(size)]) for r in range(1, size)
    ]


def gather_blocks(block, chips, planes):
    column = jnp.stack(exchange([block] * planes, "narrow"))
    plane = exchange([column] * chips, "chip")
    return plane + [exchange([b, b], "core")[1] for b in plane]


def added(parts):
    total = parts[0].astype(F32)
    for other in parts[1:]:
        total = total + other.astype(F32)
    return total


def scatter_core(keep, send):
    other = exchange([send, send], "core")[1]
    return [added([keep[r], other[r]]).astype(BF16) for r in range(keep.shape[0])]


def scatter_chips(slots):
    total = added(exchange(slots, "chip")).astype(BF16)
    return [total[r] for r in range(total.shape[0])]


PLANES = (("up",), ("q", "k"), ("v", "o"), ("down",))


def owned_kernel(parts_a, parts_b, devices):
    count = len(parts_a)

    def body(*refs):
        a_refs, b_refs, (ga_ref, gb_ref, sq_ref) = refs[:count], refs[count : 2 * count], refs[2 * count :]
        ga = added([r[...] for r in a_refs])
        gb = added([r[...] for r in b_refs])
        ga_ref[...] = ga
        gb_ref[...] = gb
        squares = jnp.sum(ga * ga) + jnp.sum(gb * gb)
        sq_ref[...] = jnp.full(sq_ref.shape, 1.0, F32) * squares

    shape_a, shape_b, shape_sq = parts_a[0].shape, parts_b[0].shape, (devices, 8, 128)
    return call(
        body,
        (1,),
        [whole(shape_a)] * count + [whole(shape_b)] * count,
        [whole(shape_a), whole(shape_b), whole(shape_sq)],
        [sds(shape_a, F32), sds(shape_b, F32), sds(shape_sq, F32)],
        1e6,
        2e6,
        "owned",
    )(*parts_a, *parts_b)


def moment_kernel(place, sq_all, vec_a, vec_b, vectors, vec_moment, ga, gb, attn_moment, up_moment, down_moment):
    own_rows, own_cols = attn_moment.shape[1:]
    own_ff = up_moment.shape[1]
    planes = len(PLANES)
    limit = clip_fraction * math.sqrt(PARAMS)

    def body(
        place_ref, sq_ref, va_ref, vb_ref, vec_ref, vm_ref, ga_ref, gb_ref, am_ref, um_ref, dm_ref,
        an_ref, un_ref, dn_ref, vn_ref, vmn_ref, norm_ref, *rest,
    ):
        slot_refs, all_ref = rest[:planes], rest[planes]
        grad_vec = va_ref[...] + vb_ref[...]
        total = jnp.sum(sq_ref[...], axis=0)[0:1, 0:1] + jnp.sum(grad_vec * grad_vec)
        norm = jnp.sqrt(total)
        norm_ref[...] = norm
        clip = limit / jnp.maximum(norm, limit)
        vec_mom = vector_decay * vm_ref[...] + clip * grad_vec
        vmn_ref[...] = vec_mom
        vn_ref[...] = vec_ref[...] - vector_rate * vec_mom
        all_ref[...] = jnp.zeros(all_ref.shape, BF16)
        for j in range(4):
            grad = ga_ref[j] if j < 3 else gb_ref[:, :own_cols]
            mom = muon_decay * am_ref[j] + clip * grad
            an_ref[j] = mom
            all_ref[1 + j // 2, :, (j % 2) * own_cols : (j % 2 + 1) * own_cols] = mom.astype(BF16)
        mom = muon_decay * um_ref[...] + clip * gb_ref[:, own_cols : own_cols + own_ff]
        un_ref[...] = mom
        all_ref[0] = mom.astype(BF16)
        mom = muon_decay * dm_ref[...].T + clip * gb_ref[:, own_cols + own_ff :]
        dn_ref[...] = mom.T
        all_ref[3] = mom.astype(BF16)
        for r in range(planes):
            slot_refs[r][...] = all_ref[place_ref[2] ^ r]

    slot = sds((own_rows, own_ff), BF16)
    operands = (sq_all, vec_a, vec_b, vectors, vec_moment, ga, gb, attn_moment, up_moment, down_moment)
    shapes = [
        sds(attn_moment.shape, F32),
        sds(up_moment.shape, F32),
        sds(down_moment.shape, F32),
        sds(vectors.shape, F32),
        sds(vectors.shape, F32),
        sds((1, 1), F32),
    ] + [slot] * planes
    return call(
        body,
        (1,),
        [SMEM] + [whole(x.shape) for x in operands],
        [whole(x.shape) for x in shapes],
        shapes,
        1e6,
        2e6,
        "moment",
        scratch=[pltpu.VMEM((planes, own_rows, own_ff), BF16)],
    )(place, *operands)


def orthogonal_kernel(place, blocks):
    chips = len(blocks) // 2
    planes, own_rows, own_ff = blocks[0].shape
    own_cols = D // planes

    def body(place_ref, *refs):
        block_refs, out_refs = refs[: len(blocks)], refs[len(blocks) : len(blocks) + planes]
        low_ref, x_ref, mix_ref, all_ref = refs[len(blocks) + planes :]
        pair = (place_ref[2] == 1) | (place_ref[2] == 2)
        own = part(place_ref[0] * 2 + place_ref[1], own_rows)

        def iterate(step, start, width, scale):
            cols = slice(start, start + width)
            gram = nt(low_ref[:, cols], low_ref[:, cols])
            if step == 0:
                eye = lax.broadcasted_iota(jnp.int32, (D, D), 0) == lax.broadcasted_iota(jnp.int32, (D, D), 1)
                scale = 1.0 / (jnp.sqrt(jnp.sum(jnp.where(eye, gram, 0.0))) + 1e-07)
                gram = gram * (scale * scale)
            low = gram.astype(BF16)
            mix = (coef_second * gram + coef_third * nn(low, low)).astype(BF16)
            mix_ref[:, :] = mix
            for c in range(start, start + width, D):
                some = slice(c, c + D)
                if step < NS_ITERS - 1:
                    old = low_ref[:, some].astype(F32) if step == 0 else x_ref[:, some]
                    new = coef_first * old + nn(mix_ref[...], low_ref[:, some])
                    if step == 0:
                        new = new * scale
                    x_ref[:, some] = new
                    low_ref[:, some] = new.astype(BF16)
                else:
                    x_ref[own, some] = coef_first * x_ref[own, some] + nn(mix_ref[own, :], low_ref[:, some])
            return scale

        @pl.when(pair)
        def _():
            for core, chip, plane, row, col in each_block(place_ref, chips, planes):
                for j in range(2):
                    low_ref[part(row, own_rows), part(col + j * planes, own_cols)] = block_refs[core * chips + chip][
                        plane, :, j * own_cols : (j + 1) * own_cols
                    ]
            scales = [None, None]
            for step in range(NS_ITERS):
                for j in range(2):
                    scales[j] = iterate(step, j * D, D, scales[j])
            for plane in range(planes):
                for j in range(2):
                    first = j * D + plane * own_cols
                    all_ref[plane, :, j * own_cols : (j + 1) * own_cols] = x_ref[own, first : first + own_cols].astype(
                        BF16
                    )

        @pl.when(jnp.logical_not(pair))
        def _():
            for core, chip, plane, row, col in each_block(place_ref, chips, planes):
                low_ref[part(row, own_rows), part(col, own_ff)] = block_refs[core * chips + chip][plane]
            scale = None
            for step in range(NS_ITERS):
                scale = iterate(step, 0, FF, scale)
            for plane in range(planes):
                all_ref[plane] = x_ref[own, plane * own_ff : (plane + 1) * own_ff].astype(BF16)

        for r in range(planes):
            out_refs[r][...] = all_ref[place_ref[2] ^ r]

    slot = sds((own_rows, own_ff), BF16)
    return call(
        body,
        (1,),
        [SMEM] + [whole(b.shape) for b in blocks],
        [whole(slot.shape)] * planes,
        [slot] * planes,
        12e9,
        3e6,
        "orthogonal",
        scratch=[
            pltpu.VMEM((D, FF), BF16),
            pltpu.VMEM((D, FF), F32),
            pltpu.VMEM((D, D), BF16),
            pltpu.VMEM((planes, own_rows, own_ff), BF16),
        ],
    )(place, *blocks)


def update_kernel(place, slots, attn_weights, up_weights, down_weights):
    planes = len(slots)
    own_rows, own_cols = attn_weights.shape[1:]
    shape_factor = math.sqrt(max(1.0, FF / D))

    def body(place_ref, *refs):
        slot_refs, (aw_ref, uw_ref, dw_ref, an_ref, un_ref, dn_ref, all_ref) = refs[:planes], refs[planes:]
        for r in range(planes):
            all_ref[place_ref[2] ^ r] = slot_refs[r][...]
        for j in range(4):
            ortho = all_ref[1 + j // 2, :, (j % 2) * own_cols : (j % 2 + 1) * own_cols].astype(F32)
            an_ref[j] = aw_ref[j] - muon_rate * ortho
        un_ref[...] = uw_ref[...] - muon_rate * all_ref[0].astype(F32)
        dn_ref[...] = dw_ref[...] - muon_rate * shape_factor * all_ref[3].astype(F32).T

    weights = (attn_weights, up_weights, down_weights)
    return call(
        body,
        (1,),
        [SMEM] + [whole(x.shape) for x in slots] + [whole(x.shape) for x in weights],
        [whole(x.shape) for x in weights],
        [sds(x.shape, F32) for x in weights],
        1e6,
        2e6,
        "update",
        scratch=[pltpu.VMEM((planes,) + slots[0].shape, BF16)],
    )(place, *slots, *weights)


def local_start(tokens, memory, bank, starts, near, cot, vectors):
    doc = jnp.cumsum(starts).astype(F32)
    x, xt, cot_t, gate = context_kernel(tokens, memory, bank, cot, vectors)
    doc_row = doc.reshape(1, LEN)
    bias_tok, bias_bank = mask_kernel(doc_row, doc.reshape(LEN, 1), near.T)
    return x, xt, cot_t, gate, doc_row, bias_tok, bias_bank


def plain_tail(sizes, grads, attn_weights, up_weights, down_weights, vectors, attn_moment, up_moment, down_moment, vec_moment):
    dp = ("chip", "core")
    grad_attn, grad_up, grad_down, grad_vectors = grads

    def owned(grad, narrow_dim, dp_dim):
        part_sum = lax.psum_scatter(grad.astype(BF16), "narrow", scatter_dimension=narrow_dim, tiled=True)
        return lax.psum_scatter(part_sum, dp, scatter_dimension=dp_dim, tiled=True).astype(F32)

    owned_attn, owned_up, owned_down = owned(grad_attn, 2, 1), owned(grad_up, 1, 0), owned(grad_down, 0, 1)
    own_squares = jnp.sum(owned_attn * owned_attn) + jnp.sum(owned_up * owned_up) + jnp.sum(owned_down * owned_down)
    vector_sum, square_sum = lax.psum((grad_vectors, own_squares), ("chip", "core", "narrow"))
    grad_norm = jnp.sqrt(square_sum + jnp.sum(vector_sum * vector_sum))
    clip_limit = clip_fraction * math.sqrt(PARAMS)
    clip_factor = clip_limit / jnp.maximum(grad_norm, clip_limit)
    attn_mom_new = muon_decay * attn_moment + clip_factor * owned_attn
    up_mom_new = muon_decay * up_moment + clip_factor * owned_up
    down_mom_new = muon_decay * down_moment + clip_factor * owned_down
    gather = lambda x, dim: lax.all_gather(x.astype(BF16), dp, axis=dim, tiled=True).astype(F32)
    ortho = (gather(attn_mom_new, 1), gather(up_mom_new, 0), gather(down_mom_new, 1))
    ortho_attn, ortho_up, ortho_down = ortho
    for iteration in range(NS_ITERS):
        gram_attn = jnp.einsum("imc,inc->imn", ortho_attn, ortho_attn, precision=highest)
        gram_up = lax.dot_general(ortho_up, ortho_up, (((1,), (1,)), ((), ())), precision=highest)
        gram_down = lax.dot_general(ortho_down, ortho_down, (((0,), (0,)), ((), ())), precision=highest)
        partial_grams = jnp.concatenate([gram_attn, gram_up[None], gram_down[None]], axis=0)
        gram_total = lax.psum(partial_grams.astype(BF16), "narrow").astype(F32)
        if iteration == 0:
            norm_scales = 1.0 / (jnp.sqrt(jnp.trace(gram_total, axis1=1, axis2=2)) + 1e-07)
            ortho_attn = ortho_attn * norm_scales[:4, None, None]
            ortho_up = ortho_up * norm_scales[4]
            ortho_down = ortho_down * norm_scales[5]
            gram_total = gram_total * (norm_scales * norm_scales)[:, None, None]
        once = jnp.einsum("imn,inc->imc", gram_total[:4], ortho_attn, precision=highest)
        twice = jnp.einsum("imn,inc->imc", gram_total[:4], once, precision=highest)
        ortho_attn = coef_first * ortho_attn + coef_second * once + coef_third * twice
        once = jnp.dot(gram_total[4], ortho_up, precision=highest)
        twice = jnp.dot(gram_total[4], once, precision=highest)
        ortho_up = coef_first * ortho_up + coef_second * once + coef_third * twice
        once = jnp.dot(ortho_down, gram_total[5], precision=highest)
        twice = jnp.dot(once, gram_total[5], precision=highest)
        ortho_down = coef_first * ortho_down + coef_second * once + coef_third * twice
    row_share = D // sizes["dp"]
    row_start = lax.axis_index(dp) * row_share
    final_attn = lax.dynamic_slice_in_dim(ortho_attn, row_start, row_share, 1)
    final_up = lax.dynamic_slice_in_dim(ortho_up, row_start, row_share, 0)
    final_down = lax.dynamic_slice_in_dim(ortho_down, row_start, row_share, 1)
    shape_factor = math.sqrt(max(1.0, FF / D))
    vector_mom_new = vector_decay * vec_moment + clip_factor * vector_sum
    return (
        attn_weights - muon_rate * final_attn,
        up_weights - muon_rate * final_up,
        down_weights - muon_rate * shape_factor * final_down,
        attn_mom_new,
        up_mom_new,
        down_mom_new,
        vectors - vector_rate * vector_mom_new,
        vector_mom_new,
        grad_norm,
    )


def per_device(
    sizes,
    tokens, memory, neighbour_bank, starts, neighbours, cotangent,
    attn_weights, up_weights, down_weights, vectors,
    attn_moment, up_moment, down_moment, vector_moment,
):
    chips, planes = sizes["dp"] // 2, sizes["narrow"]
    fast = planes == len(PLANES) and chips == 4
    memory = memory.reshape(MEM, D)
    bank = neighbour_bank.reshape(BANK, D)
    attn_low = attn_weights.astype(BF16)
    if fast:
        place = jnp.stack([lax.axis_index("chip"), lax.axis_index("core"), lax.axis_index("narrow")]).astype(jnp.int32)
        first = gather_blocks(attn_low[:3], chips, planes)
        rest = jnp.concatenate([attn_low[3], up_weights.astype(BF16), down_weights.T.astype(BF16)], axis=1)
        second = gather_blocks(rest, chips, planes)
    else:
        place = None
        full = lambda x, narrow_dim, dp_dim: lax.all_gather(
            lax.all_gather(x, ("chip", "core"), axis=dp_dim, tiled=True), "narrow", axis=narrow_dim, tiled=True
        )
        attn_full = full(attn_low, 2, 1)
        first = attn_full[:3]
        second = [attn_full[3], full(up_weights.astype(BF16), 1, 0), full(down_weights.astype(BF16), 0, 1).T]
    x, xt, cot_t, gate, doc_row, bias_tok, bias_bank = local_start(
        tokens, memory, bank, starts, neighbours, cotangent, vectors
    )
    w, q, k, v, kt, vt = project_kernel(x, first, place)
    e, local, fetched, stat, mixed, mixed_t = attend_kernel(q, k, vt, bias_tok, bias_bank, doc_row, gate, 0, NPAIR)
    out, act, gh, ffn_t, branch, gres, gmt, gain_ffn = feed_kernel(mixed, tokens, cotangent, vectors, second, place)
    if fast:
        keep_b, send_b = feed_grads_blocks(cot_t, act, ffn_t, gh, mixed_t, branch, place, chips, planes)
        slots_b = scatter_chips(scatter_core(keep_b, send_b))
    else:
        grad_down_t, grad_up, grad_o = feed_grads_kernel(cot_t, act, ffn_t, gh, mixed_t, branch)
    dq, dk, dv, gl = unattend_kernel(q, k, kt, v, e, gmt, local, fetched, stat, gate, 0, NPAIR)
    if fast:
        keep_a, send_a, grad_gate = proj_grads_kernel(xt, dq, dk, dv, gl, place, chips, planes)
    else:
        grad_qkv, grad_gate = proj_grads_kernel(xt, dq, dk, dv, gl)
    grad_in, gain_attn = input_kernel(dq, dk, dv, gl, w, tokens, memory, vectors, gres)
    grad_vectors = jnp.concatenate([gain_attn, gain_ffn, grad_gate], axis=0)
    if not fast:
        grads = (jnp.concatenate([grad_qkv, grad_o[None]], axis=0), grad_up, grad_down_t.T, grad_vectors)
        return (out, grad_in) + plain_tail(
            sizes, grads, attn_weights, up_weights, down_weights, vectors,
            attn_moment, up_moment, down_moment, vector_moment,
        )
    slots_a = scatter_core(keep_a, send_a)
    vec_chip = added(exchange([grad_vectors] * chips, "chip"))
    slots_a = scatter_chips(slots_a)
    vec_plane = added(exchange([vec_chip] * planes, "narrow"))
    vec_other = exchange([vec_plane, vec_plane], "core")[1]
    parts_a, parts_b = exchange(slots_a, "narrow"), exchange(slots_b, "narrow")
    ga, gb, squares = owned_kernel(parts_a, parts_b, chips * 2 * planes)
    sq_all = lax.all_to_all(squares, ("chip", "core", "narrow"), 0, 0)
    attn_mom, up_mom, down_mom, vec_new, vec_mom, norm, *slots = moment_kernel(
        place, sq_all, vec_plane, vec_other, vectors, vector_moment, ga, gb, attn_moment, up_moment, down_moment
    )
    columns = jnp.stack(exchange(slots, "narrow"))
    plane_blocks = exchange([columns] * chips, "chip")
    plane_blocks = plane_blocks + [exchange([b, b], "core")[1] for b in plane_blocks]
    final = exchange(orthogonal_kernel(place, plane_blocks), "narrow")
    attn_new, up_new, down_new = update_kernel(place, final, attn_weights, up_weights, down_weights)
    return (
        out, grad_in, attn_new, up_new, down_new, attn_mom, up_mom, down_mom, vec_new, vec_mom, norm.reshape(()),
    )


def solution(mesh):
    sizes = dict(mesh.shape)
    split = Mesh(
        mesh.devices.reshape(sizes["dp"] // 2, 2, sizes["narrow"]), ("chip", "core", "narrow")
    )
    dp = ("chip", "core")
    rows = ("chip", "core", "narrow")
    weights = (P(None, dp, "narrow"), P(dp, "narrow"), P("narrow", dp))
    return jax.shard_map(
        lambda *operands: per_device(sizes, *operands),
        mesh=split,
        in_specs=(P(rows, None), P(rows, None, None), P(rows, None, None), P(rows), P(rows, None), P(rows, None))
        + weights + (P(),) + weights + (P(),),
        out_specs=(P(rows, None), P(rows, None)) + weights + weights + (P(), P(), P()),
        check_vma=False,
    )
```

```python
import math

import jax
import jax.numpy as jnp
from jax import lax
from jax.experimental import pallas as pl
from jax.experimental.pallas import tpu as pltpu
from jax.sharding import Mesh, PartitionSpec as P

D = 512
H = 8
FF = 2048
MEM = 512
BANK = 512
KNB = 4
LEN = 1024
CTX = MEM + LEN
ROWS = CTX + BANK
HD = D // H
TB = 256
NT = LEN // TB
MC = MEM // TB
BC = BANK // TB
PAIR = 2 * HD
NPAIR = D // PAIR
F32 = jnp.float32
BF16 = jnp.bfloat16
NS_ITERS = 5
PARAMS = 3150848
epsilon = 1e-06
masked_score = -1e30
coef_first = 3.4445
coef_second = -4.775
coef_third = 2.0315
clip_fraction = 0.05
muon_rate = 0.5
muon_decay = 0.5
vector_rate = 0.5
vector_decay = 0.9
highest = lax.Precision.HIGHEST
VMEM_LIMIT = 60 * 1024 * 1024
SMALL = 16 * 1024 * 1024


def nn(a, b):
    return lax.dot_general(a, b, (((1,), (0,)), ((), ())), preferred_element_type=F32)


def nt(a, b):
    return lax.dot_general(a, b, (((1,), (1,)), ((), ())), preferred_element_type=F32)


def tn(a, b):
    return lax.dot_general(a, b, (((0,), (0,)), ((), ())), preferred_element_type=F32)


def rms_factor(values):
    return lax.rsqrt(jnp.mean(values * values, axis=-1, keepdims=True) + epsilon)


def whole(shape):
    return pl.BlockSpec(shape, lambda *_: (0,) * len(shape))


def call(
    body, grid, in_specs, out_specs, out_shape, flops, nbytes, name, scratch=(), trans=0, prefetch=0, after=(), alias=(),
    vmem=VMEM_LIMIT,
):
    extra, given = len(after) + len(alias), prefetch + len(in_specs)

    def with_extra(*refs):
        body(*refs[:given], *refs[given + extra :])

    made = pl.pallas_call(
        with_extra,
        grid_spec=pltpu.PrefetchScalarGridSpec(
            num_scalar_prefetch=prefetch,
            grid=grid,
            in_specs=list(in_specs) + [pl.BlockSpec(memory_space=pl.ANY)] * extra,
            out_specs=out_specs,
            scratch_shapes=list(scratch),
        ),
        out_shape=out_shape,
        input_output_aliases={given + len(after) + j: j for j in range(len(alias))},
        name=name,
        cost_estimate=pl.CostEstimate(flops=int(flops), bytes_accessed=int(nbytes), transcendentals=int(trans)),
        compiler_params=pltpu.CompilerParams(
            vmem_limit_bytes=vmem, dimension_semantics=("arbitrary",) * len(grid)
        ),
    )
    return lambda *operands: made(*operands, *after, *alias)


SMEM = pl.BlockSpec(memory_space=pltpu.SMEM)


def sds(shape, dtype):
    return jax.ShapeDtypeStruct(shape, dtype)


def context_body(tok_ref, mem_ref, bank_ref, cot_ref, vec_ref, x_ref, xt_ref, cott_ref, gate_ref):
    i = pl.program_id(0)
    gain = vec_ref[0:1, :]

    def put(rows):
        x_ref[...] = rows
        xt_ref[...] = rows.T

    def norm(values):
        wide = values.astype(F32)
        return (wide * rms_factor(wide) * gain).astype(BF16)

    @pl.when(i < MC)
    def _():
        put(norm(mem_ref[...]))

    @pl.when((i >= MC) & (i < MC + NT))
    def _():
        rows = norm(tok_ref[...])
        put(rows)
        logits = nt(vec_ref[2:10, :].astype(BF16), rows)
        gate = jax.nn.sigmoid(logits)
        for p in range(NPAIR):
            gate_ref[p] = gate[2 * p : 2 * p + 2, :]
        cott_ref[...] = cot_ref[...].T

    @pl.when(i >= MC + NT)
    def _():
        put(bank_ref[...])


def context_kernel(tokens, memory, bank, cot, vectors, after=()):
    steps = MC + NT + BC
    clip_tok = lambda i: jnp.clip(i - MC, 0, NT - 1)
    return call(
        context_body,
        (steps,),
        [
            pl.BlockSpec((TB, D), lambda i: (clip_tok(i), 0)),
            pl.BlockSpec((TB, D), lambda i: (jnp.minimum(i, MC - 1), 0)),
            pl.BlockSpec((TB, D), lambda i: (jnp.clip(i - MC - NT, 0, BC - 1), 0)),
            pl.BlockSpec((TB, D), lambda i: (clip_tok(i), 0)),
            whole((2 + H, D)),
        ],
        [
            pl.BlockSpec((TB, D), lambda i: (i, 0)),
            pl.BlockSpec((D, TB), lambda i: (0, i)),
            pl.BlockSpec((D, TB), lambda i: (0, clip_tok(i))),
            pl.BlockSpec((NPAIR, 2, TB), lambda i: (0, 0, clip_tok(i))),
        ],
        [sds((ROWS, D), BF16), sds((D, ROWS), BF16), sds((D, LEN), BF16), sds((NPAIR, 2, LEN), F32)],
        8e9,
        8e6,
        "context",
        after=after,
        vmem=SMALL,
    )(tokens, memory, bank, cot, vectors)


def mask_body(doc_row_ref, doc_col_ref, near_ref, tok_ref, bank_ref):
    i = pl.program_id(0)
    doc_row = doc_row_ref[...]

    @pl.when(i < NT)
    def _():
        keys = lax.broadcasted_iota(jnp.int32, (TB, LEN), 0) + i * TB
        rows = lax.broadcasted_iota(jnp.int32, (TB, LEN), 1)
        seen = (keys <= rows) & (doc_col_ref[...] == doc_row)
        tok_ref[...] = jnp.where(seen, 0.0, masked_score)

    @pl.when(i >= NT)
    def _():
        keys = lax.broadcasted_iota(jnp.int32, (TB, LEN), 0) + (i - NT) * TB
        count = jnp.zeros((TB, LEN), F32)
        for j in range(KNB):
            count = count + jnp.where(near_ref[j : j + 1, :] == keys, 1.0, 0.0)
        bias = jnp.where(count > 0.5, 0.0, masked_score)
        for j in range(2, KNB + 1):
            bias = jnp.where(count > j - 0.5, math.log(j), bias)
        bank_ref[...] = bias


def mask_kernel(doc_row, doc_col, near_t, after=()):
    return call(
        mask_body,
        (NT + BC,),
        [
            whole((1, LEN)),
            pl.BlockSpec((TB, 1), lambda i: (jnp.minimum(i, NT - 1), 0)),
            whole((KNB, LEN)),
        ],
        [
            pl.BlockSpec((TB, LEN), lambda i: (jnp.minimum(i, NT - 1), 0)),
            pl.BlockSpec((TB, LEN), lambda i: (jnp.clip(i - NT, 0, BC - 1), 0)),
        ],
        [sds((LEN, LEN), F32), sds((BANK, LEN), F32)],
        6e9,
        7e6,
        "masks",
        after=after,
        vmem=SMALL,
    )(doc_row, doc_col, near_t)


def each_block(place_ref, chips, planes):
    for core in range(2):
        for chip in range(chips):
            row = ((place_ref[0] ^ chip) * 2 + (place_ref[1] ^ core))
            for plane in range(planes):
                yield core, chip, plane, row, place_ref[2] ^ plane


def part(index, size):
    return pl.ds(pl.multiple_of(index * size, size), size)


def project_rows(i, x_ref, w_ref, q_ref, k_ref, v_ref, kt_ref, vt_ref):
    rows = x_ref[...]
    keys = nn(rows, w_ref[1]).astype(BF16)
    values = nn(rows, w_ref[2]).astype(BF16)
    k_ref[...] = keys
    v_ref[...] = values
    kt_ref[...] = keys.T
    vt_ref[...] = values.T

    @pl.when((i >= MC) & (i < MC + NT))
    def _():
        q_ref[...] = (nn(rows, w_ref[0]).astype(BF16).astype(F32) * (1.0 / math.sqrt(HD))).astype(BF16)


def project_kernel(x, w, place=None, after=()):
    steps = MC + NT + BC
    fast = place is not None
    if fast:
        chips, planes = len(w) // 2, w[0].shape[0]
        own_rows, own_cols = w[0].shape[1] // 3, w[0].shape[2]

    def body(*refs):
        i = pl.program_id(0)
        if not fast:
            project_rows(i, *refs)
            return
        place_ref, x_ref, *rest = refs
        blocks, (w_ref, *outs) = rest[: len(w)], rest[len(w) :]

        @pl.when(i == 0)
        def _():
            for core, chip, plane, row, col in each_block(place_ref, chips, planes):
                for j in range(3):
                    w_ref[j, part(row, own_rows), part(col, own_cols)] = blocks[core * chips + chip][
                        plane, j * own_rows : (j + 1) * own_rows, :
                    ]

        project_rows(i, x_ref, w_ref, *outs)

    out_specs = [
        pl.BlockSpec((TB, D), lambda i: (jnp.clip(i - MC, 0, NT - 1), 0)),
        pl.BlockSpec((TB, D), lambda i: (i, 0)),
        pl.BlockSpec((TB, D), lambda i: (i, 0)),
        pl.BlockSpec((D, TB), lambda i: (0, i)),
        pl.BlockSpec((D, TB), lambda i: (0, i)),
    ]
    out_shape = [
        sds((LEN, D), BF16),
        sds((ROWS, D), BF16),
        sds((ROWS, D), BF16),
        sds((D, ROWS), BF16),
        sds((D, ROWS), BF16),
    ]
    in_specs = [pl.BlockSpec((TB, D), lambda i: (i, 0))]
    if fast:
        in_specs = [SMEM] + in_specs + [whole(b.shape) for b in w]
        out_specs = [whole((3, D, D))] + out_specs
        out_shape = [sds((3, D, D), BF16)] + out_shape
        operands = (place, x, *w)
    else:
        in_specs = in_specs + [whole((3, D, D))]
        operands = (x, w)
    result = call(
        body, (steps,), in_specs, out_specs, out_shape, 11e9, 14e6, "project", after=after, vmem=24 * 1024 * 1024
    )(*operands)
    return result if fast else [w, *result]


def head_lanes(values, h):
    lanes = lax.broadcasted_iota(jnp.int32, values.shape, 1)
    keep = (lanes < HD) if h == 0 else (lanes >= HD)
    return jnp.where(keep, values, jnp.zeros_like(values))


def key_chunks(tb):
    return list(range(MC + tb + 1)), list(range(MC + NT, MC + NT + BC))


def attend_body(
    q_ref, k_ref, vt_ref, tok_ref, bank_ref, doc_ref, gate_ref,
    e_ref, local_ref, fetched_ref, stat_ref, mixed_ref, mixedt_ref, s_ref,
):
    p = pl.program_id(0)
    for tb in range(NT):
        cols = slice(tb * TB, (tb + 1) * TB)
        q_rows = q_ref[cols, :]
        mem_bias = jnp.where(doc_ref[:, cols] == 0.0, 0.0, masked_score)
        mixed_parts = []
        for h in range(2):
            q_head = head_lanes(q_rows, h)
            head_rows = slice(h * HD, (h + 1) * HD)

            def soft(chunks, slot):
                peak = jnp.full((8, TB), -3e38, F32)
                for c in chunks:
                    keys = slice(c * TB, (c + 1) * TB)
                    s = nt(k_ref[keys, :], q_head)
                    if c < MC:
                        s = s + mem_bias
                    elif c < MC + NT:
                        s = s + tok_ref[(c - MC) * TB : (c - MC + 1) * TB, cols]
                    else:
                        s = s + bank_ref[(c - MC - NT) * TB : (c - MC - NT + 1) * TB, cols]
                    s_ref[slot, keys, :] = s
                    peak = jnp.maximum(peak, jnp.max(s.reshape(TB // 8, 8, TB), axis=0))
                top = jnp.max(peak, axis=0, keepdims=True)
                total = jnp.zeros((8, TB), F32)
                result = jnp.zeros((HD, TB), F32)
                for c in chunks:
                    keys = slice(c * TB, (c + 1) * TB)
                    e = jnp.exp(s_ref[slot, keys, :] - top)
                    total = total + jnp.sum(e.reshape(TB // 8, 8, TB), axis=0)
                    low = e.astype(BF16)
                    e_ref[h, keys, cols] = low
                    result = result + nn(vt_ref[head_rows, keys], low)
                inverse = 1.0 / jnp.sum(total, axis=0, keepdims=True)
                return result * inverse, inverse

            near, far = key_chunks(tb)
            local, local_inv = soft(near, h)
            fetched, fetched_inv = soft(far, h)
            local_ref[head_rows, cols] = local
            fetched_ref[head_rows, cols] = fetched
            stat_ref[0, h : h + 1, cols] = local_inv
            stat_ref[0, 2 + h : 3 + h, cols] = fetched_inv
            gate = gate_ref[0, h : h + 1, cols]
            mixed_parts.append((1.0 - gate) * local + gate * fetched)
        mixed = jnp.concatenate(mixed_parts, axis=0)
        mixedt_ref[:, cols] = mixed.astype(BF16)
        mixed_ref[cols, :] = mixed.T.astype(BF16)


def attend_kernel(q, k, vt, bias_tok, bias_bank, doc_row, gate, first, count):
    spec_cols = lambda rows: pl.BlockSpec((rows, PAIR), lambda p: (0, p + first))
    return call(
        attend_body,
        (count,),
        [
            spec_cols(LEN),
            spec_cols(ROWS),
            pl.BlockSpec((PAIR, ROWS), lambda p: (p + first, 0)),
            whole((LEN, LEN)),
            whole((BANK, LEN)),
            whole((1, LEN)),
            pl.BlockSpec((1, 2, LEN), lambda p: (p + first, 0, 0)),
        ],
        [
            pl.BlockSpec((2, ROWS, LEN), lambda p: (p, 0, 0)),
            pl.BlockSpec((PAIR, LEN), lambda p: (p, 0)),
            pl.BlockSpec((PAIR, LEN), lambda p: (p, 0)),
            pl.BlockSpec((1, 8, LEN), lambda p: (p, 0, 0)),
            pl.BlockSpec((LEN, PAIR), lambda p: (0, p)),
            pl.BlockSpec((PAIR, LEN), lambda p: (p, 0)),
        ],
        [
            sds((2 * count, ROWS, LEN), BF16),
            sds((PAIR * count, LEN), F32),
            sds((PAIR * count, LEN), F32),
            sds((count, 8, LEN), F32),
            sds((LEN, PAIR * count), BF16),
            sds((PAIR * count, LEN), BF16),
        ],
        count * 9e9,
        count * 14e6 + 6e6,
        "attend",
        scratch=[pltpu.VMEM((2, ROWS, TB), F32)],
        trans=count * 2 * ROWS * LEN,
        vmem=40 * 1024 * 1024,
    )(q, k, vt, bias_tok, bias_bank, doc_row, gate)


def gelu_parts(x):
    square = jnp.exp(x * x * -0.5)
    z = jnp.abs(x) * 0.7071067811865476
    t = 1.0 / (1.0 + 0.3275911 * z)
    poly = t * (
        0.254829592 + t * (-0.284496736 + t * (1.421413741 + t * (-1.453152027 + t * 1.061405429)))
    )
    tail = 0.5 * poly * square
    cdf = jnp.where(x >= 0.0, 1.0 - tail, tail)
    return cdf, square * 0.3989422804014327


FC = 512


def feed_body(
    mixed_ref, tok_ref, cot_ref, wo_ref, up_ref, dt_ref, vec_ref,
    out_ref, act_ref, gh_ref, ffnt_ref, branch_ref, gres_ref, gmt_ref, gain_ref,
):
    i = pl.program_id(0)
    residual = tok_ref[...].astype(F32) + nn(mixed_ref[...], wo_ref[...])
    factor = rms_factor(residual)
    hat = residual * factor
    gain = vec_ref[1:2, :]
    ffn = (hat * gain).astype(BF16)
    ffnt_ref[...] = ffn.T
    cot = cot_ref[...]
    out = residual
    grad_ffn = jnp.zeros(residual.shape, F32)
    for c in range(FF // FC):
        cols = slice(c * FC, (c + 1) * FC)
        hidden = nn(ffn, up_ref[:, cols])
        cdf, pdf = gelu_parts(hidden)
        act = (hidden * cdf).astype(BF16)
        act_ref[:, cols] = act
        grad_act = nn(cot, dt_ref[:, cols])
        gh = (grad_act * (cdf + hidden * pdf)).astype(BF16)
        gh_ref[:, cols] = gh
        out = out + nt(act, dt_ref[:, cols])
        grad_ffn = grad_ffn + nt(gh, up_ref[:, cols])
    out_ref[...] = out.astype(BF16)
    part = jnp.sum(grad_ffn * hat, axis=0, keepdims=True)

    @pl.when(i == 0)
    def _():
        gain_ref[...] = part

    @pl.when(i > 0)
    def _():
        gain_ref[...] += part

    scaled = grad_ffn * gain
    grad_res = cot.astype(F32) + factor * (scaled - hat * jnp.mean(scaled * hat, axis=-1, keepdims=True))
    gres_ref[...] = grad_res
    branch = grad_res.astype(BF16)
    branch_ref[...] = branch
    gmt_ref[...] = nt(wo_ref[...], branch)


def feed_kernel(mixed, tokens, cot, vectors, w, place=None):
    rows = lambda width: pl.BlockSpec((TB, width), lambda i: (i, 0))
    cols = lambda height: pl.BlockSpec((height, TB), lambda i: (0, i))
    fast = place is not None
    if fast:
        chips, planes = len(w) // 2, w[0].shape[0]
        own_rows, own_o, own_ff = w[0].shape[1], D // planes, FF // planes

    def body(*refs):
        if not fast:
            mixed_ref, tok_ref, cot_ref, vec_ref, wo_ref, up_ref, dt_ref, *outs = refs
            feed_body(mixed_ref, tok_ref, cot_ref, wo_ref, up_ref, dt_ref, vec_ref, *outs)
            return
        place_ref, mixed_ref, tok_ref, cot_ref, vec_ref, *rest = refs
        blocks, outs = rest[: len(w)], rest[len(w) : -3]
        wo_ref, up_ref, dt_ref = rest[-3:]

        @pl.when(pl.program_id(0) == 0)
        def _():
            for core, chip, plane, row, col in each_block(place_ref, chips, planes):
                block = blocks[core * chips + chip]
                here = part(row, own_rows)
                wo_ref[here, part(col, own_o)] = block[plane, :, :own_o]
                up_ref[here, part(col, own_ff)] = block[plane, :, own_o : own_o + own_ff]
                dt_ref[here, part(col, own_ff)] = block[plane, :, own_o + own_ff : own_o + 2 * own_ff]

        feed_body(mixed_ref, tok_ref, cot_ref, wo_ref, up_ref, dt_ref, vec_ref, *outs)

    in_specs = [rows(D), rows(D), rows(D), whole((2 + H, D))] + [whole(b.shape) for b in w]
    scratch = []
    operands = (mixed, tokens, cot, vectors, *w)
    if fast:
        in_specs = [SMEM] + in_specs
        operands = (place, *operands)
        scratch = [pltpu.VMEM((D, D), BF16), pltpu.VMEM((D, FF), BF16), pltpu.VMEM((D, FF), BF16)]
    return call(
        body,
        (NT,),
        in_specs,
        [rows(D), rows(FF), rows(FF), cols(D), rows(D), rows(D), cols(D), whole((1, D))],
        [
            sds((LEN, D), BF16),
            sds((LEN, FF), BF16),
            sds((LEN, FF), BF16),
            sds((D, LEN), BF16),
            sds((LEN, D), BF16),
            sds((LEN, D), F32),
            sds((D, LEN), F32),
            sds((1, D), F32),
        ],
        23e9,
        22e6,
        "feed",
        scratch=scratch,
        trans=LEN * FF * 2,
        vmem=36 * 1024 * 1024,
    )(*operands)


def feed_grads_body(cott_ref, act_ref, ffnt_ref, gh_ref, mixedt_ref, branch_ref, gd_ref, gu_ref, go_ref):
    gd_ref[...] = nn(cott_ref[...], act_ref[...]).astype(BF16)
    gu_ref[...] = nn(ffnt_ref[...], gh_ref[...]).astype(BF16)
    go_ref[...] = nn(mixedt_ref[...], branch_ref[...]).astype(BF16)


def feed_grads_kernel(cot_t, act, ffn_t, gh, mixed_t, branch):
    steps = 4
    wide = lambda width: pl.BlockSpec((LEN, width // steps), lambda i: (0, i))
    out = lambda width: pl.BlockSpec((D, width // steps), lambda i: (0, i))
    return call(
        feed_grads_body,
        (steps,),
        [whole((D, LEN)), wide(FF), whole((D, LEN)), wide(FF), whole((D, LEN)), wide(D)],
        [out(FF), out(FF), out(D)],
        [sds((D, FF), BF16), sds((D, FF), BF16), sds((D, D), BF16)],
        11e9,
        17e6,
        "feed_grads",
    )(cot_t, act, ffn_t, gh, mixed_t, branch)


def feed_grads_blocks(cot_t, act, ffn_t, gh, mixed_t, branch, place, chips, planes):
    own_rows, own_o, own_ff = D // (2 * chips), D // planes, FF // planes
    width = own_o + 2 * own_ff

    def body(place_ref, cott_ref, act_ref, ffnt_ref, gh_ref, mixedt_ref, branch_ref, keep_ref, send_ref, all_ref):
        all_ref[:, :own_o] = nn(mixedt_ref[...], branch_ref[...]).astype(BF16)
        all_ref[:, own_o : own_o + own_ff] = nn(ffnt_ref[...], gh_ref[...]).astype(BF16)
        all_ref[:, own_o + own_ff :] = nn(cott_ref[...], act_ref[...]).astype(BF16)
        for chip in range(chips):
            slot = place_ref[0] ^ chip
            keep_ref[slot, 0] = all_ref[part(chip * 2 + place_ref[1], own_rows), :]
            send_ref[slot, 0] = all_ref[part(chip * 2 + 1 - place_ref[1], own_rows), :]

    wide = lambda cols: pl.BlockSpec((LEN, cols // planes), lambda i, _: (0, i))
    out = pl.BlockSpec((chips, 1, own_rows, width), lambda i, place_ref: (0, i ^ place_ref[2], 0, 0))
    shape = sds((chips, planes, own_rows, width), BF16)
    return call(
        body,
        (planes,),
        [whole((D, LEN)), wide(FF), whole((D, LEN)), wide(FF), whole((D, LEN)), wide(D)],
        [out, out],
        [shape, shape],
        11e9,
        17e6,
        "feed_grads",
        scratch=[pltpu.VMEM((D, width), BF16)],
        prefetch=1,
        vmem=24 * 1024 * 1024,
    )(place, cot_t, act, ffn_t, gh, mixed_t, branch)


def unattend_body(
    q_ref, k_ref, kt_ref, v_ref, e_ref, gmt_ref, local_ref, fetched_ref, stat_ref, gate_ref,
    dq_ref, dk_ref, dv_ref, gl_ref, ds_ref, do_ref, df_ref, dot_ref,
):
    heads = []
    for h in range(2):
        head_rows = slice(h * HD, (h + 1) * HD)
        gm = gmt_ref[head_rows, :]
        local = local_ref[head_rows, :]
        fetched = fetched_ref[head_rows, :]
        gate = gate_ref[0, h : h + 1, :]
        local_inv = stat_ref[0, h : h + 1, :]
        fetched_inv = stat_ref[0, 2 + h : 3 + h, :]
        grad_gate = jnp.sum(gm * (fetched - local), axis=0, keepdims=True)
        gl_ref[0, h : h + 1, :] = grad_gate * gate * (1.0 - gate)
        grad_local = ((1.0 - gate) * gm).astype(BF16).astype(F32)
        grad_fetched = gate * gm
        do_ref[h] = jnp.zeros((PAIR, LEN), BF16)
        df_ref[h] = jnp.zeros((PAIR, LEN), BF16)
        do_ref[h, head_rows, :] = (grad_local * local_inv).astype(BF16)
        df_ref[h, head_rows, :] = (grad_fetched * fetched_inv).astype(BF16)
        dot_ref[h : h + 1, :] = jnp.sum(grad_local * local, axis=0, keepdims=True) * local_inv
        dot_ref[2 + h : 3 + h, :] = jnp.sum(grad_fetched * fetched, axis=0, keepdims=True) * fetched_inv
    for tb in range(NT):
        cols = slice(tb * TB, (tb + 1) * TB)
        near, far = key_chunks(tb)
        dq_parts = []
        for h in range(2):
            head_rows = slice(h * HD, (h + 1) * HD)
            dq = jnp.zeros((HD, TB), F32)
            for c in near + far:
                keys = slice(c * TB, (c + 1) * TB)
                bank = c >= MC + NT
                grad_out = (df_ref if bank else do_ref)[h, :, cols]
                row = 2 + h if bank else h
                gp = nn(v_ref[keys, :], grad_out) - dot_ref[row : row + 1, cols]
                ds = (e_ref[h, keys, cols].astype(F32) * gp).astype(BF16)
                ds_ref[h, keys, cols] = ds
                dq = dq + nn(kt_ref[head_rows, keys], ds)
            dq_parts.append(dq)
        dq_pair = jnp.concatenate(dq_parts, axis=0) * (1.0 / math.sqrt(HD))
        dq_ref[cols, :] = dq_pair.T.astype(BF16)
    for c in range(ROWS // TB):
        keys = slice(c * TB, (c + 1) * TB)
        bank = c >= MC + NT
        start = (c - MC) * TB if MC <= c < MC + NT else 0
        dk = jnp.zeros((TB, PAIR), F32)
        dv = jnp.zeros((TB, PAIR), F32)
        for h in range(2):
            grad_out = (df_ref if bank else do_ref)[h, :, start:]
            dv = dv + nt(e_ref[h, keys, start:], grad_out)
            dk = dk + nn(ds_ref[h, keys, start:], head_lanes(q_ref[start:, :], h))
        dk_ref[keys, :] = dk.astype(BF16)
        dv_ref[keys, :] = dv.astype(BF16)


def unattend_kernel(q, k, kt, v, e, gmt, local, fetched, stat, gate, first, count, after=(), alias=()):
    spec_cols = lambda rows: pl.BlockSpec((rows, PAIR), lambda p: (0, p + first))
    spec_rows = lambda cols: pl.BlockSpec((PAIR, cols), lambda p: (p + first, 0))
    return call(
        unattend_body,
        (count,),
        [
            spec_cols(LEN),
            spec_cols(ROWS),
            spec_rows(ROWS),
            spec_cols(ROWS),
            pl.BlockSpec((2, ROWS, LEN), lambda p: (p + first, 0, 0)),
            spec_rows(LEN),
            spec_rows(LEN),
            spec_rows(LEN),
            pl.BlockSpec((1, 8, LEN), lambda p: (p + first, 0, 0)),
            pl.BlockSpec((1, 2, LEN), lambda p: (p + first, 0, 0)),
        ],
        [
            spec_cols(LEN),
            spec_cols(ROWS),
            spec_cols(ROWS),
            pl.BlockSpec((1, 2, LEN), lambda p: (p + first, 0, 0)),
        ],
        [
            sds((LEN, D), BF16),
            sds((ROWS, D), BF16),
            sds((ROWS, D), BF16),
            sds((NPAIR, 2, LEN), F32),
        ],
        count * 10e9,
        count * 14e6,
        "unattend",
        scratch=[
            pltpu.VMEM((2, ROWS, LEN), BF16),
            pltpu.VMEM((2, PAIR, LEN), BF16),
            pltpu.VMEM((2, PAIR, LEN), BF16),
            pltpu.VMEM((8, LEN), F32),
        ],
        after=after,
        alias=alias,
        vmem=44 * 1024 * 1024,
    )(q, k, kt, v, e, gmt, local, fetched, stat, gate)


def all_heads(gl_ref):
    return jnp.concatenate([gl_ref[p] for p in range(NPAIR)], axis=0).astype(BF16)


def proj_grads_body(xt_ref, dq_ref, dk_ref, dv_ref, gl_ref, g_ref, gate_ref):
    g_ref[0] = nn(xt_ref[:, MEM:CTX], dq_ref[...]).astype(BF16)
    g_ref[1] = nn(xt_ref[...], dk_ref[...]).astype(BF16)
    g_ref[2] = nn(xt_ref[...], dv_ref[...]).astype(BF16)

    @pl.when(pl.program_id(0) == 0)
    def _():
        gate_ref[...] = nt(all_heads(gl_ref), xt_ref[:, MEM:CTX])


def proj_grads_kernel(xt, dq, dk, dv, gl, place=None, chips=0, planes=0, after=()):
    steps = 2
    fast = place is not None
    wide = lambda rows: pl.BlockSpec((rows, D // steps), lambda i, *_: (0, i))
    in_specs = [whole((D, ROWS)), wide(LEN), wide(ROWS), wide(ROWS), whole((NPAIR, 2, LEN))]
    gate_spec, gate_shape = whole((H, D)), sds((H, D), F32)
    flops, nbytes = 8e9, 10e6
    if not fast:
        return call(
            proj_grads_body,
            (steps,),
            in_specs,
            [pl.BlockSpec((3, D, D // steps), lambda i: (0, 0, i)), gate_spec],
            [sds((3, D, D), BF16), gate_shape],
            flops,
            nbytes,
            "proj_grads",
        )(xt, dq, dk, dv, gl)
    own_rows, own_cols, group = D // (2 * chips), D // planes, planes // steps

    def body(place_ref, xt_ref, dq_ref, dk_ref, dv_ref, gl_ref, keep_ref, send_ref, gate_ref, all_ref):
        proj_grads_body(xt_ref, dq_ref, dk_ref, dv_ref, gl_ref, all_ref, gate_ref)
        for b in range(group):
            col = b ^ (place_ref[2] % group)
            cols = slice(b * own_cols, (b + 1) * own_cols)
            for chip in range(chips):
                slot = place_ref[0] ^ chip
                for j in range(3):
                    here = slice(j * own_rows, (j + 1) * own_rows)
                    keep_ref[slot, col, here, :] = all_ref[j, part(chip * 2 + place_ref[1], own_rows), cols]
                    send_ref[slot, col, here, :] = all_ref[j, part(chip * 2 + 1 - place_ref[1], own_rows), cols]

    out = pl.BlockSpec(
        (chips, group, 3 * own_rows, own_cols), lambda i, place_ref: (0, i ^ (place_ref[2] // group), 0, 0)
    )
    shape = sds((chips, planes, 3 * own_rows, own_cols), BF16)
    return call(
        body,
        (steps,),
        in_specs,
        [out, out, gate_spec],
        [shape, shape, gate_shape],
        flops,
        nbytes,
        "proj_grads",
        scratch=[pltpu.VMEM((3, D, D // steps), BF16)],
        prefetch=1,
        after=after,
        vmem=24 * 1024 * 1024,
    )(place, xt, dq, dk, dv, gl)


def input_body(dq_ref, dk_ref, dv_ref, gl_ref, w_ref, tok_ref, mem_ref, vec_ref, gres_ref, gin_ref, gain_ref):
    i = pl.program_id(0)
    gn = nt(dk_ref[...], w_ref[1]) + nt(dv_ref[...], w_ref[2])

    @pl.when(i < MC)
    def _():
        wide = mem_ref[...].astype(F32)
        part = jnp.sum(gn * (wide * rms_factor(wide)), axis=0, keepdims=True)

        @pl.when(i == 0)
        def _():
            gain_ref[...] = part

        @pl.when(i > 0)
        def _():
            gain_ref[...] += part

    @pl.when(i >= MC)
    def _():
        wide = tok_ref[...].astype(F32)
        factor = rms_factor(wide)
        hat = wide * factor
        full = gn + nt(dq_ref[...], w_ref[0]) + tn(all_heads(gl_ref), vec_ref[2:10, :].astype(BF16))
        gain_ref[...] += jnp.sum(full * hat, axis=0, keepdims=True)
        scaled = full * vec_ref[0:1, :]
        gin_ref[...] = (
            gres_ref[...] + factor * (scaled - hat * jnp.mean(scaled * hat, axis=-1, keepdims=True))
        ).astype(BF16)


def input_kernel(dq, dk, dv, gl, w, tokens, memory, vectors, gres, after=()):
    tok = lambda i: jnp.clip(i - MC, 0, NT - 1)
    rows = pl.BlockSpec((TB, D), lambda i: (tok(i), 0))
    return call(
        input_body,
        (MC + NT,),
        [
            rows,
            pl.BlockSpec((TB, D), lambda i: (i, 0)),
            pl.BlockSpec((TB, D), lambda i: (i, 0)),
            pl.BlockSpec((NPAIR, 2, TB), lambda i: (0, 0, tok(i))),
            whole((3, D, D)),
            rows,
            pl.BlockSpec((TB, D), lambda i: (jnp.minimum(i, MC - 1), 0)),
            whole((2 + H, D)),
            rows,
        ],
        [rows, whole((1, D))],
        [sds((LEN, D), BF16), sds((1, D), F32)],
        9e9,
        10e6,
        "input",
        after=after,
        vmem=SMALL,
    )(dq, dk, dv, gl, w, tokens, memory, vectors, gres)


def exchange(slots, axis):
    size = len(slots)
    return [slots[0]] + [
        lax.ppermute(slots[r], axis, [(i, i ^ r) for i in range(size)]) for r in range(1, size)
    ]


def added(parts):
    total = parts[0].astype(F32)
    for other in parts[1:]:
        total = total + other.astype(F32)
    return total


PLANES = (("up",), ("q", "k"), ("v", "o"), ("down",))
EXTRA = 16


def alone(body, operands, out_shape, name, scratch=(), place=None, after=(), flops=2e9, vmem=SMALL):
    specs = [whole(x.shape) for x in operands]
    if place is not None:
        specs, operands = [SMEM] + specs, (place, *operands)
    return call(
        body,
        (1,),
        specs,
        [whole(x.shape) for x in out_shape],
        out_shape,
        flops,
        2e6,
        name,
        scratch=scratch,
        after=after,
        vmem=vmem,
    )(*operands)


def payloads_kernel(place, attn_weights, up_weights, down_weights, attn_moment, up_moment, down_moment):
    rows, cols = attn_weights.shape[1:]
    wide = up_weights.shape[1]
    planes = len(PLANES)
    width = cols + 3 * wide

    def body(place_ref, aw_ref, uw_ref, dw_ref, am_ref, um_ref, dm_ref, first_ref, *rest):
        outs, all_ref = rest[:planes], rest[planes]
        for j in range(3):
            first_ref[j * rows : (j + 1) * rows, :] = aw_ref[j].astype(BF16)
        all_ref[...] = jnp.zeros(all_ref.shape, BF16)
        all_ref[0] = um_ref[...].astype(BF16)
        all_ref[3] = dm_ref[...].astype(BF16)
        for j in range(4):
            all_ref[1 + j // 2, :, (j % 2) * cols : (j % 2 + 1) * cols] = am_ref[j].astype(BF16)
        for r in range(planes):
            outs[r][:, :cols] = aw_ref[3].astype(BF16)
            outs[r][:, cols : cols + wide] = uw_ref[...].astype(BF16)
            outs[r][:, cols + wide : cols + 2 * wide] = dw_ref[...].astype(BF16)
            outs[r][:, cols + 2 * wide :] = all_ref[place_ref[2] ^ r]

    first, *second = alone(
        body,
        (attn_weights, up_weights, down_weights, attn_moment, up_moment, down_moment),
        [sds((3 * rows, cols), BF16)] + [sds((rows, width), BF16)] * planes,
        "payloads",
        scratch=[pltpu.VMEM((planes, rows, wide), BF16)],
        place=place,
        vmem=VMEM_LIMIT,
    )
    return first, second


def stacked(parts, after=()):
    def body(*refs):
        for r in range(len(parts)):
            refs[-1][r] = refs[r][...]

    return alone(body, parts, [sds((len(parts),) + parts[0].shape, parts[0].dtype)], "stacked", after=after)[0]


def core_blocks(plane):
    return plane + [exchange([b, b], "core")[1] for b in plane]


def fold_cores(keep, other):
    chips, planes, rows, width = keep.shape

    def body(keep_ref, other_ref, *outs):
        for chip in range(chips):
            outs[chip][...] = added([keep_ref[chip], other_ref[chip]]).astype(BF16)

    spec = pl.BlockSpec((chips, 1, rows, width), lambda i: (0, i, 0, 0))
    return call(
        body,
        (planes,),
        [spec, spec],
        [pl.BlockSpec((1, rows, width), lambda i: (i, 0, 0))] * chips,
        [sds((planes, rows, width), BF16)] * chips,
        4e9,
        7e6,
        "fold_cores",
        vmem=SMALL,
    )(keep, other)


def fold_chips(parts):
    planes, rows, width = parts[0].shape

    def body(*refs):
        for plane in range(planes):
            refs[len(parts) + plane][...] = added([r[plane] for r in refs[: len(parts)]]).astype(BF16)

    return alone(body, parts, [sds((rows, width), BF16)] * planes, "fold_chips")


VEC = 2 + H
VEC_ROWS = 128


def put_vectors(ref, first, values):
    high = values.astype(BF16)
    low = (values - high.astype(F32)).astype(BF16)
    ref[first : first + VEC_ROWS, :] = jnp.zeros((VEC_ROWS, 128), BF16)
    for j in range(4):
        lanes = slice(j * 128, (j + 1) * 128)
        ref[first + j * 16 : first + j * 16 + VEC, :] = high[:, lanes]
        ref[first + 64 + j * 16 : first + 64 + j * 16 + VEC, :] = low[:, lanes]


def get_vectors(refs, first):
    pieces = []
    for j in range(4):
        rows = lambda offset: slice(first + offset + j * 16, first + offset + j * 16 + VEC)
        pieces.append(added([r[rows(offset), :] for r in refs for offset in (0, 64)]))
    return jnp.concatenate(pieces, axis=1)


def fold_cores_first(keep, other):
    chips = keep.shape[0]

    def body(keep_ref, other_ref, *outs):
        for chip in range(chips):
            outs[chip][...] = added([keep_ref[chip], other_ref[chip]]).astype(BF16)

    return alone(body, (keep, other), [sds(keep.shape[1:], BF16)] * chips, "fold_cores_first")


def fold_chips_first(parts, gain_attn, gain_ffn, grad_gate):
    planes, rows, width = parts[0].shape
    count = len(parts)

    def body(*refs):
        ins, (ga_ref, gf_ref, gg_ref) = refs[:count], refs[count : count + 3]
        outs, vec_ref = refs[count + 3 : -1], refs[-1]
        vec_ref[0:1, :] = ga_ref[...]
        vec_ref[1:2, :] = gf_ref[...]
        vec_ref[2:VEC, :] = gg_ref[...]
        for plane in range(planes):
            outs[plane][:rows, :] = added([r[plane] for r in ins]).astype(BF16)
            put_vectors(outs[plane], rows, vec_ref[...])

    return alone(
        body,
        (*parts, gain_attn, gain_ffn, grad_gate),
        [sds((rows + VEC_ROWS, width), BF16)] * planes,
        "fold_chips_first",
        scratch=[pltpu.VMEM((VEC, D), F32)],
    )


VEC_TILE = 32


def stack_with_vectors(parts, vec):
    count, (rows, width) = len(parts), parts[0].shape

    def body(*refs):
        vec_ref, out_ref = refs[count], refs[count + 1]
        for r in range(count):
            out_ref[r * rows : (r + 1) * rows, :] = refs[r][...]
        values = vec_ref[...]
        high = values.astype(BF16)
        out_ref[count * rows :, :] = jnp.zeros((VEC_TILE, width), BF16)
        out_ref[count * rows : count * rows + VEC, :] = high
        out_ref[count * rows + 16 : count * rows + 16 + VEC, :] = (values - high.astype(F32)).astype(BF16)

    return alone(
        body, (*parts, vec), [sds((count * rows + VEC_TILE, width), BF16)], "stack_with_vectors"
    )[0]


def owned_kernel(place, parts_a, parts_b):
    planes = len(parts_a)
    size, cols = parts_a[0].shape[0] - VEC_ROWS, parts_a[0].shape[1]
    rows, width = parts_b[0].shape
    wide = (width - cols) // 2

    def body(place_ref, *refs):
        a_refs, b_refs = refs[:planes], refs[planes : 2 * planes]
        ga_ref, gb_ref, vec_ref, *rest = refs[2 * planes :]
        slots, all_ref = rest[:planes], rest[planes]
        ga = added([r[:size, :] for r in a_refs])
        gb = added([r[...] for r in b_refs])
        ga_ref[...] = ga
        gb_ref[...] = gb
        vec_ref[...] = get_vectors(a_refs, size)
        squares = jnp.sum(ga * ga, keepdims=True) + jnp.sum(gb * gb, keepdims=True)
        all_ref[...] = jnp.zeros(all_ref.shape, BF16)
        for j in range(4):
            grad = ga[j * rows : (j + 1) * rows, :] if j < 3 else gb[:, :cols]
            all_ref[1 + j // 2, :, (j % 2) * cols : (j % 2 + 1) * cols] = grad.astype(BF16)
        all_ref[0] = gb[:, cols : cols + wide].astype(BF16)
        all_ref[3] = gb[:, cols + wide :].astype(BF16)
        wide_squares = squares + jnp.zeros((EXTRA, wide), F32)
        row = lax.broadcasted_iota(jnp.int32, (EXTRA, wide), 0)
        high = wide_squares.astype(BF16).astype(F32)
        middle = (wide_squares - high).astype(BF16).astype(F32)
        low = wide_squares - high - middle
        extra = jnp.where(row == 0, high, jnp.where(row == 1, middle, jnp.where(row == 2, low, 0.0))).astype(BF16)
        for r in range(planes):
            slots[r][:rows, :] = all_ref[place_ref[2] ^ r]
            slots[r][rows:, :] = extra

    return alone(
        body,
        (*parts_a, *parts_b),
        [sds((size, cols), F32), sds((rows, width), F32), sds((VEC, D), F32)]
        + [sds((rows + EXTRA, wide), BF16)] * planes,
        "owned",
        scratch=[pltpu.VMEM((planes, rows, wide), BF16)],
        place=place,
    )


def orthogonal_kernel(place, grads, moments, vectors, vec_moment):
    count = len(grads)
    chips = count // 2
    planes, rows = moments[0].shape[:2]
    wide = grads[0].shape[1]
    slot_rows = rows + EXTRA
    cols = D // planes
    skip = moments[0].shape[2] - wide
    limit = clip_fraction * math.sqrt(PARAMS)

    def body(place_ref, *refs):
        grad_refs, moment_refs, refs = refs[:count], refs[count : 2 * count], refs[2 * count :]
        vec_ref, vm_ref, norm_ref, vn_ref, vmn_ref = refs[:5]
        outs = refs[5 : 5 + planes]
        low_ref, x_ref, mix_ref, diag_ref, all_ref = refs[5 + planes :]
        pair = (place_ref[2] == 1) | (place_ref[2] == 2)
        own = part(place_ref[0] * 2 + place_ref[1], rows)
        vec_first = planes * slot_rows
        grad_vec = jnp.zeros((VEC, D), F32)
        squares = jnp.zeros((EXTRA, wide), F32)
        for b in range(count):
            for plane in range(planes):
                squares = squares + grad_refs[b][plane * slot_rows + rows : (plane + 1) * slot_rows, :].astype(F32)
            for first in (vec_first, vec_first + 16):
                grad_vec = grad_vec + grad_refs[b][first : first + VEC, :].astype(F32)
        total = jnp.sum(squares[:, 0:1], axis=0, keepdims=True) + jnp.sum(grad_vec * grad_vec, keepdims=True)
        norm = jnp.sqrt(total)
        norm_ref[...] = norm
        clip = limit / jnp.maximum(norm, limit)
        vec_mom = vector_decay * vm_ref[...] + clip * grad_vec
        vmn_ref[...] = vec_mom
        vn_ref[...] = vec_ref[...] - vector_rate * vec_mom

        def momentum(core, chip, plane, lanes):
            b = core * chips + chip
            moment = moment_refs[b][plane, :, skip + lanes.start : skip + lanes.stop].astype(F32)
            grad = grad_refs[b][plane * slot_rows : plane * slot_rows + rows, lanes].astype(F32)
            return muon_decay * moment + clip * grad

        def mixing(gram):
            eye = lax.broadcasted_iota(jnp.int32, (D, D), 0) == lax.broadcasted_iota(jnp.int32, (D, D), 1)
            low = gram.astype(BF16)
            mix = coef_second * low.astype(F32) + coef_third * nn(low, low)
            diag_ref[...] = coef_first + jnp.sum(jnp.where(eye, mix, 0.0), axis=1, keepdims=True)
            mix_ref[...] = jnp.where(eye, 0.0, mix).astype(BF16)

        def advance(start, width, scale):
            for c in range(start, start + width, D):
                lanes = slice(c, c + D)
                new = diag_ref[...] * x_ref[:, lanes] + nn(mix_ref[...], low_ref[:, lanes])
                if scale is not None:
                    new = new * scale
                x_ref[:, lanes] = new
                low_ref[:, lanes] = new.astype(BF16)

        def first_step(start, width):
            some = slice(start, start + width)
            gram = nt(low_ref[:, some], low_ref[:, some])
            eye = lax.broadcasted_iota(jnp.int32, (D, D), 0) == lax.broadcasted_iota(jnp.int32, (D, D), 1)
            scale = 1.0 / (jnp.sqrt(jnp.sum(jnp.where(eye, gram, 0.0), keepdims=True)) + 1e-07)
            mixing(gram * (scale * scale))
            advance(start, width, scale)

        def step(start, width, last):
            some = slice(start, start + width)
            mixing(nt(low_ref[:, some], low_ref[:, some]))
            if not last:
                advance(start, width, None)
                return
            for c in range(start, start + width, D):
                lanes = slice(c, c + D)
                x_ref[own, lanes] = diag_ref[own, :] * x_ref[own, lanes] + nn(mix_ref[own, :], low_ref[:, lanes])

        def iterations(ranges):
            for start, width in ranges:
                first_step(start, width)

            def middle(_, carry):
                for start, width in ranges:
                    step(start, width, False)
                return carry

            lax.fori_loop(1, NS_ITERS - 1, middle, 0)
            for start, width in ranges:
                step(start, width, True)

        @pl.when(pair)
        def _():
            for core, chip, plane, row, col in each_block(place_ref, chips, planes):
                for j in range(2):
                    new = momentum(core, chip, plane, slice(j * cols, (j + 1) * cols))
                    x_ref[part(row, rows), part(col + j * planes, cols)] = new
                    low_ref[part(row, rows), part(col + j * planes, cols)] = new.astype(BF16)
            iterations([(0, D), (D, D)])
            for plane in range(planes):
                for j in range(2):
                    first = j * D + plane * cols
                    all_ref[plane, :, j * cols : (j + 1) * cols] = x_ref[own, first : first + cols].astype(BF16)

        @pl.when(jnp.logical_not(pair))
        def _():
            for core, chip, plane, row, col in each_block(place_ref, chips, planes):
                new = momentum(core, chip, plane, slice(0, wide))
                x_ref[part(row, rows), part(col, wide)] = new
                low_ref[part(row, rows), part(col, wide)] = new.astype(BF16)
            iterations([(0, FF)])
            for plane in range(planes):
                all_ref[plane] = x_ref[own, plane * wide : (plane + 1) * wide].astype(BF16)

        for r in range(planes):
            outs[r][...] = all_ref[place_ref[2] ^ r]

    return alone(
        body,
        (*grads, *moments, vectors, vec_moment),
        [sds((1, 1), F32), sds((VEC, D), F32), sds((VEC, D), F32)] + [sds((rows, wide), BF16)] * planes,
        "orthogonal",
        scratch=[
            pltpu.VMEM((D, FF), BF16),
            pltpu.VMEM((D, FF), F32),
            pltpu.VMEM((D, D), BF16),
            pltpu.VMEM((D, 1), F32),
            pltpu.VMEM((planes, rows, wide), BF16),
        ],
        place=place,
        flops=18e9,
        vmem=VMEM_LIMIT,
    )


def update_kernel(place, slots, norm, ga, gb, attn_moment, up_moment, down_moment, attn_weights, up_weights, down_weights):
    planes = len(slots)
    rows, cols = attn_weights.shape[1:]
    wide = up_weights.shape[1]
    shape_factor = math.sqrt(max(1.0, FF / D))
    limit = clip_fraction * math.sqrt(PARAMS)

    def body(place_ref, *refs):
        slot_refs, refs = refs[:planes], refs[planes:]
        norm_ref, ga_ref, gb_ref, am_ref, um_ref, dm_ref, aw_ref, uw_ref, dw_ref = refs[:9]
        an_ref, un_ref, dn_ref, amn_ref, umn_ref, dmn_ref, all_ref = refs[9:]
        clip = limit / jnp.maximum(norm_ref[...], limit)
        for r in range(planes):
            all_ref[place_ref[2] ^ r] = slot_refs[r][...]
        for j in range(4):
            ortho = all_ref[1 + j // 2, :, (j % 2) * cols : (j % 2 + 1) * cols].astype(F32)
            an_ref[j] = aw_ref[j] - muon_rate * ortho
            grad = ga_ref[j * rows : (j + 1) * rows, :] if j < 3 else gb_ref[:, :cols]
            amn_ref[j] = muon_decay * am_ref[j] + clip * grad
        un_ref[...] = uw_ref[...] - muon_rate * all_ref[0].astype(F32)
        umn_ref[...] = muon_decay * um_ref[...] + clip * gb_ref[:, cols : cols + wide]
        dn_ref[...] = dw_ref[...] - muon_rate * shape_factor * all_ref[3].astype(F32)
        dmn_ref[...] = muon_decay * dm_ref[...] + clip * gb_ref[:, cols + wide :]

    weights = (attn_weights, up_weights, down_weights)
    return alone(
        body,
        (*slots, norm, ga, gb, attn_moment, up_moment, down_moment, *weights),
        [sds(x.shape, F32) for x in weights] * 2,
        "update",
        scratch=[pltpu.VMEM((planes,) + slots[0].shape, BF16)],
        place=place,
    )


def documents(starts):
    doc = jnp.cumsum(starts).astype(F32)
    return doc.reshape(1, LEN), doc.reshape(LEN, 1)


def plain_tail(sizes, grads, attn_weights, up_weights, down_weights, vectors, attn_moment, up_moment, down_moment, vec_moment):
    dp = ("chip", "core")
    grad_attn, grad_up, grad_down, grad_vectors = grads

    def owned(grad, narrow_dim, dp_dim):
        part_sum = lax.psum_scatter(grad.astype(BF16), "narrow", scatter_dimension=narrow_dim, tiled=True)
        return lax.psum_scatter(part_sum, dp, scatter_dimension=dp_dim, tiled=True).astype(F32)

    owned_attn, owned_up, owned_down = owned(grad_attn, 2, 1), owned(grad_up, 1, 0), owned(grad_down, 0, 1)
    own_squares = jnp.sum(owned_attn * owned_attn) + jnp.sum(owned_up * owned_up) + jnp.sum(owned_down * owned_down)
    vector_sum, square_sum = lax.psum((grad_vectors, own_squares), ("chip", "core", "narrow"))
    grad_norm = jnp.sqrt(square_sum + jnp.sum(vector_sum * vector_sum))
    clip_limit = clip_fraction * math.sqrt(PARAMS)
    clip_factor = clip_limit / jnp.maximum(grad_norm, clip_limit)
    attn_mom_new = muon_decay * attn_moment + clip_factor * owned_attn
    up_mom_new = muon_decay * up_moment + clip_factor * owned_up
    down_mom_new = muon_decay * down_moment + clip_factor * owned_down
    gather = lambda x, dim: lax.all_gather(x.astype(BF16), dp, axis=dim, tiled=True).astype(F32)
    ortho = (gather(attn_mom_new, 1), gather(up_mom_new, 0), gather(down_mom_new, 1))
    ortho_attn, ortho_up, ortho_down = ortho
    for iteration in range(NS_ITERS):
        gram_attn = jnp.einsum("imc,inc->imn", ortho_attn, ortho_attn, precision=highest)
        gram_up = lax.dot_general(ortho_up, ortho_up, (((1,), (1,)), ((), ())), precision=highest)
        gram_down = lax.dot_general(ortho_down, ortho_down, (((0,), (0,)), ((), ())), precision=highest)
        partial_grams = jnp.concatenate([gram_attn, gram_up[None], gram_down[None]], axis=0)
        gram_total = lax.psum(partial_grams.astype(BF16), "narrow").astype(F32)
        if iteration == 0:
            norm_scales = 1.0 / (jnp.sqrt(jnp.trace(gram_total, axis1=1, axis2=2)) + 1e-07)
            ortho_attn = ortho_attn * norm_scales[:4, None, None]
            ortho_up = ortho_up * norm_scales[4]
            ortho_down = ortho_down * norm_scales[5]
            gram_total = gram_total * (norm_scales * norm_scales)[:, None, None]
        once = jnp.einsum("imn,inc->imc", gram_total[:4], ortho_attn, precision=highest)
        twice = jnp.einsum("imn,inc->imc", gram_total[:4], once, precision=highest)
        ortho_attn = coef_first * ortho_attn + coef_second * once + coef_third * twice
        once = jnp.dot(gram_total[4], ortho_up, precision=highest)
        twice = jnp.dot(gram_total[4], once, precision=highest)
        ortho_up = coef_first * ortho_up + coef_second * once + coef_third * twice
        once = jnp.dot(ortho_down, gram_total[5], precision=highest)
        twice = jnp.dot(once, gram_total[5], precision=highest)
        ortho_down = coef_first * ortho_down + coef_second * once + coef_third * twice
    row_share = D // sizes["dp"]
    row_start = lax.axis_index(dp) * row_share
    final_attn = lax.dynamic_slice_in_dim(ortho_attn, row_start, row_share, 1)
    final_up = lax.dynamic_slice_in_dim(ortho_up, row_start, row_share, 0)
    final_down = lax.dynamic_slice_in_dim(ortho_down, row_start, row_share, 1)
    shape_factor = math.sqrt(max(1.0, FF / D))
    vector_mom_new = vector_decay * vec_moment + clip_factor * vector_sum
    return (
        attn_weights - muon_rate * final_attn,
        up_weights - muon_rate * final_up,
        down_weights - muon_rate * shape_factor * final_down,
        attn_mom_new,
        up_mom_new,
        down_mom_new,
        vectors - vector_rate * vector_mom_new,
        vector_mom_new,
        grad_norm,
    )


def per_device(
    sizes,
    tokens, memory, neighbour_bank, starts, neighbours, cotangent,
    attn_weights, up_weights, down_weights, vectors,
    attn_moment, up_moment, down_moment, vector_moment,
):
    memory = memory.reshape(MEM, D)
    bank = neighbour_bank.reshape(BANK, D)
    own = (attn_weights, up_weights, down_weights)
    moments = (attn_moment, up_moment, down_moment)
    chips, planes = sizes["dp"] // 2, sizes["narrow"]
    if planes == len(PLANES) and chips == 4:
        return fast_device(
            chips, planes, tokens, memory, bank, starts, neighbours, cotangent, own, vectors, moments, vector_moment
        )
    full = lambda x, narrow_dim, dp_dim: lax.all_gather(
        lax.all_gather(x.astype(BF16), ("chip", "core"), axis=dp_dim, tiled=True), "narrow", axis=narrow_dim, tiled=True
    )
    attn_full = full(attn_weights, 2, 1)
    second = [attn_full[3], full(up_weights, 1, 0), full(down_weights, 0, 1).T]
    x, xt, cot_t, gate = context_kernel(tokens, memory, bank, cotangent, vectors)
    doc_row, doc_col = documents(starts)
    bias_tok, bias_bank = mask_kernel(doc_row, doc_col, neighbours.T)
    w, q, k, v, kt, vt = project_kernel(x, attn_full[:3])
    e, local, fetched, stat, mixed, mixed_t = attend_kernel(q, k, vt, bias_tok, bias_bank, doc_row, gate, 0, NPAIR)
    out, act, gh, ffn_t, branch, gres, gmt, gain_ffn = feed_kernel(mixed, tokens, cotangent, vectors, second)
    grad_down_t, grad_up, grad_o = feed_grads_kernel(cot_t, act, ffn_t, gh, mixed_t, branch)
    dq, dk, dv, gl = unattend_kernel(q, k, kt, v, e, gmt, local, fetched, stat, gate, 0, NPAIR)
    grad_qkv, grad_gate = proj_grads_kernel(xt, dq, dk, dv, gl)
    grad_in, gain_attn = input_kernel(dq, dk, dv, gl, w, tokens, memory, vectors, gres)
    grad_vectors = jnp.concatenate([gain_attn, gain_ffn, grad_gate], axis=0)
    grads = (jnp.concatenate([grad_qkv, grad_o[None]], axis=0), grad_up, grad_down_t.T, grad_vectors)
    return (out, grad_in) + plain_tail(sizes, grads, *own, vectors, *moments, vector_moment)


def ordered(first, second):
    return lax.optimization_barrier((first, second))[0]


def fast_device(
    chips, planes, tokens, memory, bank, starts, neighbours, cotangent, own, vectors, moments, vector_moment
):
    own, moments = own[:2] + (own[2].T,), moments[:2] + (moments[2].T,)
    place = jnp.stack([lax.axis_index("chip"), lax.axis_index("core"), lax.axis_index("narrow")]).astype(jnp.int32)
    payload, payloads = payloads_kernel(place, *own, *moments)
    near_a = exchange([payload] * planes, "narrow")
    x, xt, cot_t, gate = context_kernel(tokens, memory, bank, cotangent, vectors, after=[payload])
    doc_row, doc_col = documents(starts)
    near_t = ordered(neighbours.T, payload)
    near_a = ordered(near_a, x)
    near_b = exchange(ordered(payloads, near_a), "narrow")
    column_a = stacked(near_a)
    plane_a = exchange([column_a] * chips, "chip")
    bias_tok, bias_bank = mask_kernel(doc_row, doc_col, near_t, after=[column_a])
    first = core_blocks(ordered(plane_a, bias_tok))
    column_b = stacked(ordered(near_b, first))
    w, q, k, v, kt, vt = project_kernel(x, first, place, after=[column_b])
    plane_b = exchange([column_b] * chips, "chip")
    e, local, fetched, stat, mixed, mixed_t = attend_kernel(q, k, vt, bias_tok, bias_bank, doc_row, gate, 0, NPAIR)
    second = core_blocks(ordered(plane_b, mixed))
    out, act, gh, ffn_t, branch, gres, gmt, gain_ffn = feed_kernel(mixed, tokens, cotangent, vectors, second, place)
    keep_b, send_b = feed_grads_blocks(cot_t, act, ffn_t, gh, mixed_t, branch, place, chips, planes)
    back = (q, k, kt, v, e, gmt, local, fetched, stat, gate)
    some = unattend_kernel(*back, 0, 1, after=[keep_b])
    slots_b = fold_cores(keep_b, ordered(exchange([send_b, send_b], "core")[1], some[0]))
    dq, dk, dv, gl = unattend_kernel(*back, 1, NPAIR - 1, after=[slots_b[0]], alias=some)
    slots_b = fold_chips(ordered(exchange(slots_b, "chip"), dq))
    keep_a, send_a, grad_gate = proj_grads_kernel(xt, dq, dk, dv, gl, place, chips, planes, after=[slots_b[0]])
    slots_a = fold_cores_first(keep_a, exchange([send_a, send_a], "core")[1])
    grad_in, gain_attn = input_kernel(dq, dk, dv, gl, w, tokens, memory, vectors, gres, after=[slots_a[0]])
    parts_b, parts_a = ordered((exchange(slots_b, "narrow"), exchange(slots_a, "chip")), grad_in)
    slots_a = fold_chips_first(parts_a, gain_attn, gain_ffn, grad_gate)
    parts_a = exchange(slots_a, "narrow")
    ga, gb, vec, *slots = owned_kernel(place, parts_a, parts_b)
    grads = core_blocks(exchange([stack_with_vectors(exchange(slots, "narrow"), vec)] * chips, "chip"))
    norm, vec_new, vec_mom, *slots = orthogonal_kernel(place, grads, second, vectors, vector_moment)
    final = exchange(slots, "narrow")
    new = list(update_kernel(place, final, norm, ga, gb, *moments, *own))
    new[2], new[5] = new[2].T, new[5].T
    return (out, grad_in, *new, vec_new, vec_mom, norm.reshape(()))


def solution(mesh):
    sizes = dict(mesh.shape)
    split = Mesh(
        mesh.devices.reshape(sizes["dp"] // 2, 2, sizes["narrow"]), ("chip", "core", "narrow")
    )
    dp = ("chip", "core")
    rows = ("chip", "core", "narrow")
    weights = (P(None, dp, "narrow"), P(dp, "narrow"), P("narrow", dp))
    return jax.shard_map(
        lambda *operands: per_device(sizes, *operands),
        mesh=split,
        in_specs=(P(rows, None), P(rows, None, None), P(rows, None, None), P(rows), P(rows, None), P(rows, None))
        + weights + (P(),) + weights + (P(),),
        out_specs=(P(rows, None), P(rows, None)) + weights + weights + (P(), P(), P()),
        check_vma=False,
    )
```

```python
import math

import jax
import jax.numpy as jnp
from jax import lax
from jax.experimental import pallas as pl
from jax.experimental.pallas import tpu as pltpu
from jax.sharding import Mesh, PartitionSpec as P

D = 512
H = 8
FF = 2048
MEM = 512
BANK = 512
KNB = 4
LEN = 1024
CTX = MEM + LEN
ROWS = CTX + BANK
HD = D // H
TB = 256
NT = LEN // TB
MC = MEM // TB
BC = BANK // TB
PAIR = 2 * HD
NPAIR = D // PAIR
F32 = jnp.float32
BF16 = jnp.bfloat16
NS_ITERS = 5
PARAMS = 3150848
epsilon = 1e-06
masked_score = -1e30
coef_first = 3.4445
coef_second = -4.775
coef_third = 2.0315
clip_fraction = 0.05
muon_rate = 0.5
muon_decay = 0.5
vector_rate = 0.5
vector_decay = 0.9
highest = lax.Precision.HIGHEST
LOG2E = 1.4426950408889634
SAFE = 80.0
VMEM_LIMIT = 60 * 1024 * 1024
SMALL = 16 * 1024 * 1024


def nn(a, b):
    return lax.dot_general(a, b, (((1,), (0,)), ((), ())), preferred_element_type=F32)


def nt(a, b):
    return lax.dot_general(a, b, (((1,), (1,)), ((), ())), preferred_element_type=F32)


def tn(a, b):
    return lax.dot_general(a, b, (((0,), (0,)), ((), ())), preferred_element_type=F32)


def rms_factor(values):
    return lax.rsqrt(jnp.mean(values * values, axis=-1, keepdims=True) + epsilon)


def whole(shape):
    return pl.BlockSpec(shape, lambda *_: (0,) * len(shape))


def call(
    body, grid, in_specs, out_specs, out_shape, flops, nbytes, name, scratch=(), trans=0, prefetch=0, after=(), alias=(),
    vmem=VMEM_LIMIT,
):
    extra, given = len(after) + len(alias), prefetch + len(in_specs)

    def with_extra(*refs):
        body(*refs[:given], *refs[given + extra :])

    made = pl.pallas_call(
        with_extra,
        grid_spec=pltpu.PrefetchScalarGridSpec(
            num_scalar_prefetch=prefetch,
            grid=grid,
            in_specs=list(in_specs) + [pl.BlockSpec(memory_space=pl.ANY)] * extra,
            out_specs=out_specs,
            scratch_shapes=list(scratch),
        ),
        out_shape=out_shape,
        input_output_aliases={given + len(after) + j: j for j in range(len(alias))},
        name=name,
        cost_estimate=pl.CostEstimate(flops=int(flops), bytes_accessed=int(nbytes), transcendentals=int(trans)),
        compiler_params=pltpu.CompilerParams(
            vmem_limit_bytes=vmem, dimension_semantics=("arbitrary",) * len(grid)
        ),
    )
    return lambda *operands: made(*operands, *after, *alias)


SMEM = pl.BlockSpec(memory_space=pltpu.SMEM)


def sds(shape, dtype):
    return jax.ShapeDtypeStruct(shape, dtype)


def hbm(shape, dtype):
    return pltpu.HBM(shape, dtype)


def context_body(tok_ref, mem_ref, bank_ref, cot_ref, vec_ref, x_ref, xt_ref, cott_ref, gate_ref):
    i = pl.program_id(0)
    gain = vec_ref[0:1, :]

    def put(rows):
        x_ref[...] = rows
        xt_ref[...] = rows.T

    def norm(values):
        wide = values.astype(F32)
        return (wide * rms_factor(wide) * gain).astype(BF16)

    @pl.when(i < MC)
    def _():
        put(norm(mem_ref[...]))

    @pl.when((i >= MC) & (i < MC + NT))
    def _():
        rows = norm(tok_ref[...])
        put(rows)
        logits = nt(vec_ref[2:10, :].astype(BF16), rows)
        gate = jax.nn.sigmoid(logits)
        for p in range(NPAIR):
            gate_ref[p] = gate[2 * p : 2 * p + 2, :]
        cott_ref[...] = cot_ref[...].T

    @pl.when(i >= MC + NT)
    def _():
        put(bank_ref[...])


def context_kernel(tokens, memory, bank, cot, vectors, after=()):
    steps = MC + NT + BC
    clip_tok = lambda i: jnp.clip(i - MC, 0, NT - 1)
    return call(
        context_body,
        (steps,),
        [
            pl.BlockSpec((TB, D), lambda i: (clip_tok(i), 0)),
            pl.BlockSpec((TB, D), lambda i: (jnp.minimum(i, MC - 1), 0)),
            pl.BlockSpec((TB, D), lambda i: (jnp.clip(i - MC - NT, 0, BC - 1), 0)),
            pl.BlockSpec((TB, D), lambda i: (clip_tok(i), 0)),
            whole((2 + H, D)),
        ],
        [
            pl.BlockSpec((TB, D), lambda i: (i, 0)),
            pl.BlockSpec((D, TB), lambda i: (0, i)),
            pl.BlockSpec((D, TB), lambda i: (0, clip_tok(i))),
            pl.BlockSpec((NPAIR, 2, TB), lambda i: (0, 0, clip_tok(i))),
        ],
        [sds((ROWS, D), BF16), hbm((D, ROWS), BF16), hbm((D, LEN), BF16), hbm((NPAIR, 2, LEN), F32)],
        8e9,
        8e6,
        "context",
        after=after,
        vmem=SMALL,
    )(tokens, memory, bank, cot, vectors)


def mask_body(doc_row_ref, doc_col_ref, near_ref, tok_ref, bank_ref):
    i = pl.program_id(0)
    doc_row = doc_row_ref[...]

    @pl.when(i < NT)
    def _():
        keys = lax.broadcasted_iota(jnp.int32, (TB, LEN), 0) + i * TB
        rows = lax.broadcasted_iota(jnp.int32, (TB, LEN), 1)
        seen = (keys <= rows) & (doc_col_ref[...] == doc_row)
        tok_ref[...] = jnp.where(seen, 0.0, masked_score)

    @pl.when(i >= NT)
    def _():
        keys = lax.broadcasted_iota(jnp.int32, (TB, LEN), 0) + (i - NT) * TB
        count = jnp.zeros((TB, LEN), F32)
        for j in range(KNB):
            count = count + jnp.where(near_ref[j : j + 1, :] == keys, 1.0, 0.0)
        bias = jnp.where(count > 0.5, 0.0, masked_score)
        for j in range(2, KNB + 1):
            bias = jnp.where(count > j - 0.5, math.log2(j), bias)
        bank_ref[...] = bias


def mask_kernel(doc_row, doc_col, near_t, after=()):
    return call(
        mask_body,
        (NT + BC,),
        [
            whole((1, LEN)),
            pl.BlockSpec((TB, 1), lambda i: (jnp.minimum(i, NT - 1), 0)),
            whole((KNB, LEN)),
        ],
        [
            pl.BlockSpec((TB, LEN), lambda i: (jnp.minimum(i, NT - 1), 0)),
            pl.BlockSpec((TB, LEN), lambda i: (jnp.clip(i - NT, 0, BC - 1), 0)),
        ],
        [hbm((LEN, LEN), F32), hbm((BANK, LEN), F32)],
        6e9,
        7e6,
        "masks",
        after=after,
        vmem=SMALL,
    )(doc_row, doc_col, near_t)


def each_block(place_ref, chips, planes):
    for core in range(2):
        for chip in range(chips):
            row = ((place_ref[0] ^ chip) * 2 + (place_ref[1] ^ core))
            for plane in range(planes):
                yield core, chip, plane, row, place_ref[2] ^ plane


def part(index, size):
    return pl.ds(pl.multiple_of(index * size, size), size)


def head_squares(columns):
    wide = columns.astype(F32)
    return jnp.sum((wide * wide).reshape(H, HD, wide.shape[1]), axis=1)


def project_rows(i, x_ref, w_ref, q_ref, k_ref, v_ref, qt_ref, kt_ref, vt_ref, qn_ref, kn_ref):
    rows = x_ref[...]
    keys = nn(rows, w_ref[1]).astype(BF16)
    values = nn(rows, w_ref[2]).astype(BF16)
    keys_t = keys.T
    k_ref[...] = keys
    v_ref[...] = values
    kt_ref[...] = keys_t
    vt_ref[...] = values.T

    @pl.when(i == 0)
    def _():
        kn_ref[...] = jnp.zeros(kn_ref.shape, F32)
        qn_ref[...] = jnp.zeros(qn_ref.shape, F32)

    kn_ref[...] = jnp.maximum(kn_ref[...], head_squares(keys_t))

    @pl.when((i >= MEM // rows.shape[0]) & (i < CTX // rows.shape[0]))
    def _():
        queries = (nn(rows, w_ref[0]).astype(BF16).astype(F32) * (LOG2E / math.sqrt(HD))).astype(BF16)
        queries_t = queries.T
        q_ref[...] = queries
        qt_ref[...] = queries_t
        qn_ref[...] = jnp.maximum(qn_ref[...], head_squares(queries_t))


def project_kernel(x, w, place=None, after=()):
    rows = 2 * TB
    steps = ROWS // rows
    first_q, last_q = MEM // rows, CTX // rows - 1
    fast = place is not None
    if fast:
        chips, planes = len(w) // 2, w[0].shape[0]
        own_rows, own_cols = w[0].shape[1] // 3, w[0].shape[2]

    def body(*refs):
        i = pl.program_id(0)
        if not fast:
            project_rows(i, *refs)
            return
        place_ref, x_ref, *rest = refs
        blocks, (w_ref, *outs) = rest[: len(w)], rest[len(w) :]

        @pl.when(i == 0)
        def _():
            for core, chip, plane, row, col in each_block(place_ref, chips, planes):
                for j in range(3):
                    w_ref[j, part(row, own_rows), part(col, own_cols)] = blocks[core * chips + chip][
                        plane, j * own_rows : (j + 1) * own_rows, :
                    ]

        project_rows(i, x_ref, w_ref, *outs)

    out_specs = [
        pl.BlockSpec((rows, D), lambda i: (jnp.clip(i, first_q, last_q) - first_q, 0)),
        pl.BlockSpec((rows, D), lambda i: (i, 0)),
        pl.BlockSpec((rows, D), lambda i: (i, 0)),
        pl.BlockSpec((D, rows), lambda i: (0, jnp.clip(i, first_q, last_q) - first_q)),
        pl.BlockSpec((D, rows), lambda i: (0, i)),
        pl.BlockSpec((D, rows), lambda i: (0, i)),
        whole((H, rows)),
        whole((H, rows)),
    ]
    out_shape = [
        hbm((LEN, D), BF16),
        hbm((ROWS, D), BF16),
        hbm((ROWS, D), BF16),
        hbm((D, LEN), BF16),
        hbm((D, ROWS), BF16),
        hbm((D, ROWS), BF16),
        sds((H, rows), F32),
        sds((H, rows), F32),
    ]
    in_specs = [pl.BlockSpec((rows, D), lambda i: (i, 0))]
    if fast:
        in_specs = [SMEM] + in_specs + [whole(b.shape) for b in w]
        out_specs = [whole((3, D, D))] + out_specs
        out_shape = [hbm((3, D, D), BF16)] + out_shape
        operands = (place, x, *w)
    else:
        in_specs = in_specs + [whole((3, D, D))]
        operands = (x, w)
    result = call(
        body, (steps,), in_specs, out_specs, out_shape, 11e9, 14e6, "project", after=after, vmem=24 * 1024 * 1024
    )(*operands)
    return result if fast else [w, *result]


def head_lanes(values, h):
    lanes = lax.broadcasted_iota(jnp.int32, values.shape, 1)
    keep = (lanes < HD) if h == 0 else (lanes >= HD)
    return jnp.where(keep, values, jnp.zeros_like(values))


def key_chunks(tb):
    return list(range(MC + tb + 1)), list(range(MC + NT, MC + NT + BC))


def head_rows_of(values, h):
    zeros = jnp.zeros((HD, values.shape[1]), values.dtype)
    own = values[h * HD : (h + 1) * HD, :]
    return jnp.concatenate([own, zeros] if h == 0 else [zeros, own], axis=0)


def attend_body(
    qt_ref, k_ref, vt_ref, tok_ref, bank_ref, doc_ref, gate_ref, qn_ref, kn_ref,
    e_ref, local_ref, fetched_ref, stat_ref, mixed_ref, mixedt_ref, s_ref,
):
    units = [(tb, h) for tb in range(NT) for h in range(2)]
    far_rows = slice(CTX, ROWS)

    def near_rows(tb):
        return slice(0, MEM + (tb + 1) * TB)

    def start(u):
        tb, h = units[u]
        q_head = head_rows_of(qt_ref[:, tb * TB : (tb + 1) * TB], h)
        s_ref[u % 2, near_rows(tb), :] = nn(k_ref[near_rows(tb), :], q_head)
        s_ref[u % 2, far_rows, :] = nn(k_ref[far_rows, :], q_head)

    def biased(u, c, cols, mem_bias):
        s = s_ref[u % 2, c * TB : (c + 1) * TB, :]
        if c < MC:
            return s + mem_bias
        if c < MC + NT:
            return s + tok_ref[(c - MC) * TB : (c - MC + 1) * TB, cols]
        return s + bank_ref[(c - MC - NT) * TB : (c - MC - NT + 1) * TB, cols]

    def soft(u, chunks, cols, mem_bias, general):
        h = units[u][1]
        top = None
        if general:
            peak = jnp.full((8, TB), -3e38, F32)
            for c in chunks:
                s = biased(u, c, cols, mem_bias)
                peak = jnp.maximum(peak, jnp.max(s.reshape(TB // 8, 8, TB), axis=0))
            top = jnp.max(peak, axis=0, keepdims=True)
        total = jnp.zeros((8, TB), F32)
        for c in chunks:
            s = biased(u, c, cols, mem_bias)
            e = jnp.exp2(s - top if general else s)
            e_ref[h, c * TB : (c + 1) * TB, cols] = e.astype(BF16)
            total = total + jnp.sum(e.reshape(TB // 8, 8, TB), axis=0)
        return 1.0 / jnp.sum(total, axis=0, keepdims=True)

    def run(general):
        start(0)
        mixed_parts = []
        for u, (tb, h) in enumerate(units):
            cols = slice(tb * TB, (tb + 1) * TB)
            head_rows = slice(h * HD, (h + 1) * HD)
            if u + 1 < len(units):
                start(u + 1)
            mem_bias = jnp.where(doc_ref[:, cols] == 0.0, 0.0, masked_score)
            near, far = key_chunks(tb)
            local_inv = soft(u, near, cols, mem_bias, general)
            fetched_inv = soft(u, far, cols, mem_bias, general)
            local = nn(vt_ref[head_rows, near_rows(tb)], e_ref[h, near_rows(tb), cols]) * local_inv
            fetched = nn(vt_ref[head_rows, far_rows], e_ref[h, far_rows, cols]) * fetched_inv
            local_ref[head_rows, cols] = local
            fetched_ref[head_rows, cols] = fetched
            stat_ref[0, h : h + 1, cols] = local_inv
            stat_ref[0, 2 + h : 3 + h, cols] = fetched_inv
            gate = gate_ref[0, h : h + 1, cols]
            mixed_parts.append((1.0 - gate) * local + gate * fetched)
            if h == 1:
                mixed = jnp.concatenate(mixed_parts, axis=0)
                mixed_parts = []
                mixedt_ref[:, cols] = mixed.astype(BF16)
                mixed_ref[cols, :] = mixed.T.astype(BF16)
                if tb % 2 == 0:
                    for other in range(2):
                        e_ref[other, MEM + (tb + 1) * TB : MEM + (tb + 2) * TB, cols] = jnp.zeros((TB, TB), BF16)

    bound = jnp.max(jnp.max(qn_ref[...], axis=1, keepdims=True) * jnp.max(kn_ref[...], axis=1, keepdims=True))

    @pl.when(bound <= SAFE * SAFE)
    def _():
        run(False)

    @pl.when(jnp.logical_not(bound <= SAFE * SAFE))
    def _():
        run(True)


def attend_kernel(qt, k, vt, qn, kn, bias_tok, bias_bank, doc_row, gate, first, count):
    spec_cols = lambda rows: pl.BlockSpec((rows, PAIR), lambda p: (0, p + first))
    spec_rows = lambda cols: pl.BlockSpec((PAIR, cols), lambda p: (p + first, 0))
    return call(
        attend_body,
        (count,),
        [
            spec_rows(LEN),
            spec_cols(ROWS),
            spec_rows(ROWS),
            whole((LEN, LEN)),
            whole((BANK, LEN)),
            whole((1, LEN)),
            pl.BlockSpec((1, 2, LEN), lambda p: (p + first, 0, 0)),
            whole(qn.shape),
            whole(kn.shape),
        ],
        [
            pl.BlockSpec((2, ROWS, LEN), lambda p: (p, 0, 0)),
            pl.BlockSpec((PAIR, LEN), lambda p: (p, 0)),
            pl.BlockSpec((PAIR, LEN), lambda p: (p, 0)),
            pl.BlockSpec((1, 8, LEN), lambda p: (p, 0, 0)),
            pl.BlockSpec((LEN, PAIR), lambda p: (0, p)),
            pl.BlockSpec((PAIR, LEN), lambda p: (p, 0)),
        ],
        [
            hbm((2 * count, ROWS, LEN), BF16),
            hbm((PAIR * count, LEN), F32),
            hbm((PAIR * count, LEN), F32),
            hbm((count, 8, LEN), F32),
            hbm((LEN, PAIR * count), BF16),
            hbm((PAIR * count, LEN), BF16),
        ],
        count * 5e9,
        count * 14e6 + 6e6,
        "attend",
        scratch=[pltpu.VMEM((2, ROWS, TB), F32)],
        trans=count * 2 * ROWS * LEN,
        vmem=VMEM_LIMIT,
    )(qt, k, vt, bias_tok, bias_bank, doc_row, gate, qn, kn)


def gelu_parts(x):
    square = jnp.exp2(x * x * (-0.5 * LOG2E))
    t = 1.0 / (1.0 + (0.3275911 * 0.7071067811865476) * jnp.abs(x))
    poly = t * (
        0.127414796 + t * (-0.142248368 + t * (0.7107068705 + t * (-0.7265760135 + t * 0.5307027145)))
    )
    tail = poly * square
    cdf = jnp.where(x >= 0.0, 1.0 - tail, tail)
    return cdf, square * 0.3989422804014327


FC = 512


def feed_body(
    mixed_ref, tok_ref, cot_ref, wo_ref, up_ref, dt_ref, vec_ref,
    out_ref, act_ref, gh_ref, ffnt_ref, branch_ref, gres_ref, gmt_ref, gain_ref,
):
    i = pl.program_id(0)
    residual = tok_ref[...].astype(F32) + nn(mixed_ref[...], wo_ref[...])
    factor = rms_factor(residual)
    hat = residual * factor
    gain = vec_ref[1:2, :]
    ffn = (hat * gain).astype(BF16)
    ffnt_ref[...] = ffn.T
    cot = cot_ref[...]
    out = residual
    grad_ffn = jnp.zeros(residual.shape, F32)
    for c in range(FF // FC):
        cols = slice(c * FC, (c + 1) * FC)
        hidden = nn(ffn, up_ref[:, cols])
        cdf, pdf = gelu_parts(hidden)
        act = (hidden * cdf).astype(BF16)
        act_ref[:, cols] = act
        grad_act = nn(cot, dt_ref[:, cols])
        gh = (grad_act * (cdf + hidden * pdf)).astype(BF16)
        gh_ref[:, cols] = gh
        out = out + nt(act, dt_ref[:, cols])
        grad_ffn = grad_ffn + nt(gh, up_ref[:, cols])
    out_ref[...] = out.astype(BF16)
    part = jnp.sum(grad_ffn * hat, axis=0, keepdims=True)

    @pl.when(i == 0)
    def _():
        gain_ref[...] = part

    @pl.when(i > 0)
    def _():
        gain_ref[...] += part

    scaled = grad_ffn * gain
    grad_res = cot.astype(F32) + factor * (scaled - hat * jnp.mean(scaled * hat, axis=-1, keepdims=True))
    gres_ref[...] = grad_res
    branch = grad_res.astype(BF16)
    branch_ref[...] = branch
    gmt_ref[...] = nt(wo_ref[...], branch)


def feed_kernel(mixed, tokens, cot, vectors, w):
    rows = lambda width: pl.BlockSpec((TB, width), lambda i: (i, 0))
    cols = lambda height: pl.BlockSpec((height, TB), lambda i: (0, i))

    def body(mixed_ref, tok_ref, cot_ref, vec_ref, wo_ref, up_ref, dt_ref, *outs):
        feed_body(mixed_ref, tok_ref, cot_ref, wo_ref, up_ref, dt_ref, vec_ref, *outs)

    return call(
        body,
        (NT,),
        [rows(D), rows(D), rows(D), whole((2 + H, D))] + [whole(x.shape) for x in w],
        [rows(D), rows(FF), rows(FF), cols(D), rows(D), rows(D), cols(D), whole((1, D))],
        [
            sds((LEN, D), BF16),
            sds((LEN, FF), BF16),
            sds((LEN, FF), BF16),
            sds((D, LEN), BF16),
            sds((LEN, D), BF16),
            sds((LEN, D), F32),
            sds((D, LEN), F32),
            sds((1, D), F32),
        ],
        23e9,
        22e6,
        "feed",
        trans=LEN * FF * 2,
    )(mixed, tokens, cot, vectors, *w)


def feed_grads_body(cott_ref, act_ref, ffnt_ref, gh_ref, mixedt_ref, branch_ref, gd_ref, gu_ref, go_ref):
    gd_ref[...] = nn(cott_ref[...], act_ref[...]).astype(BF16)
    gu_ref[...] = nn(ffnt_ref[...], gh_ref[...]).astype(BF16)
    go_ref[...] = nn(mixedt_ref[...], branch_ref[...]).astype(BF16)


def feed_grads_kernel(cot_t, act, ffn_t, gh, mixed_t, branch):
    steps = 4
    wide = lambda width: pl.BlockSpec((LEN, width // steps), lambda i: (0, i))
    out = lambda width: pl.BlockSpec((D, width // steps), lambda i: (0, i))
    return call(
        feed_grads_body,
        (steps,),
        [whole((D, LEN)), wide(FF), whole((D, LEN)), wide(FF), whole((D, LEN)), wide(D)],
        [out(FF), out(FF), out(D)],
        [sds((D, FF), BF16), sds((D, FF), BF16), sds((D, D), BF16)],
        11e9,
        17e6,
        "feed_grads",
    )(cot_t, act, ffn_t, gh, mixed_t, branch)


def feed_blocks(mixed, mixed_t, tokens, cot, cot_t, vectors, w, place):
    chips, planes = len(w) // 2, w[0].shape[0]
    own_rows, own_o, own_ff = w[0].shape[1], D // planes, FF // planes
    width = own_o + 2 * own_ff
    size = 2 * TB
    row_steps = LEN // size

    def body(place_ref, mixed_ref, mixedt_ref, tok_ref, cot_ref, cott_ref, vec_ref, *rest):
        blocks, rest = rest[: len(w)], rest[len(w) :]
        out_ref, gres_ref, gmt_ref, gain_ref, keep_ref, send_ref = rest[:6]
        wo_ref, up_ref, dt_ref, act_ref, gh_ref, ffnt_ref, branch_ref, hid_ref, ga_ref, all_ref = rest[6:]
        i = pl.program_id(0)

        @pl.when(i == 0)
        def _():
            for core, chip, plane, row, col in each_block(place_ref, chips, planes):
                block = blocks[core * chips + chip]
                here = part(row, own_rows)
                wo_ref[here, part(col, own_o)] = block[plane, :, :own_o]
                up_ref[here, part(col, own_ff)] = block[plane, :, own_o : own_o + own_ff]
                dt_ref[here, part(col, own_ff)] = block[plane, :, own_o + own_ff :]

        @pl.when(i < row_steps)
        def _():
            here = part(i, size)
            residual = tok_ref[...].astype(F32) + nn(mixed_ref[...], wo_ref[...])
            factor = rms_factor(residual)
            hat = residual * factor
            gain = vec_ref[1:2, :]
            ffn = (hat * gain).astype(BF16)
            ffnt_ref[:, here] = ffn.T
            cot = cot_ref[...]

            def start(c):
                cols = slice(c * FC, (c + 1) * FC)
                hid_ref[c % 2] = nn(ffn, up_ref[:, cols])
                ga_ref[c % 2] = nn(cot, dt_ref[:, cols])

            out = residual
            grad_ffn = jnp.zeros(residual.shape, F32)
            start(0)
            for c in range(FF // FC):
                cols = slice(c * FC, (c + 1) * FC)
                if c + 1 < FF // FC:
                    start(c + 1)
                hidden = hid_ref[c % 2]
                cdf, pdf = gelu_parts(hidden)
                act_ref[here, cols] = (hidden * cdf).astype(BF16)
                gh_ref[here, cols] = (ga_ref[c % 2] * (cdf + hidden * pdf)).astype(BF16)
                out = out + nt(act_ref[here, cols], dt_ref[:, cols])
                grad_ffn = grad_ffn + nt(gh_ref[here, cols], up_ref[:, cols])
            out_ref[...] = out.astype(BF16)
            gain_part = jnp.sum(grad_ffn * hat, axis=0, keepdims=True)

            @pl.when(i == 0)
            def _():
                gain_ref[...] = gain_part

            @pl.when(i > 0)
            def _():
                gain_ref[...] += gain_part

            scaled = grad_ffn * gain
            grad_res = cot.astype(F32) + factor * (scaled - hat * jnp.mean(scaled * hat, axis=-1, keepdims=True))
            gres_ref[...] = grad_res
            branch = grad_res.astype(BF16)
            branch_ref[here, :] = branch
            gmt_ref[...] = nt(wo_ref[...], branch)

        @pl.when(i >= row_steps)
        def _():
            plane = i - row_steps
            cols = part(plane, own_ff)
            all_ref[:, :own_o] = nn(mixedt_ref[...], branch_ref[:, part(plane, own_o)]).astype(BF16)
            all_ref[:, own_o : own_o + own_ff] = nn(ffnt_ref[...], gh_ref[:, cols]).astype(BF16)
            all_ref[:, own_o + own_ff :] = nn(cott_ref[...], act_ref[:, cols]).astype(BF16)
            for chip in range(chips):
                slot = place_ref[0] ^ chip
                keep_ref[slot, 0] = all_ref[part(chip * 2 + place_ref[1], own_rows), :]
                send_ref[slot, 0] = all_ref[part(chip * 2 + 1 - place_ref[1], own_rows), :]

    row = lambda i: jnp.minimum(i, row_steps - 1)
    rows = pl.BlockSpec((size, D), lambda i, _: (row(i), 0))
    blocked = pl.BlockSpec(
        (chips, 1, own_rows, width), lambda i, place_ref: (0, jnp.maximum(i - row_steps, 0) ^ place_ref[2], 0, 0)
    )
    shape = hbm((chips, planes, own_rows, width), BF16)
    return call(
        body,
        (row_steps + planes,),
        [rows, whole((D, LEN)), rows, rows, whole((D, LEN)), whole((2 + H, D))] + [whole(b.shape) for b in w],
        [rows, rows, pl.BlockSpec((D, size), lambda i, _: (0, row(i))), whole((1, D)), blocked, blocked],
        [hbm((LEN, D), BF16), hbm((LEN, D), F32), hbm((D, LEN), F32), sds((1, D), F32), shape, shape],
        30e9,
        22e6,
        "feed",
        scratch=[
            pltpu.VMEM((D, D), BF16),
            pltpu.VMEM((D, FF), BF16),
            pltpu.VMEM((D, FF), BF16),
            pltpu.VMEM((LEN, FF), BF16),
            pltpu.VMEM((LEN, FF), BF16),
            pltpu.VMEM((D, LEN), BF16),
            pltpu.VMEM((LEN, D), BF16),
            pltpu.VMEM((2, size, FC), F32),
            pltpu.VMEM((2, size, FC), F32),
            pltpu.VMEM((D, width), BF16),
        ],
        trans=LEN * FF * 2,
        prefetch=1,
    )(place, mixed, mixed_t, tokens, cot, cot_t, vectors, *w)


def unattend_body(
    q_ref, k_ref, kt_ref, v_ref, e_ref, gmt_ref, local_ref, fetched_ref, stat_ref, gate_ref,
    dq_ref, dk_ref, dv_ref, gl_ref, ds_ref, do_ref, df_ref, dot_ref, dqt_ref, dk_acc, dv_acc, gp_ref,
):
    del k_ref

    def prepare(h):
        head_rows = slice(h * HD, (h + 1) * HD)
        gm = gmt_ref[head_rows, :]
        local = local_ref[head_rows, :]
        fetched = fetched_ref[head_rows, :]
        gate = gate_ref[0, h : h + 1, :]
        local_inv = stat_ref[0, h : h + 1, :]
        fetched_inv = stat_ref[0, 2 + h : 3 + h, :]
        grad_gate = jnp.sum(gm * (fetched - local), axis=0, keepdims=True)
        gl_ref[0, h : h + 1, :] = grad_gate * gate * (1.0 - gate)
        grad_local = ((1.0 - gate) * gm).astype(BF16).astype(F32)
        grad_fetched = gate * gm
        other = slice((1 - h) * HD, (2 - h) * HD)
        do_ref[h, other, :] = jnp.zeros((HD, LEN), BF16)
        df_ref[h, other, :] = jnp.zeros((HD, LEN), BF16)
        do_ref[h, head_rows, :] = (grad_local * local_inv).astype(BF16)
        df_ref[h, head_rows, :] = (grad_fetched * fetched_inv).astype(BF16)
        dot_ref[h : h + 1, :] = jnp.sum(grad_local * local, axis=0, keepdims=True) * local_inv
        dot_ref[2 + h : 3 + h, :] = jnp.sum(grad_fetched * fetched, axis=0, keepdims=True) * fetched_inv

    units = [(tb, h) for h in range(2) for tb in range(NT)]
    far_rows = slice(CTX, ROWS)

    def near_rows(tb):
        return slice(0, MEM + (tb + 1) * TB)

    def start(u):
        tb, h = units[u]
        cols = slice(tb * TB, (tb + 1) * TB)
        gp_ref[u % 2, near_rows(tb), :] = nn(v_ref[near_rows(tb), :], do_ref[h, :, cols])
        gp_ref[u % 2, far_rows, :] = nn(v_ref[far_rows, :], df_ref[h, :, cols])

    def rows_part(u):
        tb, h = units[u]
        cols = slice(tb * TB, (tb + 1) * TB)
        head_rows = slice(h * HD, (h + 1) * HD)
        near, far = key_chunks(tb)
        for chunks, row in ((near, h), (far, 2 + h)):
            for c in chunks:
                keys = slice(c * TB, (c + 1) * TB)
                gp = gp_ref[u % 2, keys, :] - dot_ref[row : row + 1, cols]
                ds_ref[h, keys, cols] = (e_ref[h, keys, cols].astype(F32) * gp).astype(BF16)
        if tb % 2 == 0:
            ds_ref[h, MEM + (tb + 1) * TB : MEM + (tb + 2) * TB, cols] = jnp.zeros((TB, TB), BF16)
        dq = nn(kt_ref[head_rows, near_rows(tb)], ds_ref[h, near_rows(tb), cols])
        dq = dq + nn(kt_ref[head_rows, far_rows], ds_ref[h, far_rows, cols])
        dqt_ref[head_rows, cols] = dq * (1.0 / math.sqrt(HD))

    def keys_part(h, block):
        keys = slice(block * 2 * TB, (block + 1) * 2 * TB)
        start = 2 * TB if block == 2 else 0
        grad_out = (df_ref if block == 3 else do_ref)[h, :, start:]
        dv = nt(e_ref[h, keys, start:], grad_out)
        dk = nn(ds_ref[h, keys, start:], head_lanes(q_ref[start:, :], h))
        if h == 0:
            dv_acc[keys, :] = dv
            dk_acc[keys, :] = dk
        else:
            dv_ref[keys, :] = (dv_acc[keys, :] + dv).astype(BF16)
            dk_ref[keys, :] = ((dk_acc[keys, :] + dk) * (1.0 / LOG2E)).astype(BF16)

    prepare(0)
    start(0)
    prepare(1)
    for u, (tb, h) in enumerate(units):
        if u + 1 < len(units):
            start(u + 1)
        rows_part(u)
        if h == 1:
            keys_part(0, tb)
    for block in range(4):
        keys_part(1, block)
    dq_ref[...] = dqt_ref[...].T.astype(BF16)


def unattend_kernel(q, k, kt, v, e, gmt, local, fetched, stat, gate, first, count, after=(), alias=()):
    spec_cols = lambda rows: pl.BlockSpec((rows, PAIR), lambda p: (0, p + first))
    spec_rows = lambda cols: pl.BlockSpec((PAIR, cols), lambda p: (p + first, 0))
    return call(
        unattend_body,
        (count,),
        [
            spec_cols(LEN),
            spec_cols(ROWS),
            spec_rows(ROWS),
            spec_cols(ROWS),
            pl.BlockSpec((2, ROWS, LEN), lambda p: (p + first, 0, 0)),
            spec_rows(LEN),
            spec_rows(LEN),
            spec_rows(LEN),
            pl.BlockSpec((1, 8, LEN), lambda p: (p + first, 0, 0)),
            pl.BlockSpec((1, 2, LEN), lambda p: (p + first, 0, 0)),
        ],
        [
            spec_cols(LEN),
            spec_cols(ROWS),
            spec_cols(ROWS),
            pl.BlockSpec((1, 2, LEN), lambda p: (p + first, 0, 0)),
        ],
        [
            sds((LEN, D), BF16),
            sds((ROWS, D), BF16),
            sds((ROWS, D), BF16),
            sds((NPAIR, 2, LEN), F32),
        ],
        count * 10e9,
        count * 14e6,
        "unattend",
        scratch=[
            pltpu.VMEM((2, ROWS, LEN), BF16),
            pltpu.VMEM((2, PAIR, LEN), BF16),
            pltpu.VMEM((2, PAIR, LEN), BF16),
            pltpu.VMEM((8, LEN), F32),
            pltpu.VMEM((PAIR, LEN), F32),
            pltpu.VMEM((ROWS, PAIR), F32),
            pltpu.VMEM((ROWS, PAIR), F32),
            pltpu.VMEM((2, ROWS, TB), F32),
        ],
        after=after,
        alias=alias,
        vmem=44 * 1024 * 1024,
    )(q, k, kt, v, e, gmt, local, fetched, stat, gate)


def all_heads(gl_ref):
    return jnp.concatenate([gl_ref[p] for p in range(NPAIR)], axis=0).astype(BF16)


def proj_grads_body(xt_ref, dq_ref, dk_ref, dv_ref, gl_ref, g_ref, gate_ref):
    g_ref[0] = nn(xt_ref[:, MEM:CTX], dq_ref[...]).astype(BF16)
    g_ref[1] = nn(xt_ref[...], dk_ref[...]).astype(BF16)
    g_ref[2] = nn(xt_ref[...], dv_ref[...]).astype(BF16)

    @pl.when(pl.program_id(0) == 0)
    def _():
        gate_ref[...] = nt(all_heads(gl_ref), xt_ref[:, MEM:CTX])


def proj_grads_kernel(xt, dq, dk, dv, gl, place=None, chips=0, planes=0, after=()):
    steps = 2
    fast = place is not None
    wide = lambda rows: pl.BlockSpec((rows, D // steps), lambda i, *_: (0, i))
    in_specs = [whole((D, ROWS)), wide(LEN), wide(ROWS), wide(ROWS), whole((NPAIR, 2, LEN))]
    gate_spec, gate_shape = whole((H, D)), sds((H, D), F32)
    flops, nbytes = 8e9, 10e6
    if not fast:
        return call(
            proj_grads_body,
            (steps,),
            in_specs,
            [pl.BlockSpec((3, D, D // steps), lambda i: (0, 0, i)), gate_spec],
            [sds((3, D, D), BF16), gate_shape],
            flops,
            nbytes,
            "proj_grads",
        )(xt, dq, dk, dv, gl)
    own_rows, own_cols, group = D // (2 * chips), D // planes, planes // steps

    def body(place_ref, xt_ref, dq_ref, dk_ref, dv_ref, gl_ref, keep_ref, send_ref, gate_ref, all_ref):
        proj_grads_body(xt_ref, dq_ref, dk_ref, dv_ref, gl_ref, all_ref, gate_ref)
        for b in range(group):
            col = b ^ (place_ref[2] % group)
            cols = slice(b * own_cols, (b + 1) * own_cols)
            for chip in range(chips):
                slot = place_ref[0] ^ chip
                for j in range(3):
                    here = slice(j * own_rows, (j + 1) * own_rows)
                    keep_ref[slot, col, here, :] = all_ref[j, part(chip * 2 + place_ref[1], own_rows), cols]
                    send_ref[slot, col, here, :] = all_ref[j, part(chip * 2 + 1 - place_ref[1], own_rows), cols]

    out = pl.BlockSpec(
        (chips, group, 3 * own_rows, own_cols), lambda i, place_ref: (0, i ^ (place_ref[2] // group), 0, 0)
    )
    shape = sds((chips, planes, 3 * own_rows, own_cols), BF16)
    return call(
        body,
        (steps,),
        in_specs,
        [out, out, gate_spec],
        [shape, shape, gate_shape],
        flops,
        nbytes,
        "proj_grads",
        scratch=[pltpu.VMEM((3, D, D // steps), BF16)],
        prefetch=1,
        after=after,
        vmem=24 * 1024 * 1024,
    )(place, xt, dq, dk, dv, gl)


def input_body(dq_ref, dk_ref, dv_ref, gl_ref, w_ref, tok_ref, mem_ref, vec_ref, gres_ref, gin_ref, gain_ref):
    i = pl.program_id(0)
    gn = nt(dk_ref[...], w_ref[1]) + nt(dv_ref[...], w_ref[2])

    @pl.when(i < MC)
    def _():
        wide = mem_ref[...].astype(F32)
        part = jnp.sum(gn * (wide * rms_factor(wide)), axis=0, keepdims=True)

        @pl.when(i == 0)
        def _():
            gain_ref[...] = part

        @pl.when(i > 0)
        def _():
            gain_ref[...] += part

    @pl.when(i >= MC)
    def _():
        wide = tok_ref[...].astype(F32)
        factor = rms_factor(wide)
        hat = wide * factor
        full = gn + nt(dq_ref[...], w_ref[0]) + tn(all_heads(gl_ref), vec_ref[2:10, :].astype(BF16))
        gain_ref[...] += jnp.sum(full * hat, axis=0, keepdims=True)
        scaled = full * vec_ref[0:1, :]
        gin_ref[...] = (
            gres_ref[...] + factor * (scaled - hat * jnp.mean(scaled * hat, axis=-1, keepdims=True))
        ).astype(BF16)


def input_kernel(dq, dk, dv, gl, w, tokens, memory, vectors, gres, after=()):
    tok = lambda i: jnp.clip(i - MC, 0, NT - 1)
    rows = pl.BlockSpec((TB, D), lambda i: (tok(i), 0))
    return call(
        input_body,
        (MC + NT,),
        [
            rows,
            pl.BlockSpec((TB, D), lambda i: (i, 0)),
            pl.BlockSpec((TB, D), lambda i: (i, 0)),
            pl.BlockSpec((NPAIR, 2, TB), lambda i: (0, 0, tok(i))),
            whole((3, D, D)),
            rows,
            pl.BlockSpec((TB, D), lambda i: (jnp.minimum(i, MC - 1), 0)),
            whole((2 + H, D)),
            rows,
        ],
        [rows, whole((1, D))],
        [sds((LEN, D), BF16), sds((1, D), F32)],
        9e9,
        10e6,
        "input",
        after=after,
        vmem=SMALL,
    )(dq, dk, dv, gl, w, tokens, memory, vectors, gres)


def exchange(slots, axis):
    size = len(slots)
    return [slots[0]] + [
        lax.ppermute(slots[r], axis, [(i, i ^ r) for i in range(size)]) for r in range(1, size)
    ]


def added(parts):
    total = parts[0].astype(F32)
    for other in parts[1:]:
        total = total + other.astype(F32)
    return total


PLANES = (("up",), ("q", "k"), ("v", "o"), ("down",))
EXTRA = 16


def alone(body, operands, out_shape, name, scratch=(), place=None, after=(), flops=2e9, vmem=SMALL):
    specs = [whole(x.shape) for x in operands]
    if place is not None:
        specs, operands = [SMEM] + specs, (place, *operands)
    return call(
        body,
        (1,),
        specs,
        [whole(x.shape) for x in out_shape],
        out_shape,
        flops,
        2e6,
        name,
        scratch=scratch,
        after=after,
        vmem=vmem,
    )(*operands)


def payloads_kernel(place, attn_weights, up_weights, down_weights, attn_moment, up_moment, down_moment):
    rows, cols = attn_weights.shape[1:]
    wide = up_weights.shape[1]
    planes = len(PLANES)
    width = cols + 3 * wide

    def body(place_ref, aw_ref, uw_ref, dw_ref, am_ref, um_ref, dm_ref, first_ref, *rest):
        outs, all_ref = rest[:planes], rest[planes]
        for j in range(3):
            first_ref[j * rows : (j + 1) * rows, :] = aw_ref[j].astype(BF16)
        all_ref[...] = jnp.zeros(all_ref.shape, BF16)
        all_ref[0] = um_ref[...].astype(BF16)
        all_ref[3] = dm_ref[...].astype(BF16)
        for j in range(4):
            all_ref[1 + j // 2, :, (j % 2) * cols : (j % 2 + 1) * cols] = am_ref[j].astype(BF16)
        for r in range(planes):
            outs[r][:, :cols] = aw_ref[3].astype(BF16)
            outs[r][:, cols : cols + wide] = uw_ref[...].astype(BF16)
            outs[r][:, cols + wide : cols + 2 * wide] = dw_ref[...].astype(BF16)
            outs[r][:, cols + 2 * wide :] = all_ref[place_ref[2] ^ r]

    first, *second = alone(
        body,
        (attn_weights, up_weights, down_weights, attn_moment, up_moment, down_moment),
        [sds((3 * rows, cols), BF16)] + [sds((rows, width), BF16)] * planes,
        "payloads",
        scratch=[pltpu.VMEM((planes, rows, wide), BF16)],
        place=place,
        vmem=VMEM_LIMIT,
    )
    return first, second


def stacked_pair(parts, width):
    rows = parts[0].shape[0]
    other = parts[0].shape[1] - width

    def body(*refs):
        for r in range(len(parts)):
            refs[-2][r] = refs[r][:, :width]
            refs[-1][r] = refs[r][:, width:]

    shapes = [sds((len(parts), rows, width), BF16), sds((len(parts), rows, other), BF16)]
    return alone(body, parts, shapes, "stacked_pair")


def stacked(parts, after=()):
    def body(*refs):
        for r in range(len(parts)):
            refs[-1][r] = refs[r][...]

    return alone(body, parts, [sds((len(parts),) + parts[0].shape, parts[0].dtype)], "stacked", after=after)[0]


def core_blocks(plane):
    return plane + [exchange([b, b], "core")[1] for b in plane]


def fold_cores(keep, other):
    chips, planes, rows, width = keep.shape

    def body(keep_ref, other_ref, *outs):
        for chip in range(chips):
            outs[chip][...] = added([keep_ref[chip], other_ref[chip]]).astype(BF16)

    spec = pl.BlockSpec((chips, 1, rows, width), lambda i: (0, i, 0, 0))
    return call(
        body,
        (planes,),
        [spec, spec],
        [pl.BlockSpec((1, rows, width), lambda i: (i, 0, 0))] * chips,
        [sds((planes, rows, width), BF16)] * chips,
        4e9,
        7e6,
        "fold_cores",
        vmem=SMALL,
    )(keep, other)


def fold_chips(parts):
    planes, rows, width = parts[0].shape

    def body(*refs):
        for plane in range(planes):
            refs[len(parts) + plane][...] = added([r[plane] for r in refs[: len(parts)]]).astype(BF16)

    return alone(body, parts, [sds((rows, width), BF16)] * planes, "fold_chips")


VEC = 2 + H
VEC_ROWS = 128


def put_vectors(ref, first, values):
    high = values.astype(BF16)
    low = (values - high.astype(F32)).astype(BF16)
    ref[first : first + VEC_ROWS, :] = jnp.zeros((VEC_ROWS, 128), BF16)
    for j in range(4):
        lanes = slice(j * 128, (j + 1) * 128)
        ref[first + j * 16 : first + j * 16 + VEC, :] = high[:, lanes]
        ref[first + 64 + j * 16 : first + 64 + j * 16 + VEC, :] = low[:, lanes]


def get_vectors(refs, first):
    pieces = []
    for j in range(4):
        rows = lambda offset: slice(first + offset + j * 16, first + offset + j * 16 + VEC)
        pieces.append(added([r[rows(offset), :] for r in refs for offset in (0, 64)]))
    return jnp.concatenate(pieces, axis=1)


def fold_cores_first(keep, other):
    chips = keep.shape[0]

    def body(keep_ref, other_ref, *outs):
        for chip in range(chips):
            outs[chip][...] = added([keep_ref[chip], other_ref[chip]]).astype(BF16)

    return alone(body, (keep, other), [sds(keep.shape[1:], BF16)] * chips, "fold_cores_first")


def fold_chips_first(parts, gain_attn, gain_ffn, grad_gate):
    planes, rows, width = parts[0].shape
    count = len(parts)

    def body(*refs):
        ins, (ga_ref, gf_ref, gg_ref) = refs[:count], refs[count : count + 3]
        outs, vec_ref = refs[count + 3 : -1], refs[-1]
        vec_ref[0:1, :] = ga_ref[...]
        vec_ref[1:2, :] = gf_ref[...]
        vec_ref[2:VEC, :] = gg_ref[...]
        for plane in range(planes):
            outs[plane][:rows, :] = added([r[plane] for r in ins]).astype(BF16)
            put_vectors(outs[plane], rows, vec_ref[...])

    return alone(
        body,
        (*parts, gain_attn, gain_ffn, grad_gate),
        [sds((rows + VEC_ROWS, width), BF16)] * planes,
        "fold_chips_first",
        scratch=[pltpu.VMEM((VEC, D), F32)],
    )


VEC_TILE = 32


def stack_with_vectors(parts, vec):
    count, (rows, width) = len(parts), parts[0].shape

    def body(*refs):
        vec_ref, out_ref = refs[count], refs[count + 1]
        for r in range(count):
            out_ref[r * rows : (r + 1) * rows, :] = refs[r][...]
        values = vec_ref[...]
        high = values.astype(BF16)
        out_ref[count * rows :, :] = jnp.zeros((VEC_TILE, width), BF16)
        out_ref[count * rows : count * rows + VEC, :] = high
        out_ref[count * rows + 16 : count * rows + 16 + VEC, :] = (values - high.astype(F32)).astype(BF16)

    return alone(
        body, (*parts, vec), [sds((count * rows + VEC_TILE, width), BF16)], "stack_with_vectors"
    )[0]


def owned_kernel(place, parts_a, parts_b):
    planes = len(parts_a)
    size, cols = parts_a[0].shape[0] - VEC_ROWS, parts_a[0].shape[1]
    rows, width = parts_b[0].shape
    wide = (width - cols) // 2

    def body(place_ref, *refs):
        a_refs, b_refs = refs[:planes], refs[planes : 2 * planes]
        ga_ref, gb_ref, vec_ref, *rest = refs[2 * planes :]
        slots, all_ref = rest[:planes], rest[planes]
        ga = added([r[:size, :] for r in a_refs])
        gb = added([r[...] for r in b_refs])
        ga_ref[...] = ga
        gb_ref[...] = gb
        vec_ref[...] = get_vectors(a_refs, size)
        squares = jnp.sum(ga * ga, keepdims=True) + jnp.sum(gb * gb, keepdims=True)
        all_ref[...] = jnp.zeros(all_ref.shape, BF16)
        for j in range(4):
            grad = ga[j * rows : (j + 1) * rows, :] if j < 3 else gb[:, :cols]
            all_ref[1 + j // 2, :, (j % 2) * cols : (j % 2 + 1) * cols] = grad.astype(BF16)
        all_ref[0] = gb[:, cols : cols + wide].astype(BF16)
        all_ref[3] = gb[:, cols + wide :].astype(BF16)
        wide_squares = squares + jnp.zeros((EXTRA, wide), F32)
        row = lax.broadcasted_iota(jnp.int32, (EXTRA, wide), 0)
        high = wide_squares.astype(BF16).astype(F32)
        middle = (wide_squares - high).astype(BF16).astype(F32)
        low = wide_squares - high - middle
        extra = jnp.where(row == 0, high, jnp.where(row == 1, middle, jnp.where(row == 2, low, 0.0))).astype(BF16)
        for r in range(planes):
            slots[r][:rows, :] = all_ref[place_ref[2] ^ r]
            slots[r][rows:, :] = extra

    return alone(
        body,
        (*parts_a, *parts_b),
        [sds((size, cols), F32), sds((rows, width), F32), sds((VEC, D), F32)]
        + [sds((rows + EXTRA, wide), BF16)] * planes,
        "owned",
        scratch=[pltpu.VMEM((planes, rows, wide), BF16)],
        place=place,
    )


def orthogonal_kernel(place, grads, moments, vectors, vec_moment):
    count = len(grads)
    chips = count // 2
    planes, rows = moments[0].shape[:2]
    wide = grads[0].shape[1]
    slot_rows = rows + EXTRA
    cols = D // planes
    limit = clip_fraction * math.sqrt(PARAMS)

    def body(place_ref, *refs):
        grad_refs, moment_refs, refs = refs[:count], refs[count : 2 * count], refs[2 * count :]
        vec_ref, vm_ref, norm_ref, vn_ref, vmn_ref = refs[:5]
        outs = refs[5 : 5 + planes]
        low_ref, x_ref, mix_ref, diag_ref, all_ref = refs[5 + planes :]
        pair = (place_ref[2] == 1) | (place_ref[2] == 2)
        own = part(place_ref[0] * 2 + place_ref[1], rows)
        vec_first = planes * slot_rows
        grad_vec = jnp.zeros((VEC, D), F32)
        squares = jnp.zeros((EXTRA, wide), F32)
        for b in range(count):
            for plane in range(planes):
                squares = squares + grad_refs[b][plane * slot_rows + rows : (plane + 1) * slot_rows, :].astype(F32)
            for first in (vec_first, vec_first + 16):
                grad_vec = grad_vec + grad_refs[b][first : first + VEC, :].astype(F32)
        total = jnp.sum(squares[:, 0:1], axis=0, keepdims=True) + jnp.sum(grad_vec * grad_vec, keepdims=True)
        norm = jnp.sqrt(total)
        norm_ref[...] = norm
        clip = limit / jnp.maximum(norm, limit)
        vec_mom = vector_decay * vm_ref[...] + clip * grad_vec
        vmn_ref[...] = vec_mom
        vn_ref[...] = vec_ref[...] - vector_rate * vec_mom

        def momentum(core, chip, plane, lanes):
            b = core * chips + chip
            moment = moment_refs[b][plane, :, lanes].astype(F32)
            grad = grad_refs[b][plane * slot_rows : plane * slot_rows + rows, lanes].astype(F32)
            return muon_decay * moment + clip * grad

        def gram_of(start, width):
            half = D // 2
            upper, lower = low_ref[:half, start : start + width], low_ref[half:, start : start + width]
            corner = nt(lower, upper)
            first = jnp.concatenate([nt(upper, upper), corner.T], axis=1)
            return jnp.concatenate([first, jnp.concatenate([corner, nt(lower, lower)], axis=1)], axis=0)

        def mixing(gram):
            eye = lax.broadcasted_iota(jnp.int32, (D, D), 0) == lax.broadcasted_iota(jnp.int32, (D, D), 1)
            low = gram.astype(BF16)
            mix = coef_second * low.astype(F32) + coef_third * nn(low, low)
            diag_ref[...] = coef_first + jnp.sum(jnp.where(eye, mix, 0.0), axis=1, keepdims=True)
            mix_ref[...] = jnp.where(eye, 0.0, mix).astype(BF16)

        def advance(start, width, scale):
            for c in range(start, start + width, D):
                lanes = slice(c, c + D)
                new = diag_ref[...] * x_ref[:, lanes] + nn(mix_ref[...], low_ref[:, lanes])
                if scale is not None:
                    new = new * scale
                x_ref[:, lanes] = new
                low_ref[:, lanes] = new.astype(BF16)

        def first_step(start, width):
            gram = gram_of(start, width)
            eye = lax.broadcasted_iota(jnp.int32, (D, D), 0) == lax.broadcasted_iota(jnp.int32, (D, D), 1)
            scale = 1.0 / (jnp.sqrt(jnp.sum(jnp.where(eye, gram, 0.0), keepdims=True)) + 1e-07)
            mixing(gram * (scale * scale))
            advance(start, width, scale)

        def step(start, width, last):
            mixing(gram_of(start, width))
            if not last:
                advance(start, width, None)
                return
            for c in range(start, start + width, D):
                lanes = slice(c, c + D)
                x_ref[own, lanes] = diag_ref[own, :] * x_ref[own, lanes] + nn(mix_ref[own, :], low_ref[:, lanes])

        def iterations(ranges):
            for start, width in ranges:
                first_step(start, width)

            def middle(_, carry):
                for start, width in ranges:
                    step(start, width, False)
                return carry

            lax.fori_loop(1, NS_ITERS - 1, middle, 0)
            for start, width in ranges:
                step(start, width, True)

        @pl.when(pair)
        def _():
            for core, chip, plane, row, col in each_block(place_ref, chips, planes):
                for j in range(2):
                    new = momentum(core, chip, plane, slice(j * cols, (j + 1) * cols))
                    x_ref[part(row, rows), part(col + j * planes, cols)] = new
                    low_ref[part(row, rows), part(col + j * planes, cols)] = new.astype(BF16)
            iterations([(0, D), (D, D)])
            for plane in range(planes):
                for j in range(2):
                    first = j * D + plane * cols
                    all_ref[plane, :, j * cols : (j + 1) * cols] = x_ref[own, first : first + cols].astype(BF16)

        @pl.when(jnp.logical_not(pair))
        def _():
            for core, chip, plane, row, col in each_block(place_ref, chips, planes):
                new = momentum(core, chip, plane, slice(0, wide))
                x_ref[part(row, rows), part(col, wide)] = new
                low_ref[part(row, rows), part(col, wide)] = new.astype(BF16)
            iterations([(0, FF)])
            for plane in range(planes):
                all_ref[plane] = x_ref[own, plane * wide : (plane + 1) * wide].astype(BF16)

        for r in range(planes):
            outs[r][...] = all_ref[place_ref[2] ^ r]

    return alone(
        body,
        (*grads, *moments, vectors, vec_moment),
        [sds((1, 1), F32), sds((VEC, D), F32), sds((VEC, D), F32)] + [sds((rows, wide), BF16)] * planes,
        "orthogonal",
        scratch=[
            pltpu.VMEM((D, FF), BF16),
            pltpu.VMEM((D, FF), F32),
            pltpu.VMEM((D, D), BF16),
            pltpu.VMEM((D, 1), F32),
            pltpu.VMEM((planes, rows, wide), BF16),
        ],
        place=place,
        flops=18e9,
        vmem=VMEM_LIMIT,
    )


def update_kernel(place, slots, norm, ga, gb, attn_moment, up_moment, down_moment, attn_weights, up_weights, down_weights):
    planes = len(slots)
    rows, cols = attn_weights.shape[1:]
    wide = up_weights.shape[1]
    shape_factor = math.sqrt(max(1.0, FF / D))
    limit = clip_fraction * math.sqrt(PARAMS)

    def body(place_ref, *refs):
        slot_refs, refs = refs[:planes], refs[planes:]
        norm_ref, ga_ref, gb_ref, am_ref, um_ref, dm_ref, aw_ref, uw_ref, dw_ref = refs[:9]
        an_ref, un_ref, dn_ref, amn_ref, umn_ref, dmn_ref, all_ref = refs[9:]
        clip = limit / jnp.maximum(norm_ref[...], limit)
        for r in range(planes):
            all_ref[place_ref[2] ^ r] = slot_refs[r][...]
        for j in range(4):
            ortho = all_ref[1 + j // 2, :, (j % 2) * cols : (j % 2 + 1) * cols].astype(F32)
            an_ref[j] = aw_ref[j] - muon_rate * ortho
            grad = ga_ref[j * rows : (j + 1) * rows, :] if j < 3 else gb_ref[:, :cols]
            amn_ref[j] = muon_decay * am_ref[j] + clip * grad
        un_ref[...] = uw_ref[...] - muon_rate * all_ref[0].astype(F32)
        umn_ref[...] = muon_decay * um_ref[...] + clip * gb_ref[:, cols : cols + wide]
        dn_ref[...] = dw_ref[...] - muon_rate * shape_factor * all_ref[3].astype(F32)
        dmn_ref[...] = muon_decay * dm_ref[...] + clip * gb_ref[:, cols + wide :]

    weights = (attn_weights, up_weights, down_weights)
    return alone(
        body,
        (*slots, norm, ga, gb, attn_moment, up_moment, down_moment, *weights),
        [sds(x.shape, F32) for x in weights] * 2,
        "update",
        scratch=[pltpu.VMEM((planes,) + slots[0].shape, BF16)],
        place=place,
    )


def documents(starts):
    doc = jnp.cumsum(starts).astype(F32)
    return doc.reshape(1, LEN), doc.reshape(LEN, 1)


def plain_tail(sizes, grads, attn_weights, up_weights, down_weights, vectors, attn_moment, up_moment, down_moment, vec_moment):
    dp = ("chip", "core")
    grad_attn, grad_up, grad_down, grad_vectors = grads

    def owned(grad, narrow_dim, dp_dim):
        part_sum = lax.psum_scatter(grad.astype(BF16), "narrow", scatter_dimension=narrow_dim, tiled=True)
        return lax.psum_scatter(part_sum, dp, scatter_dimension=dp_dim, tiled=True).astype(F32)

    owned_attn, owned_up, owned_down = owned(grad_attn, 2, 1), owned(grad_up, 1, 0), owned(grad_down, 0, 1)
    own_squares = jnp.sum(owned_attn * owned_attn) + jnp.sum(owned_up * owned_up) + jnp.sum(owned_down * owned_down)
    vector_sum, square_sum = lax.psum((grad_vectors, own_squares), ("chip", "core", "narrow"))
    grad_norm = jnp.sqrt(square_sum + jnp.sum(vector_sum * vector_sum))
    clip_limit = clip_fraction * math.sqrt(PARAMS)
    clip_factor = clip_limit / jnp.maximum(grad_norm, clip_limit)
    attn_mom_new = muon_decay * attn_moment + clip_factor * owned_attn
    up_mom_new = muon_decay * up_moment + clip_factor * owned_up
    down_mom_new = muon_decay * down_moment + clip_factor * owned_down
    gather = lambda x, dim: lax.all_gather(x.astype(BF16), dp, axis=dim, tiled=True).astype(F32)
    ortho = (gather(attn_mom_new, 1), gather(up_mom_new, 0), gather(down_mom_new, 1))
    ortho_attn, ortho_up, ortho_down = ortho
    for iteration in range(NS_ITERS):
        gram_attn = jnp.einsum("imc,inc->imn", ortho_attn, ortho_attn, precision=highest)
        gram_up = lax.dot_general(ortho_up, ortho_up, (((1,), (1,)), ((), ())), precision=highest)
        gram_down = lax.dot_general(ortho_down, ortho_down, (((0,), (0,)), ((), ())), precision=highest)
        partial_grams = jnp.concatenate([gram_attn, gram_up[None], gram_down[None]], axis=0)
        gram_total = lax.psum(partial_grams.astype(BF16), "narrow").astype(F32)
        if iteration == 0:
            norm_scales = 1.0 / (jnp.sqrt(jnp.trace(gram_total, axis1=1, axis2=2)) + 1e-07)
            ortho_attn = ortho_attn * norm_scales[:4, None, None]
            ortho_up = ortho_up * norm_scales[4]
            ortho_down = ortho_down * norm_scales[5]
            gram_total = gram_total * (norm_scales * norm_scales)[:, None, None]
        once = jnp.einsum("imn,inc->imc", gram_total[:4], ortho_attn, precision=highest)
        twice = jnp.einsum("imn,inc->imc", gram_total[:4], once, precision=highest)
        ortho_attn = coef_first * ortho_attn + coef_second * once + coef_third * twice
        once = jnp.dot(gram_total[4], ortho_up, precision=highest)
        twice = jnp.dot(gram_total[4], once, precision=highest)
        ortho_up = coef_first * ortho_up + coef_second * once + coef_third * twice
        once = jnp.dot(ortho_down, gram_total[5], precision=highest)
        twice = jnp.dot(once, gram_total[5], precision=highest)
        ortho_down = coef_first * ortho_down + coef_second * once + coef_third * twice
    row_share = D // sizes["dp"]
    row_start = lax.axis_index(dp) * row_share
    final_attn = lax.dynamic_slice_in_dim(ortho_attn, row_start, row_share, 1)
    final_up = lax.dynamic_slice_in_dim(ortho_up, row_start, row_share, 0)
    final_down = lax.dynamic_slice_in_dim(ortho_down, row_start, row_share, 1)
    shape_factor = math.sqrt(max(1.0, FF / D))
    vector_mom_new = vector_decay * vec_moment + clip_factor * vector_sum
    return (
        attn_weights - muon_rate * final_attn,
        up_weights - muon_rate * final_up,
        down_weights - muon_rate * shape_factor * final_down,
        attn_mom_new,
        up_mom_new,
        down_mom_new,
        vectors - vector_rate * vector_mom_new,
        vector_mom_new,
        grad_norm,
    )


def per_device(
    sizes,
    tokens, memory, neighbour_bank, starts, neighbours, cotangent,
    attn_weights, up_weights, down_weights, vectors,
    attn_moment, up_moment, down_moment, vector_moment,
):
    memory = memory.reshape(MEM, D)
    bank = neighbour_bank.reshape(BANK, D)
    own = (attn_weights, up_weights, down_weights)
    moments = (attn_moment, up_moment, down_moment)
    chips, planes = sizes["dp"] // 2, sizes["narrow"]
    if planes == len(PLANES) and chips == 4:
        return fast_device(
            chips, planes, tokens, memory, bank, starts, neighbours, cotangent, own, vectors, moments, vector_moment
        )
    full = lambda x, narrow_dim, dp_dim: lax.all_gather(
        lax.all_gather(x.astype(BF16), ("chip", "core"), axis=dp_dim, tiled=True), "narrow", axis=narrow_dim, tiled=True
    )
    attn_full = full(attn_weights, 2, 1)
    second = [attn_full[3], full(up_weights, 1, 0), full(down_weights, 0, 1).T]
    x, xt, cot_t, gate = context_kernel(tokens, memory, bank, cotangent, vectors)
    doc_row, doc_col = documents(starts)
    bias_tok, bias_bank = mask_kernel(doc_row, doc_col, neighbours.T)
    w, q, k, v, qt, kt, vt, qn, kn = project_kernel(x, attn_full[:3])
    e, local, fetched, stat, mixed, mixed_t = attend_kernel(qt, k, vt, qn, kn, bias_tok, bias_bank, doc_row, gate, 0, NPAIR)
    out, act, gh, ffn_t, branch, gres, gmt, gain_ffn = feed_kernel(mixed, tokens, cotangent, vectors, second)
    grad_down_t, grad_up, grad_o = feed_grads_kernel(cot_t, act, ffn_t, gh, mixed_t, branch)
    dq, dk, dv, gl = unattend_kernel(q, k, kt, v, e, gmt, local, fetched, stat, gate, 0, NPAIR)
    grad_qkv, grad_gate = proj_grads_kernel(xt, dq, dk, dv, gl)
    grad_in, gain_attn = input_kernel(dq, dk, dv, gl, w, tokens, memory, vectors, gres)
    grad_vectors = jnp.concatenate([gain_attn, gain_ffn, grad_gate], axis=0)
    grads = (jnp.concatenate([grad_qkv, grad_o[None]], axis=0), grad_up, grad_down_t.T, grad_vectors)
    return (out, grad_in) + plain_tail(sizes, grads, *own, vectors, *moments, vector_moment)


def ordered(first, second):
    return lax.optimization_barrier((first, second))[0]


def fast_device(
    chips, planes, tokens, memory, bank, starts, neighbours, cotangent, own, vectors, moments, vector_moment
):
    own, moments = own[:2] + (own[2].T,), moments[:2] + (moments[2].T,)
    place = jnp.stack([lax.axis_index("chip"), lax.axis_index("core"), lax.axis_index("narrow")]).astype(jnp.int32)
    payload, payloads = payloads_kernel(place, *own, *moments)
    near_a = exchange([payload] * planes, "narrow")
    doc_row, doc_col = documents(starts)
    near_t = ordered(neighbours.T, payload)
    near_b = exchange(ordered(payloads, near_a), "narrow")
    column_a = stacked(near_a)
    plane_a = exchange([column_a] * chips, "chip")
    x, xt, cot_t, gate = context_kernel(tokens, memory, bank, cotangent, vectors, after=[column_a])
    bias_tok, bias_bank = mask_kernel(doc_row, doc_col, near_t, after=[x])
    first = core_blocks(ordered(plane_a, bias_tok))
    column_b, column_m = stacked_pair(ordered(near_b, first), payloads[0].shape[1] - own[1].shape[1])
    w, q, k, v, qt, kt, vt, qn, kn = project_kernel(x, first, place, after=[column_b])
    plane_b = exchange([column_b] * chips, "chip")
    e, local, fetched, stat, mixed, mixed_t = attend_kernel(qt, k, vt, qn, kn, bias_tok, bias_bank, doc_row, gate, 0, NPAIR)
    second = core_blocks(ordered(plane_b, mixed))
    plane_m = exchange([ordered(column_m, second)] * chips, "chip")
    out, gres, gmt, gain_ffn, keep_b, send_b = feed_blocks(
        mixed, mixed_t, tokens, cotangent, cot_t, vectors, second, place
    )
    plane_m = ordered(plane_m, keep_b)
    back = (q, k, kt, v, e, gmt, local, fetched, stat, gate)
    some = unattend_kernel(*back, 0, 1, after=[keep_b])
    slots_b = fold_cores(keep_b, ordered(exchange([send_b, send_b], "core")[1], some[0]))
    all_m = core_blocks(plane_m)
    dq, dk, dv, gl = unattend_kernel(*back, 1, NPAIR - 1, after=[slots_b[0], *all_m[4:]], alias=some)
    slots_b = fold_chips(ordered(exchange(slots_b, "chip"), dq))
    keep_a, send_a, grad_gate = proj_grads_kernel(xt, dq, dk, dv, gl, place, chips, planes, after=[slots_b[0]])
    slots_a = fold_cores_first(keep_a, exchange([send_a, send_a], "core")[1])
    grad_in, gain_attn = input_kernel(dq, dk, dv, gl, w, tokens, memory, vectors, gres, after=[slots_a[0]])
    parts_a = exchange(slots_a, "chip")
    parts_b = exchange(ordered(slots_b, slots_a), "narrow")
    parts_b, parts_a = ordered((parts_b, parts_a), grad_in)
    slots_a = fold_chips_first(parts_a, gain_attn, gain_ffn, grad_gate)
    parts_a = exchange(slots_a, "narrow")
    ga, gb, vec, *slots = owned_kernel(place, parts_a, parts_b)
    grads = core_blocks(exchange([stack_with_vectors(exchange(slots, "narrow"), vec)] * chips, "chip"))
    norm, vec_new, vec_mom, *slots = orthogonal_kernel(place, grads, all_m, vectors, vector_moment)
    final = exchange(slots, "narrow")
    new = list(update_kernel(place, final, norm, ga, gb, *moments, *own))
    new[2], new[5] = new[2].T, new[5].T
    return (out, grad_in, *new, vec_new, vec_mom, norm.reshape(()))


def solution(mesh):
    sizes = dict(mesh.shape)
    split = Mesh(
        mesh.devices.reshape(sizes["dp"] // 2, 2, sizes["narrow"]), ("chip", "core", "narrow")
    )
    dp = ("chip", "core")
    rows = ("chip", "core", "narrow")
    weights = (P(None, dp, "narrow"), P(dp, "narrow"), P("narrow", dp))
    return jax.shard_map(
        lambda *operands: per_device(sizes, *operands),
        mesh=split,
        in_specs=(P(rows, None), P(rows, None, None), P(rows, None, None), P(rows), P(rows, None), P(rows, None))
        + weights + (P(),) + weights + (P(),),
        out_specs=(P(rows, None), P(rows, None)) + weights + weights + (P(), P(), P()),
        check_vma=False,
    )
```

```python
import math

import jax
import jax.numpy as jnp
from jax import lax
from jax.experimental import pallas as pl
from jax.experimental.pallas import tpu as pltpu
from jax.sharding import Mesh, PartitionSpec as P

D = 512
H = 8
FF = 2048
MEM = 512
BANK = 512
KNB = 4
LEN = 1024
CTX = MEM + LEN
ROWS = CTX + BANK
HD = D // H
TB = 256
NT = LEN // TB
MC = MEM // TB
BC = BANK // TB
PAIR = 2 * HD
NPAIR = D // PAIR
F32 = jnp.float32
BF16 = jnp.bfloat16
NS_ITERS = 5
PARAMS = 3150848
epsilon = 1e-06
masked_score = -1e30
coef_first = 3.4445
coef_second = -4.775
coef_third = 2.0315
clip_fraction = 0.05
muon_rate = 0.5
muon_decay = 0.5
vector_rate = 0.5
vector_decay = 0.9
highest = lax.Precision.HIGHEST
LOG2E = 1.4426950408889634
SAFE = 80.0
VMEM_LIMIT = 60 * 1024 * 1024
SMALL = 16 * 1024 * 1024


def nn(a, b):
    return lax.dot_general(a, b, (((1,), (0,)), ((), ())), preferred_element_type=F32)


def nt(a, b):
    return lax.dot_general(a, b, (((1,), (1,)), ((), ())), preferred_element_type=F32)


def tn(a, b):
    return lax.dot_general(a, b, (((0,), (0,)), ((), ())), preferred_element_type=F32)


def rms_factor(values):
    return lax.rsqrt(jnp.mean(values * values, axis=-1, keepdims=True) + epsilon)


def whole(shape):
    return pl.BlockSpec(shape, lambda *_: (0,) * len(shape))


def call(
    body, grid, in_specs, out_specs, out_shape, flops, nbytes, name, scratch=(), trans=0, prefetch=0, after=(), alias=(),
    vmem=VMEM_LIMIT,
):
    extra, given = len(after) + len(alias), prefetch + len(in_specs)

    def with_extra(*refs):
        body(*refs[:given], *refs[given + extra :])

    made = pl.pallas_call(
        with_extra,
        grid_spec=pltpu.PrefetchScalarGridSpec(
            num_scalar_prefetch=prefetch,
            grid=grid,
            in_specs=list(in_specs) + [pl.BlockSpec(memory_space=pl.ANY)] * extra,
            out_specs=out_specs,
            scratch_shapes=list(scratch),
        ),
        out_shape=out_shape,
        input_output_aliases={given + len(after) + j: j for j in range(len(alias))},
        name=name,
        cost_estimate=pl.CostEstimate(flops=int(flops), bytes_accessed=int(nbytes), transcendentals=int(trans)),
        compiler_params=pltpu.CompilerParams(
            vmem_limit_bytes=vmem, dimension_semantics=("arbitrary",) * len(grid)
        ),
    )
    return lambda *operands: made(*operands, *after, *alias)


SMEM = pl.BlockSpec(memory_space=pltpu.SMEM)


def sds(shape, dtype):
    return jax.ShapeDtypeStruct(shape, dtype)


def hbm(shape, dtype):
    return pltpu.HBM(shape, dtype)


def vmem(shape, dtype):
    return pltpu.VMEM(shape, dtype)


RESIDENT = pl.BlockSpec(memory_space=pltpu.VMEM)


def context_body(tok_ref, mem_ref, bank_ref, cot_ref, vec_ref, x_ref, xt_ref, cott_ref, gate_ref):
    i = pl.program_id(0)
    gain = vec_ref[0:1, :]

    def put(rows):
        x_ref[...] = rows
        xt_ref[...] = rows.T

    def norm(values):
        wide = values.astype(F32)
        return (wide * rms_factor(wide) * gain).astype(BF16)

    @pl.when(i < MC)
    def _():
        put(norm(mem_ref[...]))

    @pl.when((i >= MC) & (i < MC + NT))
    def _():
        rows = norm(tok_ref[...])
        put(rows)
        logits = nt(vec_ref[2:10, :].astype(BF16), rows)
        gate = jax.nn.sigmoid(logits)
        for p in range(NPAIR):
            gate_ref[p] = gate[2 * p : 2 * p + 2, :]
        cott_ref[...] = cot_ref[...].T

    @pl.when(i >= MC + NT)
    def _():
        put(bank_ref[...])


def context_kernel(tokens, memory, bank, cot, vectors, after=()):
    steps = MC + NT + BC
    clip_tok = lambda i: jnp.clip(i - MC, 0, NT - 1)
    return call(
        context_body,
        (steps,),
        [
            pl.BlockSpec((TB, D), lambda i: (clip_tok(i), 0)),
            pl.BlockSpec((TB, D), lambda i: (jnp.minimum(i, MC - 1), 0)),
            pl.BlockSpec((TB, D), lambda i: (jnp.clip(i - MC - NT, 0, BC - 1), 0)),
            pl.BlockSpec((TB, D), lambda i: (clip_tok(i), 0)),
            whole((2 + H, D)),
        ],
        [
            pl.BlockSpec((TB, D), lambda i: (i, 0)),
            pl.BlockSpec((D, TB), lambda i: (0, i)),
            pl.BlockSpec((D, TB), lambda i: (0, clip_tok(i))),
            pl.BlockSpec((NPAIR, 2, TB), lambda i: (0, 0, clip_tok(i))),
        ],
        [sds((ROWS, D), BF16), hbm((D, ROWS), BF16), sds((D, LEN), BF16), hbm((NPAIR, 2, LEN), F32)],
        8e9,
        8e6,
        "context",
        after=after,
        vmem=SMALL,
    )(tokens, memory, bank, cot, vectors)


def mask_body(doc_row_ref, doc_col_ref, near_ref, tok_ref, bank_ref):
    i = pl.program_id(0)
    doc_row = doc_row_ref[...]

    @pl.when(i < NT)
    def _():
        keys = lax.broadcasted_iota(jnp.int32, (TB, LEN), 0) + i * TB
        rows = lax.broadcasted_iota(jnp.int32, (TB, LEN), 1)
        seen = (keys <= rows) & (doc_col_ref[...] == doc_row)
        tok_ref[...] = jnp.where(seen, 0.0, masked_score)

    @pl.when(i >= NT)
    def _():
        keys = lax.broadcasted_iota(jnp.int32, (TB, LEN), 0) + (i - NT) * TB
        count = jnp.zeros((TB, LEN), F32)
        for j in range(KNB):
            count = count + jnp.where(near_ref[j : j + 1, :] == keys, 1.0, 0.0)
        bias = jnp.where(count > 0.5, 0.0, masked_score)
        for j in range(2, KNB + 1):
            bias = jnp.where(count > j - 0.5, math.log2(j), bias)
        bank_ref[...] = bias


def mask_kernel(doc_row, doc_col, near_t, after=()):
    return call(
        mask_body,
        (NT + BC,),
        [
            whole((1, LEN)),
            pl.BlockSpec((TB, 1), lambda i: (jnp.minimum(i, NT - 1), 0)),
            whole((KNB, LEN)),
        ],
        [
            pl.BlockSpec((TB, LEN), lambda i: (jnp.minimum(i, NT - 1), 0)),
            pl.BlockSpec((TB, LEN), lambda i: (jnp.clip(i - NT, 0, BC - 1), 0)),
        ],
        [vmem((LEN, LEN), F32), vmem((BANK, LEN), F32)],
        6e9,
        7e6,
        "masks",
        after=after,
        vmem=SMALL,
    )(doc_row, doc_col, near_t)


def each_block(place_ref, chips, planes):
    for core in range(2):
        for chip in range(chips):
            row = ((place_ref[0] ^ chip) * 2 + (place_ref[1] ^ core))
            for plane in range(planes):
                yield core, chip, plane, row, place_ref[2] ^ plane


def part(index, size):
    return pl.ds(pl.multiple_of(index * size, size), size)


def head_squares(columns):
    wide = columns.astype(F32)
    return jnp.sum((wide * wide).reshape(H, HD, wide.shape[1]), axis=1)


def project_rows(i, x_ref, w_ref, q_ref, k_ref, v_ref, qt_ref, kt_ref, vt_ref, qn_ref, kn_ref):
    rows = x_ref[...]
    keys = nn(rows, w_ref[1]).astype(BF16)
    values = nn(rows, w_ref[2]).astype(BF16)
    keys_t = keys.T
    k_ref[...] = keys
    v_ref[...] = values
    kt_ref[...] = keys_t
    vt_ref[...] = values.T

    @pl.when(i == 0)
    def _():
        kn_ref[...] = jnp.zeros(kn_ref.shape, F32)
        qn_ref[...] = jnp.zeros(qn_ref.shape, F32)

    kn_ref[...] = jnp.maximum(kn_ref[...], head_squares(keys_t))

    @pl.when((i >= MEM // rows.shape[0]) & (i < CTX // rows.shape[0]))
    def _():
        queries = (nn(rows, w_ref[0]).astype(BF16).astype(F32) * (LOG2E / math.sqrt(HD))).astype(BF16)
        queries_t = queries.T
        q_ref[...] = queries
        qt_ref[...] = queries_t
        qn_ref[...] = jnp.maximum(qn_ref[...], head_squares(queries_t))


def project_kernel(x, w, place=None, after=()):
    rows = 2 * TB
    steps = ROWS // rows
    first_q, last_q = MEM // rows, CTX // rows - 1
    fast = place is not None
    if fast:
        chips, planes = len(w) // 2, w[0].shape[0]
        own_rows, own_cols = w[0].shape[1] // 3, w[0].shape[2]

    def body(*refs):
        i = pl.program_id(0)
        if not fast:
            project_rows(i, *refs)
            return
        place_ref, x_ref, *rest = refs
        blocks, (w_ref, *outs) = rest[: len(w)], rest[len(w) :]

        @pl.when(i == 0)
        def _():
            for core, chip, plane, row, col in each_block(place_ref, chips, planes):
                for j in range(3):
                    w_ref[j, part(row, own_rows), part(col, own_cols)] = blocks[core * chips + chip][
                        plane, j * own_rows : (j + 1) * own_rows, :
                    ]

        project_rows(i, x_ref, w_ref, *outs)

    out_specs = [
        pl.BlockSpec((rows, D), lambda i: (jnp.clip(i, first_q, last_q) - first_q, 0)),
        pl.BlockSpec((rows, D), lambda i: (i, 0)),
        pl.BlockSpec((rows, D), lambda i: (i, 0)),
        pl.BlockSpec((D, rows), lambda i: (0, jnp.clip(i, first_q, last_q) - first_q)),
        pl.BlockSpec((D, rows), lambda i: (0, i)),
        pl.BlockSpec((D, rows), lambda i: (0, i)),
        whole((H, rows)),
        whole((H, rows)),
    ]
    out_shape = [
        vmem((LEN, D), BF16),
        vmem((ROWS, D), BF16),
        vmem((ROWS, D), BF16),
        vmem((D, LEN), BF16),
        vmem((D, ROWS), BF16),
        vmem((D, ROWS), BF16),
        sds((H, rows), F32),
        sds((H, rows), F32),
    ]
    in_specs = [pl.BlockSpec((rows, D), lambda i: (i, 0))]
    if fast:
        in_specs = [SMEM] + in_specs + [RESIDENT] * len(w)
        out_specs = [whole((3, D, D))] + out_specs
        out_shape = [hbm((3, D, D), BF16)] + out_shape
        operands = (place, x, *w)
    else:
        in_specs = in_specs + [whole((3, D, D))]
        operands = (x, w)
    result = call(
        body, (steps,), in_specs, out_specs, out_shape, 11e9, 14e6, "project", after=after, vmem=24 * 1024 * 1024
    )(*operands)
    return result if fast else [w, *result]


def head_lanes(values, h):
    lanes = lax.broadcasted_iota(jnp.int32, values.shape, 1)
    keep = (lanes < HD) if h == 0 else (lanes >= HD)
    return jnp.where(keep, values, jnp.zeros_like(values))


def near_count(tb):
    return MEM + (tb + 1) * TB


def seen_count(tb):
    return near_count(tb) + BANK


FAR = slice(CTX, ROWS)


def head_rows_of(values, h):
    zeros = jnp.zeros((HD, values.shape[1]), values.dtype)
    own = values[h * HD : (h + 1) * HD, :]
    return jnp.concatenate([own, zeros] if h == 0 else [zeros, own], axis=0)


def attend_body(
    qt_ref, k_ref, vt_ref, tok_ref, bank_ref, doc_ref, gate_ref, qn_ref, kn_ref,
    e0_ref, e1_ref, e2_ref, e3_ref, local_ref, fetched_ref, stat_ref, mixed_ref, mixedt_ref, s_ref,
):
    e_refs = (e0_ref, e1_ref, e2_ref, e3_ref)
    units = [(tb, h) for tb in range(NT) for h in range(2)]

    def start(u):
        tb, h = units[u]
        near = near_count(tb)
        q_head = head_rows_of(qt_ref[:, tb * TB : (tb + 1) * TB], h)
        s_ref[u % 2, :near, :] = nn(k_ref[:near, :], q_head)
        s_ref[u % 2, near : near + BANK, :] = nn(k_ref[FAR, :], q_head)

    def biased(u, row, cols, mem_bias):
        s = s_ref[u % 2, row : row + TB, :]
        near = near_count(units[u][0])
        if row < MEM:
            return s + mem_bias
        if row < near:
            return s + tok_ref[row - MEM : row - MEM + TB, cols]
        return s + bank_ref[row - near : row - near + TB, cols]

    def soft(u, first, last, cols, mem_bias, general):
        tb, h = units[u]
        top = None
        if general:
            peak = jnp.full((8, TB), -3e38, F32)
            for row in range(first, last, TB):
                s = biased(u, row, cols, mem_bias)
                peak = jnp.maximum(peak, jnp.max(s.reshape(TB // 8, 8, TB), axis=0))
            top = jnp.max(peak, axis=0, keepdims=True)
        total = jnp.zeros((8, TB), F32)
        for row in range(first, last, TB):
            s = biased(u, row, cols, mem_bias)
            e = jnp.exp2(s - top if general else s)
            e_refs[tb][h, row : row + TB, :] = e.astype(BF16)
            total = total + jnp.sum(e.reshape(TB // 8, 8, TB), axis=0)
        return 1.0 / jnp.sum(total, axis=0, keepdims=True)

    def run(general):
        start(0)
        mixed_parts = []
        for u, (tb, h) in enumerate(units):
            cols = slice(tb * TB, (tb + 1) * TB)
            head_rows = slice(h * HD, (h + 1) * HD)
            near, seen = near_count(tb), seen_count(tb)
            if u + 1 < len(units):
                start(u + 1)
            mem_bias = jnp.where(doc_ref[:, cols] == 0.0, 0.0, masked_score)
            local_inv = soft(u, 0, near, cols, mem_bias, general)
            fetched_inv = soft(u, near, seen, cols, mem_bias, general)
            local = nn(vt_ref[head_rows, :near], e_refs[tb][h, :near, :]) * local_inv
            fetched = nn(vt_ref[head_rows, FAR], e_refs[tb][h, near:, :]) * fetched_inv
            local_ref[head_rows, cols] = local.astype(BF16)
            fetched_ref[head_rows, cols] = fetched.astype(BF16)
            stat_ref[0, h : h + 1, cols] = local_inv
            stat_ref[0, 2 + h : 3 + h, cols] = fetched_inv
            gate = gate_ref[0, h : h + 1, cols]
            mixed_parts.append((1.0 - gate) * local + gate * fetched)
            if h == 1:
                mixed = jnp.concatenate(mixed_parts, axis=0)
                mixed_parts = []
                mixedt_ref[:, cols] = mixed.astype(BF16)
                mixed_ref[cols, :] = mixed.T.astype(BF16)

    bound = jnp.max(jnp.max(qn_ref[...], axis=1, keepdims=True) * jnp.max(kn_ref[...], axis=1, keepdims=True))

    @pl.when(bound <= SAFE * SAFE)
    def _():
        run(False)

    @pl.when(jnp.logical_not(bound <= SAFE * SAFE))
    def _():
        run(True)


def attend_kernel(qt, k, vt, qn, kn, bias_tok, bias_bank, doc_row, gate, first, count):
    spec_cols = lambda rows: pl.BlockSpec((rows, PAIR), lambda p: (0, p + first))
    spec_rows = lambda cols: pl.BlockSpec((PAIR, cols), lambda p: (p + first, 0))
    *e, local, fetched, stat, mixed, mixed_t = call(
        attend_body,
        (count,),
        [
            spec_rows(LEN),
            spec_cols(ROWS),
            spec_rows(ROWS),
            RESIDENT,
            RESIDENT,
            whole((1, LEN)),
            pl.BlockSpec((1, 2, LEN), lambda p: (p + first, 0, 0)),
            whole(qn.shape),
            whole(kn.shape),
        ],
        [
            *[pl.BlockSpec((2, seen_count(tb), TB), lambda p: (p, 0, 0)) for tb in range(NT)],
            pl.BlockSpec((PAIR, LEN), lambda p: (p, 0)),
            pl.BlockSpec((PAIR, LEN), lambda p: (p, 0)),
            pl.BlockSpec((1, 8, LEN), lambda p: (p, 0, 0)),
            pl.BlockSpec((LEN, PAIR), lambda p: (0, p)),
            pl.BlockSpec((PAIR, LEN), lambda p: (p, 0)),
        ],
        [
            *[hbm((2 * count, seen_count(tb), TB), BF16) for tb in range(NT)],
            hbm((PAIR * count, LEN), BF16),
            hbm((PAIR * count, LEN), BF16),
            hbm((count, 8, LEN), F32),
            vmem((LEN, PAIR * count), BF16),
            vmem((PAIR * count, LEN), BF16),
        ],
        count * 5e9,
        count * 14e6 + 6e6,
        "attend",
        scratch=[pltpu.VMEM((2, ROWS, TB), F32)],
        trans=count * 2 * ROWS * LEN,
        vmem=28 * 1024 * 1024,
    )(qt, k, vt, bias_tok, bias_bank, doc_row, gate, qn, kn)
    return e, local, fetched, stat, mixed, mixed_t


def gelu_parts(x):
    square = jnp.exp2(x * x * (-0.5 * LOG2E))
    t = 1.0 / (1.0 + (0.3275911 * 0.7071067811865476) * jnp.abs(x))
    poly = t * (
        0.127414796 + t * (-0.142248368 + t * (0.7107068705 + t * (-0.7265760135 + t * 0.5307027145)))
    )
    tail = poly * square
    cdf = jnp.where(x >= 0.0, 1.0 - tail, tail)
    return cdf, square * 0.3989422804014327


FC = 512


def feed_body(
    mixed_ref, tok_ref, cot_ref, wo_ref, up_ref, dt_ref, vec_ref,
    out_ref, act_ref, gh_ref, ffnt_ref, branch_ref, gres_ref, gmt_ref, gain_ref,
):
    i = pl.program_id(0)
    residual = tok_ref[...].astype(F32) + nn(mixed_ref[...], wo_ref[...])
    factor = rms_factor(residual)
    hat = residual * factor
    gain = vec_ref[1:2, :]
    ffn = (hat * gain).astype(BF16)
    ffnt_ref[...] = ffn.T
    cot = cot_ref[...]
    out = residual
    grad_ffn = jnp.zeros(residual.shape, F32)
    for c in range(FF // FC):
        cols = slice(c * FC, (c + 1) * FC)
        hidden = nn(ffn, up_ref[:, cols])
        cdf, pdf = gelu_parts(hidden)
        act = (hidden * cdf).astype(BF16)
        act_ref[:, cols] = act
        grad_act = nn(cot, dt_ref[:, cols])
        gh = (grad_act * (cdf + hidden * pdf)).astype(BF16)
        gh_ref[:, cols] = gh
        out = out + nt(act, dt_ref[:, cols])
        grad_ffn = grad_ffn + nt(gh, up_ref[:, cols])
    out_ref[...] = out.astype(BF16)
    part = jnp.sum(grad_ffn * hat, axis=0, keepdims=True)

    @pl.when(i == 0)
    def _():
        gain_ref[...] = part

    @pl.when(i > 0)
    def _():
        gain_ref[...] += part

    scaled = grad_ffn * gain
    grad_res = cot.astype(F32) + factor * (scaled - hat * jnp.mean(scaled * hat, axis=-1, keepdims=True))
    gres_ref[...] = grad_res
    branch = grad_res.astype(BF16)
    branch_ref[...] = branch
    gmt_ref[...] = nt(wo_ref[...], branch)


def feed_kernel(mixed, tokens, cot, vectors, w):
    rows = lambda width: pl.BlockSpec((TB, width), lambda i: (i, 0))
    cols = lambda height: pl.BlockSpec((height, TB), lambda i: (0, i))

    def body(mixed_ref, tok_ref, cot_ref, vec_ref, wo_ref, up_ref, dt_ref, *outs):
        feed_body(mixed_ref, tok_ref, cot_ref, wo_ref, up_ref, dt_ref, vec_ref, *outs)

    return call(
        body,
        (NT,),
        [rows(D), rows(D), rows(D), whole((2 + H, D))] + [whole(x.shape) for x in w],
        [rows(D), rows(FF), rows(FF), cols(D), rows(D), rows(D), cols(D), whole((1, D))],
        [
            sds((LEN, D), BF16),
            sds((LEN, FF), BF16),
            sds((LEN, FF), BF16),
            sds((D, LEN), BF16),
            sds((LEN, D), BF16),
            sds((LEN, D), F32),
            sds((D, LEN), F32),
            sds((1, D), F32),
        ],
        23e9,
        22e6,
        "feed",
        trans=LEN * FF * 2,
    )(mixed, tokens, cot, vectors, *w)


def feed_grads_body(cott_ref, act_ref, ffnt_ref, gh_ref, mixedt_ref, branch_ref, gd_ref, gu_ref, go_ref):
    gd_ref[...] = nn(cott_ref[...], act_ref[...]).astype(BF16)
    gu_ref[...] = nn(ffnt_ref[...], gh_ref[...]).astype(BF16)
    go_ref[...] = nn(mixedt_ref[...], branch_ref[...]).astype(BF16)


def feed_grads_kernel(cot_t, act, ffn_t, gh, mixed_t, branch):
    steps = 4
    wide = lambda width: pl.BlockSpec((LEN, width // steps), lambda i: (0, i))
    out = lambda width: pl.BlockSpec((D, width // steps), lambda i: (0, i))
    return call(
        feed_grads_body,
        (steps,),
        [whole((D, LEN)), wide(FF), whole((D, LEN)), wide(FF), whole((D, LEN)), wide(D)],
        [out(FF), out(FF), out(D)],
        [sds((D, FF), BF16), sds((D, FF), BF16), sds((D, D), BF16)],
        11e9,
        17e6,
        "feed_grads",
    )(cot_t, act, ffn_t, gh, mixed_t, branch)


def feed_blocks(mixed, mixed_t, tokens, cot, cot_t, vectors, w, place):
    chips, planes = len(w) // 2, w[0].shape[0]
    own_rows, own_o, own_ff = w[0].shape[1], D // planes, FF // planes
    width = own_o + 2 * own_ff
    size = 2 * TB
    row_steps = LEN // size

    def body(place_ref, mixed_ref, mixedt_ref, tok_ref, cot_ref, cott_ref, vec_ref, *rest):
        blocks, rest = rest[: len(w)], rest[len(w) :]
        out_ref, gres_ref, gmt_ref, gain_ref, keep_ref, send_ref = rest[:6]
        wo_ref, up_ref, dt_ref, act_ref, gh_ref, ffnt_ref, branch_ref, hid_ref, ga_ref, all_ref = rest[6:]
        i = pl.program_id(0)

        @pl.when(i == 0)
        def _():
            for core, chip, plane, row, col in each_block(place_ref, chips, planes):
                block = blocks[core * chips + chip]
                here = part(row, own_rows)
                wo_ref[here, part(col, own_o)] = block[plane, :, :own_o]
                up_ref[here, part(col, own_ff)] = block[plane, :, own_o : own_o + own_ff]
                dt_ref[here, part(col, own_ff)] = block[plane, :, own_o + own_ff :]

        @pl.when(i < row_steps)
        def _():
            here = part(i, size)
            residual = tok_ref[...].astype(F32) + nn(mixed_ref[...], wo_ref[...])
            factor = rms_factor(residual)
            hat = residual * factor
            gain = vec_ref[1:2, :]
            ffn = (hat * gain).astype(BF16)
            ffnt_ref[:, here] = ffn.T
            cot = cot_ref[...]

            def start(c):
                cols = slice(c * FC, (c + 1) * FC)
                hid_ref[c % 2] = nn(ffn, up_ref[:, cols])
                ga_ref[c % 2] = nn(cot, dt_ref[:, cols])

            out = residual
            grad_ffn = jnp.zeros(residual.shape, F32)
            start(0)
            for c in range(FF // FC):
                cols = slice(c * FC, (c + 1) * FC)
                if c + 1 < FF // FC:
                    start(c + 1)
                hidden = hid_ref[c % 2]
                cdf, pdf = gelu_parts(hidden)
                act_ref[here, cols] = (hidden * cdf).astype(BF16)
                gh_ref[here, cols] = (ga_ref[c % 2] * (cdf + hidden * pdf)).astype(BF16)
                out = out + nt(act_ref[here, cols], dt_ref[:, cols])
                grad_ffn = grad_ffn + nt(gh_ref[here, cols], up_ref[:, cols])
            out_ref[...] = out.astype(BF16)
            gain_part = jnp.sum(grad_ffn * hat, axis=0, keepdims=True)

            @pl.when(i == 0)
            def _():
                gain_ref[...] = gain_part

            @pl.when(i > 0)
            def _():
                gain_ref[...] += gain_part

            scaled = grad_ffn * gain
            grad_res = cot.astype(F32) + factor * (scaled - hat * jnp.mean(scaled * hat, axis=-1, keepdims=True))
            gres_ref[...] = grad_res
            branch = grad_res.astype(BF16)
            branch_ref[here, :] = branch
            gmt_ref[...] = nt(wo_ref[...], branch)

        @pl.when(i >= row_steps)
        def _():
            plane = i - row_steps
            cols = part(plane, own_ff)
            all_ref[:, :own_o] = nn(mixedt_ref[...], branch_ref[:, part(plane, own_o)]).astype(BF16)
            all_ref[:, own_o : own_o + own_ff] = nn(ffnt_ref[...], gh_ref[:, cols]).astype(BF16)
            all_ref[:, own_o + own_ff :] = nn(cott_ref[...], act_ref[:, cols]).astype(BF16)
            for chip in range(chips):
                slot = place_ref[0] ^ chip
                keep_ref[slot, 0] = all_ref[part(chip * 2 + place_ref[1], own_rows), :]
                send_ref[slot, 0] = all_ref[part(chip * 2 + 1 - place_ref[1], own_rows), :]

    row = lambda i: jnp.minimum(i, row_steps - 1)
    rows = pl.BlockSpec((size, D), lambda i, _: (row(i), 0))
    blocked = pl.BlockSpec(
        (chips, 1, own_rows, width), lambda i, place_ref: (0, jnp.maximum(i - row_steps, 0) ^ place_ref[2], 0, 0)
    )
    shape = hbm((chips, planes, own_rows, width), BF16)
    return call(
        body,
        (row_steps + planes,),
        [rows, RESIDENT, rows, rows, RESIDENT, whole((2 + H, D))] + [RESIDENT] * len(w),
        [rows, rows, pl.BlockSpec((D, size), lambda i, _: (0, row(i))), whole((1, D)), blocked, blocked],
        [hbm((LEN, D), BF16), hbm((LEN, D), F32), hbm((D, LEN), F32), sds((1, D), F32), shape, shape],
        30e9,
        22e6,
        "feed",
        scratch=[
            pltpu.VMEM((D, D), BF16),
            pltpu.VMEM((D, FF), BF16),
            pltpu.VMEM((D, FF), BF16),
            pltpu.VMEM((LEN, FF), BF16),
            pltpu.VMEM((LEN, FF), BF16),
            pltpu.VMEM((D, LEN), BF16),
            pltpu.VMEM((LEN, D), BF16),
            pltpu.VMEM((2, size, FC), F32),
            pltpu.VMEM((2, size, FC), F32),
            pltpu.VMEM((D, width), BF16),
        ],
        trans=LEN * FF * 2,
        prefetch=1,
        vmem=36 * 1024 * 1024,
    )(place, mixed, mixed_t, tokens, cot, cot_t, vectors, *w)


def unattend_body(
    q_ref, kt_ref, v_ref, e0_ref, e1_ref, e2_ref, e3_ref, gmt_ref, local_ref, fetched_ref, stat_ref, gate_ref,
    dq_ref, dk_ref, dv_ref, gl_ref, ds0_ref, ds1_ref, ds2_ref, ds3_ref, do_ref, df_ref, dot_ref, dqt_ref, dk_acc, dv_acc, gp_ref,
):
    e_refs, ds_refs = (e0_ref, e1_ref, e2_ref, e3_ref), (ds0_ref, ds1_ref, ds2_ref, ds3_ref)

    def prepare(h):
        head_rows = slice(h * HD, (h + 1) * HD)
        gm = gmt_ref[head_rows, :]
        local = local_ref[head_rows, :].astype(F32)
        fetched = fetched_ref[head_rows, :].astype(F32)
        gate = gate_ref[0, h : h + 1, :]
        local_inv = stat_ref[0, h : h + 1, :]
        fetched_inv = stat_ref[0, 2 + h : 3 + h, :]
        grad_gate = jnp.sum(gm * (fetched - local), axis=0, keepdims=True)
        gl_ref[0, h : h + 1, :] = grad_gate * gate * (1.0 - gate)
        grad_local = ((1.0 - gate) * gm).astype(BF16).astype(F32)
        grad_fetched = gate * gm
        other = slice((1 - h) * HD, (2 - h) * HD)
        do_ref[h, other, :] = jnp.zeros((HD, LEN), BF16)
        df_ref[h, other, :] = jnp.zeros((HD, LEN), BF16)
        do_ref[h, head_rows, :] = (grad_local * local_inv).astype(BF16)
        df_ref[h, head_rows, :] = (grad_fetched * fetched_inv).astype(BF16)
        dot_ref[h : h + 1, :] = jnp.sum(grad_local * local, axis=0, keepdims=True) * local_inv
        dot_ref[2 + h : 3 + h, :] = jnp.sum(grad_fetched * fetched, axis=0, keepdims=True) * fetched_inv

    units = [(tb, h) for h in range(2) for tb in range(NT)]

    def start(u):
        tb, h = units[u]
        near, cols = near_count(tb), slice(tb * TB, (tb + 1) * TB)
        gp_ref[u % 2, :near, :] = nn(v_ref[:near, :], do_ref[h, :, cols])
        gp_ref[u % 2, near : near + BANK, :] = nn(v_ref[FAR, :], df_ref[h, :, cols])

    def rows_part(u):
        tb, h = units[u]
        near, cols = near_count(tb), slice(tb * TB, (tb + 1) * TB)
        head_rows = slice(h * HD, (h + 1) * HD)
        for row in range(0, seen_count(tb), TB):
            some, which = slice(row, row + TB), h if row < near else 2 + h
            gp = gp_ref[u % 2, some, :] - dot_ref[which : which + 1, cols]
            ds_refs[tb][h, some, :] = (e_refs[tb][h, some, :].astype(F32) * gp).astype(BF16)
        dq = nn(kt_ref[head_rows, :near], ds_refs[tb][h, :near, :])
        dq = dq + nn(kt_ref[head_rows, FAR], ds_refs[tb][h, near:, :])
        dqt_ref[head_rows, cols] = dq * (1.0 / math.sqrt(HD))

    def keys_part(h, tb):
        near, cols = near_count(tb), slice(tb * TB, (tb + 1) * TB)
        q_head = head_lanes(q_ref[cols, :], h)
        pieces = (
            (slice(0, near), slice(0, near), do_ref[h, :, cols]),
            (FAR, slice(near, near + BANK), df_ref[h, :, cols]),
        )
        for keys, some, grad_out in pieces:
            dv = nt(e_refs[tb][h, some, :], grad_out)
            dk = nn(ds_refs[tb][h, some, :], q_head)
            if h == 0 and tb == NT - 1:
                dv_acc[keys, :] = dv
                dk_acc[keys, :] = dk
            else:
                dv_acc[keys, :] += dv
                dk_acc[keys, :] += dk

    prepare(0)
    start(0)
    prepare(1)
    for u, (tb, h) in enumerate(units):
        if u + 1 < len(units):
            start(u + 1)
        rows_part(u)
        if h == 1:
            keys_part(0, NT - 1 - tb)
    for tb in range(NT):
        keys_part(1, tb)
    dv_ref[...] = dv_acc[...].astype(BF16)
    dk_ref[...] = (dk_acc[...] * (1.0 / LOG2E)).astype(BF16)
    dq_ref[...] = dqt_ref[...].T.astype(BF16)


def unattend_kernel(q, kt, v, e, gmt, local, fetched, stat, gate, first, count, after=(), alias=()):
    spec_cols = lambda rows: pl.BlockSpec((rows, PAIR), lambda p: (0, p + first))
    spec_rows = lambda cols: pl.BlockSpec((PAIR, cols), lambda p: (p + first, 0))
    return call(
        unattend_body,
        (count,),
        [
            spec_cols(LEN),
            spec_rows(ROWS),
            spec_cols(ROWS),
            *[pl.BlockSpec((2, seen_count(tb), TB), lambda p: (p + first, 0, 0)) for tb in range(NT)],
            spec_rows(LEN),
            spec_rows(LEN),
            spec_rows(LEN),
            pl.BlockSpec((1, 8, LEN), lambda p: (p + first, 0, 0)),
            pl.BlockSpec((1, 2, LEN), lambda p: (p + first, 0, 0)),
        ],
        [
            spec_cols(LEN),
            spec_cols(ROWS),
            spec_cols(ROWS),
            pl.BlockSpec((1, 2, LEN), lambda p: (p + first, 0, 0)),
        ],
        [
            sds((LEN, D), BF16),
            sds((ROWS, D), BF16),
            sds((ROWS, D), BF16),
            sds((NPAIR, 2, LEN), F32),
        ],
        count * 10e9,
        count * 14e6,
        "unattend",
        scratch=[
            *[pltpu.VMEM((2, seen_count(tb), TB), BF16) for tb in range(NT)],
            pltpu.VMEM((2, PAIR, LEN), BF16),
            pltpu.VMEM((2, PAIR, LEN), BF16),
            pltpu.VMEM((8, LEN), F32),
            pltpu.VMEM((PAIR, LEN), F32),
            pltpu.VMEM((ROWS, PAIR), F32),
            pltpu.VMEM((ROWS, PAIR), F32),
            pltpu.VMEM((2, ROWS, TB), F32),
        ],
        after=after,
        alias=alias,
        vmem=36 * 1024 * 1024,
    )(q, kt, v, *e, gmt, local, fetched, stat, gate)


def all_heads(gl_ref):
    return jnp.concatenate([gl_ref[p] for p in range(NPAIR)], axis=0).astype(BF16)


def proj_grads_body(xt_ref, dq_ref, dk_ref, dv_ref, gl_ref, g_ref, gate_ref):
    g_ref[0] = nn(xt_ref[:, MEM:CTX], dq_ref[...]).astype(BF16)
    g_ref[1] = nn(xt_ref[...], dk_ref[...]).astype(BF16)
    g_ref[2] = nn(xt_ref[...], dv_ref[...]).astype(BF16)

    @pl.when(pl.program_id(0) == 0)
    def _():
        gate_ref[...] = nt(all_heads(gl_ref), xt_ref[:, MEM:CTX])


def proj_grads_kernel(xt, dq, dk, dv, gl, place=None, chips=0, planes=0, after=()):
    steps = 2
    fast = place is not None
    wide = lambda rows: pl.BlockSpec((rows, D // steps), lambda i, *_: (0, i))
    in_specs = [whole((D, ROWS)), wide(LEN), wide(ROWS), wide(ROWS), whole((NPAIR, 2, LEN))]
    gate_spec, gate_shape = whole((H, D)), sds((H, D), F32)
    flops, nbytes = 8e9, 10e6
    if not fast:
        return call(
            proj_grads_body,
            (steps,),
            in_specs,
            [pl.BlockSpec((3, D, D // steps), lambda i: (0, 0, i)), gate_spec],
            [sds((3, D, D), BF16), gate_shape],
            flops,
            nbytes,
            "proj_grads",
        )(xt, dq, dk, dv, gl)
    own_rows, own_cols, group = D // (2 * chips), D // planes, planes // steps

    def body(place_ref, xt_ref, dq_ref, dk_ref, dv_ref, gl_ref, keep_ref, send_ref, gate_ref, all_ref):
        proj_grads_body(xt_ref, dq_ref, dk_ref, dv_ref, gl_ref, all_ref, gate_ref)
        for b in range(group):
            col = b ^ (place_ref[2] % group)
            cols = slice(b * own_cols, (b + 1) * own_cols)
            for chip in range(chips):
                slot = place_ref[0] ^ chip
                for j in range(3):
                    here = slice(j * own_rows, (j + 1) * own_rows)
                    keep_ref[slot, col, here, :] = all_ref[j, part(chip * 2 + place_ref[1], own_rows), cols]
                    send_ref[slot, col, here, :] = all_ref[j, part(chip * 2 + 1 - place_ref[1], own_rows), cols]

    out = pl.BlockSpec(
        (chips, group, 3 * own_rows, own_cols), lambda i, place_ref: (0, i ^ (place_ref[2] // group), 0, 0)
    )
    shape = sds((chips, planes, 3 * own_rows, own_cols), BF16)
    return call(
        body,
        (steps,),
        in_specs,
        [out, out, gate_spec],
        [shape, shape, gate_shape],
        flops,
        nbytes,
        "proj_grads",
        scratch=[pltpu.VMEM((3, D, D // steps), BF16)],
        prefetch=1,
        after=after,
        vmem=24 * 1024 * 1024,
    )(place, xt, dq, dk, dv, gl)


def input_body(dq_ref, dk_ref, dv_ref, gl_ref, w_ref, tok_ref, mem_ref, vec_ref, gres_ref, gin_ref, gain_ref):
    i = pl.program_id(0)
    gn = nt(dk_ref[...], w_ref[1]) + nt(dv_ref[...], w_ref[2])

    @pl.when(i < MC)
    def _():
        wide = mem_ref[...].astype(F32)
        part = jnp.sum(gn * (wide * rms_factor(wide)), axis=0, keepdims=True)

        @pl.when(i == 0)
        def _():
            gain_ref[...] = part

        @pl.when(i > 0)
        def _():
            gain_ref[...] += part

    @pl.when(i >= MC)
    def _():
        wide = tok_ref[...].astype(F32)
        factor = rms_factor(wide)
        hat = wide * factor
        full = gn + nt(dq_ref[...], w_ref[0]) + tn(all_heads(gl_ref), vec_ref[2:10, :].astype(BF16))
        gain_ref[...] += jnp.sum(full * hat, axis=0, keepdims=True)
        scaled = full * vec_ref[0:1, :]
        gin_ref[...] = (
            gres_ref[...] + factor * (scaled - hat * jnp.mean(scaled * hat, axis=-1, keepdims=True))
        ).astype(BF16)


def input_kernel(dq, dk, dv, gl, w, tokens, memory, vectors, gres, after=()):
    tok = lambda i: jnp.clip(i - MC, 0, NT - 1)
    rows = pl.BlockSpec((TB, D), lambda i: (tok(i), 0))
    return call(
        input_body,
        (MC + NT,),
        [
            rows,
            pl.BlockSpec((TB, D), lambda i: (i, 0)),
            pl.BlockSpec((TB, D), lambda i: (i, 0)),
            pl.BlockSpec((NPAIR, 2, TB), lambda i: (0, 0, tok(i))),
            whole((3, D, D)),
            rows,
            pl.BlockSpec((TB, D), lambda i: (jnp.minimum(i, MC - 1), 0)),
            whole((2 + H, D)),
            rows,
        ],
        [rows, whole((1, D))],
        [sds((LEN, D), BF16), sds((1, D), F32)],
        9e9,
        10e6,
        "input",
        after=after,
        vmem=SMALL,
    )(dq, dk, dv, gl, w, tokens, memory, vectors, gres)


def exchange(slots, axis):
    size = len(slots)
    return [slots[0]] + [
        lax.ppermute(slots[r], axis, [(i, i ^ r) for i in range(size)]) for r in range(1, size)
    ]


def added(parts):
    total = parts[0].astype(F32)
    for other in parts[1:]:
        total = total + other.astype(F32)
    return total


PLANES = (("up",), ("q", "k"), ("v", "o"), ("down",))
EXTRA = 16


def alone(body, operands, out_shape, name, scratch=(), place=None, after=(), flops=2e9, vmem=SMALL, resident=0):
    specs = [RESIDENT if j < resident else whole(x.shape) for j, x in enumerate(operands)]
    if place is not None:
        specs, operands = [SMEM] + specs, (place, *operands)
    return call(
        body,
        (1,),
        specs,
        [whole(x.shape) for x in out_shape],
        out_shape,
        flops,
        2e6,
        name,
        scratch=scratch,
        after=after,
        vmem=vmem,
    )(*operands)


def payloads_kernel(place, attn_weights, up_weights, down_weights, attn_moment, up_moment, down_moment):
    rows, cols = attn_weights.shape[1:]
    wide = up_weights.shape[1]
    planes = len(PLANES)
    width = cols + 3 * wide

    def body(place_ref, aw_ref, uw_ref, dw_ref, am_ref, um_ref, dm_ref, first_ref, *rest):
        outs, all_ref = rest[:planes], rest[planes]
        for j in range(3):
            first_ref[j * rows : (j + 1) * rows, :] = aw_ref[j].astype(BF16)
        all_ref[...] = jnp.zeros(all_ref.shape, BF16)
        all_ref[0] = um_ref[...].astype(BF16)
        all_ref[3] = dm_ref[...].astype(BF16)
        for j in range(4):
            all_ref[1 + j // 2, :, (j % 2) * cols : (j % 2 + 1) * cols] = am_ref[j].astype(BF16)
        for r in range(planes):
            outs[r][:, :cols] = aw_ref[3].astype(BF16)
            outs[r][:, cols : cols + wide] = uw_ref[...].astype(BF16)
            outs[r][:, cols + wide : cols + 2 * wide] = dw_ref[...].astype(BF16)
            outs[r][:, cols + 2 * wide :] = all_ref[place_ref[2] ^ r]

    first, *second = alone(
        body,
        (attn_weights, up_weights, down_weights, attn_moment, up_moment, down_moment),
        [sds((3 * rows, cols), BF16)] + [sds((rows, width), BF16)] * planes,
        "payloads",
        scratch=[pltpu.VMEM((planes, rows, wide), BF16)],
        place=place,
        vmem=VMEM_LIMIT,
    )
    return first, second


def stacked_pair(parts, width):
    rows = parts[0].shape[0]
    other = parts[0].shape[1] - width

    def body(*refs):
        for r in range(len(parts)):
            refs[-2][r] = refs[r][:, :width]
            refs[-1][r] = refs[r][:, width:]

    shapes = [sds((len(parts), rows, width), BF16), sds((len(parts), rows, other), BF16)]
    return alone(body, parts, shapes, "stacked_pair", resident=len(parts))


def stacked(parts, after=()):
    def body(*refs):
        for r in range(len(parts)):
            refs[-1][r] = refs[r][...]

    return alone(body, parts, [sds((len(parts),) + parts[0].shape, parts[0].dtype)], "stacked", after=after, resident=len(parts))[0]


def core_blocks(plane):
    return plane + [exchange([b, b], "core")[1] for b in plane]


def fold_cores(keep, other):
    chips, planes, rows, width = keep.shape

    def body(keep_ref, other_ref, *outs):
        for chip in range(chips):
            outs[chip][...] = added([keep_ref[chip], other_ref[chip]]).astype(BF16)

    spec = pl.BlockSpec((chips, 1, rows, width), lambda i: (0, i, 0, 0))
    return call(
        body,
        (planes,),
        [spec, spec],
        [pl.BlockSpec((1, rows, width), lambda i: (i, 0, 0))] * chips,
        [sds((planes, rows, width), BF16)] * chips,
        4e9,
        7e6,
        "fold_cores",
        vmem=SMALL,
    )(keep, other)


def fold_chips(parts):
    planes, rows, width = parts[0].shape

    def body(*refs):
        for plane in range(planes):
            refs[len(parts) + plane][...] = added([r[plane] for r in refs[: len(parts)]]).astype(BF16)

    return alone(body, parts, [sds((rows, width), BF16)] * planes, "fold_chips", resident=len(parts))


VEC = 2 + H
VEC_ROWS = 128


def put_vectors(ref, first, values):
    high = values.astype(BF16)
    low = (values - high.astype(F32)).astype(BF16)
    ref[first : first + VEC_ROWS, :] = jnp.zeros((VEC_ROWS, 128), BF16)
    for j in range(4):
        lanes = slice(j * 128, (j + 1) * 128)
        ref[first + j * 16 : first + j * 16 + VEC, :] = high[:, lanes]
        ref[first + 64 + j * 16 : first + 64 + j * 16 + VEC, :] = low[:, lanes]


def get_vectors(refs, first):
    pieces = []
    for j in range(4):
        rows = lambda offset: slice(first + offset + j * 16, first + offset + j * 16 + VEC)
        pieces.append(added([r[rows(offset), :] for r in refs for offset in (0, 64)]))
    return jnp.concatenate(pieces, axis=1)


def fold_cores_first(keep, other):
    chips = keep.shape[0]

    def body(keep_ref, other_ref, *outs):
        for chip in range(chips):
            outs[chip][...] = added([keep_ref[chip], other_ref[chip]]).astype(BF16)

    return alone(body, (keep, other), [sds(keep.shape[1:], BF16)] * chips, "fold_cores_first")


def fold_chips_first(parts, gain_attn, gain_ffn, grad_gate):
    planes, rows, width = parts[0].shape
    count = len(parts)

    def body(*refs):
        ins, (ga_ref, gf_ref, gg_ref) = refs[:count], refs[count : count + 3]
        outs, vec_ref = refs[count + 3 : -1], refs[-1]
        vec_ref[0:1, :] = ga_ref[...]
        vec_ref[1:2, :] = gf_ref[...]
        vec_ref[2:VEC, :] = gg_ref[...]
        for plane in range(planes):
            outs[plane][:rows, :] = added([r[plane] for r in ins]).astype(BF16)
            put_vectors(outs[plane], rows, vec_ref[...])

    return alone(
        body,
        (*parts, gain_attn, gain_ffn, grad_gate),
        [sds((rows + VEC_ROWS, width), BF16)] * planes,
        "fold_chips_first",
        resident=count,
        scratch=[pltpu.VMEM((VEC, D), F32)],
    )


def stack_with_vectors(parts, vec):
    count, width = len(parts), parts[0].shape[1]
    rows = parts[0].shape[0] - EXTRA

    def body(*refs):
        vec_ref, out_ref = refs[count], refs[count + 1]
        for r in range(count):
            out_ref[r * rows : (r + 1) * rows, :] = refs[r][:rows, :]
        squares = added([r[rows:, :] for r in refs[:count]])
        squares = jnp.sum(squares, axis=0, keepdims=True) + jnp.zeros((EXTRA, width), F32)
        high = squares.astype(BF16).astype(F32)
        middle = (squares - high).astype(BF16).astype(F32)
        row = lax.broadcasted_iota(jnp.int32, (EXTRA, width), 0)
        extra = jnp.where(row == VEC, high, jnp.where(row == VEC + 1, middle, squares - high - middle))
        values = jnp.concatenate([vec_ref[...], jnp.zeros((EXTRA - VEC, width), F32)], axis=0)
        first = values.astype(BF16).astype(F32)
        here = count * rows
        out_ref[here : here + EXTRA, :] = jnp.where(row < VEC, first, extra).astype(BF16)
        out_ref[here + EXTRA :, :] = (values - first).astype(BF16)

    return alone(
        body, (*parts, vec), [sds((count * rows + 2 * EXTRA, width), BF16)], "stack_with_vectors", resident=count + 1
    )[0]


def owned_kernel(place, parts_a, parts_b):
    planes = len(parts_a)
    size, cols = parts_a[0].shape[0] - VEC_ROWS, parts_a[0].shape[1]
    rows, width = parts_b[0].shape
    wide = (width - cols) // 2

    def body(place_ref, *refs):
        a_refs, b_refs = refs[:planes], refs[planes : 2 * planes]
        ga_ref, gb_ref, vec_ref, *rest = refs[2 * planes :]
        slots, all_ref = rest[:planes], rest[planes]
        ga = added([r[:size, :] for r in a_refs])
        gb = added([r[...] for r in b_refs])
        ga_ref[...] = ga
        gb_ref[...] = gb
        vec_ref[...] = get_vectors(a_refs, size)
        squares = jnp.sum(ga * ga, keepdims=True) + jnp.sum(gb * gb, keepdims=True)
        all_ref[...] = jnp.zeros(all_ref.shape, BF16)
        for j in range(4):
            grad = ga[j * rows : (j + 1) * rows, :] if j < 3 else gb[:, :cols]
            all_ref[1 + j // 2, :, (j % 2) * cols : (j % 2 + 1) * cols] = grad.astype(BF16)
        all_ref[0] = gb[:, cols : cols + wide].astype(BF16)
        all_ref[3] = gb[:, cols + wide :].astype(BF16)
        wide_squares = squares + jnp.zeros((EXTRA, wide), F32)
        row = lax.broadcasted_iota(jnp.int32, (EXTRA, wide), 0)
        high = wide_squares.astype(BF16).astype(F32)
        middle = (wide_squares - high).astype(BF16).astype(F32)
        low = wide_squares - high - middle
        extra = jnp.where(row == 0, high, jnp.where(row == 1, middle, jnp.where(row == 2, low, 0.0))).astype(BF16)
        for r in range(planes):
            slots[r][:rows, :] = all_ref[place_ref[2] ^ r]
            slots[r][rows:, :] = extra

    return alone(
        body,
        (*parts_a, *parts_b),
        [sds((size, cols), F32), sds((rows, width), F32), sds((VEC, D), F32)]
        + [sds((rows + EXTRA, wide), BF16)] * planes,
        "owned",
        resident=2 * planes,
        scratch=[pltpu.VMEM((planes, rows, wide), BF16)],
        place=place,
    )


def orthogonal_kernel(place, grads, moments, vectors, vec_moment):
    count = len(grads)
    chips = count // 2
    planes, rows = moments[0].shape[:2]
    wide = grads[0].shape[1]
    cols = D // planes
    limit = clip_fraction * math.sqrt(PARAMS)

    def body(place_ref, *refs):
        grad_refs, moment_refs, refs = refs[:count], refs[count : 2 * count], refs[2 * count :]
        vec_ref, vm_ref, norm_ref, vn_ref, vmn_ref = refs[:5]
        outs = refs[5 : 5 + planes]
        low_ref, x_ref, mix_ref, diag_ref, all_ref = refs[5 + planes :]
        pair = (place_ref[2] == 1) | (place_ref[2] == 2)
        own = part(place_ref[0] * 2 + place_ref[1], rows)
        after = planes * rows
        extra = added([r[after : after + EXTRA, :] for r in grad_refs])
        grad_vec = extra[:VEC, :] + added([r[after + EXTRA : after + EXTRA + VEC, :] for r in grad_refs])
        total = jnp.sum(extra[VEC : VEC + 3, 0:1], axis=0, keepdims=True) + jnp.sum(grad_vec * grad_vec, keepdims=True)
        norm = jnp.sqrt(total)
        norm_ref[...] = norm
        clip = limit / jnp.maximum(norm, limit)
        vec_mom = vector_decay * vm_ref[...] + clip * grad_vec
        vmn_ref[...] = vec_mom
        vn_ref[...] = vec_ref[...] - vector_rate * vec_mom

        def momentum(core, chip, plane, lanes):
            b = core * chips + chip
            moment = moment_refs[b][plane, :, lanes].astype(F32)
            grad = grad_refs[b][plane * rows : (plane + 1) * rows, lanes].astype(F32)
            return muon_decay * moment + clip * grad

        def gram_of(start, width):
            half = D // 2
            upper, lower = low_ref[:half, start : start + width], low_ref[half:, start : start + width]
            corner = nt(lower, upper)
            first = jnp.concatenate([nt(upper, upper), corner.T], axis=1)
            return jnp.concatenate([first, jnp.concatenate([corner, nt(lower, lower)], axis=1)], axis=0)

        def mixing(gram):
            eye = lax.broadcasted_iota(jnp.int32, (D, D), 0) == lax.broadcasted_iota(jnp.int32, (D, D), 1)
            low = gram.astype(BF16)
            mix = coef_second * low.astype(F32) + coef_third * nn(low, low)
            diag_ref[...] = coef_first + jnp.sum(jnp.where(eye, mix, 0.0), axis=1, keepdims=True)
            mix_ref[...] = jnp.where(eye, 0.0, mix).astype(BF16)

        def advance(start, width, scale):
            for c in range(start, start + width, D):
                lanes = slice(c, c + D)
                new = diag_ref[...] * x_ref[:, lanes] + nn(mix_ref[...], low_ref[:, lanes])
                if scale is not None:
                    new = new * scale
                x_ref[:, lanes] = new
                low_ref[:, lanes] = new.astype(BF16)

        def first_step(start, width):
            gram = gram_of(start, width)
            eye = lax.broadcasted_iota(jnp.int32, (D, D), 0) == lax.broadcasted_iota(jnp.int32, (D, D), 1)
            scale = 1.0 / (jnp.sqrt(jnp.sum(jnp.where(eye, gram, 0.0), keepdims=True)) + 1e-07)
            mixing(gram * (scale * scale))
            advance(start, width, scale)

        def step(start, width, last):
            mixing(gram_of(start, width))
            if not last:
                advance(start, width, None)
                return
            for c in range(start, start + width, D):
                lanes = slice(c, c + D)
                x_ref[own, lanes] = diag_ref[own, :] * x_ref[own, lanes] + nn(mix_ref[own, :], low_ref[:, lanes])

        def iterations(ranges):
            for start, width in ranges:
                first_step(start, width)

            def middle(_, carry):
                for start, width in ranges:
                    step(start, width, False)
                return carry

            lax.fori_loop(1, NS_ITERS - 1, middle, 0)
            for start, width in ranges:
                step(start, width, True)

        @pl.when(pair)
        def _():
            for core, chip, plane, row, col in each_block(place_ref, chips, planes):
                for j in range(2):
                    new = momentum(core, chip, plane, slice(j * cols, (j + 1) * cols))
                    x_ref[part(row, rows), part(col + j * planes, cols)] = new
                    low_ref[part(row, rows), part(col + j * planes, cols)] = new.astype(BF16)
            iterations([(0, D), (D, D)])
            for plane in range(planes):
                for j in range(2):
                    first = j * D + plane * cols
                    all_ref[plane, :, j * cols : (j + 1) * cols] = x_ref[own, first : first + cols].astype(BF16)

        @pl.when(jnp.logical_not(pair))
        def _():
            for core, chip, plane, row, col in each_block(place_ref, chips, planes):
                new = momentum(core, chip, plane, slice(0, wide))
                x_ref[part(row, rows), part(col, wide)] = new
                low_ref[part(row, rows), part(col, wide)] = new.astype(BF16)
            iterations([(0, FF)])
            for plane in range(planes):
                all_ref[plane] = x_ref[own, plane * wide : (plane + 1) * wide].astype(BF16)

        for r in range(planes):
            outs[r][...] = all_ref[place_ref[2] ^ r]

    return alone(
        body,
        (*grads, *moments, vectors, vec_moment),
        [sds((1, 1), F32), sds((VEC, D), F32), sds((VEC, D), F32)] + [sds((rows, wide), BF16)] * planes,
        "orthogonal",
        scratch=[
            pltpu.VMEM((D, FF), BF16),
            pltpu.VMEM((D, FF), F32),
            pltpu.VMEM((D, D), BF16),
            pltpu.VMEM((D, 1), F32),
            pltpu.VMEM((planes, rows, wide), BF16),
        ],
        place=place,
        flops=18e9,
        vmem=24 * 1024 * 1024,
        resident=2 * count,
    )


def update_kernel(place, slots, norm, ga, gb, attn_moment, up_moment, down_moment, attn_weights, up_weights, down_weights):
    planes = len(slots)
    rows, cols = attn_weights.shape[1:]
    wide = up_weights.shape[1]
    shape_factor = math.sqrt(max(1.0, FF / D))
    limit = clip_fraction * math.sqrt(PARAMS)

    def body(place_ref, *refs):
        slot_refs, refs = refs[:planes], refs[planes:]
        norm_ref, ga_ref, gb_ref, am_ref, um_ref, dm_ref, aw_ref, uw_ref, dw_ref = refs[:9]
        an_ref, un_ref, dn_ref, amn_ref, umn_ref, dmn_ref, all_ref = refs[9:]
        clip = limit / jnp.maximum(norm_ref[...], limit)
        for r in range(planes):
            all_ref[place_ref[2] ^ r] = slot_refs[r][...]
        for j in range(4):
            ortho = all_ref[1 + j // 2, :, (j % 2) * cols : (j % 2 + 1) * cols].astype(F32)
            an_ref[j] = aw_ref[j] - muon_rate * ortho
            grad = ga_ref[j * rows : (j + 1) * rows, :] if j < 3 else gb_ref[:, :cols]
            amn_ref[j] = muon_decay * am_ref[j] + clip * grad
        un_ref[...] = uw_ref[...] - muon_rate * all_ref[0].astype(F32)
        umn_ref[...] = muon_decay * um_ref[...] + clip * gb_ref[:, cols : cols + wide]
        dn_ref[...] = dw_ref[...] - muon_rate * shape_factor * all_ref[3].astype(F32)
        dmn_ref[...] = muon_decay * dm_ref[...] + clip * gb_ref[:, cols + wide :]

    weights = (attn_weights, up_weights, down_weights)
    return alone(
        body,
        (*slots, norm, ga, gb, attn_moment, up_moment, down_moment, *weights),
        [sds(x.shape, F32) for x in weights] * 2,
        "update",
        vmem=VMEM_LIMIT,
        resident=planes,
        scratch=[pltpu.VMEM((planes,) + slots[0].shape, BF16)],
        place=place,
    )


def documents(starts):
    doc = jnp.cumsum(starts).astype(F32)
    return doc.reshape(1, LEN), doc.reshape(LEN, 1)


def plain_tail(sizes, grads, attn_weights, up_weights, down_weights, vectors, attn_moment, up_moment, down_moment, vec_moment):
    dp = ("chip", "core")
    grad_attn, grad_up, grad_down, grad_vectors = grads

    def owned(grad, narrow_dim, dp_dim):
        part_sum = lax.psum_scatter(grad.astype(BF16), "narrow", scatter_dimension=narrow_dim, tiled=True)
        return lax.psum_scatter(part_sum, dp, scatter_dimension=dp_dim, tiled=True).astype(F32)

    owned_attn, owned_up, owned_down = owned(grad_attn, 2, 1), owned(grad_up, 1, 0), owned(grad_down, 0, 1)
    own_squares = jnp.sum(owned_attn * owned_attn) + jnp.sum(owned_up * owned_up) + jnp.sum(owned_down * owned_down)
    vector_sum, square_sum = lax.psum((grad_vectors, own_squares), ("chip", "core", "narrow"))
    grad_norm = jnp.sqrt(square_sum + jnp.sum(vector_sum * vector_sum))
    clip_limit = clip_fraction * math.sqrt(PARAMS)
    clip_factor = clip_limit / jnp.maximum(grad_norm, clip_limit)
    attn_mom_new = muon_decay * attn_moment + clip_factor * owned_attn
    up_mom_new = muon_decay * up_moment + clip_factor * owned_up
    down_mom_new = muon_decay * down_moment + clip_factor * owned_down
    gather = lambda x, dim: lax.all_gather(x.astype(BF16), dp, axis=dim, tiled=True).astype(F32)
    ortho = (gather(attn_mom_new, 1), gather(up_mom_new, 0), gather(down_mom_new, 1))
    ortho_attn, ortho_up, ortho_down = ortho
    for iteration in range(NS_ITERS):
        gram_attn = jnp.einsum("imc,inc->imn", ortho_attn, ortho_attn, precision=highest)
        gram_up = lax.dot_general(ortho_up, ortho_up, (((1,), (1,)), ((), ())), precision=highest)
        gram_down = lax.dot_general(ortho_down, ortho_down, (((0,), (0,)), ((), ())), precision=highest)
        partial_grams = jnp.concatenate([gram_attn, gram_up[None], gram_down[None]], axis=0)
        gram_total = lax.psum(partial_grams.astype(BF16), "narrow").astype(F32)
        if iteration == 0:
            norm_scales = 1.0 / (jnp.sqrt(jnp.trace(gram_total, axis1=1, axis2=2)) + 1e-07)
            ortho_attn = ortho_attn * norm_scales[:4, None, None]
            ortho_up = ortho_up * norm_scales[4]
            ortho_down = ortho_down * norm_scales[5]
            gram_total = gram_total * (norm_scales * norm_scales)[:, None, None]
        once = jnp.einsum("imn,inc->imc", gram_total[:4], ortho_attn, precision=highest)
        twice = jnp.einsum("imn,inc->imc", gram_total[:4], once, precision=highest)
        ortho_attn = coef_first * ortho_attn + coef_second * once + coef_third * twice
        once = jnp.dot(gram_total[4], ortho_up, precision=highest)
        twice = jnp.dot(gram_total[4], once, precision=highest)
        ortho_up = coef_first * ortho_up + coef_second * once + coef_third * twice
        once = jnp.dot(ortho_down, gram_total[5], precision=highest)
        twice = jnp.dot(once, gram_total[5], precision=highest)
        ortho_down = coef_first * ortho_down + coef_second * once + coef_third * twice
    row_share = D // sizes["dp"]
    row_start = lax.axis_index(dp) * row_share
    final_attn = lax.dynamic_slice_in_dim(ortho_attn, row_start, row_share, 1)
    final_up = lax.dynamic_slice_in_dim(ortho_up, row_start, row_share, 0)
    final_down = lax.dynamic_slice_in_dim(ortho_down, row_start, row_share, 1)
    shape_factor = math.sqrt(max(1.0, FF / D))
    vector_mom_new = vector_decay * vec_moment + clip_factor * vector_sum
    return (
        attn_weights - muon_rate * final_attn,
        up_weights - muon_rate * final_up,
        down_weights - muon_rate * shape_factor * final_down,
        attn_mom_new,
        up_mom_new,
        down_mom_new,
        vectors - vector_rate * vector_mom_new,
        vector_mom_new,
        grad_norm,
    )


def per_device(
    sizes,
    tokens, memory, neighbour_bank, starts, neighbours, cotangent,
    attn_weights, up_weights, down_weights, vectors,
    attn_moment, up_moment, down_moment, vector_moment,
):
    memory = memory.reshape(MEM, D)
    bank = neighbour_bank.reshape(BANK, D)
    own = (attn_weights, up_weights, down_weights)
    moments = (attn_moment, up_moment, down_moment)
    chips, planes = sizes["dp"] // 2, sizes["narrow"]
    if planes == len(PLANES) and chips == 4:
        return fast_device(
            chips, planes, tokens, memory, bank, starts, neighbours, cotangent, own, vectors, moments, vector_moment
        )
    full = lambda x, narrow_dim, dp_dim: lax.all_gather(
        lax.all_gather(x.astype(BF16), ("chip", "core"), axis=dp_dim, tiled=True), "narrow", axis=narrow_dim, tiled=True
    )
    attn_full = full(attn_weights, 2, 1)
    second = [attn_full[3], full(up_weights, 1, 0), full(down_weights, 0, 1).T]
    x, xt, cot_t, gate = context_kernel(tokens, memory, bank, cotangent, vectors)
    doc_row, doc_col = documents(starts)
    bias_tok, bias_bank = mask_kernel(doc_row, doc_col, neighbours.T)
    w, q, k, v, qt, kt, vt, qn, kn = project_kernel(x, attn_full[:3])
    e, local, fetched, stat, mixed, mixed_t = attend_kernel(qt, k, vt, qn, kn, bias_tok, bias_bank, doc_row, gate, 0, NPAIR)
    out, act, gh, ffn_t, branch, gres, gmt, gain_ffn = feed_kernel(mixed, tokens, cotangent, vectors, second)
    grad_down_t, grad_up, grad_o = feed_grads_kernel(cot_t, act, ffn_t, gh, mixed_t, branch)
    dq, dk, dv, gl = unattend_kernel(q, kt, v, e, gmt, local, fetched, stat, gate, 0, NPAIR)
    grad_qkv, grad_gate = proj_grads_kernel(xt, dq, dk, dv, gl)
    grad_in, gain_attn = input_kernel(dq, dk, dv, gl, w, tokens, memory, vectors, gres)
    grad_vectors = jnp.concatenate([gain_attn, gain_ffn, grad_gate], axis=0)
    grads = (jnp.concatenate([grad_qkv, grad_o[None]], axis=0), grad_up, grad_down_t.T, grad_vectors)
    return (out, grad_in) + plain_tail(sizes, grads, *own, vectors, *moments, vector_moment)


def ordered(first, second):
    return lax.optimization_barrier((first, second))[0]


def fast_device(
    chips, planes, tokens, memory, bank, starts, neighbours, cotangent, own, vectors, moments, vector_moment
):
    own, moments = own[:2] + (own[2].T,), moments[:2] + (moments[2].T,)
    place = jnp.stack([lax.axis_index("chip"), lax.axis_index("core"), lax.axis_index("narrow")]).astype(jnp.int32)
    payload, payloads = payloads_kernel(place, *own, *moments)
    near_a = exchange([payload] * planes, "narrow")
    doc_row, doc_col = documents(starts)
    near_t = ordered(neighbours.T, payload)
    near_b = exchange(ordered(payloads, near_a), "narrow")
    column_a = stacked(near_a)
    plane_a = exchange([column_a] * chips, "chip")
    x, xt, cot_t, gate = context_kernel(tokens, memory, bank, cotangent, vectors, after=[column_a])
    bias_tok, bias_bank = mask_kernel(doc_row, doc_col, near_t, after=[x])
    first = core_blocks(ordered(plane_a, bias_tok))
    column_b, column_m = stacked_pair(ordered(near_b, first), payloads[0].shape[1] - own[1].shape[1])
    w, q, k, v, qt, kt, vt, qn, kn = project_kernel(x, first, place, after=[column_b])
    plane_b = exchange([column_b] * chips, "chip")
    e, local, fetched, stat, mixed, mixed_t = attend_kernel(qt, k, vt, qn, kn, bias_tok, bias_bank, doc_row, gate, 0, NPAIR)
    second = core_blocks(ordered(plane_b, mixed))
    plane_m = exchange([ordered(column_m, mixed)] * chips, "chip")
    out, gres, gmt, gain_ffn, keep_b, send_b = feed_blocks(
        mixed, mixed_t, tokens, cotangent, cot_t, vectors, second, place
    )
    back = (q, kt, v, e, gmt, local, fetched, stat, gate)
    some = unattend_kernel(*back, 0, 1, after=[keep_b])
    slots_b = fold_cores(keep_b, ordered(exchange([send_b, send_b], "core")[1], some[0]))
    all_m = core_blocks(ordered(plane_m, some[0]))
    dq, dk, dv, gl = unattend_kernel(*back, 1, NPAIR - 1, after=[slots_b[0], *all_m[4:]], alias=some)
    slots_b = fold_chips(ordered(exchange(slots_b, "chip"), dq))
    keep_a, send_a, grad_gate = proj_grads_kernel(xt, dq, dk, dv, gl, place, chips, planes, after=[slots_b[0]])
    slots_a = fold_cores_first(keep_a, exchange([send_a, send_a], "core")[1])
    grad_in, gain_attn = input_kernel(dq, dk, dv, gl, w, tokens, memory, vectors, gres, after=[slots_a[0]])
    parts_a = exchange(slots_a, "chip")
    parts_b = exchange(ordered(slots_b, slots_a), "narrow")
    parts_b, parts_a = ordered((parts_b, parts_a), grad_in)
    slots_a = fold_chips_first(parts_a, gain_attn, gain_ffn, grad_gate)
    parts_a = exchange(slots_a, "narrow")
    ga, gb, vec, *slots = owned_kernel(place, parts_a, parts_b)
    grads = core_blocks(exchange([stack_with_vectors(exchange(slots, "narrow"), vec)] * chips, "chip"))
    norm, vec_new, vec_mom, *slots = orthogonal_kernel(place, grads, all_m, vectors, vector_moment)
    final = exchange(slots, "narrow")
    new = list(update_kernel(place, final, norm, ga, gb, *moments, *own))
    new[2], new[5] = new[2].T, new[5].T
    return (out, grad_in, *new, vec_new, vec_mom, norm.reshape(()))


def solution(mesh):
    sizes = dict(mesh.shape)
    split = Mesh(
        mesh.devices.reshape(sizes["dp"] // 2, 2, sizes["narrow"]), ("chip", "core", "narrow")
    )
    dp = ("chip", "core")
    rows = ("chip", "core", "narrow")
    weights = (P(None, dp, "narrow"), P(dp, "narrow"), P("narrow", dp))
    return jax.shard_map(
        lambda *operands: per_device(sizes, *operands),
        mesh=split,
        in_specs=(P(rows, None), P(rows, None, None), P(rows, None, None), P(rows), P(rows, None), P(rows, None))
        + weights + (P(),) + weights + (P(),),
        out_specs=(P(rows, None), P(rows, None)) + weights + weights + (P(), P(), P()),
        check_vma=False,
    )
```

```python
import math

import jax
import jax.numpy as jnp
from jax import lax
from jax.experimental import pallas as pl
from jax.experimental.pallas import tpu as pltpu
from jax.sharding import Mesh, PartitionSpec as P

D = 512
H = 8
FF = 2048
MEM = 512
BANK = 512
KNB = 4
LEN = 1024
CTX = MEM + LEN
ROWS = CTX + BANK
HD = D // H
TB = 256
NT = LEN // TB
MC = MEM // TB
BC = BANK // TB
PAIR = 2 * HD
NPAIR = D // PAIR
F32 = jnp.float32
BF16 = jnp.bfloat16
NS_ITERS = 5
PARAMS = 3150848
epsilon = 1e-06
masked_score = -1e30
coef_first = 3.4445
coef_second = -4.775
coef_third = 2.0315
clip_fraction = 0.05
muon_rate = 0.5
muon_decay = 0.5
vector_rate = 0.5
vector_decay = 0.9
highest = lax.Precision.HIGHEST
LOG2E = 1.4426950408889634
SAFE = 80.0
VMEM_LIMIT = 60 * 1024 * 1024
SMALL = 16 * 1024 * 1024


def nn(a, b):
    return lax.dot_general(a, b, (((1,), (0,)), ((), ())), preferred_element_type=F32)


def nt(a, b):
    return lax.dot_general(a, b, (((1,), (1,)), ((), ())), preferred_element_type=F32)


def tn(a, b):
    return lax.dot_general(a, b, (((0,), (0,)), ((), ())), preferred_element_type=F32)


def rms_factor(values):
    return lax.rsqrt(jnp.mean(values * values, axis=-1, keepdims=True) + epsilon)


def whole(shape):
    return pl.BlockSpec(shape, lambda *_: (0,) * len(shape))


def call(
    body, grid, in_specs, out_specs, out_shape, flops, nbytes, name, scratch=(), trans=0, prefetch=0, after=(), alias=(),
    vmem=VMEM_LIMIT,
):
    extra, given = len(after) + len(alias), prefetch + len(in_specs)

    def with_extra(*refs):
        body(*refs[:given], *refs[given + extra :])

    made = pl.pallas_call(
        with_extra,
        grid_spec=pltpu.PrefetchScalarGridSpec(
            num_scalar_prefetch=prefetch,
            grid=grid,
            in_specs=list(in_specs) + [pl.BlockSpec(memory_space=pl.ANY)] * extra,
            out_specs=out_specs,
            scratch_shapes=list(scratch),
        ),
        out_shape=out_shape,
        input_output_aliases={given + len(after) + j: j for j in range(len(alias))},
        name=name,
        cost_estimate=pl.CostEstimate(flops=int(flops), bytes_accessed=int(nbytes), transcendentals=int(trans)),
        compiler_params=pltpu.CompilerParams(
            vmem_limit_bytes=vmem, dimension_semantics=("arbitrary",) * len(grid)
        ),
    )
    return lambda *operands: made(*operands, *after, *alias)


SMEM = pl.BlockSpec(memory_space=pltpu.SMEM)


def sds(shape, dtype):
    return jax.ShapeDtypeStruct(shape, dtype)


def hbm(shape, dtype):
    return pltpu.HBM(shape, dtype)


def vmem(shape, dtype):
    return pltpu.VMEM(shape, dtype)


RESIDENT = pl.BlockSpec(memory_space=pltpu.VMEM)


def context_body(tok_ref, mem_ref, bank_ref, cot_ref, vec_ref, x_ref, xt_ref, cott_ref, gate_ref):
    i = pl.program_id(0)
    gain = vec_ref[0:1, :]

    def put(rows):
        x_ref[...] = rows
        xt_ref[...] = rows.T

    def norm(values):
        wide = values.astype(F32)
        return (wide * rms_factor(wide) * gain).astype(BF16)

    @pl.when(i < MC)
    def _():
        put(norm(mem_ref[...]))

    @pl.when((i >= MC) & (i < MC + NT))
    def _():
        rows = norm(tok_ref[...])
        put(rows)
        logits = nt(vec_ref[2:10, :].astype(BF16), rows)
        gate = jax.nn.sigmoid(logits)
        for p in range(NPAIR):
            gate_ref[p] = gate[2 * p : 2 * p + 2, :]
        cott_ref[...] = cot_ref[...].T

    @pl.when(i >= MC + NT)
    def _():
        put(bank_ref[...])


def context_kernel(tokens, memory, bank, cot, vectors, after=()):
    steps = MC + NT + BC
    clip_tok = lambda i: jnp.clip(i - MC, 0, NT - 1)
    return call(
        context_body,
        (steps,),
        [
            pl.BlockSpec((TB, D), lambda i: (clip_tok(i), 0)),
            pl.BlockSpec((TB, D), lambda i: (jnp.minimum(i, MC - 1), 0)),
            pl.BlockSpec((TB, D), lambda i: (jnp.clip(i - MC - NT, 0, BC - 1), 0)),
            pl.BlockSpec((TB, D), lambda i: (clip_tok(i), 0)),
            whole((2 + H, D)),
        ],
        [
            pl.BlockSpec((TB, D), lambda i: (i, 0)),
            pl.BlockSpec((D, TB), lambda i: (0, i)),
            pl.BlockSpec((D, TB), lambda i: (0, clip_tok(i))),
            pl.BlockSpec((NPAIR, 2, TB), lambda i: (0, 0, clip_tok(i))),
        ],
        [sds((ROWS, D), BF16), vmem((D, ROWS), BF16), sds((D, LEN), BF16), hbm((NPAIR, 2, LEN), F32)],
        8e9,
        8e6,
        "context",
        after=after,
        vmem=SMALL,
    )(tokens, memory, bank, cot, vectors)


def mask_body(doc_row_ref, doc_col_ref, near_ref, tok_ref, bank_ref):
    i = pl.program_id(0)
    doc_row = doc_row_ref[...]

    @pl.when(i < NT)
    def _():
        keys = lax.broadcasted_iota(jnp.int32, (TB, LEN), 0) + i * TB
        rows = lax.broadcasted_iota(jnp.int32, (TB, LEN), 1)
        seen = (keys <= rows) & (doc_col_ref[...] == doc_row)
        tok_ref[...] = jnp.where(seen, 0.0, masked_score)

    @pl.when(i >= NT)
    def _():
        keys = lax.broadcasted_iota(jnp.int32, (TB, LEN), 0) + (i - NT) * TB
        count = jnp.zeros((TB, LEN), F32)
        for j in range(KNB):
            count = count + jnp.where(near_ref[j : j + 1, :] == keys, 1.0, 0.0)
        bias = jnp.where(count > 0.5, 0.0, masked_score)
        for j in range(2, KNB + 1):
            bias = jnp.where(count > j - 0.5, math.log2(j), bias)
        bank_ref[...] = bias


def mask_kernel(doc_row, doc_col, near_t, after=()):
    return call(
        mask_body,
        (NT + BC,),
        [
            whole((1, LEN)),
            pl.BlockSpec((TB, 1), lambda i: (jnp.minimum(i, NT - 1), 0)),
            whole((KNB, LEN)),
        ],
        [
            pl.BlockSpec((TB, LEN), lambda i: (jnp.minimum(i, NT - 1), 0)),
            pl.BlockSpec((TB, LEN), lambda i: (jnp.clip(i - NT, 0, BC - 1), 0)),
        ],
        [vmem((LEN, LEN), F32), vmem((BANK, LEN), F32)],
        6e9,
        7e6,
        "masks",
        after=after,
        vmem=SMALL,
    )(doc_row, doc_col, near_t)


def each_block(place_ref, chips, planes):
    for core in range(2):
        for chip in range(chips):
            row = ((place_ref[0] ^ chip) * 2 + (place_ref[1] ^ core))
            for plane in range(planes):
                yield core, chip, plane, row, place_ref[2] ^ plane


def part(index, size):
    return pl.ds(pl.multiple_of(index * size, size), size)


def head_squares(columns):
    wide = columns.astype(F32)
    return jnp.sum((wide * wide).reshape(H, HD, wide.shape[1]), axis=1)


def project_rows(i, x_ref, w_ref, q_ref, k_ref, v_ref, qt_ref, kt_ref, vt_ref, qn_ref, kn_ref):
    rows = x_ref[...]
    keys = nn(rows, w_ref[1]).astype(BF16)
    values = nn(rows, w_ref[2]).astype(BF16)
    keys_t = keys.T
    k_ref[...] = keys
    v_ref[...] = values
    kt_ref[...] = keys_t
    vt_ref[...] = values.T

    @pl.when(i == 0)
    def _():
        kn_ref[...] = jnp.zeros(kn_ref.shape, F32)
        qn_ref[...] = jnp.zeros(qn_ref.shape, F32)

    kn_ref[...] = jnp.maximum(kn_ref[...], head_squares(keys_t))

    @pl.when((i >= MEM // rows.shape[0]) & (i < CTX // rows.shape[0]))
    def _():
        queries = (nn(rows, w_ref[0]).astype(BF16).astype(F32) * (LOG2E / math.sqrt(HD))).astype(BF16)
        queries_t = queries.T
        q_ref[...] = queries
        qt_ref[...] = queries_t
        qn_ref[...] = jnp.maximum(qn_ref[...], head_squares(queries_t))


def project_kernel(x, w, place=None, after=()):
    rows = 2 * TB
    steps = ROWS // rows
    first_q, last_q = MEM // rows, CTX // rows - 1
    fast = place is not None
    if fast:
        chips, planes = len(w) // 2, w[0].shape[0]
        own_rows, own_cols = w[0].shape[1] // 3, w[0].shape[2]

    def body(*refs):
        i = pl.program_id(0)
        if not fast:
            project_rows(i, *refs)
            return
        place_ref, x_ref, *rest = refs
        blocks, (w_ref, *outs) = rest[: len(w)], rest[len(w) :]

        @pl.when(i == 0)
        def _():
            for core, chip, plane, row, col in each_block(place_ref, chips, planes):
                for j in range(3):
                    w_ref[j, part(row, own_rows), part(col, own_cols)] = blocks[core * chips + chip][
                        plane, j * own_rows : (j + 1) * own_rows, :
                    ]

        project_rows(i, x_ref, w_ref, *outs)

    out_specs = [
        pl.BlockSpec((rows, D), lambda i: (jnp.clip(i, first_q, last_q) - first_q, 0)),
        pl.BlockSpec((rows, D), lambda i: (i, 0)),
        pl.BlockSpec((rows, D), lambda i: (i, 0)),
        pl.BlockSpec((D, rows), lambda i: (0, jnp.clip(i, first_q, last_q) - first_q)),
        pl.BlockSpec((D, rows), lambda i: (0, i)),
        pl.BlockSpec((D, rows), lambda i: (0, i)),
        whole((H, rows)),
        whole((H, rows)),
    ]
    out_shape = [
        vmem((LEN, D), BF16),
        vmem((ROWS, D), BF16),
        vmem((ROWS, D), BF16),
        vmem((D, LEN), BF16),
        vmem((D, ROWS), BF16),
        vmem((D, ROWS), BF16),
        sds((H, rows), F32),
        sds((H, rows), F32),
    ]
    in_specs = [pl.BlockSpec((rows, D), lambda i: (i, 0))]
    if fast:
        in_specs = [SMEM] + in_specs + [RESIDENT] * len(w)
        out_specs = [whole((3, D, D))] + out_specs
        out_shape = [hbm((3, D, D), BF16)] + out_shape
        operands = (place, x, *w)
    else:
        in_specs = in_specs + [whole((3, D, D))]
        operands = (x, w)
    result = call(
        body, (steps,), in_specs, out_specs, out_shape, 11e9, 14e6, "project", after=after, vmem=24 * 1024 * 1024
    )(*operands)
    return result if fast else [w, *result]


def head_lanes(values, h):
    lanes = lax.broadcasted_iota(jnp.int32, values.shape, 1)
    keep = (lanes < HD) if h == 0 else (lanes >= HD)
    return jnp.where(keep, values, jnp.zeros_like(values))


def near_count(tb):
    return MEM + (tb + 1) * TB


def seen_count(tb):
    return near_count(tb) + BANK


FAR = slice(CTX, ROWS)


def head_rows_of(values, h):
    zeros = jnp.zeros((HD, values.shape[1]), values.dtype)
    own = values[h * HD : (h + 1) * HD, :]
    return jnp.concatenate([own, zeros] if h == 0 else [zeros, own], axis=0)


def attend_body(
    qt_ref, k_ref, vt_ref, tok_ref, bank_ref, doc_ref, gate_ref, qn_ref, kn_ref,
    e0_ref, e1_ref, e2_ref, e3_ref, local_ref, fetched_ref, stat_ref, mixed_ref, mixedt_ref, s_ref,
):
    e_refs = (e0_ref, e1_ref, e2_ref, e3_ref)
    units = [(tb, h) for tb in range(NT) for h in range(2)]

    def start(u):
        tb, h = units[u]
        near = near_count(tb)
        q_head = head_rows_of(qt_ref[:, tb * TB : (tb + 1) * TB], h)
        s_ref[u % 2, :near, :] = nn(k_ref[:near, :], q_head)
        s_ref[u % 2, near : near + BANK, :] = nn(k_ref[FAR, :], q_head)

    def biased(u, row, cols, mem_bias):
        s = s_ref[u % 2, row : row + TB, :]
        near = near_count(units[u][0])
        if row < MEM:
            return s + mem_bias
        if row < near:
            return s + tok_ref[row - MEM : row - MEM + TB, cols]
        return s + bank_ref[row - near : row - near + TB, cols]

    def soft(u, first, last, cols, mem_bias, general):
        tb, h = units[u]
        top = None
        if general:
            peak = jnp.full((8, TB), -3e38, F32)
            for row in range(first, last, TB):
                s = biased(u, row, cols, mem_bias)
                peak = jnp.maximum(peak, jnp.max(s.reshape(TB // 8, 8, TB), axis=0))
            top = jnp.max(peak, axis=0, keepdims=True)
        total = jnp.zeros((8, TB), F32)
        for row in range(first, last, TB):
            s = biased(u, row, cols, mem_bias)
            e = jnp.exp2(s - top if general else s)
            e_refs[tb][h, row : row + TB, :] = e.astype(BF16)
            total = total + jnp.sum(e.reshape(TB // 8, 8, TB), axis=0)
        return 1.0 / jnp.sum(total, axis=0, keepdims=True)

    def run(general):
        start(0)
        mixed_parts = []
        for u, (tb, h) in enumerate(units):
            cols = slice(tb * TB, (tb + 1) * TB)
            head_rows = slice(h * HD, (h + 1) * HD)
            near, seen = near_count(tb), seen_count(tb)
            if u + 1 < len(units):
                start(u + 1)
            mem_bias = jnp.where(doc_ref[:, cols] == 0.0, 0.0, masked_score)
            local_inv = soft(u, 0, near, cols, mem_bias, general)
            fetched_inv = soft(u, near, seen, cols, mem_bias, general)
            local = nn(vt_ref[head_rows, :near], e_refs[tb][h, :near, :]) * local_inv
            fetched = nn(vt_ref[head_rows, FAR], e_refs[tb][h, near:, :]) * fetched_inv
            local_ref[head_rows, cols] = local.astype(BF16)
            fetched_ref[head_rows, cols] = fetched.astype(BF16)
            stat_ref[0, h : h + 1, cols] = local_inv
            stat_ref[0, 2 + h : 3 + h, cols] = fetched_inv
            gate = gate_ref[0, h : h + 1, cols]
            mixed_parts.append((1.0 - gate) * local + gate * fetched)
            if h == 1:
                mixed = jnp.concatenate(mixed_parts, axis=0)
                mixed_parts = []
                mixedt_ref[:, cols] = mixed.astype(BF16)
                mixed_ref[cols, :] = mixed.T.astype(BF16)

    bound = jnp.max(jnp.max(qn_ref[...], axis=1, keepdims=True) * jnp.max(kn_ref[...], axis=1, keepdims=True))

    @pl.when(bound <= SAFE * SAFE)
    def _():
        run(False)

    @pl.when(jnp.logical_not(bound <= SAFE * SAFE))
    def _():
        run(True)


def attend_kernel(qt, k, vt, qn, kn, bias_tok, bias_bank, doc_row, gate, first, count):
    spec_cols = lambda rows: pl.BlockSpec((rows, PAIR), lambda p: (0, p + first))
    spec_rows = lambda cols: pl.BlockSpec((PAIR, cols), lambda p: (p + first, 0))
    *e, local, fetched, stat, mixed, mixed_t = call(
        attend_body,
        (count,),
        [
            spec_rows(LEN),
            spec_cols(ROWS),
            spec_rows(ROWS),
            RESIDENT,
            RESIDENT,
            whole((1, LEN)),
            pl.BlockSpec((1, 2, LEN), lambda p: (p + first, 0, 0)),
            whole(qn.shape),
            whole(kn.shape),
        ],
        [
            *[pl.BlockSpec((2, seen_count(tb), TB), lambda p: (p, 0, 0)) for tb in range(NT)],
            pl.BlockSpec((PAIR, LEN), lambda p: (p, 0)),
            pl.BlockSpec((PAIR, LEN), lambda p: (p, 0)),
            pl.BlockSpec((1, 8, LEN), lambda p: (p, 0, 0)),
            pl.BlockSpec((LEN, PAIR), lambda p: (0, p)),
            pl.BlockSpec((PAIR, LEN), lambda p: (p, 0)),
        ],
        [
            *[hbm((2 * count, seen_count(tb), TB), BF16) for tb in range(NT)],
            hbm((PAIR * count, LEN), BF16),
            hbm((PAIR * count, LEN), BF16),
            hbm((count, 8, LEN), F32),
            vmem((LEN, PAIR * count), BF16),
            vmem((PAIR * count, LEN), BF16),
        ],
        count * 5e9,
        count * 14e6 + 6e6,
        "attend",
        scratch=[pltpu.VMEM((2, ROWS, TB), F32)],
        trans=count * 2 * ROWS * LEN,
        vmem=28 * 1024 * 1024,
    )(qt, k, vt, bias_tok, bias_bank, doc_row, gate, qn, kn)
    return e, local, fetched, stat, mixed, mixed_t


def gelu_parts(x):
    square = jnp.exp2(x * x * (-0.5 * LOG2E))
    t = 1.0 / (1.0 + (0.3275911 * 0.7071067811865476) * jnp.abs(x))
    poly = t * (
        0.127414796 + t * (-0.142248368 + t * (0.7107068705 + t * (-0.7265760135 + t * 0.5307027145)))
    )
    tail = poly * square
    cdf = jnp.where(x >= 0.0, 1.0 - tail, tail)
    return cdf, square * 0.3989422804014327


FC = 512


def feed_body(
    mixed_ref, tok_ref, cot_ref, wo_ref, up_ref, dt_ref, vec_ref,
    out_ref, act_ref, gh_ref, ffnt_ref, branch_ref, gres_ref, gmt_ref, gain_ref,
):
    i = pl.program_id(0)
    residual = tok_ref[...].astype(F32) + nn(mixed_ref[...], wo_ref[...])
    factor = rms_factor(residual)
    hat = residual * factor
    gain = vec_ref[1:2, :]
    ffn = (hat * gain).astype(BF16)
    ffnt_ref[...] = ffn.T
    cot = cot_ref[...]
    out = residual
    grad_ffn = jnp.zeros(residual.shape, F32)
    for c in range(FF // FC):
        cols = slice(c * FC, (c + 1) * FC)
        hidden = nn(ffn, up_ref[:, cols])
        cdf, pdf = gelu_parts(hidden)
        act = (hidden * cdf).astype(BF16)
        act_ref[:, cols] = act
        grad_act = nn(cot, dt_ref[:, cols])
        gh = (grad_act * (cdf + hidden * pdf)).astype(BF16)
        gh_ref[:, cols] = gh
        out = out + nt(act, dt_ref[:, cols])
        grad_ffn = grad_ffn + nt(gh, up_ref[:, cols])
    out_ref[...] = out.astype(BF16)
    part = jnp.sum(grad_ffn * hat, axis=0, keepdims=True)

    @pl.when(i == 0)
    def _():
        gain_ref[...] = part

    @pl.when(i > 0)
    def _():
        gain_ref[...] += part

    scaled = grad_ffn * gain
    grad_res = cot.astype(F32) + factor * (scaled - hat * jnp.mean(scaled * hat, axis=-1, keepdims=True))
    gres_ref[...] = grad_res
    branch = grad_res.astype(BF16)
    branch_ref[...] = branch
    gmt_ref[...] = nt(wo_ref[...], branch)


def feed_kernel(mixed, tokens, cot, vectors, w):
    rows = lambda width: pl.BlockSpec((TB, width), lambda i: (i, 0))
    cols = lambda height: pl.BlockSpec((height, TB), lambda i: (0, i))

    def body(mixed_ref, tok_ref, cot_ref, vec_ref, wo_ref, up_ref, dt_ref, *outs):
        feed_body(mixed_ref, tok_ref, cot_ref, wo_ref, up_ref, dt_ref, vec_ref, *outs)

    return call(
        body,
        (NT,),
        [rows(D), rows(D), rows(D), whole((2 + H, D))] + [whole(x.shape) for x in w],
        [rows(D), rows(FF), rows(FF), cols(D), rows(D), rows(D), cols(D), whole((1, D))],
        [
            sds((LEN, D), BF16),
            sds((LEN, FF), BF16),
            sds((LEN, FF), BF16),
            sds((D, LEN), BF16),
            sds((LEN, D), BF16),
            sds((LEN, D), F32),
            sds((D, LEN), F32),
            sds((1, D), F32),
        ],
        23e9,
        22e6,
        "feed",
        trans=LEN * FF * 2,
    )(mixed, tokens, cot, vectors, *w)


def feed_grads_body(cott_ref, act_ref, ffnt_ref, gh_ref, mixedt_ref, branch_ref, gd_ref, gu_ref, go_ref):
    gd_ref[...] = nn(cott_ref[...], act_ref[...]).astype(BF16)
    gu_ref[...] = nn(ffnt_ref[...], gh_ref[...]).astype(BF16)
    go_ref[...] = nn(mixedt_ref[...], branch_ref[...]).astype(BF16)


def feed_grads_kernel(cot_t, act, ffn_t, gh, mixed_t, branch):
    steps = 4
    wide = lambda width: pl.BlockSpec((LEN, width // steps), lambda i: (0, i))
    out = lambda width: pl.BlockSpec((D, width // steps), lambda i: (0, i))
    return call(
        feed_grads_body,
        (steps,),
        [whole((D, LEN)), wide(FF), whole((D, LEN)), wide(FF), whole((D, LEN)), wide(D)],
        [out(FF), out(FF), out(D)],
        [sds((D, FF), BF16), sds((D, FF), BF16), sds((D, D), BF16)],
        11e9,
        17e6,
        "feed_grads",
    )(cot_t, act, ffn_t, gh, mixed_t, branch)


def feed_blocks(mixed, mixed_t, tokens, cot, cot_t, vectors, w, place):
    chips, planes = len(w) // 2, w[0].shape[0]
    own_rows, own_o, own_ff = w[0].shape[1], D // planes, FF // planes
    width = own_o + 2 * own_ff
    size = 2 * TB
    row_steps = LEN // size

    def body(place_ref, mixed_ref, mixedt_ref, tok_ref, cot_ref, cott_ref, vec_ref, *rest):
        blocks, rest = rest[: len(w)], rest[len(w) :]
        out_ref, gres_ref, gmt_ref, gain_ref, keep_ref, send_ref = rest[:6]
        wo_ref, up_ref, dt_ref, act_ref, gh_ref, ffnt_ref, branch_ref, hid_ref, ga_ref, all_ref = rest[6:]
        i = pl.program_id(0)

        @pl.when(i == 0)
        def _():
            for core, chip, plane, row, col in each_block(place_ref, chips, planes):
                block = blocks[core * chips + chip]
                here = part(row, own_rows)
                wo_ref[here, part(col, own_o)] = block[plane, :, :own_o]
                up_ref[here, part(col, own_ff)] = block[plane, :, own_o : own_o + own_ff]
                dt_ref[here, part(col, own_ff)] = block[plane, :, own_o + own_ff :]

        @pl.when(i < row_steps)
        def _():
            here = part(i, size)
            residual = tok_ref[...].astype(F32) + nn(mixed_ref[...], wo_ref[...])
            factor = rms_factor(residual)
            hat = residual * factor
            gain = vec_ref[1:2, :]
            ffn = (hat * gain).astype(BF16)
            ffnt_ref[:, here] = ffn.T
            cot = cot_ref[...]

            def start(c):
                cols = slice(c * FC, (c + 1) * FC)
                hid_ref[c % 2] = nn(ffn, up_ref[:, cols])
                ga_ref[c % 2] = nn(cot, dt_ref[:, cols])

            out = residual
            grad_ffn = jnp.zeros(residual.shape, F32)
            start(0)
            for c in range(FF // FC):
                cols = slice(c * FC, (c + 1) * FC)
                if c + 1 < FF // FC:
                    start(c + 1)
                hidden = hid_ref[c % 2]
                cdf, pdf = gelu_parts(hidden)
                act_ref[here, cols] = (hidden * cdf).astype(BF16)
                gh_ref[here, cols] = (ga_ref[c % 2] * (cdf + hidden * pdf)).astype(BF16)
                out = out + nt(act_ref[here, cols], dt_ref[:, cols])
                grad_ffn = grad_ffn + nt(gh_ref[here, cols], up_ref[:, cols])
            out_ref[...] = out.astype(BF16)
            gain_part = jnp.sum(grad_ffn * hat, axis=0, keepdims=True)

            @pl.when(i == 0)
            def _():
                gain_ref[...] = gain_part

            @pl.when(i > 0)
            def _():
                gain_ref[...] += gain_part

            scaled = grad_ffn * gain
            grad_res = cot.astype(F32) + factor * (scaled - hat * jnp.mean(scaled * hat, axis=-1, keepdims=True))
            gres_ref[...] = grad_res
            branch = grad_res.astype(BF16)
            branch_ref[here, :] = branch
            gmt_ref[...] = nt(wo_ref[...], branch)

        @pl.when(i >= row_steps)
        def _():
            plane = i - row_steps
            cols = part(plane, own_ff)
            all_ref[:, :own_o] = nn(mixedt_ref[...], branch_ref[:, part(plane, own_o)]).astype(BF16)
            all_ref[:, own_o : own_o + own_ff] = nn(ffnt_ref[...], gh_ref[:, cols]).astype(BF16)
            all_ref[:, own_o + own_ff :] = nn(cott_ref[...], act_ref[:, cols]).astype(BF16)
            for chip in range(chips):
                slot = place_ref[0] ^ chip
                keep_ref[slot, 0] = all_ref[part(chip * 2 + place_ref[1], own_rows), :]
                send_ref[slot, 0] = all_ref[part(chip * 2 + 1 - place_ref[1], own_rows), :]

    row = lambda i: jnp.minimum(i, row_steps - 1)
    rows = pl.BlockSpec((size, D), lambda i, _: (row(i), 0))
    blocked = pl.BlockSpec(
        (chips, 1, own_rows, width), lambda i, place_ref: (0, jnp.maximum(i - row_steps, 0) ^ place_ref[2], 0, 0)
    )
    shape = hbm((chips, planes, own_rows, width), BF16)
    return call(
        body,
        (row_steps + planes,),
        [rows, RESIDENT, rows, rows, RESIDENT, whole((2 + H, D))] + [RESIDENT] * len(w),
        [rows, rows, pl.BlockSpec((D, size), lambda i, _: (0, row(i))), whole((1, D)), blocked, blocked],
        [hbm((LEN, D), BF16), hbm((LEN, D), F32), vmem((D, LEN), F32), sds((1, D), F32), vmem((chips, planes, own_rows, width), BF16), shape],
        30e9,
        22e6,
        "feed",
        scratch=[
            pltpu.VMEM((D, D), BF16),
            pltpu.VMEM((D, FF), BF16),
            pltpu.VMEM((D, FF), BF16),
            pltpu.VMEM((LEN, FF), BF16),
            pltpu.VMEM((LEN, FF), BF16),
            pltpu.VMEM((D, LEN), BF16),
            pltpu.VMEM((LEN, D), BF16),
            pltpu.VMEM((2, size, FC), F32),
            pltpu.VMEM((2, size, FC), F32),
            pltpu.VMEM((D, width), BF16),
        ],
        trans=LEN * FF * 2,
        prefetch=1,
        vmem=36 * 1024 * 1024,
    )(place, mixed, mixed_t, tokens, cot, cot_t, vectors, *w)


def unattend_body(
    q_ref, kt_ref, v_ref, e0_ref, e1_ref, e2_ref, e3_ref, gmt_ref, local_ref, fetched_ref, stat_ref, gate_ref,
    dq_ref, dk_ref, dv_ref, gl_ref, ds0_ref, ds1_ref, ds2_ref, ds3_ref, do_ref, df_ref, dot_ref, dqt_ref, dk_acc, dv_acc, gp_ref,
):
    e_refs, ds_refs = (e0_ref, e1_ref, e2_ref, e3_ref), (ds0_ref, ds1_ref, ds2_ref, ds3_ref)

    def prepare(h):
        head_rows = slice(h * HD, (h + 1) * HD)
        gm = gmt_ref[head_rows, :]
        local = local_ref[head_rows, :].astype(F32)
        fetched = fetched_ref[head_rows, :].astype(F32)
        gate = gate_ref[0, h : h + 1, :]
        local_inv = stat_ref[0, h : h + 1, :]
        fetched_inv = stat_ref[0, 2 + h : 3 + h, :]
        grad_gate = jnp.sum(gm * (fetched - local), axis=0, keepdims=True)
        gl_ref[0, h : h + 1, :] = grad_gate * gate * (1.0 - gate)
        grad_local = ((1.0 - gate) * gm).astype(BF16).astype(F32)
        grad_fetched = gate * gm
        other = slice((1 - h) * HD, (2 - h) * HD)
        do_ref[h, other, :] = jnp.zeros((HD, LEN), BF16)
        df_ref[h, other, :] = jnp.zeros((HD, LEN), BF16)
        do_ref[h, head_rows, :] = (grad_local * local_inv).astype(BF16)
        df_ref[h, head_rows, :] = (grad_fetched * fetched_inv).astype(BF16)
        dot_ref[h : h + 1, :] = jnp.sum(grad_local * local, axis=0, keepdims=True) * local_inv
        dot_ref[2 + h : 3 + h, :] = jnp.sum(grad_fetched * fetched, axis=0, keepdims=True) * fetched_inv

    units = [(tb, h) for h in range(2) for tb in range(NT)]

    def start(u):
        tb, h = units[u]
        near, cols = near_count(tb), slice(tb * TB, (tb + 1) * TB)
        gp_ref[u % 2, :near, :] = nn(v_ref[:near, :], do_ref[h, :, cols])
        gp_ref[u % 2, near : near + BANK, :] = nn(v_ref[FAR, :], df_ref[h, :, cols])

    def rows_part(u):
        tb, h = units[u]
        near, cols = near_count(tb), slice(tb * TB, (tb + 1) * TB)
        head_rows = slice(h * HD, (h + 1) * HD)
        for row in range(0, seen_count(tb), TB):
            some, which = slice(row, row + TB), h if row < near else 2 + h
            gp = gp_ref[u % 2, some, :] - dot_ref[which : which + 1, cols]
            ds_refs[tb][h, some, :] = (e_refs[tb][h, some, :].astype(F32) * gp).astype(BF16)
        dq = nn(kt_ref[head_rows, :near], ds_refs[tb][h, :near, :])
        dq = dq + nn(kt_ref[head_rows, FAR], ds_refs[tb][h, near:, :])
        dqt_ref[head_rows, cols] = dq * (1.0 / math.sqrt(HD))

    def keys_part(h, tb):
        near, cols = near_count(tb), slice(tb * TB, (tb + 1) * TB)
        q_head = head_lanes(q_ref[cols, :], h)
        pieces = (
            (slice(0, near), slice(0, near), do_ref[h, :, cols]),
            (FAR, slice(near, near + BANK), df_ref[h, :, cols]),
        )
        for keys, some, grad_out in pieces:
            dv = nt(e_refs[tb][h, some, :], grad_out)
            dk = nn(ds_refs[tb][h, some, :], q_head)
            if h == 0 and tb == NT - 1:
                dv_acc[keys, :] = dv
                dk_acc[keys, :] = dk
            else:
                dv_acc[keys, :] += dv
                dk_acc[keys, :] += dk

    prepare(0)
    start(0)
    prepare(1)
    for u, (tb, h) in enumerate(units):
        if u + 1 < len(units):
            start(u + 1)
        rows_part(u)
        if h == 1:
            keys_part(0, NT - 1 - tb)
    for tb in range(NT):
        keys_part(1, tb)
    dv_ref[...] = dv_acc[...].astype(BF16)
    dk_ref[...] = (dk_acc[...] * (1.0 / LOG2E)).astype(BF16)
    dq_ref[...] = dqt_ref[...].T.astype(BF16)


def unattend_kernel(q, kt, v, e, gmt, local, fetched, stat, gate, first, count, after=(), alias=()):
    spec_cols = lambda rows: pl.BlockSpec((rows, PAIR), lambda p: (0, p + first))
    spec_rows = lambda cols: pl.BlockSpec((PAIR, cols), lambda p: (p + first, 0))
    return call(
        unattend_body,
        (count,),
        [
            spec_cols(LEN),
            spec_rows(ROWS),
            spec_cols(ROWS),
            *[pl.BlockSpec((2, seen_count(tb), TB), lambda p: (p + first, 0, 0)) for tb in range(NT)],
            spec_rows(LEN),
            spec_rows(LEN),
            spec_rows(LEN),
            pl.BlockSpec((1, 8, LEN), lambda p: (p + first, 0, 0)),
            pl.BlockSpec((1, 2, LEN), lambda p: (p + first, 0, 0)),
        ],
        [
            spec_cols(LEN),
            spec_cols(ROWS),
            spec_cols(ROWS),
            pl.BlockSpec((1, 2, LEN), lambda p: (p + first, 0, 0)),
        ],
        [
            sds((LEN, D), BF16),
            sds((ROWS, D), BF16),
            sds((ROWS, D), BF16),
            sds((NPAIR, 2, LEN), F32),
        ],
        count * 10e9,
        count * 14e6,
        "unattend",
        scratch=[
            *[pltpu.VMEM((2, seen_count(tb), TB), BF16) for tb in range(NT)],
            pltpu.VMEM((2, PAIR, LEN), BF16),
            pltpu.VMEM((2, PAIR, LEN), BF16),
            pltpu.VMEM((8, LEN), F32),
            pltpu.VMEM((PAIR, LEN), F32),
            pltpu.VMEM((ROWS, PAIR), F32),
            pltpu.VMEM((ROWS, PAIR), F32),
            pltpu.VMEM((2, ROWS, TB), F32),
        ],
        after=after,
        alias=alias,
        vmem=36 * 1024 * 1024,
    )(q, kt, v, *e, gmt, local, fetched, stat, gate)


def all_heads(gl_ref):
    return jnp.concatenate([gl_ref[p] for p in range(NPAIR)], axis=0).astype(BF16)


def proj_grads_body(xt_ref, dq_ref, dk_ref, dv_ref, gl_ref, g_ref, gate_ref):
    g_ref[0] = nn(xt_ref[:, MEM:CTX], dq_ref[...]).astype(BF16)
    g_ref[1] = nn(xt_ref[...], dk_ref[...]).astype(BF16)
    g_ref[2] = nn(xt_ref[...], dv_ref[...]).astype(BF16)

    @pl.when(pl.program_id(0) == 0)
    def _():
        gate_ref[...] = nt(all_heads(gl_ref), xt_ref[:, MEM:CTX])


def proj_grads_kernel(xt, dq, dk, dv, gl, place=None, chips=0, planes=0, after=()):
    steps = 2
    fast = place is not None
    wide = lambda rows: pl.BlockSpec((rows, D // steps), lambda i, *_: (0, i))
    in_specs = [whole((D, ROWS)), wide(LEN), wide(ROWS), wide(ROWS), whole((NPAIR, 2, LEN))]
    gate_spec, gate_shape = whole((H, D)), sds((H, D), F32)
    flops, nbytes = 8e9, 10e6
    if not fast:
        return call(
            proj_grads_body,
            (steps,),
            in_specs,
            [pl.BlockSpec((3, D, D // steps), lambda i: (0, 0, i)), gate_spec],
            [sds((3, D, D), BF16), gate_shape],
            flops,
            nbytes,
            "proj_grads",
        )(xt, dq, dk, dv, gl)
    own_rows, own_cols, group = D // (2 * chips), D // planes, planes // steps

    def body(place_ref, xt_ref, dq_ref, dk_ref, dv_ref, gl_ref, keep_ref, send_ref, gate_ref, all_ref):
        proj_grads_body(xt_ref, dq_ref, dk_ref, dv_ref, gl_ref, all_ref, gate_ref)
        for b in range(group):
            col = b ^ (place_ref[2] % group)
            cols = slice(b * own_cols, (b + 1) * own_cols)
            for chip in range(chips):
                slot = place_ref[0] ^ chip
                for j in range(3):
                    here = slice(j * own_rows, (j + 1) * own_rows)
                    keep_ref[slot, col, here, :] = all_ref[j, part(chip * 2 + place_ref[1], own_rows), cols]
                    send_ref[slot, col, here, :] = all_ref[j, part(chip * 2 + 1 - place_ref[1], own_rows), cols]

    out = pl.BlockSpec(
        (chips, group, 3 * own_rows, own_cols), lambda i, place_ref: (0, i ^ (place_ref[2] // group), 0, 0)
    )
    shape = sds((chips, planes, 3 * own_rows, own_cols), BF16)
    return call(
        body,
        (steps,),
        in_specs,
        [out, out, gate_spec],
        [shape, shape, gate_shape],
        flops,
        nbytes,
        "proj_grads",
        scratch=[pltpu.VMEM((3, D, D // steps), BF16)],
        prefetch=1,
        after=after,
        vmem=24 * 1024 * 1024,
    )(place, xt, dq, dk, dv, gl)


def input_body(dq_ref, dk_ref, dv_ref, gl_ref, w_ref, tok_ref, mem_ref, vec_ref, gres_ref, gin_ref, gain_ref):
    i = pl.program_id(0)
    gn = nt(dk_ref[...], w_ref[1]) + nt(dv_ref[...], w_ref[2])

    @pl.when(i < MC)
    def _():
        wide = mem_ref[...].astype(F32)
        part = jnp.sum(gn * (wide * rms_factor(wide)), axis=0, keepdims=True)

        @pl.when(i == 0)
        def _():
            gain_ref[...] = part

        @pl.when(i > 0)
        def _():
            gain_ref[...] += part

    @pl.when(i >= MC)
    def _():
        wide = tok_ref[...].astype(F32)
        factor = rms_factor(wide)
        hat = wide * factor
        full = gn + nt(dq_ref[...], w_ref[0]) + tn(all_heads(gl_ref), vec_ref[2:10, :].astype(BF16))
        gain_ref[...] += jnp.sum(full * hat, axis=0, keepdims=True)
        scaled = full * vec_ref[0:1, :]
        gin_ref[...] = (
            gres_ref[...] + factor * (scaled - hat * jnp.mean(scaled * hat, axis=-1, keepdims=True))
        ).astype(BF16)


def input_kernel(dq, dk, dv, gl, w, tokens, memory, vectors, gres, after=()):
    tok = lambda i: jnp.clip(i - MC, 0, NT - 1)
    rows = pl.BlockSpec((TB, D), lambda i: (tok(i), 0))
    return call(
        input_body,
        (MC + NT,),
        [
            rows,
            pl.BlockSpec((TB, D), lambda i: (i, 0)),
            pl.BlockSpec((TB, D), lambda i: (i, 0)),
            pl.BlockSpec((NPAIR, 2, TB), lambda i: (0, 0, tok(i))),
            whole((3, D, D)),
            rows,
            pl.BlockSpec((TB, D), lambda i: (jnp.minimum(i, MC - 1), 0)),
            whole((2 + H, D)),
            rows,
        ],
        [rows, whole((1, D))],
        [sds((LEN, D), BF16), sds((1, D), F32)],
        9e9,
        10e6,
        "input",
        after=after,
        vmem=SMALL,
    )(dq, dk, dv, gl, w, tokens, memory, vectors, gres)


def exchange(slots, axis):
    size = len(slots)
    return [slots[0]] + [
        lax.ppermute(slots[r], axis, [(i, i ^ r) for i in range(size)]) for r in range(1, size)
    ]


def added(parts):
    total = parts[0].astype(F32)
    for other in parts[1:]:
        total = total + other.astype(F32)
    return total


PLANES = (("up",), ("q", "k"), ("v", "o"), ("down",))
EXTRA = 16


def alone(body, operands, out_shape, name, scratch=(), place=None, after=(), flops=2e9, vmem=SMALL, resident=0):
    specs = [RESIDENT if j < resident else whole(x.shape) for j, x in enumerate(operands)]
    if place is not None:
        specs, operands = [SMEM] + specs, (place, *operands)
    return call(
        body,
        (1,),
        specs,
        [whole(x.shape) for x in out_shape],
        out_shape,
        flops,
        2e6,
        name,
        scratch=scratch,
        after=after,
        vmem=vmem,
    )(*operands)


def first_payload(attn_weights):
    rows, cols = attn_weights.shape[1:]

    def body(aw_ref, out_ref):
        for j in range(3):
            out_ref[j * rows : (j + 1) * rows, :] = aw_ref[j].astype(BF16)

    return alone(body, (attn_weights,), [vmem((3 * rows, cols), BF16)], "first_payload", vmem=VMEM_LIMIT)[0]


def second_payloads(place, attn_weights, up_weights, down_weights, attn_moment, up_moment, down_moment, after):
    rows, cols = attn_weights.shape[1:]
    wide = up_weights.shape[1]
    planes = len(PLANES)
    width = cols + 3 * wide

    def body(place_ref, aw_ref, uw_ref, dw_ref, am_ref, um_ref, dm_ref, *rest):
        outs, all_ref = rest[:planes], rest[planes]
        all_ref[...] = jnp.zeros(all_ref.shape, BF16)
        all_ref[0] = um_ref[...].astype(BF16)
        all_ref[3] = dm_ref[...].astype(BF16)
        for j in range(4):
            all_ref[1 + j // 2, :, (j % 2) * cols : (j % 2 + 1) * cols] = am_ref[j].astype(BF16)
        for r in range(planes):
            outs[r][:, :cols] = aw_ref[3].astype(BF16)
            outs[r][:, cols : cols + wide] = uw_ref[...].astype(BF16)
            outs[r][:, cols + wide : cols + 2 * wide] = dw_ref[...].astype(BF16)
            outs[r][:, cols + 2 * wide :] = all_ref[place_ref[2] ^ r]

    return alone(
        body,
        (attn_weights, up_weights, down_weights, attn_moment, up_moment, down_moment),
        [vmem((rows, width), BF16)] * planes,
        "second_payloads",
        scratch=[pltpu.VMEM((planes, rows, wide), BF16)],
        place=place,
        after=after,
        vmem=VMEM_LIMIT,
    )


def stacked_pair(parts, width):
    rows = parts[0].shape[0]
    other = parts[0].shape[1] - width

    def body(*refs):
        for r in range(len(parts)):
            refs[-2][r] = refs[r][:, :width]
            refs[-1][r] = refs[r][:, width:]

    shapes = [sds((len(parts), rows, width), BF16), sds((len(parts), rows, other), BF16)]
    return alone(body, parts, shapes, "stacked_pair", resident=len(parts))


def stacked(parts, after=()):
    def body(*refs):
        for r in range(len(parts)):
            refs[-1][r] = refs[r][...]

    return alone(body, parts, [sds((len(parts),) + parts[0].shape, parts[0].dtype)], "stacked", after=after, resident=len(parts))[0]


def core_blocks(plane):
    return plane + [exchange([b, b], "core")[1] for b in plane]


def fold_cores(keep, other):
    chips, planes, rows, width = keep.shape

    def body(keep_ref, other_ref, *outs):
        for chip in range(chips):
            outs[chip][...] = added([keep_ref[chip], other_ref[chip]]).astype(BF16)

    spec = pl.BlockSpec((chips, 1, rows, width), lambda i: (0, i, 0, 0))
    return call(
        body,
        (planes,),
        [spec, spec],
        [pl.BlockSpec((1, rows, width), lambda i: (i, 0, 0))] * chips,
        [sds((planes, rows, width), BF16)] * chips,
        4e9,
        7e6,
        "fold_cores",
        vmem=SMALL,
    )(keep, other)


def fold_chips(parts):
    planes, rows, width = parts[0].shape

    def body(*refs):
        for plane in range(planes):
            refs[len(parts) + plane][...] = added([r[plane] for r in refs[: len(parts)]]).astype(BF16)

    return alone(body, parts, [sds((rows, width), BF16)] * planes, "fold_chips", resident=len(parts))


VEC = 2 + H
VEC_ROWS = 128


def put_vectors(ref, first, values):
    high = values.astype(BF16)
    low = (values - high.astype(F32)).astype(BF16)
    ref[first : first + VEC_ROWS, :] = jnp.zeros((VEC_ROWS, 128), BF16)
    for j in range(4):
        lanes = slice(j * 128, (j + 1) * 128)
        ref[first + j * 16 : first + j * 16 + VEC, :] = high[:, lanes]
        ref[first + 64 + j * 16 : first + 64 + j * 16 + VEC, :] = low[:, lanes]


def get_vectors(refs, first):
    pieces = []
    for j in range(4):
        rows = lambda offset: slice(first + offset + j * 16, first + offset + j * 16 + VEC)
        pieces.append(added([r[rows(offset), :] for r in refs for offset in (0, 64)]))
    return jnp.concatenate(pieces, axis=1)


def fold_cores_first(keep, other):
    chips = keep.shape[0]

    def body(keep_ref, other_ref, *outs):
        for chip in range(chips):
            outs[chip][...] = added([keep_ref[chip], other_ref[chip]]).astype(BF16)

    return alone(body, (keep, other), [sds(keep.shape[1:], BF16)] * chips, "fold_cores_first")


def fold_chips_first(parts, gain_attn, gain_ffn, grad_gate):
    planes, rows, width = parts[0].shape
    count = len(parts)

    def body(*refs):
        ins, (ga_ref, gf_ref, gg_ref) = refs[:count], refs[count : count + 3]
        outs, vec_ref = refs[count + 3 : -1], refs[-1]
        vec_ref[0:1, :] = ga_ref[...]
        vec_ref[1:2, :] = gf_ref[...]
        vec_ref[2:VEC, :] = gg_ref[...]
        for plane in range(planes):
            outs[plane][:rows, :] = added([r[plane] for r in ins]).astype(BF16)
            put_vectors(outs[plane], rows, vec_ref[...])

    return alone(
        body,
        (*parts, gain_attn, gain_ffn, grad_gate),
        [sds((rows + VEC_ROWS, width), BF16)] * planes,
        "fold_chips_first",
        resident=count,
        scratch=[pltpu.VMEM((VEC, D), F32)],
    )


def stack_with_vectors(parts, vec):
    count, width = len(parts), parts[0].shape[1]
    rows = parts[0].shape[0] - EXTRA

    def body(*refs):
        vec_ref, out_ref = refs[count], refs[count + 1]
        for r in range(count):
            out_ref[r * rows : (r + 1) * rows, :] = refs[r][:rows, :]
        squares = added([r[rows:, :] for r in refs[:count]])
        squares = jnp.sum(squares, axis=0, keepdims=True) + jnp.zeros((EXTRA, width), F32)
        high = squares.astype(BF16).astype(F32)
        middle = (squares - high).astype(BF16).astype(F32)
        row = lax.broadcasted_iota(jnp.int32, (EXTRA, width), 0)
        extra = jnp.where(row == VEC, high, jnp.where(row == VEC + 1, middle, squares - high - middle))
        values = jnp.concatenate([vec_ref[...], jnp.zeros((EXTRA - VEC, width), F32)], axis=0)
        first = values.astype(BF16).astype(F32)
        here = count * rows
        out_ref[here : here + EXTRA, :] = jnp.where(row < VEC, first, extra).astype(BF16)
        out_ref[here + EXTRA :, :] = (values - first).astype(BF16)

    return alone(
        body, (*parts, vec), [sds((count * rows + 2 * EXTRA, width), BF16)], "stack_with_vectors", resident=count + 1
    )[0]


def owned_kernel(place, parts_a, parts_b):
    planes = len(parts_a)
    size, cols = parts_a[0].shape[0] - VEC_ROWS, parts_a[0].shape[1]
    rows, width = parts_b[0].shape
    wide = (width - cols) // 2

    def body(place_ref, *refs):
        a_refs, b_refs = refs[:planes], refs[planes : 2 * planes]
        ga_ref, gb_ref, vec_ref, *rest = refs[2 * planes :]
        slots, all_ref = rest[:planes], rest[planes]
        ga = added([r[:size, :] for r in a_refs])
        gb = added([r[...] for r in b_refs])
        ga_ref[...] = ga
        gb_ref[...] = gb
        vec_ref[...] = get_vectors(a_refs, size)
        squares = jnp.sum(ga * ga, keepdims=True) + jnp.sum(gb * gb, keepdims=True)
        all_ref[...] = jnp.zeros(all_ref.shape, BF16)
        for j in range(4):
            grad = ga[j * rows : (j + 1) * rows, :] if j < 3 else gb[:, :cols]
            all_ref[1 + j // 2, :, (j % 2) * cols : (j % 2 + 1) * cols] = grad.astype(BF16)
        all_ref[0] = gb[:, cols : cols + wide].astype(BF16)
        all_ref[3] = gb[:, cols + wide :].astype(BF16)
        wide_squares = squares + jnp.zeros((EXTRA, wide), F32)
        row = lax.broadcasted_iota(jnp.int32, (EXTRA, wide), 0)
        high = wide_squares.astype(BF16).astype(F32)
        middle = (wide_squares - high).astype(BF16).astype(F32)
        low = wide_squares - high - middle
        extra = jnp.where(row == 0, high, jnp.where(row == 1, middle, jnp.where(row == 2, low, 0.0))).astype(BF16)
        for r in range(planes):
            slots[r][:rows, :] = all_ref[place_ref[2] ^ r]
            slots[r][rows:, :] = extra

    return alone(
        body,
        (*parts_a, *parts_b),
        [hbm((size, cols), F32), hbm((rows, width), F32), sds((VEC, D), F32)]
        + [sds((rows + EXTRA, wide), BF16)] * planes,
        "owned",
        resident=2 * planes,
        scratch=[pltpu.VMEM((planes, rows, wide), BF16)],
        place=place,
    )


def orthogonal_kernel(place, grads, moments, vectors, vec_moment):
    count = len(grads)
    chips = count // 2
    planes, rows = moments[0].shape[:2]
    wide = grads[0].shape[1]
    cols = D // planes
    limit = clip_fraction * math.sqrt(PARAMS)

    def body(place_ref, *refs):
        grad_refs, moment_refs, refs = refs[:count], refs[count : 2 * count], refs[2 * count :]
        vec_ref, vm_ref, norm_ref, vn_ref, vmn_ref = refs[:5]
        outs = refs[5 : 5 + planes]
        low_ref, x_ref, mix_ref, diag_ref, all_ref = refs[5 + planes :]
        pair = (place_ref[2] == 1) | (place_ref[2] == 2)
        own = part(place_ref[0] * 2 + place_ref[1], rows)
        after = planes * rows
        extra = added([r[after : after + EXTRA, :] for r in grad_refs])
        grad_vec = extra[:VEC, :] + added([r[after + EXTRA : after + EXTRA + VEC, :] for r in grad_refs])
        total = jnp.sum(extra[VEC : VEC + 3, 0:1], axis=0, keepdims=True) + jnp.sum(grad_vec * grad_vec, keepdims=True)
        norm = jnp.sqrt(total)
        norm_ref[...] = norm
        clip = limit / jnp.maximum(norm, limit)
        vec_mom = vector_decay * vm_ref[...] + clip * grad_vec
        vmn_ref[...] = vec_mom
        vn_ref[...] = vec_ref[...] - vector_rate * vec_mom

        def momentum(core, chip, plane, lanes):
            b = core * chips + chip
            moment = moment_refs[b][plane, :, lanes].astype(F32)
            grad = grad_refs[b][plane * rows : (plane + 1) * rows, lanes].astype(F32)
            return muon_decay * moment + clip * grad

        def gram_of(start, width):
            half = D // 2
            upper, lower = low_ref[:half, start : start + width], low_ref[half:, start : start + width]
            corner = nt(lower, upper)
            first = jnp.concatenate([nt(upper, upper), corner.T], axis=1)
            return jnp.concatenate([first, jnp.concatenate([corner, nt(lower, lower)], axis=1)], axis=0)

        def mixing(gram):
            eye = lax.broadcasted_iota(jnp.int32, (D, D), 0) == lax.broadcasted_iota(jnp.int32, (D, D), 1)
            low = gram.astype(BF16)
            mix = coef_second * low.astype(F32) + coef_third * nn(low, low)
            diag_ref[...] = coef_first + jnp.sum(jnp.where(eye, mix, 0.0), axis=1, keepdims=True)
            mix_ref[...] = jnp.where(eye, 0.0, mix).astype(BF16)

        def advance(start, width, scale):
            for c in range(start, start + width, D):
                lanes = slice(c, c + D)
                new = diag_ref[...] * x_ref[:, lanes] + nn(mix_ref[...], low_ref[:, lanes])
                if scale is not None:
                    new = new * scale
                x_ref[:, lanes] = new
                low_ref[:, lanes] = new.astype(BF16)

        def first_step(start, width):
            gram = gram_of(start, width)
            eye = lax.broadcasted_iota(jnp.int32, (D, D), 0) == lax.broadcasted_iota(jnp.int32, (D, D), 1)
            scale = 1.0 / (jnp.sqrt(jnp.sum(jnp.where(eye, gram, 0.0), keepdims=True)) + 1e-07)
            mixing(gram * (scale * scale))
            advance(start, width, scale)

        def step(start, width, last):
            mixing(gram_of(start, width))
            if not last:
                advance(start, width, None)
                return
            for c in range(start, start + width, D):
                lanes = slice(c, c + D)
                x_ref[own, lanes] = diag_ref[own, :] * x_ref[own, lanes] + nn(mix_ref[own, :], low_ref[:, lanes])

        def iterations(ranges):
            for start, width in ranges:
                first_step(start, width)

            def middle(_, carry):
                for start, width in ranges:
                    step(start, width, False)
                return carry

            lax.fori_loop(1, NS_ITERS - 1, middle, 0)
            for start, width in ranges:
                step(start, width, True)

        @pl.when(pair)
        def _():
            for core, chip, plane, row, col in each_block(place_ref, chips, planes):
                for j in range(2):
                    new = momentum(core, chip, plane, slice(j * cols, (j + 1) * cols))
                    x_ref[part(row, rows), part(col + j * planes, cols)] = new
                    low_ref[part(row, rows), part(col + j * planes, cols)] = new.astype(BF16)
            iterations([(0, D), (D, D)])
            for plane in range(planes):
                for j in range(2):
                    first = j * D + plane * cols
                    all_ref[plane, :, j * cols : (j + 1) * cols] = x_ref[own, first : first + cols].astype(BF16)

        @pl.when(jnp.logical_not(pair))
        def _():
            for core, chip, plane, row, col in each_block(place_ref, chips, planes):
                new = momentum(core, chip, plane, slice(0, wide))
                x_ref[part(row, rows), part(col, wide)] = new
                low_ref[part(row, rows), part(col, wide)] = new.astype(BF16)
            iterations([(0, FF)])
            for plane in range(planes):
                all_ref[plane] = x_ref[own, plane * wide : (plane + 1) * wide].astype(BF16)

        for r in range(planes):
            outs[r][...] = all_ref[place_ref[2] ^ r]

    return alone(
        body,
        (*grads, *moments, vectors, vec_moment),
        [sds((1, 1), F32), sds((VEC, D), F32), sds((VEC, D), F32)] + [sds((rows, wide), BF16)] * planes,
        "orthogonal",
        scratch=[
            pltpu.VMEM((D, FF), BF16),
            pltpu.VMEM((D, FF), F32),
            pltpu.VMEM((D, D), BF16),
            pltpu.VMEM((D, 1), F32),
            pltpu.VMEM((planes, rows, wide), BF16),
        ],
        place=place,
        flops=18e9,
        vmem=24 * 1024 * 1024,
        resident=2 * count,
    )


def update_kernel(place, slots, norm, ga, gb, attn_moment, up_moment, down_moment, attn_weights, up_weights, down_weights):
    planes = len(slots)
    rows, cols = attn_weights.shape[1:]
    wide = up_weights.shape[1]
    shape_factor = math.sqrt(max(1.0, FF / D))
    limit = clip_fraction * math.sqrt(PARAMS)

    def body(place_ref, *refs):
        slot_refs, refs = refs[:planes], refs[planes:]
        norm_ref, ga_ref, gb_ref, am_ref, um_ref, dm_ref, aw_ref, uw_ref, dw_ref = refs[:9]
        an_ref, un_ref, dn_ref, amn_ref, umn_ref, dmn_ref, all_ref = refs[9:]
        clip = limit / jnp.maximum(norm_ref[...], limit)
        for r in range(planes):
            all_ref[place_ref[2] ^ r] = slot_refs[r][...]
        for j in range(4):
            ortho = all_ref[1 + j // 2, :, (j % 2) * cols : (j % 2 + 1) * cols].astype(F32)
            an_ref[j] = aw_ref[j] - muon_rate * ortho
            grad = ga_ref[j * rows : (j + 1) * rows, :] if j < 3 else gb_ref[:, :cols]
            amn_ref[j] = muon_decay * am_ref[j] + clip * grad
        un_ref[...] = uw_ref[...] - muon_rate * all_ref[0].astype(F32)
        umn_ref[...] = muon_decay * um_ref[...] + clip * gb_ref[:, cols : cols + wide]
        dn_ref[...] = dw_ref[...] - muon_rate * shape_factor * all_ref[3].astype(F32)
        dmn_ref[...] = muon_decay * dm_ref[...] + clip * gb_ref[:, cols + wide :]

    weights = (attn_weights, up_weights, down_weights)
    others = [
        pltpu.with_memory_space_constraint(x, pltpu.HBM)
        for x in (ga, gb, attn_moment, up_moment, down_moment, *weights)
    ]
    return alone(
        body,
        (*slots, norm, *others),
        [sds(x.shape, F32) for x in weights] * 2,
        "update",
        resident=planes,
        scratch=[pltpu.VMEM((planes,) + slots[0].shape, BF16)],
        place=place,
    )


def documents(starts):
    doc = jnp.cumsum(starts).astype(F32)
    return doc.reshape(1, LEN), doc.reshape(LEN, 1)


def plain_tail(sizes, grads, attn_weights, up_weights, down_weights, vectors, attn_moment, up_moment, down_moment, vec_moment):
    dp = ("chip", "core")
    grad_attn, grad_up, grad_down, grad_vectors = grads

    def owned(grad, narrow_dim, dp_dim):
        part_sum = lax.psum_scatter(grad.astype(BF16), "narrow", scatter_dimension=narrow_dim, tiled=True)
        return lax.psum_scatter(part_sum, dp, scatter_dimension=dp_dim, tiled=True).astype(F32)

    owned_attn, owned_up, owned_down = owned(grad_attn, 2, 1), owned(grad_up, 1, 0), owned(grad_down, 0, 1)
    own_squares = jnp.sum(owned_attn * owned_attn) + jnp.sum(owned_up * owned_up) + jnp.sum(owned_down * owned_down)
    vector_sum, square_sum = lax.psum((grad_vectors, own_squares), ("chip", "core", "narrow"))
    grad_norm = jnp.sqrt(square_sum + jnp.sum(vector_sum * vector_sum))
    clip_limit = clip_fraction * math.sqrt(PARAMS)
    clip_factor = clip_limit / jnp.maximum(grad_norm, clip_limit)
    attn_mom_new = muon_decay * attn_moment + clip_factor * owned_attn
    up_mom_new = muon_decay * up_moment + clip_factor * owned_up
    down_mom_new = muon_decay * down_moment + clip_factor * owned_down
    gather = lambda x, dim: lax.all_gather(x.astype(BF16), dp, axis=dim, tiled=True).astype(F32)
    ortho = (gather(attn_mom_new, 1), gather(up_mom_new, 0), gather(down_mom_new, 1))
    ortho_attn, ortho_up, ortho_down = ortho
    for iteration in range(NS_ITERS):
        gram_attn = jnp.einsum("imc,inc->imn", ortho_attn, ortho_attn, precision=highest)
        gram_up = lax.dot_general(ortho_up, ortho_up, (((1,), (1,)), ((), ())), precision=highest)
        gram_down = lax.dot_general(ortho_down, ortho_down, (((0,), (0,)), ((), ())), precision=highest)
        partial_grams = jnp.concatenate([gram_attn, gram_up[None], gram_down[None]], axis=0)
        gram_total = lax.psum(partial_grams.astype(BF16), "narrow").astype(F32)
        if iteration == 0:
            norm_scales = 1.0 / (jnp.sqrt(jnp.trace(gram_total, axis1=1, axis2=2)) + 1e-07)
            ortho_attn = ortho_attn * norm_scales[:4, None, None]
            ortho_up = ortho_up * norm_scales[4]
            ortho_down = ortho_down * norm_scales[5]
            gram_total = gram_total * (norm_scales * norm_scales)[:, None, None]
        once = jnp.einsum("imn,inc->imc", gram_total[:4], ortho_attn, precision=highest)
        twice = jnp.einsum("imn,inc->imc", gram_total[:4], once, precision=highest)
        ortho_attn = coef_first * ortho_attn + coef_second * once + coef_third * twice
        once = jnp.dot(gram_total[4], ortho_up, precision=highest)
        twice = jnp.dot(gram_total[4], once, precision=highest)
        ortho_up = coef_first * ortho_up + coef_second * once + coef_third * twice
        once = jnp.dot(ortho_down, gram_total[5], precision=highest)
        twice = jnp.dot(once, gram_total[5], precision=highest)
        ortho_down = coef_first * ortho_down + coef_second * once + coef_third * twice
    row_share = D // sizes["dp"]
    row_start = lax.axis_index(dp) * row_share
    final_attn = lax.dynamic_slice_in_dim(ortho_attn, row_start, row_share, 1)
    final_up = lax.dynamic_slice_in_dim(ortho_up, row_start, row_share, 0)
    final_down = lax.dynamic_slice_in_dim(ortho_down, row_start, row_share, 1)
    shape_factor = math.sqrt(max(1.0, FF / D))
    vector_mom_new = vector_decay * vec_moment + clip_factor * vector_sum
    return (
        attn_weights - muon_rate * final_attn,
        up_weights - muon_rate * final_up,
        down_weights - muon_rate * shape_factor * final_down,
        attn_mom_new,
        up_mom_new,
        down_mom_new,
        vectors - vector_rate * vector_mom_new,
        vector_mom_new,
        grad_norm,
    )


def per_device(
    sizes,
    tokens, memory, neighbour_bank, starts, neighbours, cotangent,
    attn_weights, up_weights, down_weights, vectors,
    attn_moment, up_moment, down_moment, vector_moment,
):
    memory = memory.reshape(MEM, D)
    bank = neighbour_bank.reshape(BANK, D)
    own = (attn_weights, up_weights, down_weights)
    moments = (attn_moment, up_moment, down_moment)
    chips, planes = sizes["dp"] // 2, sizes["narrow"]
    if planes == len(PLANES) and chips == 4:
        return fast_device(
            chips, planes, tokens, memory, bank, starts, neighbours, cotangent, own, vectors, moments, vector_moment
        )
    full = lambda x, narrow_dim, dp_dim: lax.all_gather(
        lax.all_gather(x.astype(BF16), ("chip", "core"), axis=dp_dim, tiled=True), "narrow", axis=narrow_dim, tiled=True
    )
    attn_full = full(attn_weights, 2, 1)
    second = [attn_full[3], full(up_weights, 1, 0), full(down_weights, 0, 1).T]
    x, xt, cot_t, gate = context_kernel(tokens, memory, bank, cotangent, vectors)
    doc_row, doc_col = documents(starts)
    bias_tok, bias_bank = mask_kernel(doc_row, doc_col, neighbours.T)
    w, q, k, v, qt, kt, vt, qn, kn = project_kernel(x, attn_full[:3])
    e, local, fetched, stat, mixed, mixed_t = attend_kernel(qt, k, vt, qn, kn, bias_tok, bias_bank, doc_row, gate, 0, NPAIR)
    out, act, gh, ffn_t, branch, gres, gmt, gain_ffn = feed_kernel(mixed, tokens, cotangent, vectors, second)
    grad_down_t, grad_up, grad_o = feed_grads_kernel(cot_t, act, ffn_t, gh, mixed_t, branch)
    dq, dk, dv, gl = unattend_kernel(q, kt, v, e, gmt, local, fetched, stat, gate, 0, NPAIR)
    grad_qkv, grad_gate = proj_grads_kernel(xt, dq, dk, dv, gl)
    grad_in, gain_attn = input_kernel(dq, dk, dv, gl, w, tokens, memory, vectors, gres)
    grad_vectors = jnp.concatenate([gain_attn, gain_ffn, grad_gate], axis=0)
    grads = (jnp.concatenate([grad_qkv, grad_o[None]], axis=0), grad_up, grad_down_t.T, grad_vectors)
    return (out, grad_in) + plain_tail(sizes, grads, *own, vectors, *moments, vector_moment)


def ordered(first, second):
    return lax.optimization_barrier((first, second))[0]


def fast_device(
    chips, planes, tokens, memory, bank, starts, neighbours, cotangent, own, vectors, moments, vector_moment
):
    own, moments = own[:2] + (own[2].T,), moments[:2] + (moments[2].T,)
    place = jnp.stack([lax.axis_index("chip"), lax.axis_index("core"), lax.axis_index("narrow")]).astype(jnp.int32)
    payload = first_payload(own[0])
    payloads = second_payloads(place, *own, *moments, after=[payload])
    near_a = exchange([payload] * planes, "narrow")
    doc_row, doc_col = documents(starts)
    near_t = ordered(neighbours.T, payload)
    near_b = exchange(ordered(payloads, near_a), "narrow")
    column_a = stacked(near_a)
    plane_a = exchange([column_a] * chips, "chip")
    x, xt, cot_t, gate = context_kernel(tokens, memory, bank, cotangent, vectors, after=[column_a])
    bias_tok, bias_bank = mask_kernel(doc_row, doc_col, near_t, after=[x])
    first = core_blocks(ordered(plane_a, bias_tok))
    column_b, column_m = stacked_pair(ordered(near_b, first), payloads[0].shape[1] - own[1].shape[1])
    w, q, k, v, qt, kt, vt, qn, kn = project_kernel(x, first, place, after=[column_b])
    plane_b = exchange([column_b] * chips, "chip")
    e, local, fetched, stat, mixed, mixed_t = attend_kernel(qt, k, vt, qn, kn, bias_tok, bias_bank, doc_row, gate, 0, NPAIR)
    second = core_blocks(ordered(plane_b, mixed))
    plane_m = exchange([ordered(column_m, mixed)] * chips, "chip")
    out, gres, gmt, gain_ffn, keep_b, send_b = feed_blocks(
        mixed, mixed_t, tokens, cotangent, cot_t, vectors, second, place
    )
    back = (q, kt, v, e, gmt, local, fetched, stat, gate)
    slots_b = fold_cores(keep_b, exchange([send_b, send_b], "core")[1])
    dq, dk, dv, gl = unattend_kernel(*back, 0, NPAIR, after=[slots_b[0]])
    all_m = core_blocks(ordered(plane_m, dq))
    slots_b = fold_chips(ordered(exchange(slots_b, "chip"), dq))
    keep_a, send_a, grad_gate = proj_grads_kernel(xt, dq, dk, dv, gl, place, chips, planes, after=[slots_b[0]])
    slots_a = fold_cores_first(keep_a, exchange([send_a, send_a], "core")[1])
    grad_in, gain_attn = input_kernel(dq, dk, dv, gl, w, tokens, memory, vectors, gres, after=[slots_a[0]])
    parts_a = exchange(slots_a, "chip")
    parts_b = exchange(ordered(slots_b, slots_a), "narrow")
    parts_b, parts_a = ordered((parts_b, parts_a), grad_in)
    slots_a = fold_chips_first(parts_a, gain_attn, gain_ffn, grad_gate)
    parts_a = exchange(slots_a, "narrow")
    ga, gb, vec, *slots = owned_kernel(place, parts_a, parts_b)
    grads = core_blocks(exchange([stack_with_vectors(exchange(slots, "narrow"), vec)] * chips, "chip"))
    norm, vec_new, vec_mom, *slots = orthogonal_kernel(place, grads, all_m, vectors, vector_moment)
    final = exchange(slots, "narrow")
    new = list(update_kernel(place, final, norm, ga, gb, *moments, *own))
    new[2], new[5] = new[2].T, new[5].T
    return (out, grad_in, *new, vec_new, vec_mom, norm.reshape(()))


def solution(mesh):
    sizes = dict(mesh.shape)
    split = Mesh(
        mesh.devices.reshape(sizes["dp"] // 2, 2, sizes["narrow"]), ("chip", "core", "narrow")
    )
    dp = ("chip", "core")
    rows = ("chip", "core", "narrow")
    weights = (P(None, dp, "narrow"), P(dp, "narrow"), P("narrow", dp))
    return jax.shard_map(
        lambda *operands: per_device(sizes, *operands),
        mesh=split,
        in_specs=(P(rows, None), P(rows, None, None), P(rows, None, None), P(rows), P(rows, None), P(rows, None))
        + weights + (P(),) + weights + (P(),),
        out_specs=(P(rows, None), P(rows, None)) + weights + weights + (P(), P(), P()),
        check_vma=False,
    )
```

```python
import math

import jax
import jax.numpy as jnp
from jax import lax
from jax.experimental import pallas as pl
from jax.experimental.pallas import tpu as pltpu
from jax.sharding import Mesh, PartitionSpec as P

D = 512
H = 8
FF = 2048
MEM = 512
BANK = 512
KNB = 4
LEN = 1024
CTX = MEM + LEN
ROWS = CTX + BANK
HD = D // H
TB = 256
NT = LEN // TB
MC = MEM // TB
BC = BANK // TB
PAIR = 2 * HD
NPAIR = D // PAIR
F32 = jnp.float32
BF16 = jnp.bfloat16
NS_ITERS = 5
PARAMS = 3150848
epsilon = 1e-06
masked_score = -1e30
coef_first = 3.4445
coef_second = -4.775
coef_third = 2.0315
clip_fraction = 0.05
muon_rate = 0.5
muon_decay = 0.5
vector_rate = 0.5
vector_decay = 0.9
highest = lax.Precision.HIGHEST
LOG2E = 1.4426950408889634
SAFE = 80.0
VMEM_LIMIT = 60 * 1024 * 1024
SMALL = 16 * 1024 * 1024


def nn(a, b):
    return lax.dot_general(a, b, (((1,), (0,)), ((), ())), preferred_element_type=F32)


def nt(a, b):
    return lax.dot_general(a, b, (((1,), (1,)), ((), ())), preferred_element_type=F32)


def tn(a, b):
    return lax.dot_general(a, b, (((0,), (0,)), ((), ())), preferred_element_type=F32)


def rms_factor(values):
    return lax.rsqrt(jnp.mean(values * values, axis=-1, keepdims=True) + epsilon)


def whole(shape):
    return pl.BlockSpec(shape, lambda *_: (0,) * len(shape))


def call(
    body, grid, in_specs, out_specs, out_shape, flops, nbytes, name, scratch=(), trans=0, prefetch=0, after=(), alias=(),
    vmem=VMEM_LIMIT,
):
    extra, given = len(after) + len(alias), prefetch + len(in_specs)

    def with_extra(*refs):
        body(*refs[:given], *refs[given + extra :])

    made = pl.pallas_call(
        with_extra,
        grid_spec=pltpu.PrefetchScalarGridSpec(
            num_scalar_prefetch=prefetch,
            grid=grid,
            in_specs=list(in_specs) + [pl.BlockSpec(memory_space=pl.ANY)] * extra,
            out_specs=out_specs,
            scratch_shapes=list(scratch),
        ),
        out_shape=out_shape,
        input_output_aliases={given + len(after) + j: j for j in range(len(alias))},
        name=name,
        cost_estimate=pl.CostEstimate(flops=int(flops), bytes_accessed=int(nbytes), transcendentals=int(trans)),
        compiler_params=pltpu.CompilerParams(
            vmem_limit_bytes=vmem, dimension_semantics=("arbitrary",) * len(grid)
        ),
    )
    return lambda *operands: made(*operands, *after, *alias)


SMEM = pl.BlockSpec(memory_space=pltpu.SMEM)


def sds(shape, dtype):
    return jax.ShapeDtypeStruct(shape, dtype)


def hbm(shape, dtype):
    return pltpu.HBM(shape, dtype)


def vmem(shape, dtype):
    return pltpu.VMEM(shape, dtype)


RESIDENT = pl.BlockSpec(memory_space=pltpu.VMEM)


def context_body(tok_ref, mem_ref, bank_ref, cot_ref, vec_ref, x_ref, xt_ref, cott_ref, gate_ref):
    i = pl.program_id(0)
    gain = vec_ref[0:1, :]

    def put(rows):
        x_ref[...] = rows
        xt_ref[...] = rows.T

    def norm(values):
        wide = values.astype(F32)
        return (wide * rms_factor(wide) * gain).astype(BF16)

    @pl.when(i < MC)
    def _():
        put(norm(mem_ref[...]))

    @pl.when((i >= MC) & (i < MC + NT))
    def _():
        rows = norm(tok_ref[...])
        put(rows)
        logits = nt(vec_ref[2:10, :].astype(BF16), rows)
        gate = jax.nn.sigmoid(logits)
        for p in range(NPAIR):
            gate_ref[p] = gate[2 * p : 2 * p + 2, :]
        cott_ref[...] = cot_ref[...].T

    @pl.when(i >= MC + NT)
    def _():
        put(bank_ref[...])


def context_kernel(tokens, memory, bank, cot, vectors, after=()):
    steps = MC + NT + BC
    clip_tok = lambda i: jnp.clip(i - MC, 0, NT - 1)
    return call(
        context_body,
        (steps,),
        [
            pl.BlockSpec((TB, D), lambda i: (clip_tok(i), 0)),
            pl.BlockSpec((TB, D), lambda i: (jnp.minimum(i, MC - 1), 0)),
            pl.BlockSpec((TB, D), lambda i: (jnp.clip(i - MC - NT, 0, BC - 1), 0)),
            pl.BlockSpec((TB, D), lambda i: (clip_tok(i), 0)),
            whole((2 + H, D)),
        ],
        [
            pl.BlockSpec((TB, D), lambda i: (i, 0)),
            pl.BlockSpec((D, TB), lambda i: (0, i)),
            pl.BlockSpec((D, TB), lambda i: (0, clip_tok(i))),
            pl.BlockSpec((NPAIR, 2, TB), lambda i: (0, 0, clip_tok(i))),
        ],
        [sds((ROWS, D), BF16), vmem((D, ROWS), BF16), sds((D, LEN), BF16), hbm((NPAIR, 2, LEN), F32)],
        8e9,
        8e6,
        "context",
        after=after,
        vmem=SMALL,
    )(tokens, memory, bank, cot, vectors)


def mask_body(doc_row_ref, doc_col_ref, near_ref, tok_ref, bank_ref):
    i = pl.program_id(0)
    doc_row = doc_row_ref[...]

    @pl.when(i < NT)
    def _():
        keys = lax.broadcasted_iota(jnp.int32, (TB, LEN), 0) + i * TB
        rows = lax.broadcasted_iota(jnp.int32, (TB, LEN), 1)
        seen = (keys <= rows) & (doc_col_ref[...] == doc_row)
        tok_ref[...] = jnp.where(seen, 0.0, masked_score)

    @pl.when(i >= NT)
    def _():
        keys = lax.broadcasted_iota(jnp.int32, (TB, LEN), 0) + (i - NT) * TB
        count = jnp.zeros((TB, LEN), F32)
        for j in range(KNB):
            count = count + jnp.where(near_ref[j : j + 1, :] == keys, 1.0, 0.0)
        bias = jnp.where(count > 0.5, 0.0, masked_score)
        for j in range(2, KNB + 1):
            bias = jnp.where(count > j - 0.5, math.log2(j), bias)
        bank_ref[...] = bias


def mask_kernel(doc_row, doc_col, near_t, after=()):
    return call(
        mask_body,
        (NT + BC,),
        [
            whole((1, LEN)),
            pl.BlockSpec((TB, 1), lambda i: (jnp.minimum(i, NT - 1), 0)),
            whole((KNB, LEN)),
        ],
        [
            pl.BlockSpec((TB, LEN), lambda i: (jnp.minimum(i, NT - 1), 0)),
            pl.BlockSpec((TB, LEN), lambda i: (jnp.clip(i - NT, 0, BC - 1), 0)),
        ],
        [vmem((LEN, LEN), F32), vmem((BANK, LEN), F32)],
        6e9,
        7e6,
        "masks",
        after=after,
        vmem=SMALL,
    )(doc_row, doc_col, near_t)


def each_block(place_ref, chips, planes):
    for core in range(2):
        for chip in range(chips):
            row = ((place_ref[0] ^ chip) * 2 + (place_ref[1] ^ core))
            for plane in range(planes):
                yield core, chip, plane, row, place_ref[2] ^ plane


def part(index, size):
    return pl.ds(pl.multiple_of(index * size, size), size)


def head_squares(columns):
    wide = columns.astype(F32)
    return jnp.sum((wide * wide).reshape(H, HD, wide.shape[1]), axis=1)


def project_rows(i, x_ref, w_ref, q_ref, k_ref, v_ref, qt_ref, kt_ref, vt_ref, qn_ref, kn_ref):
    rows = x_ref[...]
    keys = nn(rows, w_ref[1]).astype(BF16)
    values = nn(rows, w_ref[2]).astype(BF16)
    keys_t = keys.T
    k_ref[...] = keys
    v_ref[...] = values
    kt_ref[...] = keys_t
    vt_ref[...] = values.T

    @pl.when(i == 0)
    def _():
        kn_ref[...] = jnp.zeros(kn_ref.shape, F32)
        qn_ref[...] = jnp.zeros(qn_ref.shape, F32)

    kn_ref[...] = jnp.maximum(kn_ref[...], head_squares(keys_t))

    @pl.when((i >= MEM // rows.shape[0]) & (i < CTX // rows.shape[0]))
    def _():
        queries = (nn(rows, w_ref[0]).astype(BF16).astype(F32) * (LOG2E / math.sqrt(HD))).astype(BF16)
        queries_t = queries.T
        q_ref[...] = queries
        qt_ref[...] = queries_t
        qn_ref[...] = jnp.maximum(qn_ref[...], head_squares(queries_t))


def project_kernel(x, w, place=None, after=()):
    rows = 2 * TB
    steps = ROWS // rows
    first_q, last_q = MEM // rows, CTX // rows - 1
    fast = place is not None
    if fast:
        chips, planes = len(w) // 2, w[0].shape[0]
        own_rows, own_cols = w[0].shape[1] // 3, w[0].shape[2]

    def body(*refs):
        i = pl.program_id(0)
        if not fast:
            project_rows(i, *refs)
            return
        place_ref, x_ref, *rest = refs
        blocks, (w_ref, *outs) = rest[: len(w)], rest[len(w) :]

        @pl.when(i == 0)
        def _():
            for core, chip, plane, row, col in each_block(place_ref, chips, planes):
                for j in range(3):
                    w_ref[j, part(row, own_rows), part(col, own_cols)] = blocks[core * chips + chip][
                        plane, j * own_rows : (j + 1) * own_rows, :
                    ]

        project_rows(i, x_ref, w_ref, *outs)

    out_specs = [
        pl.BlockSpec((rows, D), lambda i: (jnp.clip(i, first_q, last_q) - first_q, 0)),
        pl.BlockSpec((rows, D), lambda i: (i, 0)),
        pl.BlockSpec((rows, D), lambda i: (i, 0)),
        pl.BlockSpec((D, rows), lambda i: (0, jnp.clip(i, first_q, last_q) - first_q)),
        pl.BlockSpec((D, rows), lambda i: (0, i)),
        pl.BlockSpec((D, rows), lambda i: (0, i)),
        whole((H, rows)),
        whole((H, rows)),
    ]
    out_shape = [
        vmem((LEN, D), BF16),
        vmem((ROWS, D), BF16),
        vmem((ROWS, D), BF16),
        vmem((D, LEN), BF16),
        vmem((D, ROWS), BF16),
        vmem((D, ROWS), BF16),
        sds((H, rows), F32),
        sds((H, rows), F32),
    ]
    in_specs = [pl.BlockSpec((rows, D), lambda i: (i, 0))]
    if fast:
        in_specs = [SMEM] + in_specs + [RESIDENT] * len(w)
        out_specs = [whole((3, D, D))] + out_specs
        out_shape = [hbm((3, D, D), BF16)] + out_shape
        operands = (place, x, *w)
    else:
        in_specs = in_specs + [whole((3, D, D))]
        operands = (x, w)
    result = call(
        body, (steps,), in_specs, out_specs, out_shape, 11e9, 14e6, "project", after=after, vmem=24 * 1024 * 1024
    )(*operands)
    return result if fast else [w, *result]


def head_lanes(values, h):
    lanes = lax.broadcasted_iota(jnp.int32, values.shape, 1)
    keep = (lanes < HD) if h == 0 else (lanes >= HD)
    return jnp.where(keep, values, jnp.zeros_like(values))


def near_count(tb):
    return MEM + (tb + 1) * TB


def seen_count(tb):
    return near_count(tb) + BANK


FAR = slice(CTX, ROWS)


def head_rows_of(values, h):
    zeros = jnp.zeros((HD, values.shape[1]), values.dtype)
    own = values[h * HD : (h + 1) * HD, :]
    return jnp.concatenate([own, zeros] if h == 0 else [zeros, own], axis=0)


def attend_body(
    qt_ref, k_ref, vt_ref, tok_ref, bank_ref, doc_ref, gate_ref, qn_ref, kn_ref,
    e0_ref, e1_ref, e2_ref, e3_ref, local_ref, fetched_ref, stat_ref, mixed_ref, mixedt_ref, s_ref,
):
    e_refs = (e0_ref, e1_ref, e2_ref, e3_ref)
    units = [(tb, h) for tb in range(NT) for h in range(2)]

    def start(u):
        tb, h = units[u]
        near = near_count(tb)
        q_head = head_rows_of(qt_ref[:, tb * TB : (tb + 1) * TB], h)
        s_ref[u % 2, :near, :] = nn(k_ref[:near, :], q_head)
        s_ref[u % 2, near : near + BANK, :] = nn(k_ref[FAR, :], q_head)

    def biased(u, row, cols, mem_bias):
        s = s_ref[u % 2, row : row + TB, :]
        near = near_count(units[u][0])
        if row < MEM:
            return s + mem_bias
        if row < near:
            return s + tok_ref[row - MEM : row - MEM + TB, cols]
        return s + bank_ref[row - near : row - near + TB, cols]

    def soft(u, first, last, cols, mem_bias, general):
        tb, h = units[u]
        top = None
        if general:
            peak = jnp.full((8, TB), -3e38, F32)
            for row in range(first, last, TB):
                s = biased(u, row, cols, mem_bias)
                peak = jnp.maximum(peak, jnp.max(s.reshape(TB // 8, 8, TB), axis=0))
            top = jnp.max(peak, axis=0, keepdims=True)
        total = jnp.zeros((8, TB), F32)
        for row in range(first, last, TB):
            s = biased(u, row, cols, mem_bias)
            e = jnp.exp2(s - top if general else s)
            e_refs[tb][h, row : row + TB, :] = e.astype(BF16)
            total = total + jnp.sum(e.reshape(TB // 8, 8, TB), axis=0)
        return 1.0 / jnp.sum(total, axis=0, keepdims=True)

    def run(general):
        start(0)
        mixed_parts = []
        for u, (tb, h) in enumerate(units):
            cols = slice(tb * TB, (tb + 1) * TB)
            head_rows = slice(h * HD, (h + 1) * HD)
            near, seen = near_count(tb), seen_count(tb)
            if u + 1 < len(units):
                start(u + 1)
            mem_bias = jnp.where(doc_ref[:, cols] == 0.0, 0.0, masked_score)
            local_inv = soft(u, 0, near, cols, mem_bias, general)
            fetched_inv = soft(u, near, seen, cols, mem_bias, general)
            local = nn(vt_ref[head_rows, :near], e_refs[tb][h, :near, :]) * local_inv
            fetched = nn(vt_ref[head_rows, FAR], e_refs[tb][h, near:, :]) * fetched_inv
            local_ref[head_rows, cols] = local.astype(BF16)
            fetched_ref[head_rows, cols] = fetched.astype(BF16)
            stat_ref[0, h : h + 1, cols] = local_inv
            stat_ref[0, 2 + h : 3 + h, cols] = fetched_inv
            gate = gate_ref[0, h : h + 1, cols]
            mixed_parts.append((1.0 - gate) * local + gate * fetched)
            if h == 1:
                mixed = jnp.concatenate(mixed_parts, axis=0)
                mixed_parts = []
                mixedt_ref[:, cols] = mixed.astype(BF16)
                mixed_ref[cols, :] = mixed.T.astype(BF16)

    bound = jnp.max(jnp.max(qn_ref[...], axis=1, keepdims=True) * jnp.max(kn_ref[...], axis=1, keepdims=True))

    @pl.when(bound <= SAFE * SAFE)
    def _():
        run(False)

    @pl.when(jnp.logical_not(bound <= SAFE * SAFE))
    def _():
        run(True)


def attend_kernel(qt, k, vt, qn, kn, bias_tok, bias_bank, doc_row, gate, first, count):
    spec_cols = lambda rows: pl.BlockSpec((rows, PAIR), lambda p: (0, p + first))
    spec_rows = lambda cols: pl.BlockSpec((PAIR, cols), lambda p: (p + first, 0))
    *e, local, fetched, stat, mixed, mixed_t = call(
        attend_body,
        (count,),
        [
            spec_rows(LEN),
            spec_cols(ROWS),
            spec_rows(ROWS),
            RESIDENT,
            RESIDENT,
            whole((1, LEN)),
            pl.BlockSpec((1, 2, LEN), lambda p: (p + first, 0, 0)),
            whole(qn.shape),
            whole(kn.shape),
        ],
        [
            *[pl.BlockSpec((2, seen_count(tb), TB), lambda p: (p, 0, 0)) for tb in range(NT)],
            pl.BlockSpec((PAIR, LEN), lambda p: (p, 0)),
            pl.BlockSpec((PAIR, LEN), lambda p: (p, 0)),
            pl.BlockSpec((1, 8, LEN), lambda p: (p, 0, 0)),
            pl.BlockSpec((LEN, PAIR), lambda p: (0, p)),
            pl.BlockSpec((PAIR, LEN), lambda p: (p, 0)),
        ],
        [
            *[hbm((2 * count, seen_count(tb), TB), BF16) for tb in range(NT)],
            hbm((PAIR * count, LEN), BF16),
            hbm((PAIR * count, LEN), BF16),
            hbm((count, 8, LEN), F32),
            vmem((LEN, PAIR * count), BF16),
            vmem((PAIR * count, LEN), BF16),
        ],
        count * 5e9,
        count * 14e6 + 6e6,
        "attend",
        scratch=[pltpu.VMEM((2, ROWS, TB), F32)],
        trans=count * 2 * ROWS * LEN,
        vmem=28 * 1024 * 1024,
    )(qt, k, vt, bias_tok, bias_bank, doc_row, gate, qn, kn)
    return e, local, fetched, stat, mixed, mixed_t


def gelu_parts(x):
    square = jnp.exp2(x * x * (-0.5 * LOG2E))
    t = 1.0 / (1.0 + (0.3275911 * 0.7071067811865476) * jnp.abs(x))
    poly = t * (
        0.127414796 + t * (-0.142248368 + t * (0.7107068705 + t * (-0.7265760135 + t * 0.5307027145)))
    )
    tail = poly * square
    cdf = jnp.where(x >= 0.0, 1.0 - tail, tail)
    return cdf, square * 0.3989422804014327


FC = 512


def feed_body(
    mixed_ref, tok_ref, cot_ref, wo_ref, up_ref, dt_ref, vec_ref,
    out_ref, act_ref, gh_ref, ffnt_ref, branch_ref, gres_ref, gmt_ref, gain_ref,
):
    i = pl.program_id(0)
    residual = tok_ref[...].astype(F32) + nn(mixed_ref[...], wo_ref[...])
    factor = rms_factor(residual)
    hat = residual * factor
    gain = vec_ref[1:2, :]
    ffn = (hat * gain).astype(BF16)
    ffnt_ref[...] = ffn.T
    cot = cot_ref[...]
    out = residual
    grad_ffn = jnp.zeros(residual.shape, F32)
    for c in range(FF // FC):
        cols = slice(c * FC, (c + 1) * FC)
        hidden = nn(ffn, up_ref[:, cols])
        cdf, pdf = gelu_parts(hidden)
        act = (hidden * cdf).astype(BF16)
        act_ref[:, cols] = act
        grad_act = nn(cot, dt_ref[:, cols])
        gh = (grad_act * (cdf + hidden * pdf)).astype(BF16)
        gh_ref[:, cols] = gh
        out = out + nt(act, dt_ref[:, cols])
        grad_ffn = grad_ffn + nt(gh, up_ref[:, cols])
    out_ref[...] = out.astype(BF16)
    part = jnp.sum(grad_ffn * hat, axis=0, keepdims=True)

    @pl.when(i == 0)
    def _():
        gain_ref[...] = part

    @pl.when(i > 0)
    def _():
        gain_ref[...] += part

    scaled = grad_ffn * gain
    grad_res = cot.astype(F32) + factor * (scaled - hat * jnp.mean(scaled * hat, axis=-1, keepdims=True))
    gres_ref[...] = grad_res
    branch = grad_res.astype(BF16)
    branch_ref[...] = branch
    gmt_ref[...] = nt(wo_ref[...], branch)


def feed_kernel(mixed, tokens, cot, vectors, w):
    rows = lambda width: pl.BlockSpec((TB, width), lambda i: (i, 0))
    cols = lambda height: pl.BlockSpec((height, TB), lambda i: (0, i))

    def body(mixed_ref, tok_ref, cot_ref, vec_ref, wo_ref, up_ref, dt_ref, *outs):
        feed_body(mixed_ref, tok_ref, cot_ref, wo_ref, up_ref, dt_ref, vec_ref, *outs)

    return call(
        body,
        (NT,),
        [rows(D), rows(D), rows(D), whole((2 + H, D))] + [whole(x.shape) for x in w],
        [rows(D), rows(FF), rows(FF), cols(D), rows(D), rows(D), cols(D), whole((1, D))],
        [
            sds((LEN, D), BF16),
            sds((LEN, FF), BF16),
            sds((LEN, FF), BF16),
            sds((D, LEN), BF16),
            sds((LEN, D), BF16),
            sds((LEN, D), F32),
            sds((D, LEN), F32),
            sds((1, D), F32),
        ],
        23e9,
        22e6,
        "feed",
        trans=LEN * FF * 2,
    )(mixed, tokens, cot, vectors, *w)


def feed_grads_body(cott_ref, act_ref, ffnt_ref, gh_ref, mixedt_ref, branch_ref, gd_ref, gu_ref, go_ref):
    gd_ref[...] = nn(cott_ref[...], act_ref[...]).astype(BF16)
    gu_ref[...] = nn(ffnt_ref[...], gh_ref[...]).astype(BF16)
    go_ref[...] = nn(mixedt_ref[...], branch_ref[...]).astype(BF16)


def feed_grads_kernel(cot_t, act, ffn_t, gh, mixed_t, branch):
    steps = 4
    wide = lambda width: pl.BlockSpec((LEN, width // steps), lambda i: (0, i))
    out = lambda width: pl.BlockSpec((D, width // steps), lambda i: (0, i))
    return call(
        feed_grads_body,
        (steps,),
        [whole((D, LEN)), wide(FF), whole((D, LEN)), wide(FF), whole((D, LEN)), wide(D)],
        [out(FF), out(FF), out(D)],
        [sds((D, FF), BF16), sds((D, FF), BF16), sds((D, D), BF16)],
        11e9,
        17e6,
        "feed_grads",
    )(cot_t, act, ffn_t, gh, mixed_t, branch)


def feed_blocks(mixed, mixed_t, tokens, cot, cot_t, vectors, w, place):
    chips, planes = len(w) // 2, w[0].shape[0]
    own_rows, own_o, own_ff = w[0].shape[1], D // planes, FF // planes
    width = own_o + 2 * own_ff
    size = 2 * TB
    row_steps = LEN // size

    def body(place_ref, mixed_ref, mixedt_ref, tok_ref, cot_ref, cott_ref, vec_ref, *rest):
        blocks, rest = rest[: len(w)], rest[len(w) :]
        out_ref, gres_ref, gmt_ref, gain_ref, keep_ref, send_ref = rest[:6]
        wo_ref, up_ref, dt_ref, act_ref, gh_ref, ffnt_ref, branch_ref, hid_ref, ga_ref, all_ref = rest[6:]
        i = pl.program_id(0)

        @pl.when(i == 0)
        def _():
            for core, chip, plane, row, col in each_block(place_ref, chips, planes):
                block = blocks[core * chips + chip]
                here = part(row, own_rows)
                wo_ref[here, part(col, own_o)] = block[plane, :, :own_o]
                up_ref[here, part(col, own_ff)] = block[plane, :, own_o : own_o + own_ff]
                dt_ref[here, part(col, own_ff)] = block[plane, :, own_o + own_ff :]

        @pl.when(i < row_steps)
        def _():
            here = part(i, size)
            residual = tok_ref[...].astype(F32) + nn(mixed_ref[...], wo_ref[...])
            factor = rms_factor(residual)
            hat = residual * factor
            gain = vec_ref[1:2, :]
            ffn = (hat * gain).astype(BF16)
            ffnt_ref[:, here] = ffn.T
            cot = cot_ref[...]

            def start(c):
                cols = slice(c * FC, (c + 1) * FC)
                hid_ref[c % 2] = nn(ffn, up_ref[:, cols])
                ga_ref[c % 2] = nn(cot, dt_ref[:, cols])

            out = residual
            grad_ffn = jnp.zeros(residual.shape, F32)
            start(0)
            for c in range(FF // FC):
                cols = slice(c * FC, (c + 1) * FC)
                if c + 1 < FF // FC:
                    start(c + 1)
                hidden = hid_ref[c % 2]
                cdf, pdf = gelu_parts(hidden)
                act_ref[here, cols] = (hidden * cdf).astype(BF16)
                gh_ref[here, cols] = (ga_ref[c % 2] * (cdf + hidden * pdf)).astype(BF16)
                out = out + nt(act_ref[here, cols], dt_ref[:, cols])
                grad_ffn = grad_ffn + nt(gh_ref[here, cols], up_ref[:, cols])
            out_ref[...] = out.astype(BF16)
            gain_part = jnp.sum(grad_ffn * hat, axis=0, keepdims=True)

            @pl.when(i == 0)
            def _():
                gain_ref[...] = gain_part

            @pl.when(i > 0)
            def _():
                gain_ref[...] += gain_part

            scaled = grad_ffn * gain
            grad_res = cot.astype(F32) + factor * (scaled - hat * jnp.mean(scaled * hat, axis=-1, keepdims=True))
            gres_ref[...] = grad_res
            branch = grad_res.astype(BF16)
            branch_ref[here, :] = branch
            gmt_ref[...] = nt(wo_ref[...], branch)

        @pl.when(i >= row_steps)
        def _():
            plane = i - row_steps
            cols = part(plane, own_ff)
            all_ref[:, :own_o] = nn(mixedt_ref[...], branch_ref[:, part(plane, own_o)]).astype(BF16)
            all_ref[:, own_o : own_o + own_ff] = nn(ffnt_ref[...], gh_ref[:, cols]).astype(BF16)
            all_ref[:, own_o + own_ff :] = nn(cott_ref[...], act_ref[:, cols]).astype(BF16)
            for chip in range(chips):
                slot = place_ref[0] ^ chip
                keep_ref[slot, 0] = all_ref[part(chip * 2 + place_ref[1], own_rows), :]
                send_ref[slot, 0] = all_ref[part(chip * 2 + 1 - place_ref[1], own_rows), :]

    row = lambda i: jnp.minimum(i, row_steps - 1)
    rows = pl.BlockSpec((size, D), lambda i, _: (row(i), 0))
    blocked = pl.BlockSpec(
        (chips, 1, own_rows, width), lambda i, place_ref: (0, jnp.maximum(i - row_steps, 0) ^ place_ref[2], 0, 0)
    )
    shape = hbm((chips, planes, own_rows, width), BF16)
    return call(
        body,
        (row_steps + planes,),
        [rows, RESIDENT, rows, rows, RESIDENT, whole((2 + H, D))] + [RESIDENT] * len(w),
        [rows, rows, pl.BlockSpec((D, size), lambda i, _: (0, row(i))), whole((1, D)), blocked, blocked],
        [hbm((LEN, D), BF16), hbm((LEN, D), F32), vmem((D, LEN), F32), sds((1, D), F32), vmem((chips, planes, own_rows, width), BF16), shape],
        30e9,
        22e6,
        "feed",
        scratch=[
            pltpu.VMEM((D, D), BF16),
            pltpu.VMEM((D, FF), BF16),
            pltpu.VMEM((D, FF), BF16),
            pltpu.VMEM((LEN, FF), BF16),
            pltpu.VMEM((LEN, FF), BF16),
            pltpu.VMEM((D, LEN), BF16),
            pltpu.VMEM((LEN, D), BF16),
            pltpu.VMEM((2, size, FC), F32),
            pltpu.VMEM((2, size, FC), F32),
            pltpu.VMEM((D, width), BF16),
        ],
        trans=LEN * FF * 2,
        prefetch=1,
        vmem=36 * 1024 * 1024,
    )(place, mixed, mixed_t, tokens, cot, cot_t, vectors, *w)


def unattend_body(
    q_ref, kt_ref, v_ref, e0_ref, e1_ref, e2_ref, e3_ref, gmt_ref, local_ref, fetched_ref, stat_ref, gate_ref,
    dq_ref, dk_ref, dv_ref, gl_ref, ds0_ref, ds1_ref, ds2_ref, ds3_ref, do_ref, df_ref, dot_ref, dqt_ref, dk_acc, dv_acc, gp_ref,
):
    e_refs, ds_refs = (e0_ref, e1_ref, e2_ref, e3_ref), (ds0_ref, ds1_ref, ds2_ref, ds3_ref)

    def prepare(h):
        head_rows = slice(h * HD, (h + 1) * HD)
        gm = gmt_ref[head_rows, :]
        local = local_ref[head_rows, :].astype(F32)
        fetched = fetched_ref[head_rows, :].astype(F32)
        gate = gate_ref[0, h : h + 1, :]
        local_inv = stat_ref[0, h : h + 1, :]
        fetched_inv = stat_ref[0, 2 + h : 3 + h, :]
        grad_gate = jnp.sum(gm * (fetched - local), axis=0, keepdims=True)
        gl_ref[0, h : h + 1, :] = grad_gate * gate * (1.0 - gate)
        grad_local = ((1.0 - gate) * gm).astype(BF16).astype(F32)
        grad_fetched = gate * gm
        other = slice((1 - h) * HD, (2 - h) * HD)
        do_ref[h, other, :] = jnp.zeros((HD, LEN), BF16)
        df_ref[h, other, :] = jnp.zeros((HD, LEN), BF16)
        do_ref[h, head_rows, :] = (grad_local * local_inv).astype(BF16)
        df_ref[h, head_rows, :] = (grad_fetched * fetched_inv).astype(BF16)
        dot_ref[h : h + 1, :] = jnp.sum(grad_local * local, axis=0, keepdims=True) * local_inv
        dot_ref[2 + h : 3 + h, :] = jnp.sum(grad_fetched * fetched, axis=0, keepdims=True) * fetched_inv

    units = [(tb, h) for h in range(2) for tb in range(NT)]

    def start(u):
        tb, h = units[u]
        near, cols = near_count(tb), slice(tb * TB, (tb + 1) * TB)
        gp_ref[u % 2, :near, :] = nn(v_ref[:near, :], do_ref[h, :, cols])
        gp_ref[u % 2, near : near + BANK, :] = nn(v_ref[FAR, :], df_ref[h, :, cols])

    def rows_part(u):
        tb, h = units[u]
        near, cols = near_count(tb), slice(tb * TB, (tb + 1) * TB)
        head_rows = slice(h * HD, (h + 1) * HD)
        for row in range(0, seen_count(tb), TB):
            some, which = slice(row, row + TB), h if row < near else 2 + h
            gp = gp_ref[u % 2, some, :] - dot_ref[which : which + 1, cols]
            ds_refs[tb][h, some, :] = (e_refs[tb][h, some, :].astype(F32) * gp).astype(BF16)
        dq = nn(kt_ref[head_rows, :near], ds_refs[tb][h, :near, :])
        dq = dq + nn(kt_ref[head_rows, FAR], ds_refs[tb][h, near:, :])
        dqt_ref[head_rows, cols] = dq * (1.0 / math.sqrt(HD))

    def keys_part(h, tb):
        near, cols = near_count(tb), slice(tb * TB, (tb + 1) * TB)
        q_head = head_lanes(q_ref[cols, :], h)
        pieces = (
            (slice(0, near), slice(0, near), do_ref[h, :, cols]),
            (FAR, slice(near, near + BANK), df_ref[h, :, cols]),
        )
        for keys, some, grad_out in pieces:
            dv = nt(e_refs[tb][h, some, :], grad_out)
            dk = nn(ds_refs[tb][h, some, :], q_head)
            if h == 0 and tb == NT - 1:
                dv_acc[keys, :] = dv
                dk_acc[keys, :] = dk
            else:
                dv_acc[keys, :] += dv
                dk_acc[keys, :] += dk

    prepare(0)
    start(0)
    prepare(1)
    for u, (tb, h) in enumerate(units):
        if u + 1 < len(units):
            start(u + 1)
        rows_part(u)
        if h == 1:
            keys_part(0, NT - 1 - tb)
    for tb in range(NT):
        keys_part(1, tb)
    dv_ref[...] = dv_acc[...].astype(BF16)
    dk_ref[...] = (dk_acc[...] * (1.0 / LOG2E)).astype(BF16)
    dq_ref[...] = dqt_ref[...].T.astype(BF16)


def unattend_kernel(q, kt, v, e, gmt, local, fetched, stat, gate, first, count, after=(), alias=()):
    spec_cols = lambda rows: pl.BlockSpec((rows, PAIR), lambda p: (0, p + first))
    spec_rows = lambda cols: pl.BlockSpec((PAIR, cols), lambda p: (p + first, 0))
    return call(
        unattend_body,
        (count,),
        [
            spec_cols(LEN),
            spec_rows(ROWS),
            spec_cols(ROWS),
            *[pl.BlockSpec((2, seen_count(tb), TB), lambda p: (p + first, 0, 0)) for tb in range(NT)],
            spec_rows(LEN),
            spec_rows(LEN),
            spec_rows(LEN),
            pl.BlockSpec((1, 8, LEN), lambda p: (p + first, 0, 0)),
            pl.BlockSpec((1, 2, LEN), lambda p: (p + first, 0, 0)),
        ],
        [
            spec_cols(LEN),
            spec_cols(ROWS),
            spec_cols(ROWS),
            pl.BlockSpec((1, 2, LEN), lambda p: (p + first, 0, 0)),
        ],
        [
            sds((LEN, D), BF16),
            sds((ROWS, D), BF16),
            sds((ROWS, D), BF16),
            sds((NPAIR, 2, LEN), F32),
        ],
        count * 10e9,
        count * 14e6,
        "unattend",
        scratch=[
            *[pltpu.VMEM((2, seen_count(tb), TB), BF16) for tb in range(NT)],
            pltpu.VMEM((2, PAIR, LEN), BF16),
            pltpu.VMEM((2, PAIR, LEN), BF16),
            pltpu.VMEM((8, LEN), F32),
            pltpu.VMEM((PAIR, LEN), F32),
            pltpu.VMEM((ROWS, PAIR), F32),
            pltpu.VMEM((ROWS, PAIR), F32),
            pltpu.VMEM((2, ROWS, TB), F32),
        ],
        after=after,
        alias=alias,
        vmem=36 * 1024 * 1024,
    )(q, kt, v, *e, gmt, local, fetched, stat, gate)


def all_heads(gl_ref):
    return jnp.concatenate([gl_ref[p] for p in range(NPAIR)], axis=0).astype(BF16)


def proj_grads_body(xt_ref, dq_ref, dk_ref, dv_ref, gl_ref, g_ref, gate_ref):
    g_ref[0] = nn(xt_ref[:, MEM:CTX], dq_ref[...]).astype(BF16)
    g_ref[1] = nn(xt_ref[...], dk_ref[...]).astype(BF16)
    g_ref[2] = nn(xt_ref[...], dv_ref[...]).astype(BF16)

    @pl.when(pl.program_id(0) == 0)
    def _():
        gate_ref[...] = nt(all_heads(gl_ref), xt_ref[:, MEM:CTX])


def proj_grads_kernel(xt, dq, dk, dv, gl, place=None, chips=0, planes=0, after=()):
    steps = 2
    fast = place is not None
    wide = lambda rows: pl.BlockSpec((rows, D // steps), lambda i, *_: (0, i))
    in_specs = [whole((D, ROWS)), wide(LEN), wide(ROWS), wide(ROWS), whole((NPAIR, 2, LEN))]
    gate_spec, gate_shape = whole((H, D)), sds((H, D), F32)
    flops, nbytes = 8e9, 10e6
    if not fast:
        return call(
            proj_grads_body,
            (steps,),
            in_specs,
            [pl.BlockSpec((3, D, D // steps), lambda i: (0, 0, i)), gate_spec],
            [sds((3, D, D), BF16), gate_shape],
            flops,
            nbytes,
            "proj_grads",
        )(xt, dq, dk, dv, gl)
    own_rows, own_cols, group = D // (2 * chips), D // planes, planes // steps

    def body(place_ref, xt_ref, dq_ref, dk_ref, dv_ref, gl_ref, keep_ref, send_ref, gate_ref, all_ref):
        proj_grads_body(xt_ref, dq_ref, dk_ref, dv_ref, gl_ref, all_ref, gate_ref)
        for b in range(group):
            col = b ^ (place_ref[2] % group)
            cols = slice(b * own_cols, (b + 1) * own_cols)
            for chip in range(chips):
                slot = place_ref[0] ^ chip
                for j in range(3):
                    here = slice(j * own_rows, (j + 1) * own_rows)
                    keep_ref[slot, col, here, :] = all_ref[j, part(chip * 2 + place_ref[1], own_rows), cols]
                    send_ref[slot, col, here, :] = all_ref[j, part(chip * 2 + 1 - place_ref[1], own_rows), cols]

    out = pl.BlockSpec(
        (chips, group, 3 * own_rows, own_cols), lambda i, place_ref: (0, i ^ (place_ref[2] // group), 0, 0)
    )
    shape = sds((chips, planes, 3 * own_rows, own_cols), BF16)
    return call(
        body,
        (steps,),
        in_specs,
        [out, out, gate_spec],
        [shape, shape, gate_shape],
        flops,
        nbytes,
        "proj_grads",
        scratch=[pltpu.VMEM((3, D, D // steps), BF16)],
        prefetch=1,
        after=after,
        vmem=24 * 1024 * 1024,
    )(place, xt, dq, dk, dv, gl)


def input_body(dq_ref, dk_ref, dv_ref, gl_ref, w_ref, tok_ref, mem_ref, vec_ref, gres_ref, gin_ref, gain_ref):
    i = pl.program_id(0)
    gn = nt(dk_ref[...], w_ref[1]) + nt(dv_ref[...], w_ref[2])

    @pl.when(i < MC)
    def _():
        wide = mem_ref[...].astype(F32)
        part = jnp.sum(gn * (wide * rms_factor(wide)), axis=0, keepdims=True)

        @pl.when(i == 0)
        def _():
            gain_ref[...] = part

        @pl.when(i > 0)
        def _():
            gain_ref[...] += part

    @pl.when(i >= MC)
    def _():
        wide = tok_ref[...].astype(F32)
        factor = rms_factor(wide)
        hat = wide * factor
        full = gn + nt(dq_ref[...], w_ref[0]) + tn(all_heads(gl_ref), vec_ref[2:10, :].astype(BF16))
        gain_ref[...] += jnp.sum(full * hat, axis=0, keepdims=True)
        scaled = full * vec_ref[0:1, :]
        gin_ref[...] = (
            gres_ref[...] + factor * (scaled - hat * jnp.mean(scaled * hat, axis=-1, keepdims=True))
        ).astype(BF16)


def input_kernel(dq, dk, dv, gl, w, tokens, memory, vectors, gres, after=()):
    tok = lambda i: jnp.clip(i - MC, 0, NT - 1)
    rows = pl.BlockSpec((TB, D), lambda i: (tok(i), 0))
    return call(
        input_body,
        (MC + NT,),
        [
            rows,
            pl.BlockSpec((TB, D), lambda i: (i, 0)),
            pl.BlockSpec((TB, D), lambda i: (i, 0)),
            pl.BlockSpec((NPAIR, 2, TB), lambda i: (0, 0, tok(i))),
            whole((3, D, D)),
            rows,
            pl.BlockSpec((TB, D), lambda i: (jnp.minimum(i, MC - 1), 0)),
            whole((2 + H, D)),
            rows,
        ],
        [rows, whole((1, D))],
        [sds((LEN, D), BF16), sds((1, D), F32)],
        9e9,
        10e6,
        "input",
        after=after,
        vmem=SMALL,
    )(dq, dk, dv, gl, w, tokens, memory, vectors, gres)


def exchange(slots, axis):
    size = len(slots)
    return [slots[0]] + [
        lax.ppermute(slots[r], axis, [(i, i ^ r) for i in range(size)]) for r in range(1, size)
    ]


def added(parts):
    total = parts[0].astype(F32)
    for other in parts[1:]:
        total = total + other.astype(F32)
    return total


PLANES = (("up",), ("q", "k"), ("v", "o"), ("down",))
EXTRA = 16


def alone(body, operands, out_shape, name, scratch=(), place=None, after=(), flops=2e9, vmem=SMALL, resident=0):
    specs = [RESIDENT if j < resident else whole(x.shape) for j, x in enumerate(operands)]
    if place is not None:
        specs, operands = [SMEM] + specs, (place, *operands)
    return call(
        body,
        (1,),
        specs,
        [whole(x.shape) for x in out_shape],
        out_shape,
        flops,
        2e6,
        name,
        scratch=scratch,
        after=after,
        vmem=vmem,
    )(*operands)


def first_payload(attn_weights):
    rows, cols = attn_weights.shape[1:]

    def body(aw_ref, out_ref):
        for j in range(3):
            out_ref[j * rows : (j + 1) * rows, :] = aw_ref[j].astype(BF16)

    return alone(body, (attn_weights,), [vmem((3 * rows, cols), BF16)], "first_payload", vmem=VMEM_LIMIT)[0]


def second_payloads(place, attn_weights, up_weights, down_weights, attn_moment, up_moment, down_moment, after):
    rows, cols = attn_weights.shape[1:]
    wide = up_weights.shape[1]
    planes = len(PLANES)
    width = cols + 3 * wide

    def body(place_ref, aw_ref, uw_ref, dw_ref, am_ref, um_ref, dm_ref, *rest):
        outs, all_ref = rest[:planes], rest[planes]
        all_ref[...] = jnp.zeros(all_ref.shape, BF16)
        all_ref[0] = um_ref[...].astype(BF16)
        all_ref[3] = dm_ref[...].astype(BF16)
        for j in range(4):
            all_ref[1 + j // 2, :, (j % 2) * cols : (j % 2 + 1) * cols] = am_ref[j].astype(BF16)
        for r in range(planes):
            outs[r][:, :cols] = aw_ref[3].astype(BF16)
            outs[r][:, cols : cols + wide] = uw_ref[...].astype(BF16)
            outs[r][:, cols + wide : cols + 2 * wide] = dw_ref[...].astype(BF16)
            outs[r][:, cols + 2 * wide :] = all_ref[place_ref[2] ^ r]

    return alone(
        body,
        (attn_weights, up_weights, down_weights, attn_moment, up_moment, down_moment),
        [vmem((rows, width), BF16)] * planes,
        "second_payloads",
        scratch=[pltpu.VMEM((planes, rows, wide), BF16)],
        place=place,
        after=after,
        vmem=VMEM_LIMIT,
    )


def stacked_pair(parts, width):
    rows = parts[0].shape[0]
    other = parts[0].shape[1] - width

    def body(*refs):
        for r in range(len(parts)):
            refs[-2][r] = refs[r][:, :width]
            refs[-1][r] = refs[r][:, width:]

    shapes = [sds((len(parts), rows, width), BF16), sds((len(parts), rows, other), BF16)]
    return alone(body, parts, shapes, "stacked_pair", resident=len(parts))


def stacked(parts, after=()):
    def body(*refs):
        for r in range(len(parts)):
            refs[-1][r] = refs[r][...]

    return alone(body, parts, [sds((len(parts),) + parts[0].shape, parts[0].dtype)], "stacked", after=after, resident=len(parts))[0]


def core_blocks(plane):
    return plane + [exchange([b, b], "core")[1] for b in plane]


def fold_cores(keep, other):
    chips, planes, rows, width = keep.shape

    def body(keep_ref, other_ref, *outs):
        for chip in range(chips):
            outs[chip][...] = added([keep_ref[chip], other_ref[chip]]).astype(BF16)

    spec = pl.BlockSpec((chips, 1, rows, width), lambda i: (0, i, 0, 0))
    return call(
        body,
        (planes,),
        [spec, spec],
        [pl.BlockSpec((1, rows, width), lambda i: (i, 0, 0))] * chips,
        [sds((planes, rows, width), BF16)] * chips,
        4e9,
        7e6,
        "fold_cores",
        vmem=SMALL,
    )(keep, other)


def fold_chips(parts):
    planes, rows, width = parts[0].shape

    def body(*refs):
        for plane in range(planes):
            refs[len(parts) + plane][...] = added([r[plane] for r in refs[: len(parts)]]).astype(BF16)

    return alone(body, parts, [sds((rows, width), BF16)] * planes, "fold_chips", resident=len(parts))


VEC = 2 + H
VEC_ROWS = 128


def put_vectors(ref, first, values):
    high = values.astype(BF16)
    low = (values - high.astype(F32)).astype(BF16)
    ref[first : first + VEC_ROWS, :] = jnp.zeros((VEC_ROWS, 128), BF16)
    for j in range(4):
        lanes = slice(j * 128, (j + 1) * 128)
        ref[first + j * 16 : first + j * 16 + VEC, :] = high[:, lanes]
        ref[first + 64 + j * 16 : first + 64 + j * 16 + VEC, :] = low[:, lanes]


def get_vectors(refs, first):
    pieces = []
    for j in range(4):
        rows = lambda offset: slice(first + offset + j * 16, first + offset + j * 16 + VEC)
        pieces.append(added([r[rows(offset), :] for r in refs for offset in (0, 64)]))
    return jnp.concatenate(pieces, axis=1)


def fold_cores_first(keep, other):
    chips = keep.shape[0]

    def body(keep_ref, other_ref, *outs):
        for chip in range(chips):
            outs[chip][...] = added([keep_ref[chip], other_ref[chip]]).astype(BF16)

    return alone(body, (keep, other), [sds(keep.shape[1:], BF16)] * chips, "fold_cores_first")


def fold_chips_first(parts, gain_attn, gain_ffn, grad_gate):
    planes, rows, width = parts[0].shape
    count = len(parts)

    def body(*refs):
        ins, (ga_ref, gf_ref, gg_ref) = refs[:count], refs[count : count + 3]
        outs, vec_ref = refs[count + 3 : -1], refs[-1]
        vec_ref[0:1, :] = ga_ref[...]
        vec_ref[1:2, :] = gf_ref[...]
        vec_ref[2:VEC, :] = gg_ref[...]
        for plane in range(planes):
            outs[plane][:rows, :] = added([r[plane] for r in ins]).astype(BF16)
            put_vectors(outs[plane], rows, vec_ref[...])

    return alone(
        body,
        (*parts, gain_attn, gain_ffn, grad_gate),
        [sds((rows + VEC_ROWS, width), BF16)] * planes,
        "fold_chips_first",
        resident=count,
        scratch=[pltpu.VMEM((VEC, D), F32)],
    )


def stack_with_vectors(parts, vec):
    count, width = len(parts), parts[0].shape[1]
    rows = parts[0].shape[0] - EXTRA

    def body(*refs):
        vec_ref, out_ref = refs[count], refs[count + 1]
        for r in range(count):
            out_ref[r * rows : (r + 1) * rows, :] = refs[r][:rows, :]
        squares = added([r[rows:, :] for r in refs[:count]])
        squares = jnp.sum(squares, axis=0, keepdims=True) + jnp.zeros((EXTRA, width), F32)
        high = squares.astype(BF16).astype(F32)
        middle = (squares - high).astype(BF16).astype(F32)
        row = lax.broadcasted_iota(jnp.int32, (EXTRA, width), 0)
        extra = jnp.where(row == VEC, high, jnp.where(row == VEC + 1, middle, squares - high - middle))
        values = jnp.concatenate([vec_ref[...], jnp.zeros((EXTRA - VEC, width), F32)], axis=0)
        first = values.astype(BF16).astype(F32)
        here = count * rows
        out_ref[here : here + EXTRA, :] = jnp.where(row < VEC, first, extra).astype(BF16)
        out_ref[here + EXTRA :, :] = (values - first).astype(BF16)

    return alone(
        body, (*parts, vec), [sds((count * rows + 2 * EXTRA, width), BF16)], "stack_with_vectors", resident=count + 1
    )[0]


def owned_kernel(place, parts_a, parts_b):
    planes = len(parts_a)
    size, cols = parts_a[0].shape[0] - VEC_ROWS, parts_a[0].shape[1]
    rows, width = parts_b[0].shape
    wide = (width - cols) // 2

    def body(place_ref, *refs):
        a_refs, b_refs = refs[:planes], refs[planes : 2 * planes]
        ga_ref, gb_ref, vec_ref, *rest = refs[2 * planes :]
        slots, all_ref = rest[:planes], rest[planes]
        ga = added([r[:size, :] for r in a_refs])
        gb = added([r[...] for r in b_refs])
        ga_ref[...] = ga
        gb_ref[...] = gb
        vec_ref[...] = get_vectors(a_refs, size)
        squares = jnp.sum(ga * ga, keepdims=True) + jnp.sum(gb * gb, keepdims=True)
        all_ref[...] = jnp.zeros(all_ref.shape, BF16)
        for j in range(4):
            grad = ga[j * rows : (j + 1) * rows, :] if j < 3 else gb[:, :cols]
            all_ref[1 + j // 2, :, (j % 2) * cols : (j % 2 + 1) * cols] = grad.astype(BF16)
        all_ref[0] = gb[:, cols : cols + wide].astype(BF16)
        all_ref[3] = gb[:, cols + wide :].astype(BF16)
        wide_squares = squares + jnp.zeros((EXTRA, wide), F32)
        row = lax.broadcasted_iota(jnp.int32, (EXTRA, wide), 0)
        high = wide_squares.astype(BF16).astype(F32)
        middle = (wide_squares - high).astype(BF16).astype(F32)
        low = wide_squares - high - middle
        extra = jnp.where(row == 0, high, jnp.where(row == 1, middle, jnp.where(row == 2, low, 0.0))).astype(BF16)
        for r in range(planes):
            slots[r][:rows, :] = all_ref[place_ref[2] ^ r]
            slots[r][rows:, :] = extra

    return alone(
        body,
        (*parts_a, *parts_b),
        [hbm((size, cols), F32), hbm((rows, width), F32), sds((VEC, D), F32)]
        + [sds((rows + EXTRA, wide), BF16)] * planes,
        "owned",
        resident=2 * planes,
        scratch=[pltpu.VMEM((planes, rows, wide), BF16)],
        place=place,
    )


def orthogonal_kernel(place, grads, moments, vectors, vec_moment):
    count = len(grads)
    chips = count // 2
    planes, rows = moments[0].shape[:2]
    wide = grads[0].shape[1]
    cols = D // planes
    limit = clip_fraction * math.sqrt(PARAMS)

    def body(place_ref, *refs):
        grad_refs, moment_refs, refs = refs[:count], refs[count : 2 * count], refs[2 * count :]
        vec_ref, vm_ref, norm_ref, vn_ref, vmn_ref = refs[:5]
        outs = refs[5 : 5 + planes]
        low_ref, x_ref, mix_ref, diag_ref, all_ref = refs[5 + planes :]
        pair = (place_ref[2] == 1) | (place_ref[2] == 2)
        own = part(place_ref[0] * 2 + place_ref[1], rows)
        after = planes * rows
        extra = added([r[after : after + EXTRA, :] for r in grad_refs])
        grad_vec = extra[:VEC, :] + added([r[after + EXTRA : after + EXTRA + VEC, :] for r in grad_refs])
        total = jnp.sum(extra[VEC : VEC + 3, 0:1], axis=0, keepdims=True) + jnp.sum(grad_vec * grad_vec, keepdims=True)
        norm = jnp.sqrt(total)
        norm_ref[...] = norm
        clip = limit / jnp.maximum(norm, limit)
        vec_mom = vector_decay * vm_ref[...] + clip * grad_vec
        vmn_ref[...] = vec_mom
        vn_ref[...] = vec_ref[...] - vector_rate * vec_mom

        def momentum(core, chip, plane, lanes):
            b = core * chips + chip
            moment = moment_refs[b][plane, :, lanes].astype(F32)
            grad = grad_refs[b][plane * rows : (plane + 1) * rows, lanes].astype(F32)
            return muon_decay * moment + clip * grad

        def gram_of(start, width):
            half = D // 2
            upper, lower = low_ref[:half, start : start + width], low_ref[half:, start : start + width]
            corner = nt(lower, upper)
            first = jnp.concatenate([nt(upper, upper), corner.T], axis=1)
            return jnp.concatenate([first, jnp.concatenate([corner, nt(lower, lower)], axis=1)], axis=0)

        def mixing(gram):
            eye = lax.broadcasted_iota(jnp.int32, (D, D), 0) == lax.broadcasted_iota(jnp.int32, (D, D), 1)
            low = gram.astype(BF16)
            mix = coef_second * low.astype(F32) + coef_third * nn(low, low)
            diag_ref[...] = coef_first + jnp.sum(jnp.where(eye, mix, 0.0), axis=1, keepdims=True)
            mix_ref[...] = jnp.where(eye, 0.0, mix).astype(BF16)

        def advance(start, width, scale):
            for c in range(start, start + width, D):
                lanes = slice(c, c + D)
                new = diag_ref[...] * x_ref[:, lanes] + nn(mix_ref[...], low_ref[:, lanes])
                if scale is not None:
                    new = new * scale
                x_ref[:, lanes] = new
                low_ref[:, lanes] = new.astype(BF16)

        def first_step(start, width):
            gram = gram_of(start, width)
            eye = lax.broadcasted_iota(jnp.int32, (D, D), 0) == lax.broadcasted_iota(jnp.int32, (D, D), 1)
            scale = 1.0 / (jnp.sqrt(jnp.sum(jnp.where(eye, gram, 0.0), keepdims=True)) + 1e-07)
            mixing(gram * (scale * scale))
            advance(start, width, scale)

        def step(start, width, last):
            mixing(gram_of(start, width))
            if not last:
                advance(start, width, None)
                return
            for c in range(start, start + width, D):
                lanes = slice(c, c + D)
                x_ref[own, lanes] = diag_ref[own, :] * x_ref[own, lanes] + nn(mix_ref[own, :], low_ref[:, lanes])

        def iterations(ranges):
            for start, width in ranges:
                first_step(start, width)

            def middle(_, carry):
                for start, width in ranges:
                    step(start, width, False)
                return carry

            lax.fori_loop(1, NS_ITERS - 1, middle, 0)
            for start, width in ranges:
                step(start, width, True)

        @pl.when(pair)
        def _():
            for core, chip, plane, row, col in each_block(place_ref, chips, planes):
                for j in range(2):
                    new = momentum(core, chip, plane, slice(j * cols, (j + 1) * cols))
                    x_ref[part(row, rows), part(col + j * planes, cols)] = new
                    low_ref[part(row, rows), part(col + j * planes, cols)] = new.astype(BF16)
            iterations([(0, D), (D, D)])
            for plane in range(planes):
                for j in range(2):
                    first = j * D + plane * cols
                    all_ref[plane, :, j * cols : (j + 1) * cols] = x_ref[own, first : first + cols].astype(BF16)

        @pl.when(jnp.logical_not(pair))
        def _():
            for core, chip, plane, row, col in each_block(place_ref, chips, planes):
                new = momentum(core, chip, plane, slice(0, wide))
                x_ref[part(row, rows), part(col, wide)] = new
                low_ref[part(row, rows), part(col, wide)] = new.astype(BF16)
            iterations([(0, FF)])
            for plane in range(planes):
                all_ref[plane] = x_ref[own, plane * wide : (plane + 1) * wide].astype(BF16)

        for r in range(planes):
            outs[r][...] = all_ref[place_ref[2] ^ r]

    return alone(
        body,
        (*grads, *moments, vectors, vec_moment),
        [sds((1, 1), F32), sds((VEC, D), F32), sds((VEC, D), F32)] + [sds((rows, wide), BF16)] * planes,
        "orthogonal",
        scratch=[
            pltpu.VMEM((D, FF), BF16),
            pltpu.VMEM((D, FF), F32),
            pltpu.VMEM((D, D), BF16),
            pltpu.VMEM((D, 1), F32),
            pltpu.VMEM((planes, rows, wide), BF16),
        ],
        place=place,
        flops=18e9,
        vmem=24 * 1024 * 1024,
        resident=2 * count,
    )


def outside(arrays):
    return [pltpu.with_memory_space_constraint(x, pltpu.HBM) for x in arrays]


def moments_kernel(norm, ga, gb, attn_moment, up_moment, down_moment, after):
    rows, cols = attn_moment.shape[1:]
    wide = up_moment.shape[1]
    limit = clip_fraction * math.sqrt(PARAMS)

    def body(norm_ref, ga_ref, gb_ref, am_ref, um_ref, dm_ref, amn_ref, umn_ref, dmn_ref):
        clip = limit / jnp.maximum(norm_ref[...], limit)
        for j in range(4):
            grad = ga_ref[j * rows : (j + 1) * rows, :] if j < 3 else gb_ref[:, :cols]
            amn_ref[j] = muon_decay * am_ref[j] + clip * grad
        umn_ref[...] = muon_decay * um_ref[...] + clip * gb_ref[:, cols : cols + wide]
        dmn_ref[...] = muon_decay * dm_ref[...] + clip * gb_ref[:, cols + wide :]

    moments = (attn_moment, up_moment, down_moment)
    return alone(
        body,
        (norm, *outside((ga, gb, *moments))),
        [sds(x.shape, F32) for x in moments],
        "moments",
        after=after,
    )


def update_kernel(place, slots, attn_weights, up_weights, down_weights):
    planes = len(slots)
    cols = attn_weights.shape[2]
    shape_factor = math.sqrt(max(1.0, FF / D))

    def body(place_ref, *refs):
        slot_refs, (aw_ref, uw_ref, dw_ref, an_ref, un_ref, dn_ref, all_ref) = refs[:planes], refs[planes:]
        for r in range(planes):
            all_ref[place_ref[2] ^ r] = slot_refs[r][...]
        for j in range(4):
            ortho = all_ref[1 + j // 2, :, (j % 2) * cols : (j % 2 + 1) * cols].astype(F32)
            an_ref[j] = aw_ref[j] - muon_rate * ortho
        un_ref[...] = uw_ref[...] - muon_rate * all_ref[0].astype(F32)
        dn_ref[...] = dw_ref[...] - muon_rate * shape_factor * all_ref[3].astype(F32)

    weights = (attn_weights, up_weights, down_weights)
    return alone(
        body,
        (*slots, *outside(weights)),
        [sds(x.shape, F32) for x in weights],
        "update",
        resident=planes,
        scratch=[pltpu.VMEM((planes,) + slots[0].shape, BF16)],
        place=place,
    )


def documents(starts):
    doc = jnp.cumsum(starts).astype(F32)
    return doc.reshape(1, LEN), doc.reshape(LEN, 1)


def plain_tail(sizes, grads, attn_weights, up_weights, down_weights, vectors, attn_moment, up_moment, down_moment, vec_moment):
    dp = ("chip", "core")
    grad_attn, grad_up, grad_down, grad_vectors = grads

    def owned(grad, narrow_dim, dp_dim):
        part_sum = lax.psum_scatter(grad.astype(BF16), "narrow", scatter_dimension=narrow_dim, tiled=True)
        return lax.psum_scatter(part_sum, dp, scatter_dimension=dp_dim, tiled=True).astype(F32)

    owned_attn, owned_up, owned_down = owned(grad_attn, 2, 1), owned(grad_up, 1, 0), owned(grad_down, 0, 1)
    own_squares = jnp.sum(owned_attn * owned_attn) + jnp.sum(owned_up * owned_up) + jnp.sum(owned_down * owned_down)
    vector_sum, square_sum = lax.psum((grad_vectors, own_squares), ("chip", "core", "narrow"))
    grad_norm = jnp.sqrt(square_sum + jnp.sum(vector_sum * vector_sum))
    clip_limit = clip_fraction * math.sqrt(PARAMS)
    clip_factor = clip_limit / jnp.maximum(grad_norm, clip_limit)
    attn_mom_new = muon_decay * attn_moment + clip_factor * owned_attn
    up_mom_new = muon_decay * up_moment + clip_factor * owned_up
    down_mom_new = muon_decay * down_moment + clip_factor * owned_down
    gather = lambda x, dim: lax.all_gather(x.astype(BF16), dp, axis=dim, tiled=True).astype(F32)
    ortho = (gather(attn_mom_new, 1), gather(up_mom_new, 0), gather(down_mom_new, 1))
    ortho_attn, ortho_up, ortho_down = ortho
    for iteration in range(NS_ITERS):
        gram_attn = jnp.einsum("imc,inc->imn", ortho_attn, ortho_attn, precision=highest)
        gram_up = lax.dot_general(ortho_up, ortho_up, (((1,), (1,)), ((), ())), precision=highest)
        gram_down = lax.dot_general(ortho_down, ortho_down, (((0,), (0,)), ((), ())), precision=highest)
        partial_grams = jnp.concatenate([gram_attn, gram_up[None], gram_down[None]], axis=0)
        gram_total = lax.psum(partial_grams.astype(BF16), "narrow").astype(F32)
        if iteration == 0:
            norm_scales = 1.0 / (jnp.sqrt(jnp.trace(gram_total, axis1=1, axis2=2)) + 1e-07)
            ortho_attn = ortho_attn * norm_scales[:4, None, None]
            ortho_up = ortho_up * norm_scales[4]
            ortho_down = ortho_down * norm_scales[5]
            gram_total = gram_total * (norm_scales * norm_scales)[:, None, None]
        once = jnp.einsum("imn,inc->imc", gram_total[:4], ortho_attn, precision=highest)
        twice = jnp.einsum("imn,inc->imc", gram_total[:4], once, precision=highest)
        ortho_attn = coef_first * ortho_attn + coef_second * once + coef_third * twice
        once = jnp.dot(gram_total[4], ortho_up, precision=highest)
        twice = jnp.dot(gram_total[4], once, precision=highest)
        ortho_up = coef_first * ortho_up + coef_second * once + coef_third * twice
        once = jnp.dot(ortho_down, gram_total[5], precision=highest)
        twice = jnp.dot(once, gram_total[5], precision=highest)
        ortho_down = coef_first * ortho_down + coef_second * once + coef_third * twice
    row_share = D // sizes["dp"]
    row_start = lax.axis_index(dp) * row_share
    final_attn = lax.dynamic_slice_in_dim(ortho_attn, row_start, row_share, 1)
    final_up = lax.dynamic_slice_in_dim(ortho_up, row_start, row_share, 0)
    final_down = lax.dynamic_slice_in_dim(ortho_down, row_start, row_share, 1)
    shape_factor = math.sqrt(max(1.0, FF / D))
    vector_mom_new = vector_decay * vec_moment + clip_factor * vector_sum
    return (
        attn_weights - muon_rate * final_attn,
        up_weights - muon_rate * final_up,
        down_weights - muon_rate * shape_factor * final_down,
        attn_mom_new,
        up_mom_new,
        down_mom_new,
        vectors - vector_rate * vector_mom_new,
        vector_mom_new,
        grad_norm,
    )


def per_device(
    sizes,
    tokens, memory, neighbour_bank, starts, neighbours, cotangent,
    attn_weights, up_weights, down_weights, vectors,
    attn_moment, up_moment, down_moment, vector_moment,
):
    memory = memory.reshape(MEM, D)
    bank = neighbour_bank.reshape(BANK, D)
    own = (attn_weights, up_weights, down_weights)
    moments = (attn_moment, up_moment, down_moment)
    chips, planes = sizes["dp"] // 2, sizes["narrow"]
    if planes == len(PLANES) and chips == 4:
        return fast_device(
            chips, planes, tokens, memory, bank, starts, neighbours, cotangent, own, vectors, moments, vector_moment
        )
    full = lambda x, narrow_dim, dp_dim: lax.all_gather(
        lax.all_gather(x.astype(BF16), ("chip", "core"), axis=dp_dim, tiled=True), "narrow", axis=narrow_dim, tiled=True
    )
    attn_full = full(attn_weights, 2, 1)
    second = [attn_full[3], full(up_weights, 1, 0), full(down_weights, 0, 1).T]
    x, xt, cot_t, gate = context_kernel(tokens, memory, bank, cotangent, vectors)
    doc_row, doc_col = documents(starts)
    bias_tok, bias_bank = mask_kernel(doc_row, doc_col, neighbours.T)
    w, q, k, v, qt, kt, vt, qn, kn = project_kernel(x, attn_full[:3])
    e, local, fetched, stat, mixed, mixed_t = attend_kernel(qt, k, vt, qn, kn, bias_tok, bias_bank, doc_row, gate, 0, NPAIR)
    out, act, gh, ffn_t, branch, gres, gmt, gain_ffn = feed_kernel(mixed, tokens, cotangent, vectors, second)
    grad_down_t, grad_up, grad_o = feed_grads_kernel(cot_t, act, ffn_t, gh, mixed_t, branch)
    dq, dk, dv, gl = unattend_kernel(q, kt, v, e, gmt, local, fetched, stat, gate, 0, NPAIR)
    grad_qkv, grad_gate = proj_grads_kernel(xt, dq, dk, dv, gl)
    grad_in, gain_attn = input_kernel(dq, dk, dv, gl, w, tokens, memory, vectors, gres)
    grad_vectors = jnp.concatenate([gain_attn, gain_ffn, grad_gate], axis=0)
    grads = (jnp.concatenate([grad_qkv, grad_o[None]], axis=0), grad_up, grad_down_t.T, grad_vectors)
    return (out, grad_in) + plain_tail(sizes, grads, *own, vectors, *moments, vector_moment)


def ordered(first, second):
    return lax.optimization_barrier((first, second))[0]


def fast_device(
    chips, planes, tokens, memory, bank, starts, neighbours, cotangent, own, vectors, moments, vector_moment
):
    own, moments = own[:2] + (own[2].T,), moments[:2] + (moments[2].T,)
    place = jnp.stack([lax.axis_index("chip"), lax.axis_index("core"), lax.axis_index("narrow")]).astype(jnp.int32)
    payload = first_payload(own[0])
    payloads = second_payloads(place, *own, *moments, after=[payload])
    near_a = exchange([payload] * planes, "narrow")
    doc_row, doc_col = documents(starts)
    near_t = ordered(neighbours.T, payload)
    near_b = exchange(ordered(payloads, near_a), "narrow")
    column_a = stacked(near_a)
    plane_a = exchange([column_a] * chips, "chip")
    x, xt, cot_t, gate = context_kernel(tokens, memory, bank, cotangent, vectors, after=[column_a])
    bias_tok, bias_bank = mask_kernel(doc_row, doc_col, near_t, after=[x])
    first = core_blocks(ordered(plane_a, bias_tok))
    column_b, column_m = stacked_pair(ordered(near_b, first), payloads[0].shape[1] - own[1].shape[1])
    w, q, k, v, qt, kt, vt, qn, kn = project_kernel(x, first, place, after=[column_b])
    plane_b = exchange([column_b] * chips, "chip")
    e, local, fetched, stat, mixed, mixed_t = attend_kernel(qt, k, vt, qn, kn, bias_tok, bias_bank, doc_row, gate, 0, NPAIR)
    second = core_blocks(ordered(plane_b, mixed))
    plane_m = exchange([ordered(column_m, mixed)] * chips, "chip")
    out, gres, gmt, gain_ffn, keep_b, send_b = feed_blocks(
        mixed, mixed_t, tokens, cotangent, cot_t, vectors, second, place
    )
    back = (q, kt, v, e, gmt, local, fetched, stat, gate)
    slots_b = fold_cores(keep_b, exchange([send_b, send_b], "core")[1])
    dq, dk, dv, gl = unattend_kernel(*back, 0, NPAIR, after=[slots_b[0]])
    all_m = core_blocks(ordered(plane_m, dq))
    slots_b = fold_chips(ordered(exchange(slots_b, "chip"), dq))
    keep_a, send_a, grad_gate = proj_grads_kernel(xt, dq, dk, dv, gl, place, chips, planes, after=[slots_b[0]])
    slots_a = fold_cores_first(keep_a, exchange([send_a, send_a], "core")[1])
    grad_in, gain_attn = input_kernel(dq, dk, dv, gl, w, tokens, memory, vectors, gres, after=[slots_a[0]])
    parts_a = exchange(slots_a, "chip")
    parts_b = exchange(slots_b, "narrow")
    parts_b, parts_a = ordered((parts_b, parts_a), grad_in)
    slots_a = fold_chips_first(parts_a, gain_attn, gain_ffn, grad_gate)
    parts_a = exchange(slots_a, "narrow")
    ga, gb, vec, *slots = owned_kernel(place, parts_a, parts_b)
    grads = core_blocks(exchange([stack_with_vectors(exchange(slots, "narrow"), vec)] * chips, "chip"))
    norm, vec_new, vec_mom, *slots = orthogonal_kernel(place, grads, all_m, vectors, vector_moment)
    final = exchange(slots, "narrow")
    attn_mom, up_mom, down_mom = moments_kernel(norm, ga, gb, *moments, after=[slots[0]])
    attn_new, up_new, down_new = update_kernel(place, ordered(final, attn_mom), *own)
    new = (attn_new, up_new, down_new.T, attn_mom, up_mom, down_mom.T)
    return (out, grad_in, *new, vec_new, vec_mom, norm.reshape(()))


def solution(mesh):
    sizes = dict(mesh.shape)
    split = Mesh(
        mesh.devices.reshape(sizes["dp"] // 2, 2, sizes["narrow"]), ("chip", "core", "narrow")
    )
    dp = ("chip", "core")
    rows = ("chip", "core", "narrow")
    weights = (P(None, dp, "narrow"), P(dp, "narrow"), P("narrow", dp))
    return jax.shard_map(
        lambda *operands: per_device(sizes, *operands),
        mesh=split,
        in_specs=(P(rows, None), P(rows, None, None), P(rows, None, None), P(rows), P(rows, None), P(rows, None))
        + weights + (P(),) + weights + (P(),),
        out_specs=(P(rows, None), P(rows, None)) + weights + weights + (P(), P(), P()),
        check_vma=False,
    )
```

```python
import math

import jax
import jax.numpy as jnp
from jax import lax
from jax.experimental import pallas as pl
from jax.experimental.pallas import tpu as pltpu
from jax.sharding import Mesh, PartitionSpec as P

D = 512
H = 8
FF = 2048
MEM = 512
BANK = 512
KNB = 4
LEN = 1024
CTX = MEM + LEN
ROWS = CTX + BANK
HD = D // H
TB = 256
NT = LEN // TB
MC = MEM // TB
BC = BANK // TB
PAIR = 2 * HD
NPAIR = D // PAIR
F32 = jnp.float32
BF16 = jnp.bfloat16
NS_ITERS = 5
PARAMS = 3150848
epsilon = 1e-06
masked_score = -1e30
coef_first = 3.4445
coef_second = -4.775
coef_third = 2.0315
clip_fraction = 0.05
muon_rate = 0.5
muon_decay = 0.5
vector_rate = 0.5
vector_decay = 0.9
highest = lax.Precision.HIGHEST
LOG2E = 1.4426950408889634
SAFE = 80.0
VMEM_LIMIT = 60 * 1024 * 1024
SMALL = 16 * 1024 * 1024


def nn(a, b):
    return lax.dot_general(a, b, (((1,), (0,)), ((), ())), preferred_element_type=F32)


def nt(a, b):
    return lax.dot_general(a, b, (((1,), (1,)), ((), ())), preferred_element_type=F32)


def tn(a, b):
    return lax.dot_general(a, b, (((0,), (0,)), ((), ())), preferred_element_type=F32)


def rms_factor(values):
    return lax.rsqrt(jnp.mean(values * values, axis=-1, keepdims=True) + epsilon)


def whole(shape):
    return pl.BlockSpec(shape, lambda *_: (0,) * len(shape))


def call(
    body, grid, in_specs, out_specs, out_shape, flops, nbytes, name, scratch=(), trans=0, prefetch=0, after=(), alias=(),
    vmem=VMEM_LIMIT,
):
    extra, given = len(after) + len(alias), prefetch + len(in_specs)

    def with_extra(*refs):
        body(*refs[:given], *refs[given + extra :])

    made = pl.pallas_call(
        with_extra,
        grid_spec=pltpu.PrefetchScalarGridSpec(
            num_scalar_prefetch=prefetch,
            grid=grid,
            in_specs=list(in_specs) + [pl.BlockSpec(memory_space=pl.ANY)] * extra,
            out_specs=out_specs,
            scratch_shapes=list(scratch),
        ),
        out_shape=out_shape,
        input_output_aliases={given + len(after) + j: j for j in range(len(alias))},
        name=name,
        cost_estimate=pl.CostEstimate(flops=int(flops), bytes_accessed=int(nbytes), transcendentals=int(trans)),
        compiler_params=pltpu.CompilerParams(
            vmem_limit_bytes=vmem, dimension_semantics=("arbitrary",) * len(grid)
        ),
    )
    return lambda *operands: made(*operands, *after, *alias)


SMEM = pl.BlockSpec(memory_space=pltpu.SMEM)


def sds(shape, dtype):
    return jax.ShapeDtypeStruct(shape, dtype)


def hbm(shape, dtype):
    return pltpu.HBM(shape, dtype)


def vmem(shape, dtype):
    return pltpu.VMEM(shape, dtype)


RESIDENT = pl.BlockSpec(memory_space=pltpu.VMEM)


def context_body(tok_ref, mem_ref, bank_ref, cot_ref, vec_ref, x_ref, xt_ref, cott_ref, gate_ref):
    i = pl.program_id(0)
    gain = vec_ref[0:1, :]

    def put(rows):
        x_ref[...] = rows
        xt_ref[...] = rows.T

    def norm(values):
        wide = values.astype(F32)
        return (wide * rms_factor(wide) * gain).astype(BF16)

    @pl.when(i < MC)
    def _():
        put(norm(mem_ref[...]))

    @pl.when((i >= MC) & (i < MC + NT))
    def _():
        rows = norm(tok_ref[...])
        put(rows)
        logits = nt(vec_ref[2:10, :].astype(BF16), rows)
        gate = jax.nn.sigmoid(logits)
        for p in range(NPAIR):
            gate_ref[p] = gate[2 * p : 2 * p + 2, :]
        cott_ref[...] = cot_ref[...].T

    @pl.when(i >= MC + NT)
    def _():
        put(bank_ref[...])


def context_kernel(tokens, memory, bank, cot, vectors, after=()):
    steps = MC + NT + BC
    clip_tok = lambda i: jnp.clip(i - MC, 0, NT - 1)
    return call(
        context_body,
        (steps,),
        [
            pl.BlockSpec((TB, D), lambda i: (clip_tok(i), 0)),
            pl.BlockSpec((TB, D), lambda i: (jnp.minimum(i, MC - 1), 0)),
            pl.BlockSpec((TB, D), lambda i: (jnp.clip(i - MC - NT, 0, BC - 1), 0)),
            pl.BlockSpec((TB, D), lambda i: (clip_tok(i), 0)),
            whole((2 + H, D)),
        ],
        [
            pl.BlockSpec((TB, D), lambda i: (i, 0)),
            pl.BlockSpec((D, TB), lambda i: (0, i)),
            pl.BlockSpec((D, TB), lambda i: (0, clip_tok(i))),
            pl.BlockSpec((NPAIR, 2, TB), lambda i: (0, 0, clip_tok(i))),
        ],
        [sds((ROWS, D), BF16), hbm((D, ROWS), BF16), sds((D, LEN), BF16), hbm((NPAIR, 2, LEN), F32)],
        8e9,
        8e6,
        "context",
        after=after,
        vmem=SMALL,
    )(tokens, memory, bank, cot, vectors)


def mask_body(doc_row_ref, doc_col_ref, near_ref, tok_ref, bank_ref):
    i = pl.program_id(0)
    doc_row = doc_row_ref[...]

    @pl.when(i < NT)
    def _():
        keys = lax.broadcasted_iota(jnp.int32, (TB, LEN), 0) + i * TB
        rows = lax.broadcasted_iota(jnp.int32, (TB, LEN), 1)
        seen = (keys <= rows) & (doc_col_ref[...] == doc_row)
        tok_ref[...] = jnp.where(seen, 0.0, masked_score)

    @pl.when(i >= NT)
    def _():
        keys = lax.broadcasted_iota(jnp.int32, (TB, LEN), 0) + (i - NT) * TB
        count = jnp.zeros((TB, LEN), F32)
        for j in range(KNB):
            count = count + jnp.where(near_ref[j : j + 1, :] == keys, 1.0, 0.0)
        bias = jnp.where(count > 0.5, 0.0, masked_score)
        for j in range(2, KNB + 1):
            bias = jnp.where(count > j - 0.5, math.log2(j), bias)
        bank_ref[...] = bias


def mask_kernel(doc_row, doc_col, near_t, after=()):
    return call(
        mask_body,
        (NT + BC,),
        [
            whole((1, LEN)),
            pl.BlockSpec((TB, 1), lambda i: (jnp.minimum(i, NT - 1), 0)),
            whole((KNB, LEN)),
        ],
        [
            pl.BlockSpec((TB, LEN), lambda i: (jnp.minimum(i, NT - 1), 0)),
            pl.BlockSpec((TB, LEN), lambda i: (jnp.clip(i - NT, 0, BC - 1), 0)),
        ],
        [vmem((LEN, LEN), F32), vmem((BANK, LEN), F32)],
        6e9,
        7e6,
        "masks",
        after=after,
        vmem=SMALL,
    )(doc_row, doc_col, near_t)


def each_block(place_ref, chips, planes):
    for core in range(2):
        for chip in range(chips):
            row = ((place_ref[0] ^ chip) * 2 + (place_ref[1] ^ core))
            for plane in range(planes):
                yield core, chip, plane, row, place_ref[2] ^ plane


def part(index, size):
    return pl.ds(pl.multiple_of(index * size, size), size)


def head_squares(columns):
    wide = columns.astype(F32)
    return jnp.sum((wide * wide).reshape(H, HD, wide.shape[1]), axis=1)


def project_rows(i, x_ref, w_ref, q_ref, k_ref, v_ref, qt_ref, kt_ref, vt_ref, qn_ref, kn_ref):
    rows = x_ref[...]
    keys = nn(rows, w_ref[1]).astype(BF16)
    values = nn(rows, w_ref[2]).astype(BF16)
    keys_t = keys.T
    k_ref[...] = keys
    v_ref[...] = values
    kt_ref[...] = keys_t
    vt_ref[...] = values.T

    @pl.when(i == 0)
    def _():
        kn_ref[...] = jnp.zeros(kn_ref.shape, F32)
        qn_ref[...] = jnp.zeros(qn_ref.shape, F32)

    kn_ref[...] = jnp.maximum(kn_ref[...], head_squares(keys_t))

    @pl.when((i >= MEM // rows.shape[0]) & (i < CTX // rows.shape[0]))
    def _():
        queries = (nn(rows, w_ref[0]).astype(BF16).astype(F32) * (LOG2E / math.sqrt(HD))).astype(BF16)
        queries_t = queries.T
        q_ref[...] = queries
        qt_ref[...] = queries_t
        qn_ref[...] = jnp.maximum(qn_ref[...], head_squares(queries_t))


def project_kernel(x, w, place=None, after=()):
    rows = 2 * TB
    steps = ROWS // rows
    first_q, last_q = MEM // rows, CTX // rows - 1
    fast = place is not None
    if fast:
        chips, planes = len(w) // 2, w[0].shape[0]
        own_rows, own_cols = w[0].shape[1] // 3, w[0].shape[2]

    def body(*refs):
        i = pl.program_id(0)
        if not fast:
            project_rows(i, *refs)
            return
        place_ref, x_ref, *rest = refs
        blocks, (w_ref, *outs) = rest[: len(w)], rest[len(w) :]

        @pl.when(i == 0)
        def _():
            for core, chip, plane, row, col in each_block(place_ref, chips, planes):
                for j in range(3):
                    w_ref[j, part(row, own_rows), part(col, own_cols)] = blocks[core * chips + chip][
                        plane, j * own_rows : (j + 1) * own_rows, :
                    ]

        project_rows(i, x_ref, w_ref, *outs)

    out_specs = [
        pl.BlockSpec((rows, D), lambda i: (jnp.clip(i, first_q, last_q) - first_q, 0)),
        pl.BlockSpec((rows, D), lambda i: (i, 0)),
        pl.BlockSpec((rows, D), lambda i: (i, 0)),
        pl.BlockSpec((D, rows), lambda i: (0, jnp.clip(i, first_q, last_q) - first_q)),
        pl.BlockSpec((D, rows), lambda i: (0, i)),
        pl.BlockSpec((D, rows), lambda i: (0, i)),
        whole((H, rows)),
        whole((H, rows)),
    ]
    out_shape = [
        hbm((LEN, D), BF16),
        vmem((ROWS, D), BF16),
        vmem((ROWS, D), BF16),
        vmem((D, LEN), BF16),
        hbm((D, ROWS), BF16),
        vmem((D, ROWS), BF16),
        sds((H, rows), F32),
        sds((H, rows), F32),
    ]
    in_specs = [pl.BlockSpec((rows, D), lambda i: (i, 0))]
    if fast:
        in_specs = [SMEM] + in_specs + [RESIDENT] * len(w)
        out_specs = [whole((3, D, D))] + out_specs
        out_shape = [hbm((3, D, D), BF16)] + out_shape
        operands = (place, x, *w)
    else:
        in_specs = in_specs + [whole((3, D, D))]
        operands = (x, w)
    result = call(
        body, (steps,), in_specs, out_specs, out_shape, 11e9, 14e6, "project", after=after, vmem=24 * 1024 * 1024
    )(*operands)
    return result if fast else [w, *result]


def head_lanes(values, h):
    lanes = lax.broadcasted_iota(jnp.int32, values.shape, 1)
    keep = (lanes < HD) if h == 0 else (lanes >= HD)
    return jnp.where(keep, values, jnp.zeros_like(values))


def near_count(tb):
    return MEM + (tb + 1) * TB


def seen_count(tb):
    return near_count(tb) + BANK


FAR = slice(CTX, ROWS)


def head_rows_of(values, h):
    zeros = jnp.zeros((HD, values.shape[1]), values.dtype)
    own = values[h * HD : (h + 1) * HD, :]
    return jnp.concatenate([own, zeros] if h == 0 else [zeros, own], axis=0)


def attend_body(
    qt_ref, k_ref, vt_ref, tok_ref, bank_ref, doc_ref, gate_ref, qn_ref, kn_ref,
    e0_ref, e1_ref, e2_ref, e3_ref, local_ref, fetched_ref, stat_ref, mixed_ref, mixedt_ref, s_ref,
):
    e_refs = (e0_ref, e1_ref, e2_ref, e3_ref)
    units = [(tb, h) for tb in range(NT) for h in range(2)]

    def start(u):
        tb, h = units[u]
        near = near_count(tb)
        q_head = head_rows_of(qt_ref[:, tb * TB : (tb + 1) * TB], h)
        s_ref[u % 2, :near, :] = nn(k_ref[:near, :], q_head)
        s_ref[u % 2, near : near + BANK, :] = nn(k_ref[FAR, :], q_head)

    def biased(u, row, cols, mem_bias):
        s = s_ref[u % 2, row : row + TB, :]
        near = near_count(units[u][0])
        if row < MEM:
            return s + mem_bias
        if row < near:
            return s + tok_ref[row - MEM : row - MEM + TB, cols]
        return s + bank_ref[row - near : row - near + TB, cols]

    def soft(u, first, last, cols, mem_bias, general):
        tb, h = units[u]
        top = None
        if general:
            peak = jnp.full((8, TB), -3e38, F32)
            for row in range(first, last, TB):
                s = biased(u, row, cols, mem_bias)
                peak = jnp.maximum(peak, jnp.max(s.reshape(TB // 8, 8, TB), axis=0))
            top = jnp.max(peak, axis=0, keepdims=True)
        total = jnp.zeros((8, TB), F32)
        for row in range(first, last, TB):
            s = biased(u, row, cols, mem_bias)
            e = jnp.exp2(s - top if general else s)
            e_refs[tb][h, row : row + TB, :] = e.astype(BF16)
            total = total + jnp.sum(e.reshape(TB // 8, 8, TB), axis=0)
        return 1.0 / jnp.sum(total, axis=0, keepdims=True)

    def run(general):
        start(0)
        mixed_parts = []
        for u, (tb, h) in enumerate(units):
            cols = slice(tb * TB, (tb + 1) * TB)
            head_rows = slice(h * HD, (h + 1) * HD)
            near, seen = near_count(tb), seen_count(tb)
            if u + 1 < len(units):
                start(u + 1)
            mem_bias = jnp.where(doc_ref[:, cols] == 0.0, 0.0, masked_score)
            local_inv = soft(u, 0, near, cols, mem_bias, general)
            fetched_inv = soft(u, near, seen, cols, mem_bias, general)
            local = nn(vt_ref[head_rows, :near], e_refs[tb][h, :near, :]) * local_inv
            fetched = nn(vt_ref[head_rows, FAR], e_refs[tb][h, near:, :]) * fetched_inv
            local_ref[head_rows, cols] = local.astype(BF16)
            fetched_ref[head_rows, cols] = fetched.astype(BF16)
            stat_ref[0, h : h + 1, cols] = local_inv
            stat_ref[0, 2 + h : 3 + h, cols] = fetched_inv
            gate = gate_ref[0, h : h + 1, cols]
            mixed_parts.append((1.0 - gate) * local + gate * fetched)
            if h == 1:
                mixed = jnp.concatenate(mixed_parts, axis=0)
                mixed_parts = []
                mixedt_ref[:, cols] = mixed.astype(BF16)
                mixed_ref[cols, :] = mixed.T.astype(BF16)

    bound = jnp.max(jnp.max(qn_ref[...], axis=1, keepdims=True) * jnp.max(kn_ref[...], axis=1, keepdims=True))

    @pl.when(bound <= SAFE * SAFE)
    def _():
        run(False)

    @pl.when(jnp.logical_not(bound <= SAFE * SAFE))
    def _():
        run(True)


def attend_kernel(qt, k, vt, qn, kn, bias_tok, bias_bank, doc_row, gate, first, count):
    spec_cols = lambda rows: pl.BlockSpec((rows, PAIR), lambda p: (0, p + first))
    spec_rows = lambda cols: pl.BlockSpec((PAIR, cols), lambda p: (p + first, 0))
    *e, local, fetched, stat, mixed, mixed_t = call(
        attend_body,
        (count,),
        [
            spec_rows(LEN),
            spec_cols(ROWS),
            spec_rows(ROWS),
            RESIDENT,
            RESIDENT,
            whole((1, LEN)),
            pl.BlockSpec((1, 2, LEN), lambda p: (p + first, 0, 0)),
            whole(qn.shape),
            whole(kn.shape),
        ],
        [
            *[pl.BlockSpec((2, seen_count(tb), TB), lambda p: (p, 0, 0)) for tb in range(NT)],
            pl.BlockSpec((PAIR, LEN), lambda p: (p, 0)),
            pl.BlockSpec((PAIR, LEN), lambda p: (p, 0)),
            pl.BlockSpec((1, 8, LEN), lambda p: (p, 0, 0)),
            pl.BlockSpec((LEN, PAIR), lambda p: (0, p)),
            pl.BlockSpec((PAIR, LEN), lambda p: (p, 0)),
        ],
        [
            *[hbm((2 * count, seen_count(tb), TB), BF16) for tb in range(NT)],
            hbm((PAIR * count, LEN), BF16),
            hbm((PAIR * count, LEN), BF16),
            hbm((count, 8, LEN), F32),
            vmem((LEN, PAIR * count), BF16),
            vmem((PAIR * count, LEN), BF16),
        ],
        count * 5e9,
        count * 14e6 + 6e6,
        "attend",
        scratch=[pltpu.VMEM((2, ROWS, TB), F32)],
        trans=count * 2 * ROWS * LEN,
        vmem=28 * 1024 * 1024,
    )(qt, k, vt, bias_tok, bias_bank, doc_row, gate, qn, kn)
    return e, local, fetched, stat, mixed, mixed_t


def gelu_parts(x):
    square = jnp.exp2(x * x * (-0.5 * LOG2E))
    t = 1.0 / (1.0 + (0.3275911 * 0.7071067811865476) * jnp.abs(x))
    poly = t * (
        0.127414796 + t * (-0.142248368 + t * (0.7107068705 + t * (-0.7265760135 + t * 0.5307027145)))
    )
    tail = poly * square
    cdf = jnp.where(x >= 0.0, 1.0 - tail, tail)
    return cdf, square * 0.3989422804014327


FC = 512


def feed_body(
    mixed_ref, tok_ref, cot_ref, wo_ref, up_ref, dt_ref, vec_ref,
    out_ref, act_ref, gh_ref, ffnt_ref, branch_ref, gres_ref, gmt_ref, gain_ref,
):
    i = pl.program_id(0)
    residual = tok_ref[...].astype(F32) + nn(mixed_ref[...], wo_ref[...])
    factor = rms_factor(residual)
    hat = residual * factor
    gain = vec_ref[1:2, :]
    ffn = (hat * gain).astype(BF16)
    ffnt_ref[...] = ffn.T
    cot = cot_ref[...]
    out = residual
    grad_ffn = jnp.zeros(residual.shape, F32)
    for c in range(FF // FC):
        cols = slice(c * FC, (c + 1) * FC)
        hidden = nn(ffn, up_ref[:, cols])
        cdf, pdf = gelu_parts(hidden)
        act = (hidden * cdf).astype(BF16)
        act_ref[:, cols] = act
        grad_act = nn(cot, dt_ref[:, cols])
        gh = (grad_act * (cdf + hidden * pdf)).astype(BF16)
        gh_ref[:, cols] = gh
        out = out + nt(act, dt_ref[:, cols])
        grad_ffn = grad_ffn + nt(gh, up_ref[:, cols])
    out_ref[...] = out.astype(BF16)
    part = jnp.sum(grad_ffn * hat, axis=0, keepdims=True)

    @pl.when(i == 0)
    def _():
        gain_ref[...] = part

    @pl.when(i > 0)
    def _():
        gain_ref[...] += part

    scaled = grad_ffn * gain
    grad_res = cot.astype(F32) + factor * (scaled - hat * jnp.mean(scaled * hat, axis=-1, keepdims=True))
    gres_ref[...] = grad_res
    branch = grad_res.astype(BF16)
    branch_ref[...] = branch
    gmt_ref[...] = nt(wo_ref[...], branch)


def feed_kernel(mixed, tokens, cot, vectors, w):
    rows = lambda width: pl.BlockSpec((TB, width), lambda i: (i, 0))
    cols = lambda height: pl.BlockSpec((height, TB), lambda i: (0, i))

    def body(mixed_ref, tok_ref, cot_ref, vec_ref, wo_ref, up_ref, dt_ref, *outs):
        feed_body(mixed_ref, tok_ref, cot_ref, wo_ref, up_ref, dt_ref, vec_ref, *outs)

    return call(
        body,
        (NT,),
        [rows(D), rows(D), rows(D), whole((2 + H, D))] + [whole(x.shape) for x in w],
        [rows(D), rows(FF), rows(FF), cols(D), rows(D), rows(D), cols(D), whole((1, D))],
        [
            sds((LEN, D), BF16),
            sds((LEN, FF), BF16),
            sds((LEN, FF), BF16),
            sds((D, LEN), BF16),
            sds((LEN, D), BF16),
            sds((LEN, D), F32),
            sds((D, LEN), F32),
            sds((1, D), F32),
        ],
        23e9,
        22e6,
        "feed",
        trans=LEN * FF * 2,
    )(mixed, tokens, cot, vectors, *w)


def feed_grads_body(cott_ref, act_ref, ffnt_ref, gh_ref, mixedt_ref, branch_ref, gd_ref, gu_ref, go_ref):
    gd_ref[...] = nn(cott_ref[...], act_ref[...]).astype(BF16)
    gu_ref[...] = nn(ffnt_ref[...], gh_ref[...]).astype(BF16)
    go_ref[...] = nn(mixedt_ref[...], branch_ref[...]).astype(BF16)


def feed_grads_kernel(cot_t, act, ffn_t, gh, mixed_t, branch):
    steps = 4
    wide = lambda width: pl.BlockSpec((LEN, width // steps), lambda i: (0, i))
    out = lambda width: pl.BlockSpec((D, width // steps), lambda i: (0, i))
    return call(
        feed_grads_body,
        (steps,),
        [whole((D, LEN)), wide(FF), whole((D, LEN)), wide(FF), whole((D, LEN)), wide(D)],
        [out(FF), out(FF), out(D)],
        [sds((D, FF), BF16), sds((D, FF), BF16), sds((D, D), BF16)],
        11e9,
        17e6,
        "feed_grads",
    )(cot_t, act, ffn_t, gh, mixed_t, branch)


def feed_blocks(mixed, mixed_t, tokens, cot, cot_t, vectors, w, place):
    chips, planes = len(w) // 2, w[0].shape[0]
    own_rows, own_o, own_ff = w[0].shape[1], D // planes, FF // planes
    width = own_o + 2 * own_ff
    size = 2 * TB
    row_steps = LEN // size

    def body(place_ref, mixed_ref, mixedt_ref, tok_ref, cot_ref, cott_ref, vec_ref, *rest):
        blocks, rest = rest[: len(w)], rest[len(w) :]
        gres_ref, gmt_ref, gain_ref, keep_ref, send_ref, res_ref, act_out, dt_out = rest[:8]
        wo_ref, up_ref, dt_ref, act_ref, gh_ref, ffnt_ref, branch_ref, hid_ref, ga_ref, all_ref, sems = rest[8:]
        i = pl.program_id(0)
        leave = (pltpu.make_async_copy(act_ref, act_out, sems.at[0]), pltpu.make_async_copy(dt_ref, dt_out, sems.at[1]))

        @pl.when(i == 0)
        def _():
            for core, chip, plane, row, col in each_block(place_ref, chips, planes):
                block = blocks[core * chips + chip]
                here = part(row, own_rows)
                wo_ref[here, part(col, own_o)] = block[plane, :, :own_o]
                up_ref[here, part(col, own_ff)] = block[plane, :, own_o : own_o + own_ff]
                dt_ref[here, part(col, own_ff)] = block[plane, :, own_o + own_ff :]

        @pl.when(i < row_steps)
        def _():
            here = part(i, size)
            residual = tok_ref[...].astype(F32) + nn(mixed_ref[...], wo_ref[...])
            factor = rms_factor(residual)
            hat = residual * factor
            gain = vec_ref[1:2, :]
            ffn = (hat * gain).astype(BF16)
            ffnt_ref[:, here] = ffn.T
            cot = cot_ref[...]

            def start(c):
                cols = slice(c * FC, (c + 1) * FC)
                hid_ref[c % 2] = nn(ffn, up_ref[:, cols])
                ga_ref[c % 2] = nn(cot, dt_ref[:, cols])

            grad_ffn = jnp.zeros(residual.shape, F32)
            start(0)
            for c in range(FF // FC):
                cols = slice(c * FC, (c + 1) * FC)
                if c + 1 < FF // FC:
                    start(c + 1)
                hidden = hid_ref[c % 2]
                cdf, pdf = gelu_parts(hidden)
                act_ref[here, cols] = (hidden * cdf).astype(BF16)
                gh_ref[here, cols] = (ga_ref[c % 2] * (cdf + hidden * pdf)).astype(BF16)
                grad_ffn = grad_ffn + nt(gh_ref[here, cols], up_ref[:, cols])
            res_ref[...] = residual
            gain_part = jnp.sum(grad_ffn * hat, axis=0, keepdims=True)

            @pl.when(i == 0)
            def _():
                gain_ref[...] = gain_part

            @pl.when(i > 0)
            def _():
                gain_ref[...] += gain_part

            scaled = grad_ffn * gain
            grad_res = cot.astype(F32) + factor * (scaled - hat * jnp.mean(scaled * hat, axis=-1, keepdims=True))
            gres_ref[...] = grad_res
            branch = grad_res.astype(BF16)
            branch_ref[here, :] = branch
            gmt_ref[...] = nt(wo_ref[...], branch)

        @pl.when(i == row_steps)
        def _():
            for copy in leave:
                copy.start()

        @pl.when(i == row_steps + planes - 1)
        def _():
            for copy in leave:
                copy.wait()

        @pl.when(i >= row_steps)
        def _():
            plane = i - row_steps
            cols = part(plane, own_ff)
            all_ref[:, :own_o] = nn(mixedt_ref[...], branch_ref[:, part(plane, own_o)]).astype(BF16)
            all_ref[:, own_o : own_o + own_ff] = nn(ffnt_ref[...], gh_ref[:, cols]).astype(BF16)
            all_ref[:, own_o + own_ff :] = nn(cott_ref[...], act_ref[:, cols]).astype(BF16)
            for chip in range(chips):
                slot = place_ref[0] ^ chip
                keep_ref[slot, 0] = all_ref[part(chip * 2 + place_ref[1], own_rows), :]
                send_ref[slot, 0] = all_ref[part(chip * 2 + 1 - place_ref[1], own_rows), :]

    row = lambda i: jnp.minimum(i, row_steps - 1)
    rows = pl.BlockSpec((size, D), lambda i, _: (row(i), 0))
    blocked = pl.BlockSpec(
        (chips, 1, own_rows, width), lambda i, place_ref: (0, jnp.maximum(i - row_steps, 0) ^ place_ref[2], 0, 0)
    )
    shape = hbm((chips, planes, own_rows, width), BF16)
    return call(
        body,
        (row_steps + planes,),
        [rows, RESIDENT, rows, rows, RESIDENT, whole((2 + H, D))] + [RESIDENT] * len(w),
        [rows, pl.BlockSpec((D, size), lambda i, _: (0, row(i))), whole((1, D)), blocked, blocked, rows]
        + [pl.BlockSpec(memory_space=pl.ANY)] * 2,
        [
            hbm((LEN, D), F32),
            vmem((D, LEN), F32),
            sds((1, D), F32),
            vmem((chips, planes, own_rows, width), BF16),
            shape,
            hbm((LEN, D), F32),
            hbm((LEN, FF), BF16),
            hbm((D, FF), BF16),
        ],
        30e9,
        22e6,
        "feed",
        scratch=[
            pltpu.VMEM((D, D), BF16),
            pltpu.VMEM((D, FF), BF16),
            pltpu.VMEM((D, FF), BF16),
            pltpu.VMEM((LEN, FF), BF16),
            pltpu.VMEM((LEN, FF), BF16),
            pltpu.VMEM((D, LEN), BF16),
            pltpu.VMEM((LEN, D), BF16),
            pltpu.VMEM((2, size, FC), F32),
            pltpu.VMEM((2, size, FC), F32),
            pltpu.VMEM((D, width), BF16),
            pltpu.SemaphoreType.DMA((2,)),
        ],
        trans=LEN * FF * 2,
        prefetch=1,
        vmem=36 * 1024 * 1024,
    )(place, mixed, mixed_t, tokens, cot, cot_t, vectors, *w)


def output_kernel(residual, act, down_t, after):
    size = 2 * TB

    def body(res_ref, act_ref, dt_ref, out_ref):
        out_ref[...] = (res_ref[...] + nt(act_ref[...], dt_ref[...])).astype(BF16)

    rows = lambda width: pl.BlockSpec((size, width), lambda i: (i, 0))
    return call(
        body,
        (LEN // size,),
        [rows(D), rows(FF), whole((D, FF))],
        rows(D),
        hbm((LEN, D), BF16),
        6e9,
        10e6,
        "output",
        after=after,
        vmem=SMALL,
    )(residual, act, down_t)


def unattend_body(
    q_ref, kt_ref, v_ref, e0_ref, e1_ref, e2_ref, e3_ref, gmt_ref, local_ref, fetched_ref, stat_ref, gate_ref,
    dq_ref, dk_ref, dv_ref, gl_ref, ds0_ref, ds1_ref, ds2_ref, ds3_ref, do_ref, df_ref, dot_ref, dqt_ref, dk_acc, dv_acc, gp_ref,
):
    e_refs, ds_refs = (e0_ref, e1_ref, e2_ref, e3_ref), (ds0_ref, ds1_ref, ds2_ref, ds3_ref)

    def prepare(h):
        head_rows = slice(h * HD, (h + 1) * HD)
        gm = gmt_ref[head_rows, :]
        local = local_ref[head_rows, :].astype(F32)
        fetched = fetched_ref[head_rows, :].astype(F32)
        gate = gate_ref[0, h : h + 1, :]
        local_inv = stat_ref[0, h : h + 1, :]
        fetched_inv = stat_ref[0, 2 + h : 3 + h, :]
        grad_gate = jnp.sum(gm * (fetched - local), axis=0, keepdims=True)
        gl_ref[0, h : h + 1, :] = grad_gate * gate * (1.0 - gate)
        grad_local = ((1.0 - gate) * gm).astype(BF16).astype(F32)
        grad_fetched = gate * gm
        other = slice((1 - h) * HD, (2 - h) * HD)
        do_ref[h, other, :] = jnp.zeros((HD, LEN), BF16)
        df_ref[h, other, :] = jnp.zeros((HD, LEN), BF16)
        do_ref[h, head_rows, :] = (grad_local * local_inv).astype(BF16)
        df_ref[h, head_rows, :] = (grad_fetched * fetched_inv).astype(BF16)
        dot_ref[h : h + 1, :] = jnp.sum(grad_local * local, axis=0, keepdims=True) * local_inv
        dot_ref[2 + h : 3 + h, :] = jnp.sum(grad_fetched * fetched, axis=0, keepdims=True) * fetched_inv

    units = [(tb, h) for h in range(2) for tb in range(NT)]

    def start(u):
        tb, h = units[u]
        near, cols = near_count(tb), slice(tb * TB, (tb + 1) * TB)
        gp_ref[u % 2, :near, :] = nn(v_ref[:near, :], do_ref[h, :, cols])
        gp_ref[u % 2, near : near + BANK, :] = nn(v_ref[FAR, :], df_ref[h, :, cols])

    def rows_part(u):
        tb, h = units[u]
        near, cols = near_count(tb), slice(tb * TB, (tb + 1) * TB)
        head_rows = slice(h * HD, (h + 1) * HD)
        for row in range(0, seen_count(tb), TB):
            some, which = slice(row, row + TB), h if row < near else 2 + h
            gp = gp_ref[u % 2, some, :] - dot_ref[which : which + 1, cols]
            ds_refs[tb][h, some, :] = (e_refs[tb][h, some, :].astype(F32) * gp).astype(BF16)
        dq = nn(kt_ref[head_rows, :near], ds_refs[tb][h, :near, :])
        dq = dq + nn(kt_ref[head_rows, FAR], ds_refs[tb][h, near:, :])
        dqt_ref[head_rows, cols] = dq * (1.0 / math.sqrt(HD))

    def keys_part(h, tb):
        near, cols = near_count(tb), slice(tb * TB, (tb + 1) * TB)
        q_head = head_lanes(q_ref[cols, :], h)
        pieces = (
            (slice(0, near), slice(0, near), do_ref[h, :, cols]),
            (FAR, slice(near, near + BANK), df_ref[h, :, cols]),
        )
        for keys, some, grad_out in pieces:
            dv = nt(e_refs[tb][h, some, :], grad_out)
            dk = nn(ds_refs[tb][h, some, :], q_head)
            if h == 0 and tb == NT - 1:
                dv_acc[keys, :] = dv
                dk_acc[keys, :] = dk
            else:
                dv_acc[keys, :] += dv
                dk_acc[keys, :] += dk

    prepare(0)
    start(0)
    prepare(1)
    for u, (tb, h) in enumerate(units):
        if u + 1 < len(units):
            start(u + 1)
        rows_part(u)
        if h == 1:
            keys_part(0, NT - 1 - tb)
    for tb in range(NT):
        keys_part(1, tb)
    dv_ref[...] = dv_acc[...].astype(BF16)
    dk_ref[...] = (dk_acc[...] * (1.0 / LOG2E)).astype(BF16)
    dq_ref[...] = dqt_ref[...].T.astype(BF16)


def unattend_kernel(q, kt, v, e, gmt, local, fetched, stat, gate, first, count, after=(), alias=()):
    spec_cols = lambda rows: pl.BlockSpec((rows, PAIR), lambda p: (0, p + first))
    spec_rows = lambda cols: pl.BlockSpec((PAIR, cols), lambda p: (p + first, 0))
    return call(
        unattend_body,
        (count,),
        [
            spec_cols(LEN),
            spec_rows(ROWS),
            spec_cols(ROWS),
            *[pl.BlockSpec((2, seen_count(tb), TB), lambda p: (p + first, 0, 0)) for tb in range(NT)],
            spec_rows(LEN),
            spec_rows(LEN),
            spec_rows(LEN),
            pl.BlockSpec((1, 8, LEN), lambda p: (p + first, 0, 0)),
            pl.BlockSpec((1, 2, LEN), lambda p: (p + first, 0, 0)),
        ],
        [
            spec_cols(LEN),
            spec_cols(ROWS),
            spec_cols(ROWS),
            pl.BlockSpec((1, 2, LEN), lambda p: (p + first, 0, 0)),
        ],
        [
            sds((LEN, D), BF16),
            sds((ROWS, D), BF16),
            sds((ROWS, D), BF16),
            sds((NPAIR, 2, LEN), F32),
        ],
        count * 10e9,
        count * 14e6,
        "unattend",
        scratch=[
            *[pltpu.VMEM((2, seen_count(tb), TB), BF16) for tb in range(NT)],
            pltpu.VMEM((2, PAIR, LEN), BF16),
            pltpu.VMEM((2, PAIR, LEN), BF16),
            pltpu.VMEM((8, LEN), F32),
            pltpu.VMEM((PAIR, LEN), F32),
            pltpu.VMEM((ROWS, PAIR), F32),
            pltpu.VMEM((ROWS, PAIR), F32),
            pltpu.VMEM((2, ROWS, TB), F32),
        ],
        after=after,
        alias=alias,
        vmem=36 * 1024 * 1024,
    )(q, kt, v, *e, gmt, local, fetched, stat, gate)


def all_heads(gl_ref):
    return jnp.concatenate([gl_ref[p] for p in range(NPAIR)], axis=0).astype(BF16)


def proj_grads_body(xt_ref, dq_ref, dk_ref, dv_ref, gl_ref, g_ref, gate_ref):
    g_ref[0] = nn(xt_ref[:, MEM:CTX], dq_ref[...]).astype(BF16)
    g_ref[1] = nn(xt_ref[...], dk_ref[...]).astype(BF16)
    g_ref[2] = nn(xt_ref[...], dv_ref[...]).astype(BF16)

    @pl.when(pl.program_id(0) == 0)
    def _():
        gate_ref[...] = nt(all_heads(gl_ref), xt_ref[:, MEM:CTX])


def proj_grads_kernel(xt, dq, dk, dv, gl, place=None, chips=0, planes=0, after=()):
    steps = 2
    fast = place is not None
    wide = lambda rows: pl.BlockSpec((rows, D // steps), lambda i, *_: (0, i))
    in_specs = [whole((D, ROWS)), wide(LEN), wide(ROWS), wide(ROWS), whole((NPAIR, 2, LEN))]
    gate_spec, gate_shape = whole((H, D)), sds((H, D), F32)
    flops, nbytes = 8e9, 10e6
    if not fast:
        return call(
            proj_grads_body,
            (steps,),
            in_specs,
            [pl.BlockSpec((3, D, D // steps), lambda i: (0, 0, i)), gate_spec],
            [sds((3, D, D), BF16), gate_shape],
            flops,
            nbytes,
            "proj_grads",
        )(xt, dq, dk, dv, gl)
    own_rows, own_cols, group = D // (2 * chips), D // planes, planes // steps

    def body(place_ref, xt_ref, dq_ref, dk_ref, dv_ref, gl_ref, keep_ref, send_ref, gate_ref, all_ref):
        proj_grads_body(xt_ref, dq_ref, dk_ref, dv_ref, gl_ref, all_ref, gate_ref)
        for b in range(group):
            col = b ^ (place_ref[2] % group)
            cols = slice(b * own_cols, (b + 1) * own_cols)
            for chip in range(chips):
                slot = place_ref[0] ^ chip
                for j in range(3):
                    here = slice(j * own_rows, (j + 1) * own_rows)
                    keep_ref[slot, col, here, :] = all_ref[j, part(chip * 2 + place_ref[1], own_rows), cols]
                    send_ref[slot, col, here, :] = all_ref[j, part(chip * 2 + 1 - place_ref[1], own_rows), cols]

    out = pl.BlockSpec(
        (chips, group, 3 * own_rows, own_cols), lambda i, place_ref: (0, i ^ (place_ref[2] // group), 0, 0)
    )
    shape = sds((chips, planes, 3 * own_rows, own_cols), BF16)
    return call(
        body,
        (steps,),
        in_specs,
        [out, out, gate_spec],
        [shape, shape, gate_shape],
        flops,
        nbytes,
        "proj_grads",
        scratch=[pltpu.VMEM((3, D, D // steps), BF16)],
        prefetch=1,
        after=after,
        vmem=24 * 1024 * 1024,
    )(place, xt, dq, dk, dv, gl)


def input_body(dq_ref, dk_ref, dv_ref, gl_ref, w_ref, tok_ref, mem_ref, vec_ref, gres_ref, gin_ref, gain_ref):
    i = pl.program_id(0)
    gn = nt(dk_ref[...], w_ref[1]) + nt(dv_ref[...], w_ref[2])

    @pl.when(i < MC)
    def _():
        wide = mem_ref[...].astype(F32)
        part = jnp.sum(gn * (wide * rms_factor(wide)), axis=0, keepdims=True)

        @pl.when(i == 0)
        def _():
            gain_ref[...] = part

        @pl.when(i > 0)
        def _():
            gain_ref[...] += part

    @pl.when(i >= MC)
    def _():
        wide = tok_ref[...].astype(F32)
        factor = rms_factor(wide)
        hat = wide * factor
        full = gn + nt(dq_ref[...], w_ref[0]) + tn(all_heads(gl_ref), vec_ref[2:10, :].astype(BF16))
        gain_ref[...] += jnp.sum(full * hat, axis=0, keepdims=True)
        scaled = full * vec_ref[0:1, :]
        gin_ref[...] = (
            gres_ref[...] + factor * (scaled - hat * jnp.mean(scaled * hat, axis=-1, keepdims=True))
        ).astype(BF16)


def input_kernel(dq, dk, dv, gl, w, tokens, memory, vectors, gres, after=()):
    tok = lambda i: jnp.clip(i - MC, 0, NT - 1)
    rows = pl.BlockSpec((TB, D), lambda i: (tok(i), 0))
    return call(
        input_body,
        (MC + NT,),
        [
            rows,
            pl.BlockSpec((TB, D), lambda i: (i, 0)),
            pl.BlockSpec((TB, D), lambda i: (i, 0)),
            pl.BlockSpec((NPAIR, 2, TB), lambda i: (0, 0, tok(i))),
            whole((3, D, D)),
            rows,
            pl.BlockSpec((TB, D), lambda i: (jnp.minimum(i, MC - 1), 0)),
            whole((2 + H, D)),
            rows,
        ],
        [rows, whole((1, D))],
        [sds((LEN, D), BF16), sds((1, D), F32)],
        9e9,
        10e6,
        "input",
        after=after,
        vmem=SMALL,
    )(dq, dk, dv, gl, w, tokens, memory, vectors, gres)


def exchange(slots, axis):
    size = len(slots)
    return [slots[0]] + [
        lax.ppermute(slots[r], axis, [(i, i ^ r) for i in range(size)]) for r in range(1, size)
    ]


def added(parts):
    total = parts[0].astype(F32)
    for other in parts[1:]:
        total = total + other.astype(F32)
    return total


PLANES = (("up",), ("q", "k"), ("v", "o"), ("down",))
EXTRA = 16


def alone(body, operands, out_shape, name, scratch=(), place=None, after=(), flops=2e9, vmem=SMALL, resident=0):
    specs = [RESIDENT if j < resident else whole(x.shape) for j, x in enumerate(operands)]
    if place is not None:
        specs, operands = [SMEM] + specs, (place, *operands)
    return call(
        body,
        (1,),
        specs,
        [whole(x.shape) for x in out_shape],
        out_shape,
        flops,
        2e6,
        name,
        scratch=scratch,
        after=after,
        vmem=vmem,
    )(*operands)


def first_payload(attn_weights):
    rows, cols = attn_weights.shape[1:]

    def body(aw_ref, out_ref):
        for j in range(3):
            out_ref[j * rows : (j + 1) * rows, :] = aw_ref[j].astype(BF16)

    return alone(body, (attn_weights,), [vmem((3 * rows, cols), BF16)], "first_payload", vmem=VMEM_LIMIT)[0]


def second_payloads(place, attn_weights, up_weights, down_weights, attn_moment, up_moment, down_moment, after):
    rows, cols = attn_weights.shape[1:]
    wide = up_weights.shape[1]
    planes = len(PLANES)
    width = cols + 3 * wide

    def body(place_ref, aw_ref, uw_ref, dw_ref, am_ref, um_ref, dm_ref, *rest):
        outs, all_ref = rest[:planes], rest[planes]
        all_ref[...] = jnp.zeros(all_ref.shape, BF16)
        all_ref[0] = um_ref[...].astype(BF16)
        all_ref[3] = dm_ref[...].astype(BF16)
        for j in range(4):
            all_ref[1 + j // 2, :, (j % 2) * cols : (j % 2 + 1) * cols] = am_ref[j].astype(BF16)
        for r in range(planes):
            outs[r][:, :cols] = aw_ref[3].astype(BF16)
            outs[r][:, cols : cols + wide] = uw_ref[...].astype(BF16)
            outs[r][:, cols + wide : cols + 2 * wide] = dw_ref[...].astype(BF16)
            outs[r][:, cols + 2 * wide :] = all_ref[place_ref[2] ^ r]

    return alone(
        body,
        (attn_weights, up_weights, down_weights, attn_moment, up_moment, down_moment),
        [vmem((rows, width), BF16)] * planes,
        "second_payloads",
        scratch=[pltpu.VMEM((planes, rows, wide), BF16)],
        place=place,
        after=after,
        vmem=VMEM_LIMIT,
    )


def stacked_pair(parts, width):
    rows = parts[0].shape[0]
    other = parts[0].shape[1] - width

    def body(*refs):
        for r in range(len(parts)):
            refs[-2][r] = refs[r][:, :width]
            refs[-1][r] = refs[r][:, width:]

    shapes = [sds((len(parts), rows, width), BF16), sds((len(parts), rows, other), BF16)]
    return alone(body, parts, shapes, "stacked_pair", resident=len(parts))


def stacked(parts, after=()):
    def body(*refs):
        for r in range(len(parts)):
            refs[-1][r] = refs[r][...]

    return alone(body, parts, [sds((len(parts),) + parts[0].shape, parts[0].dtype)], "stacked", after=after, resident=len(parts))[0]


def core_blocks(plane):
    return plane + [exchange([b, b], "core")[1] for b in plane]


def fold_cores(keep, other):
    chips, planes, rows, width = keep.shape

    def body(keep_ref, other_ref, *outs):
        for chip in range(chips):
            outs[chip][...] = added([keep_ref[chip], other_ref[chip]]).astype(BF16)

    spec = pl.BlockSpec((chips, 1, rows, width), lambda i: (0, i, 0, 0))
    return call(
        body,
        (planes,),
        [spec, spec],
        [pl.BlockSpec((1, rows, width), lambda i: (i, 0, 0))] * chips,
        [sds((planes, rows, width), BF16)] * chips,
        4e9,
        7e6,
        "fold_cores",
        vmem=SMALL,
    )(keep, other)


def fold_chips(parts):
    planes, rows, width = parts[0].shape

    def body(*refs):
        for plane in range(planes):
            refs[len(parts) + plane][...] = added([r[plane] for r in refs[: len(parts)]]).astype(BF16)

    return alone(body, parts, [sds((rows, width), BF16)] * planes, "fold_chips", resident=len(parts))


VEC = 2 + H
VEC_ROWS = 128


def put_vectors(ref, first, values):
    high = values.astype(BF16)
    low = (values - high.astype(F32)).astype(BF16)
    ref[first : first + VEC_ROWS, :] = jnp.zeros((VEC_ROWS, 128), BF16)
    for j in range(4):
        lanes = slice(j * 128, (j + 1) * 128)
        ref[first + j * 16 : first + j * 16 + VEC, :] = high[:, lanes]
        ref[first + 64 + j * 16 : first + 64 + j * 16 + VEC, :] = low[:, lanes]


def get_vectors(refs, first):
    pieces = []
    for j in range(4):
        rows = lambda offset: slice(first + offset + j * 16, first + offset + j * 16 + VEC)
        pieces.append(added([r[rows(offset), :] for r in refs for offset in (0, 64)]))
    return jnp.concatenate(pieces, axis=1)


def fold_cores_first(keep, other):
    chips = keep.shape[0]

    def body(keep_ref, other_ref, *outs):
        for chip in range(chips):
            outs[chip][...] = added([keep_ref[chip], other_ref[chip]]).astype(BF16)

    return alone(body, (keep, other), [sds(keep.shape[1:], BF16)] * chips, "fold_cores_first")


def fold_chips_first(parts, gain_attn, gain_ffn, grad_gate):
    planes, rows, width = parts[0].shape
    count = len(parts)

    def body(*refs):
        ins, (ga_ref, gf_ref, gg_ref) = refs[:count], refs[count : count + 3]
        outs, vec_ref = refs[count + 3 : -1], refs[-1]
        vec_ref[0:1, :] = ga_ref[...]
        vec_ref[1:2, :] = gf_ref[...]
        vec_ref[2:VEC, :] = gg_ref[...]
        for plane in range(planes):
            outs[plane][:rows, :] = added([r[plane] for r in ins]).astype(BF16)
            put_vectors(outs[plane], rows, vec_ref[...])

    return alone(
        body,
        (*parts, gain_attn, gain_ffn, grad_gate),
        [sds((rows + VEC_ROWS, width), BF16)] * planes,
        "fold_chips_first",
        resident=count,
        scratch=[pltpu.VMEM((VEC, D), F32)],
    )


def stack_with_vectors(parts, vec, after):
    count, width = len(parts), parts[0].shape[1]
    rows = parts[0].shape[0] - EXTRA

    def body(*refs):
        vec_ref, out_ref = refs[count], refs[count + 1]
        for r in range(count):
            out_ref[r * rows : (r + 1) * rows, :] = refs[r][:rows, :]
        squares = added([r[rows:, :] for r in refs[:count]])
        squares = jnp.sum(squares, axis=0, keepdims=True) + jnp.zeros((EXTRA, width), F32)
        high = squares.astype(BF16).astype(F32)
        middle = (squares - high).astype(BF16).astype(F32)
        row = lax.broadcasted_iota(jnp.int32, (EXTRA, width), 0)
        extra = jnp.where(row == VEC, high, jnp.where(row == VEC + 1, middle, squares - high - middle))
        values = jnp.concatenate([vec_ref[...], jnp.zeros((EXTRA - VEC, width), F32)], axis=0)
        first = values.astype(BF16).astype(F32)
        here = count * rows
        out_ref[here : here + EXTRA, :] = jnp.where(row < VEC, first, extra).astype(BF16)
        out_ref[here + EXTRA :, :] = (values - first).astype(BF16)

    return alone(
        body, (*parts, vec), [sds((count * rows + 2 * EXTRA, width), BF16)], "stack_with_vectors", after=after, resident=count + 1
    )[0]


def owned_kernel(place, parts_a, parts_b):
    planes = len(parts_a)
    size, cols = parts_a[0].shape[0] - VEC_ROWS, parts_a[0].shape[1]
    rows, width = parts_b[0].shape
    wide = (width - cols) // 2

    def body(place_ref, *refs):
        a_refs, b_refs = refs[:planes], refs[planes : 2 * planes]
        ga_ref, gb_ref, vec_ref, *rest = refs[2 * planes :]
        slots, all_ref = rest[:planes], rest[planes]
        ga = added([r[:size, :] for r in a_refs])
        gb = added([r[...] for r in b_refs])
        ga_ref[...] = ga
        gb_ref[...] = gb
        vec_ref[...] = get_vectors(a_refs, size)
        squares = jnp.sum(ga * ga, keepdims=True) + jnp.sum(gb * gb, keepdims=True)
        all_ref[...] = jnp.zeros(all_ref.shape, BF16)
        for j in range(4):
            grad = ga[j * rows : (j + 1) * rows, :] if j < 3 else gb[:, :cols]
            all_ref[1 + j // 2, :, (j % 2) * cols : (j % 2 + 1) * cols] = grad.astype(BF16)
        all_ref[0] = gb[:, cols : cols + wide].astype(BF16)
        all_ref[3] = gb[:, cols + wide :].astype(BF16)
        wide_squares = squares + jnp.zeros((EXTRA, wide), F32)
        row = lax.broadcasted_iota(jnp.int32, (EXTRA, wide), 0)
        high = wide_squares.astype(BF16).astype(F32)
        middle = (wide_squares - high).astype(BF16).astype(F32)
        low = wide_squares - high - middle
        extra = jnp.where(row == 0, high, jnp.where(row == 1, middle, jnp.where(row == 2, low, 0.0))).astype(BF16)
        for r in range(planes):
            slots[r][:rows, :] = all_ref[place_ref[2] ^ r]
            slots[r][rows:, :] = extra

    return alone(
        body,
        (*parts_a, *parts_b),
        [hbm((size, cols), F32), hbm((rows, width), F32), sds((VEC, D), F32)]
        + [sds((rows + EXTRA, wide), BF16)] * planes,
        "owned",
        resident=2 * planes,
        scratch=[pltpu.VMEM((planes, rows, wide), BF16)],
        place=place,
    )


def orthogonal_kernel(place, grads, moments, vectors, vec_moment, after):
    count = len(grads)
    chips = count // 2
    planes, rows, wide = moments[0].shape[1:]
    cols = D // planes
    limit = clip_fraction * math.sqrt(PARAMS)

    def body(place_ref, *refs):
        grad_refs, moment_refs, refs = refs[:count], refs[count : count + 2], refs[count + 2 :]
        vec_ref, vm_ref, norm_ref, vn_ref, vmn_ref = refs[:5]
        outs = refs[5 : 5 + planes]
        low_ref, x_ref, mix_ref, diag_ref, all_ref = refs[5 + planes :]
        pair = (place_ref[2] == 1) | (place_ref[2] == 2)
        own = part(place_ref[0] * 2 + place_ref[1], rows)
        after = planes * rows
        extra = added([r[after : after + EXTRA, :] for r in grad_refs])
        grad_vec = extra[:VEC, :] + added([r[after + EXTRA : after + EXTRA + VEC, :] for r in grad_refs])
        total = jnp.sum(extra[VEC : VEC + 3, 0:1], axis=0, keepdims=True) + jnp.sum(grad_vec * grad_vec, keepdims=True)
        norm = jnp.sqrt(total)
        norm_ref[...] = norm
        clip = limit / jnp.maximum(norm, limit)
        vec_mom = vector_decay * vm_ref[...] + clip * grad_vec
        vmn_ref[...] = vec_mom
        vn_ref[...] = vec_ref[...] - vector_rate * vec_mom

        def momentum(core, chip, plane, lanes):
            b = core * chips + chip
            moment = moment_refs[core][chip, plane, :, lanes].astype(F32)
            grad = grad_refs[b][plane * rows : (plane + 1) * rows, lanes].astype(F32)
            return muon_decay * moment + clip * grad

        def gram_of(start, width):
            half = D // 2
            upper, lower = low_ref[:half, start : start + width], low_ref[half:, start : start + width]
            corner = nt(lower, upper)
            first = jnp.concatenate([nt(upper, upper), corner.T], axis=1)
            return jnp.concatenate([first, jnp.concatenate([corner, nt(lower, lower)], axis=1)], axis=0)

        def mixing(gram):
            eye = lax.broadcasted_iota(jnp.int32, (D, D), 0) == lax.broadcasted_iota(jnp.int32, (D, D), 1)
            low = gram.astype(BF16)
            mix = coef_second * low.astype(F32) + coef_third * nn(low, low)
            diag_ref[...] = coef_first + jnp.sum(jnp.where(eye, mix, 0.0), axis=1, keepdims=True)
            mix_ref[...] = jnp.where(eye, 0.0, mix).astype(BF16)

        def advance(start, width, scale):
            for c in range(start, start + width, D):
                lanes = slice(c, c + D)
                new = diag_ref[...] * x_ref[:, lanes] + nn(mix_ref[...], low_ref[:, lanes])
                if scale is not None:
                    new = new * scale
                x_ref[:, lanes] = new
                low_ref[:, lanes] = new.astype(BF16)

        def first_step(start, width):
            gram = gram_of(start, width)
            eye = lax.broadcasted_iota(jnp.int32, (D, D), 0) == lax.broadcasted_iota(jnp.int32, (D, D), 1)
            scale = 1.0 / (jnp.sqrt(jnp.sum(jnp.where(eye, gram, 0.0), keepdims=True)) + 1e-07)
            mixing(gram * (scale * scale))
            advance(start, width, scale)

        def step(start, width, last):
            mixing(gram_of(start, width))
            if not last:
                advance(start, width, None)
                return
            for c in range(start, start + width, D):
                lanes = slice(c, c + D)
                x_ref[own, lanes] = diag_ref[own, :] * x_ref[own, lanes] + nn(mix_ref[own, :], low_ref[:, lanes])

        def iterations(ranges):
            for start, width in ranges:
                first_step(start, width)

            def middle(_, carry):
                for start, width in ranges:
                    step(start, width, False)
                return carry

            lax.fori_loop(1, NS_ITERS - 1, middle, 0)
            for start, width in ranges:
                step(start, width, True)

        @pl.when(pair)
        def _():
            for core, chip, plane, row, col in each_block(place_ref, chips, planes):
                for j in range(2):
                    new = momentum(core, chip, plane, slice(j * cols, (j + 1) * cols))
                    x_ref[part(row, rows), part(col + j * planes, cols)] = new
                    low_ref[part(row, rows), part(col + j * planes, cols)] = new.astype(BF16)
            iterations([(0, D), (D, D)])
            for plane in range(planes):
                for j in range(2):
                    first = j * D + plane * cols
                    all_ref[plane, :, j * cols : (j + 1) * cols] = x_ref[own, first : first + cols].astype(BF16)

        @pl.when(jnp.logical_not(pair))
        def _():
            for core, chip, plane, row, col in each_block(place_ref, chips, planes):
                new = momentum(core, chip, plane, slice(0, wide))
                x_ref[part(row, rows), part(col, wide)] = new
                low_ref[part(row, rows), part(col, wide)] = new.astype(BF16)
            iterations([(0, FF)])
            for plane in range(planes):
                all_ref[plane] = x_ref[own, plane * wide : (plane + 1) * wide].astype(BF16)

        for r in range(planes):
            outs[r][...] = all_ref[place_ref[2] ^ r]

    return alone(
        body,
        (*grads, *moments, vectors, vec_moment),
        [sds((1, 1), F32), sds((VEC, D), F32), sds((VEC, D), F32)] + [sds((rows, wide), BF16)] * planes,
        "orthogonal",
        scratch=[
            pltpu.VMEM((D, FF), BF16),
            pltpu.VMEM((D, FF), F32),
            pltpu.VMEM((D, D), BF16),
            pltpu.VMEM((D, 1), F32),
            pltpu.VMEM((planes, rows, wide), BF16),
        ],
        place=place,
        after=after,
        flops=18e9,
        vmem=24 * 1024 * 1024,
        resident=count + 2,
    )


def outside(arrays):
    return [pltpu.with_memory_space_constraint(x, pltpu.HBM) for x in arrays]


def moments_kernel(norm, ga, gb, attn_moment, up_moment, down_moment, after):
    rows, cols = attn_moment.shape[1:]
    wide = up_moment.shape[1]
    limit = clip_fraction * math.sqrt(PARAMS)

    def body(norm_ref, ga_ref, gb_ref, am_ref, um_ref, dm_ref, amn_ref, umn_ref, dmn_ref):
        clip = limit / jnp.maximum(norm_ref[...], limit)
        for j in range(4):
            grad = ga_ref[j * rows : (j + 1) * rows, :] if j < 3 else gb_ref[:, :cols]
            amn_ref[j] = muon_decay * am_ref[j] + clip * grad
        umn_ref[...] = muon_decay * um_ref[...] + clip * gb_ref[:, cols : cols + wide]
        dmn_ref[...] = muon_decay * dm_ref[...] + clip * gb_ref[:, cols + wide :]

    moments = (attn_moment, up_moment, down_moment)
    return alone(
        body,
        (norm, *outside((ga, gb, *moments))),
        [sds(x.shape, F32) for x in moments],
        "moments",
        after=after,
    )


def update_kernel(place, slots, attn_weights, up_weights, down_weights):
    planes = len(slots)
    cols = attn_weights.shape[2]
    shape_factor = math.sqrt(max(1.0, FF / D))

    def body(place_ref, *refs):
        slot_refs, (aw_ref, uw_ref, dw_ref, an_ref, un_ref, dn_ref, all_ref) = refs[:planes], refs[planes:]
        for r in range(planes):
            all_ref[place_ref[2] ^ r] = slot_refs[r][...]
        for j in range(4):
            ortho = all_ref[1 + j // 2, :, (j % 2) * cols : (j % 2 + 1) * cols].astype(F32)
            an_ref[j] = aw_ref[j] - muon_rate * ortho
        un_ref[...] = uw_ref[...] - muon_rate * all_ref[0].astype(F32)
        dn_ref[...] = dw_ref[...] - muon_rate * shape_factor * all_ref[3].astype(F32)

    weights = (attn_weights, up_weights, down_weights)
    return alone(
        body,
        (*slots, *outside(weights)),
        [sds(x.shape, F32) for x in weights],
        "update",
        resident=planes,
        scratch=[pltpu.VMEM((planes,) + slots[0].shape, BF16)],
        place=place,
    )


def documents(starts):
    doc = jnp.cumsum(starts).astype(F32)
    return doc.reshape(1, LEN), doc.reshape(LEN, 1)


def plain_tail(sizes, grads, attn_weights, up_weights, down_weights, vectors, attn_moment, up_moment, down_moment, vec_moment):
    dp = ("chip", "core")
    grad_attn, grad_up, grad_down, grad_vectors = grads

    def owned(grad, narrow_dim, dp_dim):
        part_sum = lax.psum_scatter(grad.astype(BF16), "narrow", scatter_dimension=narrow_dim, tiled=True)
        return lax.psum_scatter(part_sum, dp, scatter_dimension=dp_dim, tiled=True).astype(F32)

    owned_attn, owned_up, owned_down = owned(grad_attn, 2, 1), owned(grad_up, 1, 0), owned(grad_down, 0, 1)
    own_squares = jnp.sum(owned_attn * owned_attn) + jnp.sum(owned_up * owned_up) + jnp.sum(owned_down * owned_down)
    vector_sum, square_sum = lax.psum((grad_vectors, own_squares), ("chip", "core", "narrow"))
    grad_norm = jnp.sqrt(square_sum + jnp.sum(vector_sum * vector_sum))
    clip_limit = clip_fraction * math.sqrt(PARAMS)
    clip_factor = clip_limit / jnp.maximum(grad_norm, clip_limit)
    attn_mom_new = muon_decay * attn_moment + clip_factor * owned_attn
    up_mom_new = muon_decay * up_moment + clip_factor * owned_up
    down_mom_new = muon_decay * down_moment + clip_factor * owned_down
    gather = lambda x, dim: lax.all_gather(x.astype(BF16), dp, axis=dim, tiled=True).astype(F32)
    ortho = (gather(attn_mom_new, 1), gather(up_mom_new, 0), gather(down_mom_new, 1))
    ortho_attn, ortho_up, ortho_down = ortho
    for iteration in range(NS_ITERS):
        gram_attn = jnp.einsum("imc,inc->imn", ortho_attn, ortho_attn, precision=highest)
        gram_up = lax.dot_general(ortho_up, ortho_up, (((1,), (1,)), ((), ())), precision=highest)
        gram_down = lax.dot_general(ortho_down, ortho_down, (((0,), (0,)), ((), ())), precision=highest)
        partial_grams = jnp.concatenate([gram_attn, gram_up[None], gram_down[None]], axis=0)
        gram_total = lax.psum(partial_grams.astype(BF16), "narrow").astype(F32)
        if iteration == 0:
            norm_scales = 1.0 / (jnp.sqrt(jnp.trace(gram_total, axis1=1, axis2=2)) + 1e-07)
            ortho_attn = ortho_attn * norm_scales[:4, None, None]
            ortho_up = ortho_up * norm_scales[4]
            ortho_down = ortho_down * norm_scales[5]
            gram_total = gram_total * (norm_scales * norm_scales)[:, None, None]
        once = jnp.einsum("imn,inc->imc", gram_total[:4], ortho_attn, precision=highest)
        twice = jnp.einsum("imn,inc->imc", gram_total[:4], once, precision=highest)
        ortho_attn = coef_first * ortho_attn + coef_second * once + coef_third * twice
        once = jnp.dot(gram_total[4], ortho_up, precision=highest)
        twice = jnp.dot(gram_total[4], once, precision=highest)
        ortho_up = coef_first * ortho_up + coef_second * once + coef_third * twice
        once = jnp.dot(ortho_down, gram_total[5], precision=highest)
        twice = jnp.dot(once, gram_total[5], precision=highest)
        ortho_down = coef_first * ortho_down + coef_second * once + coef_third * twice
    row_share = D // sizes["dp"]
    row_start = lax.axis_index(dp) * row_share
    final_attn = lax.dynamic_slice_in_dim(ortho_attn, row_start, row_share, 1)
    final_up = lax.dynamic_slice_in_dim(ortho_up, row_start, row_share, 0)
    final_down = lax.dynamic_slice_in_dim(ortho_down, row_start, row_share, 1)
    shape_factor = math.sqrt(max(1.0, FF / D))
    vector_mom_new = vector_decay * vec_moment + clip_factor * vector_sum
    return (
        attn_weights - muon_rate * final_attn,
        up_weights - muon_rate * final_up,
        down_weights - muon_rate * shape_factor * final_down,
        attn_mom_new,
        up_mom_new,
        down_mom_new,
        vectors - vector_rate * vector_mom_new,
        vector_mom_new,
        grad_norm,
    )


def per_device(
    sizes,
    tokens, memory, neighbour_bank, starts, neighbours, cotangent,
    attn_weights, up_weights, down_weights, vectors,
    attn_moment, up_moment, down_moment, vector_moment,
):
    memory = memory.reshape(MEM, D)
    bank = neighbour_bank.reshape(BANK, D)
    own = (attn_weights, up_weights, down_weights)
    moments = (attn_moment, up_moment, down_moment)
    chips, planes = sizes["dp"] // 2, sizes["narrow"]
    if planes == len(PLANES) and chips == 4:
        return fast_device(
            chips, planes, tokens, memory, bank, starts, neighbours, cotangent, own, vectors, moments, vector_moment
        )
    full = lambda x, narrow_dim, dp_dim: lax.all_gather(
        lax.all_gather(x.astype(BF16), ("chip", "core"), axis=dp_dim, tiled=True), "narrow", axis=narrow_dim, tiled=True
    )
    attn_full = full(attn_weights, 2, 1)
    second = [attn_full[3], full(up_weights, 1, 0), full(down_weights, 0, 1).T]
    x, xt, cot_t, gate = context_kernel(tokens, memory, bank, cotangent, vectors)
    doc_row, doc_col = documents(starts)
    bias_tok, bias_bank = mask_kernel(doc_row, doc_col, neighbours.T)
    w, q, k, v, qt, kt, vt, qn, kn = project_kernel(x, attn_full[:3])
    e, local, fetched, stat, mixed, mixed_t = attend_kernel(qt, k, vt, qn, kn, bias_tok, bias_bank, doc_row, gate, 0, NPAIR)
    out, act, gh, ffn_t, branch, gres, gmt, gain_ffn = feed_kernel(mixed, tokens, cotangent, vectors, second)
    grad_down_t, grad_up, grad_o = feed_grads_kernel(cot_t, act, ffn_t, gh, mixed_t, branch)
    dq, dk, dv, gl = unattend_kernel(q, kt, v, e, gmt, local, fetched, stat, gate, 0, NPAIR)
    grad_qkv, grad_gate = proj_grads_kernel(xt, dq, dk, dv, gl)
    grad_in, gain_attn = input_kernel(dq, dk, dv, gl, w, tokens, memory, vectors, gres)
    grad_vectors = jnp.concatenate([gain_attn, gain_ffn, grad_gate], axis=0)
    grads = (jnp.concatenate([grad_qkv, grad_o[None]], axis=0), grad_up, grad_down_t.T, grad_vectors)
    return (out, grad_in) + plain_tail(sizes, grads, *own, vectors, *moments, vector_moment)


def ordered(first, second):
    return lax.optimization_barrier((first, second))[0]


def fast_device(
    chips, planes, tokens, memory, bank, starts, neighbours, cotangent, own, vectors, moments, vector_moment
):
    own, moments = own[:2] + (own[2].T,), moments[:2] + (moments[2].T,)
    place = jnp.stack([lax.axis_index("chip"), lax.axis_index("core"), lax.axis_index("narrow")]).astype(jnp.int32)
    payload = first_payload(own[0])
    payloads = second_payloads(place, *own, *moments, after=[payload])
    near_a = exchange([payload] * planes, "narrow")
    doc_row, doc_col = documents(starts)
    near_t = ordered(neighbours.T, payload)
    near_b = exchange(ordered(payloads, near_a), "narrow")
    column_a = stacked(near_a)
    plane_a = exchange([column_a] * chips, "chip")
    x, xt, cot_t, gate = context_kernel(tokens, memory, bank, cotangent, vectors, after=[column_a])
    bias_tok, bias_bank = mask_kernel(doc_row, doc_col, near_t, after=[x])
    first = core_blocks(ordered(plane_a, bias_tok))
    column_b, column_m = stacked_pair(ordered(near_b, first), payloads[0].shape[1] - own[1].shape[1])
    w, q, k, v, qt, kt, vt, qn, kn = project_kernel(x, first, place, after=[column_b])
    plane_b = exchange([column_b] * chips, "chip")
    e, local, fetched, stat, mixed, mixed_t = attend_kernel(qt, k, vt, qn, kn, bias_tok, bias_bank, doc_row, gate, 0, NPAIR)
    own_b = exchange([column_b, column_b], "core")[1]
    late_b = ordered(plane_b[1:], mixed)
    second = [column_b, *late_b, own_b] + [exchange([b, b], "core")[1] for b in late_b]
    gres, gmt, gain_ffn, keep_b, send_b, residual, act, down_t = feed_blocks(
        mixed, mixed_t, tokens, cotangent, cot_t, vectors, second, place
    )
    q, kt, xt = outside((q, kt, xt))
    back = (q, kt, v, e, gmt, local, fetched, stat, gate)
    slots_b = fold_cores(keep_b, exchange([send_b, send_b], "core")[1])
    dq, dk, dv, gl = unattend_kernel(*back, 0, NPAIR, after=[slots_b[0]])
    slots_b = fold_chips(ordered(exchange(slots_b, "chip"), dq))
    keep_a, send_a, grad_gate = proj_grads_kernel(xt, dq, dk, dv, gl, place, chips, planes, after=[slots_b[0]])
    slots_a = fold_cores_first(keep_a, exchange([send_a, send_a], "core")[1])
    grad_in, gain_attn = input_kernel(dq, dk, dv, gl, w, tokens, memory, vectors, gres, after=[slots_a[0]])
    parts_a = exchange(slots_a, "chip")
    parts_b = exchange(slots_b, "narrow")
    parts_b, parts_a = ordered((parts_b, parts_a), grad_in)
    slots_a = fold_chips_first(parts_a, gain_attn, gain_ffn, grad_gate)
    plane_m = exchange([ordered(column_m, slots_a[0])] * chips, "chip")
    parts_a = exchange(slots_a, "narrow")
    whole_m = stacked(plane_m)
    all_m = exchange([whole_m, whole_m], "core")
    ga, gb, vec, *slots = owned_kernel(place, parts_a, parts_b)
    column_g = stack_with_vectors(exchange(slots, "narrow"), vec, after=[whole_m])
    plane_g = exchange([column_g] * chips, "chip")
    out = output_kernel(*outside((residual, act, down_t)), after=[column_g])
    grads = core_blocks(ordered(plane_g, out))
    norm, vec_new, vec_mom, *slots = orthogonal_kernel(place, grads, all_m, vectors, vector_moment, [])
    final = exchange(slots, "narrow")
    attn_mom, up_mom, down_mom = moments_kernel(norm, ga, gb, *moments, after=[slots[0]])
    attn_new, up_new, down_new = update_kernel(place, ordered(final, attn_mom), *own)
    new = (attn_new, up_new, down_new.T, attn_mom, up_mom, down_mom.T)
    return (out, grad_in, *new, vec_new, vec_mom, norm.reshape(()))


def solution(mesh):
    sizes = dict(mesh.shape)
    split = Mesh(
        mesh.devices.reshape(sizes["dp"] // 2, 2, sizes["narrow"]), ("chip", "core", "narrow")
    )
    dp = ("chip", "core")
    rows = ("chip", "core", "narrow")
    weights = (P(None, dp, "narrow"), P(dp, "narrow"), P("narrow", dp))
    return jax.shard_map(
        lambda *operands: per_device(sizes, *operands),
        mesh=split,
        in_specs=(P(rows, None), P(rows, None, None), P(rows, None, None), P(rows), P(rows, None), P(rows, None))
        + weights + (P(),) + weights + (P(),),
        out_specs=(P(rows, None), P(rows, None)) + weights + weights + (P(), P(), P()),
        check_vma=False,
    )
```

```python
import math

import jax
import jax.numpy as jnp
from jax import lax
from jax.experimental import pallas as pl
from jax.experimental.pallas import tpu as pltpu
from jax.sharding import Mesh, PartitionSpec as P

D = 512
H = 8
FF = 2048
MEM = 512
BANK = 512
KNB = 4
LEN = 1024
CTX = MEM + LEN
ROWS = CTX + BANK
HD = D // H
TB = 256
NT = LEN // TB
MC = MEM // TB
BC = BANK // TB
PAIR = 2 * HD
NPAIR = D // PAIR
F32 = jnp.float32
BF16 = jnp.bfloat16
NS_ITERS = 5
PARAMS = 3150848
epsilon = 1e-06
masked_score = -1e30
coef_first = 3.4445
coef_second = -4.775
coef_third = 2.0315
clip_fraction = 0.05
muon_rate = 0.5
muon_decay = 0.5
vector_rate = 0.5
vector_decay = 0.9
highest = lax.Precision.HIGHEST
LOG2E = 1.4426950408889634
SAFE = 80.0
VMEM_LIMIT = 60 * 1024 * 1024
SMALL = 16 * 1024 * 1024


def nn(a, b):
    return lax.dot_general(a, b, (((1,), (0,)), ((), ())), preferred_element_type=F32)


def nt(a, b):
    return lax.dot_general(a, b, (((1,), (1,)), ((), ())), preferred_element_type=F32)


def tn(a, b):
    return lax.dot_general(a, b, (((0,), (0,)), ((), ())), preferred_element_type=F32)


def rms_factor(values):
    return lax.rsqrt(jnp.mean(values * values, axis=-1, keepdims=True) + epsilon)


def whole(shape):
    return pl.BlockSpec(shape, lambda *_: (0,) * len(shape))


def call(
    body, grid, in_specs, out_specs, out_shape, flops, nbytes, name, scratch=(), trans=0, prefetch=0, after=(), alias=(),
    vmem=VMEM_LIMIT,
):
    extra, given = len(after) + len(alias), prefetch + len(in_specs)

    def with_extra(*refs):
        body(*refs[:given], *refs[given + extra :])

    made = pl.pallas_call(
        with_extra,
        grid_spec=pltpu.PrefetchScalarGridSpec(
            num_scalar_prefetch=prefetch,
            grid=grid,
            in_specs=list(in_specs) + [pl.BlockSpec(memory_space=pl.ANY)] * extra,
            out_specs=out_specs,
            scratch_shapes=list(scratch),
        ),
        out_shape=out_shape,
        input_output_aliases={given + len(after) + j: j for j in range(len(alias))},
        name=name,
        cost_estimate=pl.CostEstimate(flops=int(flops), bytes_accessed=int(nbytes), transcendentals=int(trans)),
        compiler_params=pltpu.CompilerParams(
            vmem_limit_bytes=vmem, dimension_semantics=("arbitrary",) * len(grid)
        ),
    )
    return lambda *operands: made(*operands, *after, *alias)


SMEM = pl.BlockSpec(memory_space=pltpu.SMEM)


def sds(shape, dtype):
    return jax.ShapeDtypeStruct(shape, dtype)


def hbm(shape, dtype):
    return pltpu.HBM(shape, dtype)


def vmem(shape, dtype):
    return pltpu.VMEM(shape, dtype)


RESIDENT = pl.BlockSpec(memory_space=pltpu.VMEM)


def context_body(tok_ref, mem_ref, bank_ref, cot_ref, vec_ref, x_ref, xt_ref, cott_ref, gate_ref):
    i = pl.program_id(0)
    gain = vec_ref[0:1, :]

    def put(rows):
        x_ref[...] = rows
        xt_ref[...] = rows.T

    def norm(values):
        wide = values.astype(F32)
        return (wide * rms_factor(wide) * gain).astype(BF16)

    @pl.when(i < MC)
    def _():
        put(norm(mem_ref[...]))

    @pl.when((i >= MC) & (i < MC + NT))
    def _():
        rows = norm(tok_ref[...])
        put(rows)
        logits = nt(vec_ref[2:10, :].astype(BF16), rows)
        gate = jax.nn.sigmoid(logits)
        for p in range(NPAIR):
            gate_ref[p] = gate[2 * p : 2 * p + 2, :]
        cott_ref[...] = cot_ref[...].T

    @pl.when(i >= MC + NT)
    def _():
        put(bank_ref[...])


def context_kernel(tokens, memory, bank, cot, vectors, after=()):
    steps = MC + NT + BC
    clip_tok = lambda i: jnp.clip(i - MC, 0, NT - 1)
    return call(
        context_body,
        (steps,),
        [
            pl.BlockSpec((TB, D), lambda i: (clip_tok(i), 0)),
            pl.BlockSpec((TB, D), lambda i: (jnp.minimum(i, MC - 1), 0)),
            pl.BlockSpec((TB, D), lambda i: (jnp.clip(i - MC - NT, 0, BC - 1), 0)),
            pl.BlockSpec((TB, D), lambda i: (clip_tok(i), 0)),
            whole((2 + H, D)),
        ],
        [
            pl.BlockSpec((TB, D), lambda i: (i, 0)),
            pl.BlockSpec((D, TB), lambda i: (0, i)),
            pl.BlockSpec((D, TB), lambda i: (0, clip_tok(i))),
            pl.BlockSpec((NPAIR, 2, TB), lambda i: (0, 0, clip_tok(i))),
        ],
        [sds((ROWS, D), BF16), hbm((D, ROWS), BF16), sds((D, LEN), BF16), hbm((NPAIR, 2, LEN), F32)],
        8e9,
        8e6,
        "context",
        after=after,
        vmem=SMALL,
    )(tokens, memory, bank, cot, vectors)


def mask_body(doc_row_ref, doc_col_ref, near_ref, tok_ref, bank_ref):
    i = pl.program_id(0)
    doc_row = doc_row_ref[...]

    @pl.when(i < NT)
    def _():
        keys = lax.broadcasted_iota(jnp.int32, (TB, LEN), 0) + i * TB
        rows = lax.broadcasted_iota(jnp.int32, (TB, LEN), 1)
        seen = (keys <= rows) & (doc_col_ref[...] == doc_row)
        tok_ref[...] = jnp.where(seen, 0.0, masked_score)

    @pl.when(i >= NT)
    def _():
        keys = lax.broadcasted_iota(jnp.int32, (TB, LEN), 0) + (i - NT) * TB
        count = jnp.zeros((TB, LEN), F32)
        for j in range(KNB):
            count = count + jnp.where(near_ref[j : j + 1, :] == keys, 1.0, 0.0)
        bias = jnp.where(count > 0.5, 0.0, masked_score)
        for j in range(2, KNB + 1):
            bias = jnp.where(count > j - 0.5, math.log2(j), bias)
        bank_ref[...] = bias


def mask_kernel(doc_row, doc_col, near_t, after=()):
    return call(
        mask_body,
        (NT + BC,),
        [
            whole((1, LEN)),
            pl.BlockSpec((TB, 1), lambda i: (jnp.minimum(i, NT - 1), 0)),
            whole((KNB, LEN)),
        ],
        [
            pl.BlockSpec((TB, LEN), lambda i: (jnp.minimum(i, NT - 1), 0)),
            pl.BlockSpec((TB, LEN), lambda i: (jnp.clip(i - NT, 0, BC - 1), 0)),
        ],
        [vmem((LEN, LEN), F32), vmem((BANK, LEN), F32)],
        6e9,
        7e6,
        "masks",
        after=after,
        vmem=SMALL,
    )(doc_row, doc_col, near_t)


def each_block(place_ref, chips, planes):
    for core in range(2):
        for chip in range(chips):
            row = ((place_ref[0] ^ chip) * 2 + (place_ref[1] ^ core))
            for plane in range(planes):
                yield core, chip, plane, row, place_ref[2] ^ plane


def part(index, size):
    return pl.ds(pl.multiple_of(index * size, size), size)


def head_squares(columns):
    wide = columns.astype(F32)
    return jnp.sum((wide * wide).reshape(H, HD, wide.shape[1]), axis=1)


def project_rows(i, x_ref, w_ref, q_ref, k_ref, v_ref, qt_ref, kt_ref, vt_ref, qn_ref, kn_ref):
    rows = x_ref[...]
    keys = nn(rows, w_ref[1]).astype(BF16)
    values = nn(rows, w_ref[2]).astype(BF16)
    keys_t = keys.T
    k_ref[...] = keys
    v_ref[...] = values
    kt_ref[...] = keys_t
    vt_ref[...] = values.T

    @pl.when(i == 0)
    def _():
        kn_ref[...] = jnp.zeros(kn_ref.shape, F32)
        qn_ref[...] = jnp.zeros(qn_ref.shape, F32)

    kn_ref[...] = jnp.maximum(kn_ref[...], head_squares(keys_t))

    @pl.when((i >= MEM // rows.shape[0]) & (i < CTX // rows.shape[0]))
    def _():
        queries = (nn(rows, w_ref[0]).astype(BF16).astype(F32) * (LOG2E / math.sqrt(HD))).astype(BF16)
        queries_t = queries.T
        q_ref[...] = queries
        qt_ref[...] = queries_t
        qn_ref[...] = jnp.maximum(qn_ref[...], head_squares(queries_t))


def project_kernel(x, w, place=None, after=()):
    rows = 2 * TB
    steps = ROWS // rows
    first_q, last_q = MEM // rows, CTX // rows - 1
    fast = place is not None
    if fast:
        chips, planes = len(w) // 2, w[0].shape[0]
        own_rows, own_cols = w[0].shape[1] // 3, w[0].shape[2]

    def body(*refs):
        i = pl.program_id(0)
        if not fast:
            project_rows(i, *refs)
            return
        place_ref, x_ref, *rest = refs
        blocks, (w_ref, *outs) = rest[: len(w)], rest[len(w) :]

        @pl.when(i == 0)
        def _():
            for core, chip, plane, row, col in each_block(place_ref, chips, planes):
                for j in range(3):
                    w_ref[j, part(row, own_rows), part(col, own_cols)] = blocks[core * chips + chip][
                        plane, j * own_rows : (j + 1) * own_rows, :
                    ]

        project_rows(i, x_ref, w_ref, *outs)

    out_specs = [
        pl.BlockSpec((rows, D), lambda i: (jnp.clip(i, first_q, last_q) - first_q, 0)),
        pl.BlockSpec((rows, D), lambda i: (i, 0)),
        pl.BlockSpec((rows, D), lambda i: (i, 0)),
        pl.BlockSpec((D, rows), lambda i: (0, jnp.clip(i, first_q, last_q) - first_q)),
        pl.BlockSpec((D, rows), lambda i: (0, i)),
        pl.BlockSpec((D, rows), lambda i: (0, i)),
        whole((H, rows)),
        whole((H, rows)),
    ]
    out_shape = [
        hbm((LEN, D), BF16),
        vmem((ROWS, D), BF16),
        vmem((ROWS, D), BF16),
        vmem((D, LEN), BF16),
        hbm((D, ROWS), BF16),
        vmem((D, ROWS), BF16),
        sds((H, rows), F32),
        sds((H, rows), F32),
    ]
    in_specs = [pl.BlockSpec((rows, D), lambda i: (i, 0))]
    if fast:
        in_specs = [SMEM] + in_specs + [RESIDENT] * len(w)
        out_specs = [whole((3, D, D))] + out_specs
        out_shape = [hbm((3, D, D), BF16)] + out_shape
        operands = (place, x, *w)
    else:
        in_specs = in_specs + [whole((3, D, D))]
        operands = (x, w)
    result = call(
        body, (steps,), in_specs, out_specs, out_shape, 11e9, 14e6, "project", after=after, vmem=24 * 1024 * 1024
    )(*operands)
    return result if fast else [w, *result]


def head_lanes(values, h):
    lanes = lax.broadcasted_iota(jnp.int32, values.shape, 1)
    keep = (lanes < HD) if h == 0 else (lanes >= HD)
    return jnp.where(keep, values, jnp.zeros_like(values))


def near_count(tb):
    return MEM + (tb + 1) * TB


def seen_count(tb):
    return near_count(tb) + BANK


FAR = slice(CTX, ROWS)


def head_rows_of(values, h):
    zeros = jnp.zeros((HD, values.shape[1]), values.dtype)
    own = values[h * HD : (h + 1) * HD, :]
    return jnp.concatenate([own, zeros] if h == 0 else [zeros, own], axis=0)


def attend_body(
    qt_ref, k_ref, vt_ref, tok_ref, bank_ref, doc_ref, gate_ref, qn_ref, kn_ref,
    e0_ref, e1_ref, e2_ref, e3_ref, local_ref, fetched_ref, stat_ref, mixed_ref, mixedt_ref, s_ref,
):
    e_refs = (e0_ref, e1_ref, e2_ref, e3_ref)
    units = [(tb, h) for tb in range(NT) for h in range(2)]

    def start(u):
        tb, h = units[u]
        near = near_count(tb)
        q_head = head_rows_of(qt_ref[:, tb * TB : (tb + 1) * TB], h)
        s_ref[u % 2, :near, :] = nn(k_ref[:near, :], q_head)
        s_ref[u % 2, near : near + BANK, :] = nn(k_ref[FAR, :], q_head)

    def biased(u, row, cols, mem_bias):
        s = s_ref[u % 2, row : row + TB, :]
        near = near_count(units[u][0])
        if row < MEM:
            return s + mem_bias
        if row < near:
            return s + tok_ref[row - MEM : row - MEM + TB, cols]
        return s + bank_ref[row - near : row - near + TB, cols]

    def soft(u, first, last, cols, mem_bias, general):
        tb, h = units[u]
        top = None
        if general:
            peak = jnp.full((8, TB), -3e38, F32)
            for row in range(first, last, TB):
                s = biased(u, row, cols, mem_bias)
                peak = jnp.maximum(peak, jnp.max(s.reshape(TB // 8, 8, TB), axis=0))
            top = jnp.max(peak, axis=0, keepdims=True)
        total = jnp.zeros((8, TB), F32)
        for row in range(first, last, TB):
            s = biased(u, row, cols, mem_bias)
            e = jnp.exp2(s - top if general else s)
            e_refs[tb][h, row : row + TB, :] = e.astype(BF16)
            total = total + jnp.sum(e.reshape(TB // 8, 8, TB), axis=0)
        return 1.0 / jnp.sum(total, axis=0, keepdims=True)

    def run(general):
        start(0)
        mixed_parts = []
        for u, (tb, h) in enumerate(units):
            cols = slice(tb * TB, (tb + 1) * TB)
            head_rows = slice(h * HD, (h + 1) * HD)
            near, seen = near_count(tb), seen_count(tb)
            if u + 1 < len(units):
                start(u + 1)
            mem_bias = jnp.where(doc_ref[:, cols] == 0.0, 0.0, masked_score)
            local_inv = soft(u, 0, near, cols, mem_bias, general)
            fetched_inv = soft(u, near, seen, cols, mem_bias, general)
            local = nn(vt_ref[head_rows, :near], e_refs[tb][h, :near, :]) * local_inv
            fetched = nn(vt_ref[head_rows, FAR], e_refs[tb][h, near:, :]) * fetched_inv
            local_ref[head_rows, cols] = local.astype(BF16)
            fetched_ref[head_rows, cols] = fetched.astype(BF16)
            stat_ref[0, h : h + 1, cols] = local_inv
            stat_ref[0, 2 + h : 3 + h, cols] = fetched_inv
            gate = gate_ref[0, h : h + 1, cols]
            mixed_parts.append((1.0 - gate) * local + gate * fetched)
            if h == 1:
                mixed = jnp.concatenate(mixed_parts, axis=0)
                mixed_parts = []
                mixedt_ref[:, cols] = mixed.astype(BF16)
                mixed_ref[cols, :] = mixed.T.astype(BF16)

    bound = jnp.max(jnp.max(qn_ref[...], axis=1, keepdims=True) * jnp.max(kn_ref[...], axis=1, keepdims=True))

    @pl.when(bound <= SAFE * SAFE)
    def _():
        run(False)

    @pl.when(jnp.logical_not(bound <= SAFE * SAFE))
    def _():
        run(True)


def attend_kernel(qt, k, vt, qn, kn, bias_tok, bias_bank, doc_row, gate, first, count):
    spec_cols = lambda rows: pl.BlockSpec((rows, PAIR), lambda p: (0, p + first))
    spec_rows = lambda cols: pl.BlockSpec((PAIR, cols), lambda p: (p + first, 0))
    *e, local, fetched, stat, mixed, mixed_t = call(
        attend_body,
        (count,),
        [
            spec_rows(LEN),
            spec_cols(ROWS),
            spec_rows(ROWS),
            RESIDENT,
            RESIDENT,
            whole((1, LEN)),
            pl.BlockSpec((1, 2, LEN), lambda p: (p + first, 0, 0)),
            whole(qn.shape),
            whole(kn.shape),
        ],
        [
            *[pl.BlockSpec((2, seen_count(tb), TB), lambda p: (p, 0, 0)) for tb in range(NT)],
            pl.BlockSpec((PAIR, LEN), lambda p: (p, 0)),
            pl.BlockSpec((PAIR, LEN), lambda p: (p, 0)),
            pl.BlockSpec((1, 8, LEN), lambda p: (p, 0, 0)),
            pl.BlockSpec((LEN, PAIR), lambda p: (0, p)),
            pl.BlockSpec((PAIR, LEN), lambda p: (p, 0)),
        ],
        [
            *[hbm((2 * count, seen_count(tb), TB), BF16) for tb in range(NT)],
            hbm((PAIR * count, LEN), BF16),
            hbm((PAIR * count, LEN), BF16),
            hbm((count, 8, LEN), F32),
            vmem((LEN, PAIR * count), BF16),
            vmem((PAIR * count, LEN), BF16),
        ],
        count * 5e9,
        count * 14e6 + 6e6,
        "attend",
        scratch=[pltpu.VMEM((2, ROWS, TB), F32)],
        trans=count * 2 * ROWS * LEN,
        vmem=28 * 1024 * 1024,
    )(qt, k, vt, bias_tok, bias_bank, doc_row, gate, qn, kn)
    return e, local, fetched, stat, mixed, mixed_t


def gelu_parts(x):
    square = jnp.exp2(x * x * (-0.5 * LOG2E))
    t = 1.0 / (1.0 + (0.3275911 * 0.7071067811865476) * jnp.abs(x))
    poly = t * (
        0.127414796 + t * (-0.142248368 + t * (0.7107068705 + t * (-0.7265760135 + t * 0.5307027145)))
    )
    tail = poly * square
    cdf = jnp.where(x >= 0.0, 1.0 - tail, tail)
    return cdf, square * 0.3989422804014327


FC = 512


def feed_body(
    mixed_ref, tok_ref, cot_ref, wo_ref, up_ref, dt_ref, vec_ref,
    out_ref, act_ref, gh_ref, ffnt_ref, branch_ref, gres_ref, gmt_ref, gain_ref,
):
    i = pl.program_id(0)
    residual = tok_ref[...].astype(F32) + nn(mixed_ref[...], wo_ref[...])
    factor = rms_factor(residual)
    hat = residual * factor
    gain = vec_ref[1:2, :]
    ffn = (hat * gain).astype(BF16)
    ffnt_ref[...] = ffn.T
    cot = cot_ref[...]
    out = residual
    grad_ffn = jnp.zeros(residual.shape, F32)
    for c in range(FF // FC):
        cols = slice(c * FC, (c + 1) * FC)
        hidden = nn(ffn, up_ref[:, cols])
        cdf, pdf = gelu_parts(hidden)
        act = (hidden * cdf).astype(BF16)
        act_ref[:, cols] = act
        grad_act = nn(cot, dt_ref[:, cols])
        gh = (grad_act * (cdf + hidden * pdf)).astype(BF16)
        gh_ref[:, cols] = gh
        out = out + nt(act, dt_ref[:, cols])
        grad_ffn = grad_ffn + nt(gh, up_ref[:, cols])
    out_ref[...] = out.astype(BF16)
    part = jnp.sum(grad_ffn * hat, axis=0, keepdims=True)

    @pl.when(i == 0)
    def _():
        gain_ref[...] = part

    @pl.when(i > 0)
    def _():
        gain_ref[...] += part

    scaled = grad_ffn * gain
    grad_res = cot.astype(F32) + factor * (scaled - hat * jnp.mean(scaled * hat, axis=-1, keepdims=True))
    gres_ref[...] = grad_res
    branch = grad_res.astype(BF16)
    branch_ref[...] = branch
    gmt_ref[...] = nt(wo_ref[...], branch)


def feed_kernel(mixed, tokens, cot, vectors, w):
    rows = lambda width: pl.BlockSpec((TB, width), lambda i: (i, 0))
    cols = lambda height: pl.BlockSpec((height, TB), lambda i: (0, i))

    def body(mixed_ref, tok_ref, cot_ref, vec_ref, wo_ref, up_ref, dt_ref, *outs):
        feed_body(mixed_ref, tok_ref, cot_ref, wo_ref, up_ref, dt_ref, vec_ref, *outs)

    return call(
        body,
        (NT,),
        [rows(D), rows(D), rows(D), whole((2 + H, D))] + [whole(x.shape) for x in w],
        [rows(D), rows(FF), rows(FF), cols(D), rows(D), rows(D), cols(D), whole((1, D))],
        [
            sds((LEN, D), BF16),
            sds((LEN, FF), BF16),
            sds((LEN, FF), BF16),
            sds((D, LEN), BF16),
            sds((LEN, D), BF16),
            sds((LEN, D), F32),
            sds((D, LEN), F32),
            sds((1, D), F32),
        ],
        23e9,
        22e6,
        "feed",
        trans=LEN * FF * 2,
    )(mixed, tokens, cot, vectors, *w)


def feed_grads_body(cott_ref, act_ref, ffnt_ref, gh_ref, mixedt_ref, branch_ref, gd_ref, gu_ref, go_ref):
    gd_ref[...] = nn(cott_ref[...], act_ref[...]).astype(BF16)
    gu_ref[...] = nn(ffnt_ref[...], gh_ref[...]).astype(BF16)
    go_ref[...] = nn(mixedt_ref[...], branch_ref[...]).astype(BF16)


def feed_grads_kernel(cot_t, act, ffn_t, gh, mixed_t, branch):
    steps = 4
    wide = lambda width: pl.BlockSpec((LEN, width // steps), lambda i: (0, i))
    out = lambda width: pl.BlockSpec((D, width // steps), lambda i: (0, i))
    return call(
        feed_grads_body,
        (steps,),
        [whole((D, LEN)), wide(FF), whole((D, LEN)), wide(FF), whole((D, LEN)), wide(D)],
        [out(FF), out(FF), out(D)],
        [sds((D, FF), BF16), sds((D, FF), BF16), sds((D, D), BF16)],
        11e9,
        17e6,
        "feed_grads",
    )(cot_t, act, ffn_t, gh, mixed_t, branch)


def feed_blocks(mixed, mixed_t, tokens, cot, cot_t, vectors, w, place):
    chips, planes = len(w) // 2, w[0].shape[0]
    own_rows, own_o, own_ff = w[0].shape[1], D // planes, FF // planes
    width = own_o + 2 * own_ff
    size = 2 * TB
    row_steps = LEN // size

    def body(place_ref, mixed_ref, mixedt_ref, tok_ref, cot_ref, cott_ref, vec_ref, *rest):
        blocks, rest = rest[: len(w)], rest[len(w) :]
        gres_ref, gmt_ref, gain_ref, keep_ref, send_ref, res_ref, act_out, dt_out = rest[:8]
        wo_ref, up_ref, dt_ref, act_ref, gh_ref, ffnt_ref, branch_ref, hid_ref, ga_ref, all_ref, sems = rest[8:]
        i = pl.program_id(0)
        leave = (pltpu.make_async_copy(act_ref, act_out, sems.at[0]), pltpu.make_async_copy(dt_ref, dt_out, sems.at[1]))

        @pl.when(i == 0)
        def _():
            for core, chip, plane, row, col in each_block(place_ref, chips, planes):
                block = blocks[core * chips + chip]
                here = part(row, own_rows)
                wo_ref[here, part(col, own_o)] = block[plane, :, :own_o]
                up_ref[here, part(col, own_ff)] = block[plane, :, own_o : own_o + own_ff]
                dt_ref[here, part(col, own_ff)] = block[plane, :, own_o + own_ff :]

        @pl.when(i < row_steps)
        def _():
            here = part(i, size)
            residual = tok_ref[...].astype(F32) + nn(mixed_ref[...], wo_ref[...])
            factor = rms_factor(residual)
            hat = residual * factor
            gain = vec_ref[1:2, :]
            ffn = (hat * gain).astype(BF16)
            ffnt_ref[:, here] = ffn.T
            cot = cot_ref[...]

            def start(c):
                cols = slice(c * FC, (c + 1) * FC)
                hid_ref[c % 2] = nn(ffn, up_ref[:, cols])
                ga_ref[c % 2] = nn(cot, dt_ref[:, cols])

            grad_ffn = jnp.zeros(residual.shape, F32)
            start(0)
            for c in range(FF // FC):
                cols = slice(c * FC, (c + 1) * FC)
                if c + 1 < FF // FC:
                    start(c + 1)
                hidden = hid_ref[c % 2]
                cdf, pdf = gelu_parts(hidden)
                act_ref[here, cols] = (hidden * cdf).astype(BF16)
                gh_ref[here, cols] = (ga_ref[c % 2] * (cdf + hidden * pdf)).astype(BF16)
                grad_ffn = grad_ffn + nt(gh_ref[here, cols], up_ref[:, cols])
            res_ref[...] = residual
            gain_part = jnp.sum(grad_ffn * hat, axis=0, keepdims=True)

            @pl.when(i == 0)
            def _():
                gain_ref[...] = gain_part

            @pl.when(i > 0)
            def _():
                gain_ref[...] += gain_part

            scaled = grad_ffn * gain
            grad_res = cot.astype(F32) + factor * (scaled - hat * jnp.mean(scaled * hat, axis=-1, keepdims=True))
            gres_ref[...] = grad_res
            branch = grad_res.astype(BF16)
            branch_ref[here, :] = branch
            gmt_ref[...] = nt(wo_ref[...], branch)

        @pl.when(i == row_steps)
        def _():
            for copy in leave:
                copy.start()

        @pl.when(i == row_steps + planes - 1)
        def _():
            for copy in leave:
                copy.wait()

        @pl.when(i >= row_steps)
        def _():
            plane = i - row_steps
            cols = part(plane, own_ff)
            all_ref[:, :own_o] = nn(mixedt_ref[...], branch_ref[:, part(plane, own_o)]).astype(BF16)
            all_ref[:, own_o : own_o + own_ff] = nn(ffnt_ref[...], gh_ref[:, cols]).astype(BF16)
            all_ref[:, own_o + own_ff :] = nn(cott_ref[...], act_ref[:, cols]).astype(BF16)
            for chip in range(chips):
                slot = place_ref[0] ^ chip
                keep_ref[slot, 0] = all_ref[part(chip * 2 + place_ref[1], own_rows), :]
                send_ref[slot, 0] = all_ref[part(chip * 2 + 1 - place_ref[1], own_rows), :]

    row = lambda i: jnp.minimum(i, row_steps - 1)
    rows = pl.BlockSpec((size, D), lambda i, _: (row(i), 0))
    blocked = pl.BlockSpec(
        (chips, 1, own_rows, width), lambda i, place_ref: (0, jnp.maximum(i - row_steps, 0) ^ place_ref[2], 0, 0)
    )
    shape = hbm((chips, planes, own_rows, width), BF16)
    return call(
        body,
        (row_steps + planes,),
        [rows, RESIDENT, rows, rows, RESIDENT, whole((2 + H, D))] + [RESIDENT] * len(w),
        [rows, pl.BlockSpec((D, size), lambda i, _: (0, row(i))), whole((1, D)), blocked, blocked, rows]
        + [pl.BlockSpec(memory_space=pl.ANY)] * 2,
        [
            hbm((LEN, D), F32),
            vmem((D, LEN), F32),
            sds((1, D), F32),
            vmem((chips, planes, own_rows, width), BF16),
            shape,
            hbm((LEN, D), F32),
            hbm((LEN, FF), BF16),
            hbm((D, FF), BF16),
        ],
        30e9,
        22e6,
        "feed",
        scratch=[
            pltpu.VMEM((D, D), BF16),
            pltpu.VMEM((D, FF), BF16),
            pltpu.VMEM((D, FF), BF16),
            pltpu.VMEM((LEN, FF), BF16),
            pltpu.VMEM((LEN, FF), BF16),
            pltpu.VMEM((D, LEN), BF16),
            pltpu.VMEM((LEN, D), BF16),
            pltpu.VMEM((2, size, FC), F32),
            pltpu.VMEM((2, size, FC), F32),
            pltpu.VMEM((D, width), BF16),
            pltpu.SemaphoreType.DMA((2,)),
        ],
        trans=LEN * FF * 2,
        prefetch=1,
        vmem=36 * 1024 * 1024,
    )(place, mixed, mixed_t, tokens, cot, cot_t, vectors, *w)


def output_kernel(residual, act, down_t, after):
    size = 2 * TB

    def body(res_ref, act_ref, dt_ref, out_ref):
        out_ref[...] = (res_ref[...] + nt(act_ref[...], dt_ref[...])).astype(BF16)

    rows = lambda width: pl.BlockSpec((size, width), lambda i: (i, 0))
    return call(
        body,
        (LEN // size,),
        [rows(D), rows(FF), whole((D, FF))],
        rows(D),
        hbm((LEN, D), BF16),
        6e9,
        10e6,
        "output",
        after=after,
        vmem=SMALL,
    )(residual, act, down_t)


def prepare_body(gmt_ref, local_ref, fetched_ref, stat_ref, gate_ref, do_ref, df_ref, dot_ref, gl_ref):
    for h in range(2):
        head_rows = slice(h * HD, (h + 1) * HD)
        gm = gmt_ref[head_rows, :]
        local = local_ref[head_rows, :].astype(F32)
        fetched = fetched_ref[head_rows, :].astype(F32)
        gate = gate_ref[0, h : h + 1, :]
        local_inv = stat_ref[0, h : h + 1, :]
        fetched_inv = stat_ref[0, 2 + h : 3 + h, :]
        grad_gate = jnp.sum(gm * (fetched - local), axis=0, keepdims=True)
        gl_ref[0, h : h + 1, :] = grad_gate * gate * (1.0 - gate)
        grad_local = ((1.0 - gate) * gm).astype(BF16).astype(F32)
        grad_fetched = gate * gm
        do_ref[head_rows, :] = (grad_local * local_inv).astype(BF16)
        df_ref[head_rows, :] = (grad_fetched * fetched_inv).astype(BF16)
        dot_ref[0, h : h + 1, :] = jnp.sum(grad_local * local, axis=0, keepdims=True) * local_inv
        dot_ref[0, 2 + h : 3 + h, :] = jnp.sum(grad_fetched * fetched, axis=0, keepdims=True) * fetched_inv


def prepare_kernel(gmt, local, fetched, stat, gate):
    rows = pl.BlockSpec((PAIR, LEN), lambda p: (p, 0))
    few = pl.BlockSpec((1, 8, LEN), lambda p: (p, 0, 0))
    two = pl.BlockSpec((1, 2, LEN), lambda p: (p, 0, 0))
    return call(
        prepare_body,
        (NPAIR,),
        [rows, rows, rows, few, two],
        [rows, rows, few, two],
        [hbm((D, LEN), BF16), hbm((D, LEN), BF16), hbm((NPAIR, 8, LEN), F32), hbm((NPAIR, 2, LEN), F32)],
        4e9,
        8e6,
        "prepare",
        vmem=SMALL,
    )(gmt, local, fetched, stat, gate)


def unattend_body(
    q_ref, kt_ref, v_ref, e0_ref, e1_ref, e2_ref, e3_ref, dol_ref, dfl_ref, dots_ref,
    dq_ref, dk_ref, dv_ref, ds0_ref, ds1_ref, ds2_ref, ds3_ref, do_ref, df_ref, dqt_ref, dk_acc, dv_acc, gp_ref,
):
    e_refs, ds_refs = (e0_ref, e1_ref, e2_ref, e3_ref), (ds0_ref, ds1_ref, ds2_ref, ds3_ref)
    dot_ref = dots_ref.at[0]
    for h in range(2):
        own, other = slice(h * HD, (h + 1) * HD), slice((1 - h) * HD, (2 - h) * HD)
        for to_ref, from_ref in ((do_ref, dol_ref), (df_ref, dfl_ref)):
            to_ref[h, own, :] = from_ref[own, :]
            to_ref[h, other, :] = jnp.zeros((HD, LEN), BF16)

    units = [(tb, h) for h in range(2) for tb in range(NT)]

    def start(u):
        tb, h = units[u]
        near, cols = near_count(tb), slice(tb * TB, (tb + 1) * TB)
        gp_ref[u % 2, :near, :] = nn(v_ref[:near, :], do_ref[h, :, cols])
        gp_ref[u % 2, near : near + BANK, :] = nn(v_ref[FAR, :], df_ref[h, :, cols])

    def rows_part(u):
        tb, h = units[u]
        near, cols = near_count(tb), slice(tb * TB, (tb + 1) * TB)
        head_rows = slice(h * HD, (h + 1) * HD)
        for row in range(0, seen_count(tb), TB):
            some, which = slice(row, row + TB), h if row < near else 2 + h
            gp = gp_ref[u % 2, some, :] - dot_ref[which : which + 1, cols]
            ds_refs[tb][h, some, :] = (e_refs[tb][h, some, :].astype(F32) * gp).astype(BF16)
        dq = nn(kt_ref[head_rows, :near], ds_refs[tb][h, :near, :])
        dq = dq + nn(kt_ref[head_rows, FAR], ds_refs[tb][h, near:, :])
        dqt_ref[head_rows, cols] = dq * (1.0 / math.sqrt(HD))

    def keys_part(h, tb):
        near, cols = near_count(tb), slice(tb * TB, (tb + 1) * TB)
        q_head = head_lanes(q_ref[cols, :], h)
        pieces = (
            (slice(0, near), slice(0, near), do_ref[h, :, cols]),
            (FAR, slice(near, near + BANK), df_ref[h, :, cols]),
        )
        for keys, some, grad_out in pieces:
            dv = nt(e_refs[tb][h, some, :], grad_out)
            dk = nn(ds_refs[tb][h, some, :], q_head)
            if h == 0 and tb == NT - 1:
                dv_acc[keys, :] = dv
                dk_acc[keys, :] = dk
            else:
                dv_acc[keys, :] += dv
                dk_acc[keys, :] += dk

    start(0)
    for u, (tb, h) in enumerate(units):
        if u + 1 < len(units):
            start(u + 1)
        rows_part(u)
        if h == 1:
            keys_part(0, NT - 1 - tb)
    for tb in range(NT):
        keys_part(1, tb)
    dv_ref[...] = dv_acc[...].astype(BF16)
    dk_ref[...] = (dk_acc[...] * (1.0 / LOG2E)).astype(BF16)
    dq_ref[...] = dqt_ref[...].T.astype(BF16)


def unattend_kernel(q, kt, v, e, grad_local, grad_fetched, dots, first, count, after=(), alias=()):
    spec_cols = lambda rows: pl.BlockSpec((rows, PAIR), lambda p: (0, p + first))
    spec_rows = lambda cols: pl.BlockSpec((PAIR, cols), lambda p: (p + first, 0))
    return call(
        unattend_body,
        (count,),
        [
            spec_cols(LEN),
            spec_rows(ROWS),
            spec_cols(ROWS),
            *[pl.BlockSpec((2, seen_count(tb), TB), lambda p: (p + first, 0, 0)) for tb in range(NT)],
            spec_rows(LEN),
            spec_rows(LEN),
            pl.BlockSpec((1, 8, LEN), lambda p: (p + first, 0, 0)),
        ],
        [
            spec_cols(LEN),
            spec_cols(ROWS),
            spec_cols(ROWS),
        ],
        [
            sds((LEN, D), BF16),
            sds((ROWS, D), BF16),
            sds((ROWS, D), BF16),
        ],
        count * 10e9,
        count * 14e6,
        "unattend",
        scratch=[
            *[pltpu.VMEM((2, seen_count(tb), TB), BF16) for tb in range(NT)],
            pltpu.VMEM((2, PAIR, LEN), BF16),
            pltpu.VMEM((2, PAIR, LEN), BF16),
            pltpu.VMEM((PAIR, LEN), F32),
            pltpu.VMEM((ROWS, PAIR), F32),
            pltpu.VMEM((ROWS, PAIR), F32),
            pltpu.VMEM((2, ROWS, TB), F32),
        ],
        after=after,
        alias=alias,
        vmem=36 * 1024 * 1024,
    )(q, kt, v, *e, grad_local, grad_fetched, dots)


def all_heads(gl_ref):
    return jnp.concatenate([gl_ref[p] for p in range(NPAIR)], axis=0).astype(BF16)


def proj_grads_body(xt_ref, dq_ref, dk_ref, dv_ref, gl_ref, g_ref, gate_ref):
    g_ref[0] = nn(xt_ref[:, MEM:CTX], dq_ref[...]).astype(BF16)
    g_ref[1] = nn(xt_ref[...], dk_ref[...]).astype(BF16)
    g_ref[2] = nn(xt_ref[...], dv_ref[...]).astype(BF16)

    @pl.when(pl.program_id(0) == 0)
    def _():
        gate_ref[...] = nt(all_heads(gl_ref), xt_ref[:, MEM:CTX])


def proj_grads_kernel(xt, dq, dk, dv, gl, place=None, chips=0, planes=0, after=()):
    steps = 2
    fast = place is not None
    wide = lambda rows: pl.BlockSpec((rows, D // steps), lambda i, *_: (0, i))
    in_specs = [whole((D, ROWS)), wide(LEN), wide(ROWS), wide(ROWS), whole((NPAIR, 2, LEN))]
    gate_spec, gate_shape = whole((H, D)), sds((H, D), F32)
    flops, nbytes = 8e9, 10e6
    if not fast:
        return call(
            proj_grads_body,
            (steps,),
            in_specs,
            [pl.BlockSpec((3, D, D // steps), lambda i: (0, 0, i)), gate_spec],
            [sds((3, D, D), BF16), gate_shape],
            flops,
            nbytes,
            "proj_grads",
        )(xt, dq, dk, dv, gl)
    own_rows, own_cols, group = D // (2 * chips), D // planes, planes // steps

    def body(place_ref, xt_ref, dq_ref, dk_ref, dv_ref, gl_ref, keep_ref, send_ref, gate_ref, all_ref):
        proj_grads_body(xt_ref, dq_ref, dk_ref, dv_ref, gl_ref, all_ref, gate_ref)
        for b in range(group):
            col = b ^ (place_ref[2] % group)
            cols = slice(b * own_cols, (b + 1) * own_cols)
            for chip in range(chips):
                slot = place_ref[0] ^ chip
                for j in range(3):
                    here = slice(j * own_rows, (j + 1) * own_rows)
                    keep_ref[slot, col, here, :] = all_ref[j, part(chip * 2 + place_ref[1], own_rows), cols]
                    send_ref[slot, col, here, :] = all_ref[j, part(chip * 2 + 1 - place_ref[1], own_rows), cols]

    out = pl.BlockSpec(
        (chips, group, 3 * own_rows, own_cols), lambda i, place_ref: (0, i ^ (place_ref[2] // group), 0, 0)
    )
    shape = sds((chips, planes, 3 * own_rows, own_cols), BF16)
    return call(
        body,
        (steps,),
        in_specs,
        [out, out, gate_spec],
        [shape, shape, gate_shape],
        flops,
        nbytes,
        "proj_grads",
        scratch=[pltpu.VMEM((3, D, D // steps), BF16)],
        prefetch=1,
        after=after,
        vmem=24 * 1024 * 1024,
    )(place, xt, dq, dk, dv, gl)


def input_body(dq_ref, dk_ref, dv_ref, gl_ref, w_ref, tok_ref, mem_ref, vec_ref, gres_ref, gin_ref, gain_ref):
    i = pl.program_id(0)
    gn = nt(dk_ref[...], w_ref[1]) + nt(dv_ref[...], w_ref[2])

    @pl.when(i < MC)
    def _():
        wide = mem_ref[...].astype(F32)
        part = jnp.sum(gn * (wide * rms_factor(wide)), axis=0, keepdims=True)

        @pl.when(i == 0)
        def _():
            gain_ref[...] = part

        @pl.when(i > 0)
        def _():
            gain_ref[...] += part

    @pl.when(i >= MC)
    def _():
        wide = tok_ref[...].astype(F32)
        factor = rms_factor(wide)
        hat = wide * factor
        full = gn + nt(dq_ref[...], w_ref[0]) + tn(all_heads(gl_ref), vec_ref[2:10, :].astype(BF16))
        gain_ref[...] += jnp.sum(full * hat, axis=0, keepdims=True)
        scaled = full * vec_ref[0:1, :]
        gin_ref[...] = (
            gres_ref[...] + factor * (scaled - hat * jnp.mean(scaled * hat, axis=-1, keepdims=True))
        ).astype(BF16)


def input_kernel(dq, dk, dv, gl, w, tokens, memory, vectors, gres, after=()):
    tok = lambda i: jnp.clip(i - MC, 0, NT - 1)
    rows = pl.BlockSpec((TB, D), lambda i: (tok(i), 0))
    return call(
        input_body,
        (MC + NT,),
        [
            rows,
            pl.BlockSpec((TB, D), lambda i: (i, 0)),
            pl.BlockSpec((TB, D), lambda i: (i, 0)),
            pl.BlockSpec((NPAIR, 2, TB), lambda i: (0, 0, tok(i))),
            whole((3, D, D)),
            rows,
            pl.BlockSpec((TB, D), lambda i: (jnp.minimum(i, MC - 1), 0)),
            whole((2 + H, D)),
            rows,
        ],
        [rows, whole((1, D))],
        [sds((LEN, D), BF16), sds((1, D), F32)],
        9e9,
        10e6,
        "input",
        after=after,
        vmem=SMALL,
    )(dq, dk, dv, gl, w, tokens, memory, vectors, gres)


def exchange(slots, axis):
    size = len(slots)
    return [slots[0]] + [
        lax.ppermute(slots[r], axis, [(i, i ^ r) for i in range(size)]) for r in range(1, size)
    ]


def added(parts):
    total = parts[0].astype(F32)
    for other in parts[1:]:
        total = total + other.astype(F32)
    return total


PLANES = (("up",), ("q", "k"), ("v", "o"), ("down",))
EXTRA = 16


def alone(body, operands, out_shape, name, scratch=(), place=None, after=(), flops=2e9, vmem=SMALL, resident=0):
    specs = [RESIDENT if j < resident else whole(x.shape) for j, x in enumerate(operands)]
    if place is not None:
        specs, operands = [SMEM] + specs, (place, *operands)
    return call(
        body,
        (1,),
        specs,
        [whole(x.shape) for x in out_shape],
        out_shape,
        flops,
        2e6,
        name,
        scratch=scratch,
        after=after,
        vmem=vmem,
    )(*operands)


def first_payload(attn_weights):
    rows, cols = attn_weights.shape[1:]

    def body(aw_ref, out_ref):
        for j in range(3):
            out_ref[j * rows : (j + 1) * rows, :] = aw_ref[j].astype(BF16)

    return alone(body, (attn_weights,), [vmem((3 * rows, cols), BF16)], "first_payload", vmem=VMEM_LIMIT)[0]


def second_payloads(place, attn_weights, up_weights, down_weights, attn_moment, up_moment, down_moment, after):
    rows, cols = attn_weights.shape[1:]
    wide = up_weights.shape[1]
    planes = len(PLANES)
    width = cols + 3 * wide

    def body(place_ref, aw_ref, uw_ref, dw_ref, am_ref, um_ref, dm_ref, *rest):
        outs, all_ref = rest[:planes], rest[planes]
        all_ref[...] = jnp.zeros(all_ref.shape, BF16)
        all_ref[0] = um_ref[...].astype(BF16)
        all_ref[3] = dm_ref[...].astype(BF16)
        for j in range(4):
            all_ref[1 + j // 2, :, (j % 2) * cols : (j % 2 + 1) * cols] = am_ref[j].astype(BF16)
        for r in range(planes):
            outs[r][:, :cols] = aw_ref[3].astype(BF16)
            outs[r][:, cols : cols + wide] = uw_ref[...].astype(BF16)
            outs[r][:, cols + wide : cols + 2 * wide] = dw_ref[...].astype(BF16)
            outs[r][:, cols + 2 * wide :] = all_ref[place_ref[2] ^ r]

    return alone(
        body,
        (attn_weights, up_weights, down_weights, attn_moment, up_moment, down_moment),
        [vmem((rows, width), BF16)] * planes,
        "second_payloads",
        scratch=[pltpu.VMEM((planes, rows, wide), BF16)],
        place=place,
        after=after,
        vmem=VMEM_LIMIT,
    )


def stacked_pair(parts, width):
    rows = parts[0].shape[0]
    other = parts[0].shape[1] - width

    def body(*refs):
        for r in range(len(parts)):
            refs[-2][r] = refs[r][:, :width]
            refs[-1][r] = refs[r][:, width:]

    shapes = [sds((len(parts), rows, width), BF16), sds((len(parts), rows, other), BF16)]
    return alone(body, parts, shapes, "stacked_pair", resident=len(parts))


def stacked(parts, after=()):
    def body(*refs):
        for r in range(len(parts)):
            refs[-1][r] = refs[r][...]

    return alone(body, parts, [sds((len(parts),) + parts[0].shape, parts[0].dtype)], "stacked", after=after, resident=len(parts))[0]


def core_blocks(plane):
    return plane + [exchange([b, b], "core")[1] for b in plane]


def fold_cores(keep, other):
    chips, planes, rows, width = keep.shape

    def body(keep_ref, other_ref, *outs):
        for chip in range(chips):
            outs[chip][...] = added([keep_ref[chip], other_ref[chip]]).astype(BF16)

    spec = pl.BlockSpec((chips, 1, rows, width), lambda i: (0, i, 0, 0))
    return call(
        body,
        (planes,),
        [spec, spec],
        [pl.BlockSpec((1, rows, width), lambda i: (i, 0, 0))] * chips,
        [sds((planes, rows, width), BF16)] * chips,
        4e9,
        7e6,
        "fold_cores",
        vmem=SMALL,
    )(keep, other)


def fold_chips(parts):
    planes, rows, width = parts[0].shape

    def body(*refs):
        for plane in range(planes):
            refs[len(parts) + plane][...] = added([r[plane] for r in refs[: len(parts)]]).astype(BF16)

    return alone(body, parts, [sds((rows, width), BF16)] * planes, "fold_chips", resident=len(parts))


VEC = 2 + H
VEC_ROWS = 128


def put_vectors(ref, first, values):
    high = values.astype(BF16)
    low = (values - high.astype(F32)).astype(BF16)
    ref[first : first + VEC_ROWS, :] = jnp.zeros((VEC_ROWS, 128), BF16)
    for j in range(4):
        lanes = slice(j * 128, (j + 1) * 128)
        ref[first + j * 16 : first + j * 16 + VEC, :] = high[:, lanes]
        ref[first + 64 + j * 16 : first + 64 + j * 16 + VEC, :] = low[:, lanes]


def get_vectors(refs, first):
    pieces = []
    for j in range(4):
        rows = lambda offset: slice(first + offset + j * 16, first + offset + j * 16 + VEC)
        pieces.append(added([r[rows(offset), :] for r in refs for offset in (0, 64)]))
    return jnp.concatenate(pieces, axis=1)


def fold_cores_first(keep, other):
    chips = keep.shape[0]

    def body(keep_ref, other_ref, *outs):
        for chip in range(chips):
            outs[chip][...] = added([keep_ref[chip], other_ref[chip]]).astype(BF16)

    return alone(body, (keep, other), [sds(keep.shape[1:], BF16)] * chips, "fold_cores_first")


def fold_chips_first(parts, gain_attn, gain_ffn, grad_gate):
    planes, rows, width = parts[0].shape
    count = len(parts)

    def body(*refs):
        ins, (ga_ref, gf_ref, gg_ref) = refs[:count], refs[count : count + 3]
        outs, vec_ref = refs[count + 3 : -1], refs[-1]
        vec_ref[0:1, :] = ga_ref[...]
        vec_ref[1:2, :] = gf_ref[...]
        vec_ref[2:VEC, :] = gg_ref[...]
        for plane in range(planes):
            outs[plane][:rows, :] = added([r[plane] for r in ins]).astype(BF16)
            put_vectors(outs[plane], rows, vec_ref[...])

    return alone(
        body,
        (*parts, gain_attn, gain_ffn, grad_gate),
        [sds((rows + VEC_ROWS, width), BF16)] * planes,
        "fold_chips_first",
        resident=count,
        scratch=[pltpu.VMEM((VEC, D), F32)],
    )


def stack_with_vectors(parts, vec, after):
    count, width = len(parts), parts[0].shape[1]
    rows = parts[0].shape[0] - EXTRA

    def body(*refs):
        vec_ref, out_ref = refs[count], refs[count + 1]
        for r in range(count):
            out_ref[r * rows : (r + 1) * rows, :] = refs[r][:rows, :]
        squares = added([r[rows:, :] for r in refs[:count]])
        squares = jnp.sum(squares, axis=0, keepdims=True) + jnp.zeros((EXTRA, width), F32)
        high = squares.astype(BF16).astype(F32)
        middle = (squares - high).astype(BF16).astype(F32)
        row = lax.broadcasted_iota(jnp.int32, (EXTRA, width), 0)
        extra = jnp.where(row == VEC, high, jnp.where(row == VEC + 1, middle, squares - high - middle))
        values = jnp.concatenate([vec_ref[...], jnp.zeros((EXTRA - VEC, width), F32)], axis=0)
        first = values.astype(BF16).astype(F32)
        here = count * rows
        out_ref[here : here + EXTRA, :] = jnp.where(row < VEC, first, extra).astype(BF16)
        out_ref[here + EXTRA :, :] = (values - first).astype(BF16)

    return alone(
        body, (*parts, vec), [sds((count * rows + 2 * EXTRA, width), BF16)], "stack_with_vectors", after=after, resident=count + 1
    )[0]


def owned_kernel(place, parts_a, parts_b):
    planes = len(parts_a)
    size, cols = parts_a[0].shape[0] - VEC_ROWS, parts_a[0].shape[1]
    rows, width = parts_b[0].shape
    wide = (width - cols) // 2

    def body(place_ref, *refs):
        a_refs, b_refs = refs[:planes], refs[planes : 2 * planes]
        ga_ref, gb_ref, vec_ref, *rest = refs[2 * planes :]
        slots, all_ref = rest[:planes], rest[planes]
        ga = added([r[:size, :] for r in a_refs])
        gb = added([r[...] for r in b_refs])
        ga_ref[...] = ga
        gb_ref[...] = gb
        vec_ref[...] = get_vectors(a_refs, size)
        squares = jnp.sum(ga * ga, keepdims=True) + jnp.sum(gb * gb, keepdims=True)
        all_ref[...] = jnp.zeros(all_ref.shape, BF16)
        for j in range(4):
            grad = ga[j * rows : (j + 1) * rows, :] if j < 3 else gb[:, :cols]
            all_ref[1 + j // 2, :, (j % 2) * cols : (j % 2 + 1) * cols] = grad.astype(BF16)
        all_ref[0] = gb[:, cols : cols + wide].astype(BF16)
        all_ref[3] = gb[:, cols + wide :].astype(BF16)
        wide_squares = squares + jnp.zeros((EXTRA, wide), F32)
        row = lax.broadcasted_iota(jnp.int32, (EXTRA, wide), 0)
        high = wide_squares.astype(BF16).astype(F32)
        middle = (wide_squares - high).astype(BF16).astype(F32)
        low = wide_squares - high - middle
        extra = jnp.where(row == 0, high, jnp.where(row == 1, middle, jnp.where(row == 2, low, 0.0))).astype(BF16)
        for r in range(planes):
            slots[r][:rows, :] = all_ref[place_ref[2] ^ r]
            slots[r][rows:, :] = extra

    return alone(
        body,
        (*parts_a, *parts_b),
        [hbm((size, cols), F32), hbm((rows, width), F32), sds((VEC, D), F32)]
        + [sds((rows + EXTRA, wide), BF16)] * planes,
        "owned",
        resident=2 * planes,
        scratch=[pltpu.VMEM((planes, rows, wide), BF16)],
        place=place,
    )


def orthogonal_kernel(place, grads, moments, vectors, vec_moment, after):
    count = len(grads)
    chips = count // 2
    planes, rows, wide = moments[0].shape[1:]
    cols = D // planes
    limit = clip_fraction * math.sqrt(PARAMS)

    def body(place_ref, *refs):
        grad_refs, moment_refs, refs = refs[:count], refs[count : count + 2], refs[count + 2 :]
        vec_ref, vm_ref, norm_ref, vn_ref, vmn_ref = refs[:5]
        outs = refs[5 : 5 + planes]
        low_ref, x_ref, mix_ref, diag_ref, all_ref = refs[5 + planes :]
        pair = (place_ref[2] == 1) | (place_ref[2] == 2)
        own = part(place_ref[0] * 2 + place_ref[1], rows)
        after = planes * rows
        extra = added([r[after : after + EXTRA, :] for r in grad_refs])
        grad_vec = extra[:VEC, :] + added([r[after + EXTRA : after + EXTRA + VEC, :] for r in grad_refs])
        total = jnp.sum(extra[VEC : VEC + 3, 0:1], axis=0, keepdims=True) + jnp.sum(grad_vec * grad_vec, keepdims=True)
        norm = jnp.sqrt(total)
        norm_ref[...] = norm
        clip = limit / jnp.maximum(norm, limit)
        vec_mom = vector_decay * vm_ref[...] + clip * grad_vec
        vmn_ref[...] = vec_mom
        vn_ref[...] = vec_ref[...] - vector_rate * vec_mom

        def momentum(core, chip, plane, lanes):
            b = core * chips + chip
            moment = moment_refs[core][chip, plane, :, lanes].astype(F32)
            grad = grad_refs[b][plane * rows : (plane + 1) * rows, lanes].astype(F32)
            return muon_decay * moment + clip * grad

        def gram_of(start, width):
            half = D // 2
            upper, lower = low_ref[:half, start : start + width], low_ref[half:, start : start + width]
            corner = nt(lower, upper)
            first = jnp.concatenate([nt(upper, upper), corner.T], axis=1)
            return jnp.concatenate([first, jnp.concatenate([corner, nt(lower, lower)], axis=1)], axis=0)

        def mixing(gram):
            eye = lax.broadcasted_iota(jnp.int32, (D, D), 0) == lax.broadcasted_iota(jnp.int32, (D, D), 1)
            low = gram.astype(BF16)
            mix = coef_second * low.astype(F32) + coef_third * nn(low, low)
            diag_ref[...] = coef_first + jnp.sum(jnp.where(eye, mix, 0.0), axis=1, keepdims=True)
            mix_ref[...] = jnp.where(eye, 0.0, mix).astype(BF16)

        def advance(start, width, scale):
            for c in range(start, start + width, D):
                lanes = slice(c, c + D)
                new = diag_ref[...] * x_ref[:, lanes] + nn(mix_ref[...], low_ref[:, lanes])
                if scale is not None:
                    new = new * scale
                x_ref[:, lanes] = new
                low_ref[:, lanes] = new.astype(BF16)

        def first_step(start, width):
            gram = gram_of(start, width)
            eye = lax.broadcasted_iota(jnp.int32, (D, D), 0) == lax.broadcasted_iota(jnp.int32, (D, D), 1)
            scale = 1.0 / (jnp.sqrt(jnp.sum(jnp.where(eye, gram, 0.0), keepdims=True)) + 1e-07)
            mixing(gram * (scale * scale))
            advance(start, width, scale)

        def step(start, width):
            mixing(gram_of(start, width))
            advance(start, width, None)

        def last_step(start, width):
            mix_ref[...] = gram_of(start, width).astype(BF16)
            low = mix_ref[own, :]
            mix = coef_second * low.astype(F32) + coef_third * nn(low, mix_ref[...])
            row = lax.broadcasted_iota(jnp.int32, (rows, D), 0) + (place_ref[0] * 2 + place_ref[1]) * rows
            eye = row == lax.broadcasted_iota(jnp.int32, (rows, D), 1)
            diag = coef_first + jnp.sum(jnp.where(eye, mix, 0.0), axis=1, keepdims=True)
            mix = jnp.where(eye, 0.0, mix).astype(BF16)
            for c in range(start, start + width, D):
                lanes = slice(c, c + D)
                x_ref[own, lanes] = diag * x_ref[own, lanes] + nn(mix, low_ref[:, lanes])

        def iterations(ranges):
            for start, width in ranges:
                first_step(start, width)

            def middle(_, carry):
                for start, width in ranges:
                    step(start, width)
                return carry

            lax.fori_loop(1, NS_ITERS - 1, middle, 0)
            for start, width in ranges:
                last_step(start, width)

        @pl.when(pair)
        def _():
            for core, chip, plane, row, col in each_block(place_ref, chips, planes):
                for j in range(2):
                    new = momentum(core, chip, plane, slice(j * cols, (j + 1) * cols))
                    x_ref[part(row, rows), part(col + j * planes, cols)] = new
                    low_ref[part(row, rows), part(col + j * planes, cols)] = new.astype(BF16)
            iterations([(0, D), (D, D)])
            for plane in range(planes):
                for j in range(2):
                    first = j * D + plane * cols
                    all_ref[plane, :, j * cols : (j + 1) * cols] = x_ref[own, first : first + cols].astype(BF16)

        @pl.when(jnp.logical_not(pair))
        def _():
            for core, chip, plane, row, col in each_block(place_ref, chips, planes):
                new = momentum(core, chip, plane, slice(0, wide))
                x_ref[part(row, rows), part(col, wide)] = new
                low_ref[part(row, rows), part(col, wide)] = new.astype(BF16)
            iterations([(0, FF)])
            for plane in range(planes):
                all_ref[plane] = x_ref[own, plane * wide : (plane + 1) * wide].astype(BF16)

        for r in range(planes):
            outs[r][...] = all_ref[place_ref[2] ^ r]

    return alone(
        body,
        (*grads, *moments, vectors, vec_moment),
        [sds((1, 1), F32), sds((VEC, D), F32), sds((VEC, D), F32)] + [sds((rows, wide), BF16)] * planes,
        "orthogonal",
        scratch=[
            pltpu.VMEM((D, FF), BF16),
            pltpu.VMEM((D, FF), F32),
            pltpu.VMEM((D, D), BF16),
            pltpu.VMEM((D, 1), F32),
            pltpu.VMEM((planes, rows, wide), BF16),
        ],
        place=place,
        after=after,
        flops=18e9,
        vmem=24 * 1024 * 1024,
        resident=count + 2,
    )


def outside(arrays):
    return [pltpu.with_memory_space_constraint(x, pltpu.HBM) for x in arrays]


def moments_kernel(norm, ga, gb, attn_moment, up_moment, down_moment, after):
    rows, cols = attn_moment.shape[1:]
    wide = up_moment.shape[1]
    limit = clip_fraction * math.sqrt(PARAMS)

    def body(norm_ref, ga_ref, gb_ref, am_ref, um_ref, dm_ref, amn_ref, umn_ref, dmn_ref):
        clip = limit / jnp.maximum(norm_ref[...], limit)
        for j in range(4):
            grad = ga_ref[j * rows : (j + 1) * rows, :] if j < 3 else gb_ref[:, :cols]
            amn_ref[j] = muon_decay * am_ref[j] + clip * grad
        umn_ref[...] = muon_decay * um_ref[...] + clip * gb_ref[:, cols : cols + wide]
        dmn_ref[...] = muon_decay * dm_ref[...] + clip * gb_ref[:, cols + wide :]

    moments = (attn_moment, up_moment, down_moment)
    return alone(
        body,
        (norm, *outside((ga, gb, *moments))),
        [sds(x.shape, F32) for x in moments],
        "moments",
        after=after,
    )


def update_kernel(place, slots, attn_weights, up_weights, down_weights):
    planes = len(slots)
    cols = attn_weights.shape[2]
    shape_factor = math.sqrt(max(1.0, FF / D))

    def body(place_ref, *refs):
        slot_refs, (aw_ref, uw_ref, dw_ref, an_ref, un_ref, dn_ref, all_ref) = refs[:planes], refs[planes:]
        for r in range(planes):
            all_ref[place_ref[2] ^ r] = slot_refs[r][...]
        for j in range(4):
            ortho = all_ref[1 + j // 2, :, (j % 2) * cols : (j % 2 + 1) * cols].astype(F32)
            an_ref[j] = aw_ref[j] - muon_rate * ortho
        un_ref[...] = uw_ref[...] - muon_rate * all_ref[0].astype(F32)
        dn_ref[...] = dw_ref[...] - muon_rate * shape_factor * all_ref[3].astype(F32)

    weights = (attn_weights, up_weights, down_weights)
    return alone(
        body,
        (*slots, *outside(weights)),
        [sds(x.shape, F32) for x in weights],
        "update",
        resident=planes,
        scratch=[pltpu.VMEM((planes,) + slots[0].shape, BF16)],
        place=place,
    )


def documents(starts):
    doc = jnp.cumsum(starts).astype(F32)
    return doc.reshape(1, LEN), doc.reshape(LEN, 1)


def plain_tail(sizes, grads, attn_weights, up_weights, down_weights, vectors, attn_moment, up_moment, down_moment, vec_moment):
    dp = ("chip", "core")
    grad_attn, grad_up, grad_down, grad_vectors = grads

    def owned(grad, narrow_dim, dp_dim):
        part_sum = lax.psum_scatter(grad.astype(BF16), "narrow", scatter_dimension=narrow_dim, tiled=True)
        return lax.psum_scatter(part_sum, dp, scatter_dimension=dp_dim, tiled=True).astype(F32)

    owned_attn, owned_up, owned_down = owned(grad_attn, 2, 1), owned(grad_up, 1, 0), owned(grad_down, 0, 1)
    own_squares = jnp.sum(owned_attn * owned_attn) + jnp.sum(owned_up * owned_up) + jnp.sum(owned_down * owned_down)
    vector_sum, square_sum = lax.psum((grad_vectors, own_squares), ("chip", "core", "narrow"))
    grad_norm = jnp.sqrt(square_sum + jnp.sum(vector_sum * vector_sum))
    clip_limit = clip_fraction * math.sqrt(PARAMS)
    clip_factor = clip_limit / jnp.maximum(grad_norm, clip_limit)
    attn_mom_new = muon_decay * attn_moment + clip_factor * owned_attn
    up_mom_new = muon_decay * up_moment + clip_factor * owned_up
    down_mom_new = muon_decay * down_moment + clip_factor * owned_down
    gather = lambda x, dim: lax.all_gather(x.astype(BF16), dp, axis=dim, tiled=True).astype(F32)
    ortho = (gather(attn_mom_new, 1), gather(up_mom_new, 0), gather(down_mom_new, 1))
    ortho_attn, ortho_up, ortho_down = ortho
    for iteration in range(NS_ITERS):
        gram_attn = jnp.einsum("imc,inc->imn", ortho_attn, ortho_attn, precision=highest)
        gram_up = lax.dot_general(ortho_up, ortho_up, (((1,), (1,)), ((), ())), precision=highest)
        gram_down = lax.dot_general(ortho_down, ortho_down, (((0,), (0,)), ((), ())), precision=highest)
        partial_grams = jnp.concatenate([gram_attn, gram_up[None], gram_down[None]], axis=0)
        gram_total = lax.psum(partial_grams.astype(BF16), "narrow").astype(F32)
        if iteration == 0:
            norm_scales = 1.0 / (jnp.sqrt(jnp.trace(gram_total, axis1=1, axis2=2)) + 1e-07)
            ortho_attn = ortho_attn * norm_scales[:4, None, None]
            ortho_up = ortho_up * norm_scales[4]
            ortho_down = ortho_down * norm_scales[5]
            gram_total = gram_total * (norm_scales * norm_scales)[:, None, None]
        once = jnp.einsum("imn,inc->imc", gram_total[:4], ortho_attn, precision=highest)
        twice = jnp.einsum("imn,inc->imc", gram_total[:4], once, precision=highest)
        ortho_attn = coef_first * ortho_attn + coef_second * once + coef_third * twice
        once = jnp.dot(gram_total[4], ortho_up, precision=highest)
        twice = jnp.dot(gram_total[4], once, precision=highest)
        ortho_up = coef_first * ortho_up + coef_second * once + coef_third * twice
        once = jnp.dot(ortho_down, gram_total[5], precision=highest)
        twice = jnp.dot(once, gram_total[5], precision=highest)
        ortho_down = coef_first * ortho_down + coef_second * once + coef_third * twice
    row_share = D // sizes["dp"]
    row_start = lax.axis_index(dp) * row_share
    final_attn = lax.dynamic_slice_in_dim(ortho_attn, row_start, row_share, 1)
    final_up = lax.dynamic_slice_in_dim(ortho_up, row_start, row_share, 0)
    final_down = lax.dynamic_slice_in_dim(ortho_down, row_start, row_share, 1)
    shape_factor = math.sqrt(max(1.0, FF / D))
    vector_mom_new = vector_decay * vec_moment + clip_factor * vector_sum
    return (
        attn_weights - muon_rate * final_attn,
        up_weights - muon_rate * final_up,
        down_weights - muon_rate * shape_factor * final_down,
        attn_mom_new,
        up_mom_new,
        down_mom_new,
        vectors - vector_rate * vector_mom_new,
        vector_mom_new,
        grad_norm,
    )


def per_device(
    sizes,
    tokens, memory, neighbour_bank, starts, neighbours, cotangent,
    attn_weights, up_weights, down_weights, vectors,
    attn_moment, up_moment, down_moment, vector_moment,
):
    memory = memory.reshape(MEM, D)
    bank = neighbour_bank.reshape(BANK, D)
    own = (attn_weights, up_weights, down_weights)
    moments = (attn_moment, up_moment, down_moment)
    chips, planes = sizes["dp"] // 2, sizes["narrow"]
    if planes == len(PLANES) and chips == 4:
        return fast_device(
            chips, planes, tokens, memory, bank, starts, neighbours, cotangent, own, vectors, moments, vector_moment
        )
    full = lambda x, narrow_dim, dp_dim: lax.all_gather(
        lax.all_gather(x.astype(BF16), ("chip", "core"), axis=dp_dim, tiled=True), "narrow", axis=narrow_dim, tiled=True
    )
    attn_full = full(attn_weights, 2, 1)
    second = [attn_full[3], full(up_weights, 1, 0), full(down_weights, 0, 1).T]
    x, xt, cot_t, gate = context_kernel(tokens, memory, bank, cotangent, vectors)
    doc_row, doc_col = documents(starts)
    bias_tok, bias_bank = mask_kernel(doc_row, doc_col, neighbours.T)
    w, q, k, v, qt, kt, vt, qn, kn = project_kernel(x, attn_full[:3])
    e, local, fetched, stat, mixed, mixed_t = attend_kernel(qt, k, vt, qn, kn, bias_tok, bias_bank, doc_row, gate, 0, NPAIR)
    out, act, gh, ffn_t, branch, gres, gmt, gain_ffn = feed_kernel(mixed, tokens, cotangent, vectors, second)
    grad_down_t, grad_up, grad_o = feed_grads_kernel(cot_t, act, ffn_t, gh, mixed_t, branch)
    *back, gl = prepare_kernel(gmt, local, fetched, stat, gate)
    dq, dk, dv = unattend_kernel(q, kt, v, e, *back, 0, NPAIR)
    grad_qkv, grad_gate = proj_grads_kernel(xt, dq, dk, dv, gl)
    grad_in, gain_attn = input_kernel(dq, dk, dv, gl, w, tokens, memory, vectors, gres)
    grad_vectors = jnp.concatenate([gain_attn, gain_ffn, grad_gate], axis=0)
    grads = (jnp.concatenate([grad_qkv, grad_o[None]], axis=0), grad_up, grad_down_t.T, grad_vectors)
    return (out, grad_in) + plain_tail(sizes, grads, *own, vectors, *moments, vector_moment)


def ordered(first, second):
    return lax.optimization_barrier((first, second))[0]


def fast_device(
    chips, planes, tokens, memory, bank, starts, neighbours, cotangent, own, vectors, moments, vector_moment
):
    own, moments = own[:2] + (own[2].T,), moments[:2] + (moments[2].T,)
    place = jnp.stack([lax.axis_index("chip"), lax.axis_index("core"), lax.axis_index("narrow")]).astype(jnp.int32)
    payload = first_payload(own[0])
    payloads = second_payloads(place, *own, *moments, after=[payload])
    near_a = exchange([payload] * planes, "narrow")
    doc_row, doc_col = documents(starts)
    near_t = ordered(neighbours.T, payload)
    near_b = exchange(ordered(payloads, near_a), "narrow")
    column_a = stacked(near_a)
    plane_a = exchange([column_a] * chips, "chip")
    x, xt, cot_t, gate = context_kernel(tokens, memory, bank, cotangent, vectors, after=[column_a])
    bias_tok, bias_bank = mask_kernel(doc_row, doc_col, near_t, after=[x])
    first = core_blocks(ordered(plane_a, bias_tok))
    column_b, column_m = stacked_pair(ordered(near_b, first), payloads[0].shape[1] - own[1].shape[1])
    w, q, k, v, qt, kt, vt, qn, kn = project_kernel(x, first, place, after=[column_b])
    plane_b = exchange([column_b] * chips, "chip")
    e, local, fetched, stat, mixed, mixed_t = attend_kernel(qt, k, vt, qn, kn, bias_tok, bias_bank, doc_row, gate, 0, NPAIR)
    own_b = exchange([column_b, column_b], "core")[1]
    late_b = ordered(plane_b[1:], mixed)
    second = [column_b, *late_b, own_b] + [exchange([b, b], "core")[1] for b in late_b]
    gres, gmt, gain_ffn, keep_b, send_b, residual, act, down_t = feed_blocks(
        mixed, mixed_t, tokens, cotangent, cot_t, vectors, second, place
    )
    q, kt, xt = outside((q, kt, xt))
    *back, gl = prepare_kernel(gmt, local, fetched, stat, gate)
    other_b = ordered(exchange([send_b, send_b], "core")[1], back[0])
    slots_b = fold_cores(keep_b, other_b)
    dq, dk, dv = unattend_kernel(q, kt, v, e, *back, 0, NPAIR, after=[slots_b[0]])
    slots_b = fold_chips(ordered(exchange(slots_b, "chip"), dq))
    keep_a, send_a, grad_gate = proj_grads_kernel(xt, dq, dk, dv, gl, place, chips, planes, after=[slots_b[0]])
    slots_a = fold_cores_first(keep_a, exchange([send_a, send_a], "core")[1])
    grad_in, gain_attn = input_kernel(dq, dk, dv, gl, w, tokens, memory, vectors, gres, after=[slots_a[0]])
    parts_a = exchange(slots_a, "chip")
    parts_b = exchange([slots_b[0], ordered(slots_b[1], grad_in), *slots_b[2:]], "narrow")
    parts_a = ordered(parts_a, grad_in)
    slots_a = fold_chips_first(parts_a, gain_attn, gain_ffn, grad_gate)
    plane_m = exchange([ordered(column_m, slots_a[0])] * chips, "chip")
    parts_a = exchange(slots_a, "narrow")
    whole_m = stacked(plane_m)
    all_m = exchange([whole_m, whole_m], "core")
    ga, gb, vec, *slots = owned_kernel(place, parts_a, parts_b)
    column_g = stack_with_vectors(exchange(slots, "narrow"), vec, after=[whole_m])
    plane_g = exchange([column_g] * chips, "chip")
    out = output_kernel(*outside((residual, act, down_t)), after=[column_g])
    grads = core_blocks(ordered(plane_g, out))
    norm, vec_new, vec_mom, *slots = orthogonal_kernel(place, grads, all_m, vectors, vector_moment, [])
    final = exchange(slots, "narrow")
    attn_mom, up_mom, down_mom = moments_kernel(norm, ga, gb, *moments, after=[slots[0]])
    attn_new, up_new, down_new = update_kernel(place, ordered(final, attn_mom), *own)
    new = (attn_new, up_new, down_new.T, attn_mom, up_mom, down_mom.T)
    return (out, grad_in, *new, vec_new, vec_mom, norm.reshape(()))


def solution(mesh):
    sizes = dict(mesh.shape)
    split = Mesh(
        mesh.devices.reshape(sizes["dp"] // 2, 2, sizes["narrow"]), ("chip", "core", "narrow")
    )
    dp = ("chip", "core")
    rows = ("chip", "core", "narrow")
    weights = (P(None, dp, "narrow"), P(dp, "narrow"), P("narrow", dp))
    return jax.shard_map(
        lambda *operands: per_device(sizes, *operands),
        mesh=split,
        in_specs=(P(rows, None), P(rows, None, None), P(rows, None, None), P(rows), P(rows, None), P(rows, None))
        + weights + (P(),) + weights + (P(),),
        out_specs=(P(rows, None), P(rows, None)) + weights + weights + (P(), P(), P()),
        check_vma=False,
    )
```

```python
import math

import jax
import jax.numpy as jnp
from jax import lax
from jax.experimental import pallas as pl
from jax.experimental.pallas import tpu as pltpu
from jax.sharding import Mesh, PartitionSpec as P

D = 512
H = 8
FF = 2048
MEM = 512
BANK = 512
KNB = 4
LEN = 1024
CTX = MEM + LEN
ROWS = CTX + BANK
HD = D // H
TB = 256
NT = LEN // TB
MC = MEM // TB
BC = BANK // TB
PAIR = 2 * HD
NPAIR = D // PAIR
F32 = jnp.float32
BF16 = jnp.bfloat16
NS_ITERS = 5
PARAMS = 3150848
epsilon = 1e-06
masked_score = -1e30
coef_first = 3.4445
coef_second = -4.775
coef_third = 2.0315
clip_fraction = 0.05
muon_rate = 0.5
muon_decay = 0.5
vector_rate = 0.5
vector_decay = 0.9
highest = lax.Precision.HIGHEST
LOG2E = 1.4426950408889634
SAFE = 80.0
VMEM_LIMIT = 60 * 1024 * 1024
SMALL = 16 * 1024 * 1024


def nn(a, b):
    return lax.dot_general(a, b, (((1,), (0,)), ((), ())), preferred_element_type=F32)


def nt(a, b):
    return lax.dot_general(a, b, (((1,), (1,)), ((), ())), preferred_element_type=F32)


def tn(a, b):
    return lax.dot_general(a, b, (((0,), (0,)), ((), ())), preferred_element_type=F32)


def rms_factor(values):
    return lax.rsqrt(jnp.mean(values * values, axis=-1, keepdims=True) + epsilon)


def whole(shape):
    return pl.BlockSpec(shape, lambda *_: (0,) * len(shape))


def call(
    body, grid, in_specs, out_specs, out_shape, flops, nbytes, name, scratch=(), trans=0, prefetch=0, after=(), alias=(),
    vmem=VMEM_LIMIT,
):
    extra, given = len(after) + len(alias), prefetch + len(in_specs)

    def with_extra(*refs):
        body(*refs[:given], *refs[given + extra :])

    made = pl.pallas_call(
        with_extra,
        grid_spec=pltpu.PrefetchScalarGridSpec(
            num_scalar_prefetch=prefetch,
            grid=grid,
            in_specs=list(in_specs) + [pl.BlockSpec(memory_space=pl.ANY)] * extra,
            out_specs=out_specs,
            scratch_shapes=list(scratch),
        ),
        out_shape=out_shape,
        input_output_aliases={given + len(after) + j: j for j in range(len(alias))},
        name=name,
        cost_estimate=pl.CostEstimate(flops=int(flops), bytes_accessed=int(nbytes), transcendentals=int(trans)),
        compiler_params=pltpu.CompilerParams(
            vmem_limit_bytes=vmem, dimension_semantics=("arbitrary",) * len(grid)
        ),
    )
    return lambda *operands: made(*operands, *after, *alias)


SMEM = pl.BlockSpec(memory_space=pltpu.SMEM)


def sds(shape, dtype):
    return jax.ShapeDtypeStruct(shape, dtype)


def hbm(shape, dtype):
    return pltpu.HBM(shape, dtype)


def vmem(shape, dtype):
    return pltpu.VMEM(shape, dtype)


RESIDENT = pl.BlockSpec(memory_space=pltpu.VMEM)


def context_body(tok_ref, mem_ref, bank_ref, cot_ref, vec_ref, x_ref, xt_ref, cott_ref, gate_ref):
    i = pl.program_id(0)
    gain = vec_ref[0:1, :]

    def put(rows):
        x_ref[...] = rows
        xt_ref[...] = rows.T

    def norm(values):
        wide = values.astype(F32)
        return (wide * rms_factor(wide) * gain).astype(BF16)

    @pl.when(i < MC)
    def _():
        put(norm(mem_ref[...]))

    @pl.when((i >= MC) & (i < MC + NT))
    def _():
        rows = norm(tok_ref[...])
        put(rows)
        logits = nt(vec_ref[2:10, :].astype(BF16), rows)
        gate = jax.nn.sigmoid(logits)
        for p in range(NPAIR):
            gate_ref[p] = gate[2 * p : 2 * p + 2, :]
        cott_ref[...] = cot_ref[...].T

    @pl.when(i >= MC + NT)
    def _():
        put(bank_ref[...])


def context_kernel(tokens, memory, bank, cot, vectors, after=()):
    steps = MC + NT + BC
    clip_tok = lambda i: jnp.clip(i - MC, 0, NT - 1)
    return call(
        context_body,
        (steps,),
        [
            pl.BlockSpec((TB, D), lambda i: (clip_tok(i), 0)),
            pl.BlockSpec((TB, D), lambda i: (jnp.minimum(i, MC - 1), 0)),
            pl.BlockSpec((TB, D), lambda i: (jnp.clip(i - MC - NT, 0, BC - 1), 0)),
            pl.BlockSpec((TB, D), lambda i: (clip_tok(i), 0)),
            whole((2 + H, D)),
        ],
        [
            pl.BlockSpec((TB, D), lambda i: (i, 0)),
            pl.BlockSpec((D, TB), lambda i: (0, i)),
            pl.BlockSpec((D, TB), lambda i: (0, clip_tok(i))),
            pl.BlockSpec((NPAIR, 2, TB), lambda i: (0, 0, clip_tok(i))),
        ],
        [sds((ROWS, D), BF16), hbm((D, ROWS), BF16), sds((D, LEN), BF16), hbm((NPAIR, 2, LEN), F32)],
        8e9,
        8e6,
        "context",
        after=after,
        vmem=SMALL,
    )(tokens, memory, bank, cot, vectors)


def mask_body(doc_row_ref, doc_col_ref, near_ref, tok_ref, bank_ref):
    i = pl.program_id(0)
    doc_row = doc_row_ref[...]

    @pl.when(i < NT)
    def _():
        keys = lax.broadcasted_iota(jnp.int32, (TB, LEN), 0) + i * TB
        rows = lax.broadcasted_iota(jnp.int32, (TB, LEN), 1)
        seen = (keys <= rows) & (doc_col_ref[...] == doc_row)
        tok_ref[...] = jnp.where(seen, 0.0, masked_score)

    @pl.when(i >= NT)
    def _():
        keys = lax.broadcasted_iota(jnp.int32, (TB, LEN), 0) + (i - NT) * TB
        count = jnp.zeros((TB, LEN), F32)
        for j in range(KNB):
            count = count + jnp.where(near_ref[j : j + 1, :] == keys, 1.0, 0.0)
        bias = jnp.where(count > 0.5, 0.0, masked_score)
        for j in range(2, KNB + 1):
            bias = jnp.where(count > j - 0.5, math.log2(j), bias)
        bank_ref[...] = bias


def mask_kernel(doc_row, doc_col, near_t, after=()):
    return call(
        mask_body,
        (NT + BC,),
        [
            whole((1, LEN)),
            pl.BlockSpec((TB, 1), lambda i: (jnp.minimum(i, NT - 1), 0)),
            whole((KNB, LEN)),
        ],
        [
            pl.BlockSpec((TB, LEN), lambda i: (jnp.minimum(i, NT - 1), 0)),
            pl.BlockSpec((TB, LEN), lambda i: (jnp.clip(i - NT, 0, BC - 1), 0)),
        ],
        [vmem((LEN, LEN), F32), vmem((BANK, LEN), F32)],
        6e9,
        7e6,
        "masks",
        after=after,
        vmem=SMALL,
    )(doc_row, doc_col, near_t)


def each_block(place_ref, chips, planes):
    for core in range(2):
        for chip in range(chips):
            row = ((place_ref[0] ^ chip) * 2 + (place_ref[1] ^ core))
            for plane in range(planes):
                yield core, chip, plane, row, place_ref[2] ^ plane


def part(index, size):
    return pl.ds(pl.multiple_of(index * size, size), size)


def head_squares(columns):
    wide = columns.astype(F32)
    return jnp.sum((wide * wide).reshape(H, HD, wide.shape[1]), axis=1)


def project_rows(i, x_ref, w_ref, q_ref, k_ref, v_ref, qt_ref, kt_ref, vt_ref, qn_ref, kn_ref):
    rows = x_ref[...]
    keys = nn(rows, w_ref[1]).astype(BF16)
    values = nn(rows, w_ref[2]).astype(BF16)
    keys_t = keys.T
    k_ref[...] = keys
    v_ref[...] = values
    kt_ref[...] = keys_t
    vt_ref[...] = values.T

    @pl.when(i == 0)
    def _():
        kn_ref[...] = jnp.zeros(kn_ref.shape, F32)
        qn_ref[...] = jnp.zeros(qn_ref.shape, F32)

    kn_ref[...] = jnp.maximum(kn_ref[...], head_squares(keys_t))

    @pl.when((i >= MEM // rows.shape[0]) & (i < CTX // rows.shape[0]))
    def _():
        queries = (nn(rows, w_ref[0]).astype(BF16).astype(F32) * (LOG2E / math.sqrt(HD))).astype(BF16)
        queries_t = queries.T
        q_ref[...] = queries
        qt_ref[...] = queries_t
        qn_ref[...] = jnp.maximum(qn_ref[...], head_squares(queries_t))


def project_kernel(x, w, place=None, after=()):
    rows = 2 * TB
    steps = ROWS // rows
    first_q, last_q = MEM // rows, CTX // rows - 1
    fast = place is not None
    if fast:
        chips, planes = len(w) // 2, w[0].shape[0]
        own_rows, own_cols = w[0].shape[1] // 3, w[0].shape[2]

    def body(*refs):
        i = pl.program_id(0)
        if not fast:
            project_rows(i, *refs)
            return
        place_ref, x_ref, *rest = refs
        blocks, (w_ref, *outs) = rest[: len(w)], rest[len(w) :]

        @pl.when(i == 0)
        def _():
            for core, chip, plane, row, col in each_block(place_ref, chips, planes):
                for j in range(3):
                    w_ref[j, part(row, own_rows), part(col, own_cols)] = blocks[core * chips + chip][
                        plane, j * own_rows : (j + 1) * own_rows, :
                    ]

        project_rows(i, x_ref, w_ref, *outs)

    out_specs = [
        pl.BlockSpec((rows, D), lambda i: (jnp.clip(i, first_q, last_q) - first_q, 0)),
        pl.BlockSpec((rows, D), lambda i: (i, 0)),
        pl.BlockSpec((rows, D), lambda i: (i, 0)),
        pl.BlockSpec((D, rows), lambda i: (0, jnp.clip(i, first_q, last_q) - first_q)),
        pl.BlockSpec((D, rows), lambda i: (0, i)),
        pl.BlockSpec((D, rows), lambda i: (0, i)),
        whole((H, rows)),
        whole((H, rows)),
    ]
    out_shape = [
        hbm((LEN, D), BF16),
        vmem((ROWS, D), BF16),
        vmem((ROWS, D), BF16),
        vmem((D, LEN), BF16),
        hbm((D, ROWS), BF16),
        vmem((D, ROWS), BF16),
        sds((H, rows), F32),
        sds((H, rows), F32),
    ]
    in_specs = [pl.BlockSpec((rows, D), lambda i: (i, 0))]
    if fast:
        in_specs = [SMEM] + in_specs + [RESIDENT] * len(w)
        out_specs = [whole((3, D, D))] + out_specs
        out_shape = [hbm((3, D, D), BF16)] + out_shape
        operands = (place, x, *w)
    else:
        in_specs = in_specs + [whole((3, D, D))]
        operands = (x, w)
    result = call(
        body, (steps,), in_specs, out_specs, out_shape, 11e9, 14e6, "project", after=after, vmem=24 * 1024 * 1024
    )(*operands)
    return result if fast else [w, *result]


def head_lanes(values, h):
    lanes = lax.broadcasted_iota(jnp.int32, values.shape, 1)
    keep = (lanes < HD) if h == 0 else (lanes >= HD)
    return jnp.where(keep, values, jnp.zeros_like(values))


def near_count(tb):
    return MEM + (tb + 1) * TB


def seen_count(tb):
    return near_count(tb) + BANK


FAR = slice(CTX, ROWS)


def head_rows_of(values, h):
    zeros = jnp.zeros((HD, values.shape[1]), values.dtype)
    own = values[h * HD : (h + 1) * HD, :]
    return jnp.concatenate([own, zeros] if h == 0 else [zeros, own], axis=0)


def attend_body(
    qt_ref, k_ref, vt_ref, tok_ref, bank_ref, doc_ref, gate_ref, qn_ref, kn_ref,
    e0_ref, e1_ref, e2_ref, e3_ref, local_ref, fetched_ref, stat_ref, mixed_ref, mixedt_ref, s_ref,
):
    e_refs = (e0_ref, e1_ref, e2_ref, e3_ref)
    units = [(tb, h) for tb in range(NT) for h in range(2)]

    def start(u):
        tb, h = units[u]
        near = near_count(tb)
        q_head = head_rows_of(qt_ref[:, tb * TB : (tb + 1) * TB], h)
        s_ref[u % 2, :near, :] = nn(k_ref[:near, :], q_head)
        s_ref[u % 2, near : near + BANK, :] = nn(k_ref[FAR, :], q_head)

    def biased(u, row, cols, mem_bias):
        s = s_ref[u % 2, row : row + TB, :]
        near = near_count(units[u][0])
        if row < MEM:
            return s + mem_bias
        if row < near:
            return s + tok_ref[row - MEM : row - MEM + TB, cols]
        return s + bank_ref[row - near : row - near + TB, cols]

    def soft(u, first, last, cols, mem_bias, general):
        tb, h = units[u]
        top = None
        if general:
            peak = jnp.full((8, TB), -3e38, F32)
            for row in range(first, last, TB):
                s = biased(u, row, cols, mem_bias)
                peak = jnp.maximum(peak, jnp.max(s.reshape(TB // 8, 8, TB), axis=0))
            top = jnp.max(peak, axis=0, keepdims=True)
        total = jnp.zeros((8, TB), F32)
        for row in range(first, last, TB):
            s = biased(u, row, cols, mem_bias)
            e = jnp.exp2(s - top if general else s)
            e_refs[tb][h, row : row + TB, :] = e.astype(BF16)
            total = total + jnp.sum(e.reshape(TB // 8, 8, TB), axis=0)
        return 1.0 / jnp.sum(total, axis=0, keepdims=True)

    def run(general):
        start(0)
        mixed_parts = []
        for u, (tb, h) in enumerate(units):
            cols = slice(tb * TB, (tb + 1) * TB)
            head_rows = slice(h * HD, (h + 1) * HD)
            near, seen = near_count(tb), seen_count(tb)
            if u + 1 < len(units):
                start(u + 1)
            mem_bias = jnp.where(doc_ref[:, cols] == 0.0, 0.0, masked_score)
            local_inv = soft(u, 0, near, cols, mem_bias, general)
            fetched_inv = soft(u, near, seen, cols, mem_bias, general)
            local = nn(vt_ref[head_rows, :near], e_refs[tb][h, :near, :]) * local_inv
            fetched = nn(vt_ref[head_rows, FAR], e_refs[tb][h, near:, :]) * fetched_inv
            local_ref[head_rows, cols] = local.astype(BF16)
            fetched_ref[head_rows, cols] = fetched.astype(BF16)
            stat_ref[0, h : h + 1, cols] = local_inv
            stat_ref[0, 2 + h : 3 + h, cols] = fetched_inv
            gate = gate_ref[0, h : h + 1, cols]
            mixed_parts.append((1.0 - gate) * local + gate * fetched)
            if h == 1:
                mixed = jnp.concatenate(mixed_parts, axis=0)
                mixed_parts = []
                mixedt_ref[:, cols] = mixed.astype(BF16)
                mixed_ref[cols, :] = mixed.T.astype(BF16)

    bound = jnp.max(jnp.max(qn_ref[...], axis=1, keepdims=True) * jnp.max(kn_ref[...], axis=1, keepdims=True))

    @pl.when(bound <= SAFE * SAFE)
    def _():
        run(False)

    @pl.when(jnp.logical_not(bound <= SAFE * SAFE))
    def _():
        run(True)


def attend_kernel(qt, k, vt, qn, kn, bias_tok, bias_bank, doc_row, gate, first, count):
    spec_cols = lambda rows: pl.BlockSpec((rows, PAIR), lambda p: (0, p + first))
    spec_rows = lambda cols: pl.BlockSpec((PAIR, cols), lambda p: (p + first, 0))
    *e, local, fetched, stat, mixed, mixed_t = call(
        attend_body,
        (count,),
        [
            spec_rows(LEN),
            spec_cols(ROWS),
            spec_rows(ROWS),
            RESIDENT,
            RESIDENT,
            whole((1, LEN)),
            pl.BlockSpec((1, 2, LEN), lambda p: (p + first, 0, 0)),
            whole(qn.shape),
            whole(kn.shape),
        ],
        [
            *[pl.BlockSpec((2, seen_count(tb), TB), lambda p: (p, 0, 0)) for tb in range(NT)],
            pl.BlockSpec((PAIR, LEN), lambda p: (p, 0)),
            pl.BlockSpec((PAIR, LEN), lambda p: (p, 0)),
            pl.BlockSpec((1, 8, LEN), lambda p: (p, 0, 0)),
            pl.BlockSpec((LEN, PAIR), lambda p: (0, p)),
            pl.BlockSpec((PAIR, LEN), lambda p: (p, 0)),
        ],
        [
            *[hbm((2 * count, seen_count(tb), TB), BF16) for tb in range(NT)],
            hbm((PAIR * count, LEN), BF16),
            hbm((PAIR * count, LEN), BF16),
            hbm((count, 8, LEN), F32),
            vmem((LEN, PAIR * count), BF16),
            vmem((PAIR * count, LEN), BF16),
        ],
        count * 5e9,
        count * 14e6 + 6e6,
        "attend",
        scratch=[pltpu.VMEM((2, ROWS, TB), F32)],
        trans=count * 2 * ROWS * LEN,
        vmem=28 * 1024 * 1024,
    )(qt, k, vt, bias_tok, bias_bank, doc_row, gate, qn, kn)
    return e, local, fetched, stat, mixed, mixed_t


def gelu_parts(x):
    square = jnp.exp2(x * x * (-0.5 * LOG2E))
    t = 1.0 / (1.0 + (0.3275911 * 0.7071067811865476) * jnp.abs(x))
    poly = t * (
        0.127414796 + t * (-0.142248368 + t * (0.7107068705 + t * (-0.7265760135 + t * 0.5307027145)))
    )
    tail = poly * square
    cdf = jnp.where(x >= 0.0, 1.0 - tail, tail)
    return cdf, square * 0.3989422804014327


FC = 512


def feed_body(
    mixed_ref, tok_ref, cot_ref, wo_ref, up_ref, dt_ref, vec_ref,
    out_ref, act_ref, gh_ref, ffnt_ref, branch_ref, gres_ref, gmt_ref, gain_ref,
):
    i = pl.program_id(0)
    residual = tok_ref[...].astype(F32) + nn(mixed_ref[...], wo_ref[...])
    factor = rms_factor(residual)
    hat = residual * factor
    gain = vec_ref[1:2, :]
    ffn = (hat * gain).astype(BF16)
    ffnt_ref[...] = ffn.T
    cot = cot_ref[...]
    out = residual
    grad_ffn = jnp.zeros(residual.shape, F32)
    for c in range(FF // FC):
        cols = slice(c * FC, (c + 1) * FC)
        hidden = nn(ffn, up_ref[:, cols])
        cdf, pdf = gelu_parts(hidden)
        act = (hidden * cdf).astype(BF16)
        act_ref[:, cols] = act
        grad_act = nn(cot, dt_ref[:, cols])
        gh = (grad_act * (cdf + hidden * pdf)).astype(BF16)
        gh_ref[:, cols] = gh
        out = out + nt(act, dt_ref[:, cols])
        grad_ffn = grad_ffn + nt(gh, up_ref[:, cols])
    out_ref[...] = out.astype(BF16)
    part = jnp.sum(grad_ffn * hat, axis=0, keepdims=True)

    @pl.when(i == 0)
    def _():
        gain_ref[...] = part

    @pl.when(i > 0)
    def _():
        gain_ref[...] += part

    scaled = grad_ffn * gain
    grad_res = cot.astype(F32) + factor * (scaled - hat * jnp.mean(scaled * hat, axis=-1, keepdims=True))
    gres_ref[...] = grad_res
    branch = grad_res.astype(BF16)
    branch_ref[...] = branch
    gmt_ref[...] = nt(wo_ref[...], branch)


def feed_kernel(mixed, tokens, cot, vectors, w):
    rows = lambda width: pl.BlockSpec((TB, width), lambda i: (i, 0))
    cols = lambda height: pl.BlockSpec((height, TB), lambda i: (0, i))

    def body(mixed_ref, tok_ref, cot_ref, vec_ref, wo_ref, up_ref, dt_ref, *outs):
        feed_body(mixed_ref, tok_ref, cot_ref, wo_ref, up_ref, dt_ref, vec_ref, *outs)

    return call(
        body,
        (NT,),
        [rows(D), rows(D), rows(D), whole((2 + H, D))] + [whole(x.shape) for x in w],
        [rows(D), rows(FF), rows(FF), cols(D), rows(D), rows(D), cols(D), whole((1, D))],
        [
            sds((LEN, D), BF16),
            sds((LEN, FF), BF16),
            sds((LEN, FF), BF16),
            sds((D, LEN), BF16),
            sds((LEN, D), BF16),
            sds((LEN, D), F32),
            sds((D, LEN), F32),
            sds((1, D), F32),
        ],
        23e9,
        22e6,
        "feed",
        trans=LEN * FF * 2,
    )(mixed, tokens, cot, vectors, *w)


def feed_grads_body(cott_ref, act_ref, ffnt_ref, gh_ref, mixedt_ref, branch_ref, gd_ref, gu_ref, go_ref):
    gd_ref[...] = nn(cott_ref[...], act_ref[...]).astype(BF16)
    gu_ref[...] = nn(ffnt_ref[...], gh_ref[...]).astype(BF16)
    go_ref[...] = nn(mixedt_ref[...], branch_ref[...]).astype(BF16)


def feed_grads_kernel(cot_t, act, ffn_t, gh, mixed_t, branch):
    steps = 4
    wide = lambda width: pl.BlockSpec((LEN, width // steps), lambda i: (0, i))
    out = lambda width: pl.BlockSpec((D, width // steps), lambda i: (0, i))
    return call(
        feed_grads_body,
        (steps,),
        [whole((D, LEN)), wide(FF), whole((D, LEN)), wide(FF), whole((D, LEN)), wide(D)],
        [out(FF), out(FF), out(D)],
        [sds((D, FF), BF16), sds((D, FF), BF16), sds((D, D), BF16)],
        11e9,
        17e6,
        "feed_grads",
    )(cot_t, act, ffn_t, gh, mixed_t, branch)


def feed_blocks(mixed, mixed_t, tokens, cot, cot_t, vectors, w, place):
    chips, planes = len(w) // 2, w[0].shape[0]
    own_rows, own_o, own_ff = w[0].shape[1], D // planes, FF // planes
    width = own_o + 2 * own_ff
    size = 2 * TB
    row_steps = LEN // size

    def body(place_ref, mixed_ref, mixedt_ref, tok_ref, cot_ref, cott_ref, vec_ref, *rest):
        blocks, rest = rest[: len(w)], rest[len(w) :]
        gres_ref, gmt_ref, gain_ref, keep_ref, send_ref, res_ref, act_out, dt_out = rest[:8]
        wo_ref, up_ref, dt_ref, act_ref, gh_ref, ffnt_ref, branch_ref, hid_ref, ga_ref, all_ref, sems = rest[8:]
        i = pl.program_id(0)
        leave = (pltpu.make_async_copy(act_ref, act_out, sems.at[0]), pltpu.make_async_copy(dt_ref, dt_out, sems.at[1]))

        @pl.when(i == 0)
        def _():
            for core, chip, plane, row, col in each_block(place_ref, chips, planes):
                block = blocks[core * chips + chip]
                here = part(row, own_rows)
                wo_ref[here, part(col, own_o)] = block[plane, :, :own_o]
                up_ref[here, part(col, own_ff)] = block[plane, :, own_o : own_o + own_ff]
                dt_ref[here, part(col, own_ff)] = block[plane, :, own_o + own_ff :]

        @pl.when(i < row_steps)
        def _():
            here = part(i, size)
            residual = tok_ref[...].astype(F32) + nn(mixed_ref[...], wo_ref[...])
            factor = rms_factor(residual)
            hat = residual * factor
            gain = vec_ref[1:2, :]
            ffn = (hat * gain).astype(BF16)
            ffnt_ref[:, here] = ffn.T
            cot = cot_ref[...]

            def start(c):
                cols = slice(c * FC, (c + 1) * FC)
                hid_ref[c % 2] = nn(ffn, up_ref[:, cols])
                ga_ref[c % 2] = nn(cot, dt_ref[:, cols])

            grad_ffn = jnp.zeros(residual.shape, F32)
            start(0)
            for c in range(FF // FC):
                cols = slice(c * FC, (c + 1) * FC)
                if c + 1 < FF // FC:
                    start(c + 1)
                hidden = hid_ref[c % 2]
                cdf, pdf = gelu_parts(hidden)
                act_ref[here, cols] = (hidden * cdf).astype(BF16)
                gh_ref[here, cols] = (ga_ref[c % 2] * (cdf + hidden * pdf)).astype(BF16)
                grad_ffn = grad_ffn + nt(gh_ref[here, cols], up_ref[:, cols])
            res_ref[...] = residual
            gain_part = jnp.sum(grad_ffn * hat, axis=0, keepdims=True)

            @pl.when(i == 0)
            def _():
                gain_ref[...] = gain_part

            @pl.when(i > 0)
            def _():
                gain_ref[...] += gain_part

            scaled = grad_ffn * gain
            grad_res = cot.astype(F32) + factor * (scaled - hat * jnp.mean(scaled * hat, axis=-1, keepdims=True))
            gres_ref[...] = grad_res
            branch = grad_res.astype(BF16)
            branch_ref[here, :] = branch
            gmt_ref[...] = nt(wo_ref[...], branch)

        @pl.when(i == row_steps)
        def _():
            for copy in leave:
                copy.start()

        @pl.when(i == row_steps + planes - 1)
        def _():
            for copy in leave:
                copy.wait()

        @pl.when(i >= row_steps)
        def _():
            plane = i - row_steps
            cols = part(plane, own_ff)
            all_ref[:, :own_o] = nn(mixedt_ref[...], branch_ref[:, part(plane, own_o)]).astype(BF16)
            all_ref[:, own_o : own_o + own_ff] = nn(ffnt_ref[...], gh_ref[:, cols]).astype(BF16)
            all_ref[:, own_o + own_ff :] = nn(cott_ref[...], act_ref[:, cols]).astype(BF16)
            for chip in range(chips):
                slot = place_ref[0] ^ chip
                keep_ref[slot, 0] = all_ref[part(chip * 2 + place_ref[1], own_rows), :]
                send_ref[slot, 0] = all_ref[part(chip * 2 + 1 - place_ref[1], own_rows), :]

    row = lambda i: jnp.minimum(i, row_steps - 1)
    rows = pl.BlockSpec((size, D), lambda i, _: (row(i), 0))
    blocked = pl.BlockSpec(
        (chips, 1, own_rows, width), lambda i, place_ref: (0, jnp.maximum(i - row_steps, 0) ^ place_ref[2], 0, 0)
    )
    shape = hbm((chips, planes, own_rows, width), BF16)
    return call(
        body,
        (row_steps + planes,),
        [rows, RESIDENT, rows, rows, RESIDENT, whole((2 + H, D))] + [RESIDENT] * len(w),
        [rows, pl.BlockSpec((D, size), lambda i, _: (0, row(i))), whole((1, D)), blocked, blocked, rows]
        + [pl.BlockSpec(memory_space=pl.ANY)] * 2,
        [
            hbm((LEN, D), F32),
            vmem((D, LEN), F32),
            sds((1, D), F32),
            vmem((chips, planes, own_rows, width), BF16),
            shape,
            hbm((LEN, D), F32),
            hbm((LEN, FF), BF16),
            hbm((D, FF), BF16),
        ],
        30e9,
        22e6,
        "feed",
        scratch=[
            pltpu.VMEM((D, D), BF16),
            pltpu.VMEM((D, FF), BF16),
            pltpu.VMEM((D, FF), BF16),
            pltpu.VMEM((LEN, FF), BF16),
            pltpu.VMEM((LEN, FF), BF16),
            pltpu.VMEM((D, LEN), BF16),
            pltpu.VMEM((LEN, D), BF16),
            pltpu.VMEM((2, size, FC), F32),
            pltpu.VMEM((2, size, FC), F32),
            pltpu.VMEM((D, width), BF16),
            pltpu.SemaphoreType.DMA((2,)),
        ],
        trans=LEN * FF * 2,
        prefetch=1,
        vmem=36 * 1024 * 1024,
    )(place, mixed, mixed_t, tokens, cot, cot_t, vectors, *w)


def output_kernel(residual, act, down_t, after):
    size = 2 * TB

    def body(res_ref, act_ref, dt_ref, out_ref):
        out_ref[...] = (res_ref[...] + nt(act_ref[...], dt_ref[...])).astype(BF16)

    rows = lambda width: pl.BlockSpec((size, width), lambda i: (i, 0))
    return call(
        body,
        (LEN // size,),
        [rows(D), rows(FF), whole((D, FF))],
        rows(D),
        hbm((LEN, D), BF16),
        6e9,
        10e6,
        "output",
        after=after,
        vmem=SMALL,
    )(residual, act, down_t)


def prepare_body(gmt_ref, local_ref, fetched_ref, stat_ref, gate_ref, do_ref, df_ref, dot_ref, gl_ref):
    for h in range(2):
        head_rows = slice(h * HD, (h + 1) * HD)
        gm = gmt_ref[head_rows, :]
        local = local_ref[head_rows, :].astype(F32)
        fetched = fetched_ref[head_rows, :].astype(F32)
        gate = gate_ref[0, h : h + 1, :]
        local_inv = stat_ref[0, h : h + 1, :]
        fetched_inv = stat_ref[0, 2 + h : 3 + h, :]
        grad_gate = jnp.sum(gm * (fetched - local), axis=0, keepdims=True)
        gl_ref[0, h : h + 1, :] = grad_gate * gate * (1.0 - gate)
        grad_local = ((1.0 - gate) * gm).astype(BF16).astype(F32)
        grad_fetched = gate * gm
        do_ref[head_rows, :] = (grad_local * local_inv).astype(BF16)
        df_ref[head_rows, :] = (grad_fetched * fetched_inv).astype(BF16)
        dot_ref[0, h : h + 1, :] = jnp.sum(grad_local * local, axis=0, keepdims=True) * local_inv
        dot_ref[0, 2 + h : 3 + h, :] = jnp.sum(grad_fetched * fetched, axis=0, keepdims=True) * fetched_inv


def prepare_kernel(gmt, local, fetched, stat, gate):
    rows = pl.BlockSpec((PAIR, LEN), lambda p: (p, 0))
    few = pl.BlockSpec((1, 8, LEN), lambda p: (p, 0, 0))
    two = pl.BlockSpec((1, 2, LEN), lambda p: (p, 0, 0))
    return call(
        prepare_body,
        (NPAIR,),
        [rows, rows, rows, few, two],
        [rows, rows, few, two],
        [hbm((D, LEN), BF16), hbm((D, LEN), BF16), hbm((NPAIR, 8, LEN), F32), hbm((NPAIR, 2, LEN), F32)],
        4e9,
        8e6,
        "prepare",
        vmem=SMALL,
    )(gmt, local, fetched, stat, gate)


def unattend_body(
    q_ref, kt_ref, v_ref, e0_ref, e1_ref, e2_ref, e3_ref, dol_ref, dfl_ref, dots_ref,
    dq_ref, dk_ref, dv_ref, ds0_ref, ds1_ref, ds2_ref, ds3_ref, do_ref, df_ref, dqt_ref, dk_acc, dv_acc, gp_ref,
):
    e_refs, ds_refs = (e0_ref, e1_ref, e2_ref, e3_ref), (ds0_ref, ds1_ref, ds2_ref, ds3_ref)
    dot_ref = dots_ref.at[0]
    for h in range(2):
        own, other = slice(h * HD, (h + 1) * HD), slice((1 - h) * HD, (2 - h) * HD)
        for to_ref, from_ref in ((do_ref, dol_ref), (df_ref, dfl_ref)):
            to_ref[h, own, :] = from_ref[own, :]
            to_ref[h, other, :] = jnp.zeros((HD, LEN), BF16)

    units = [(tb, h) for h in range(2) for tb in range(NT)]

    def start(u):
        tb, h = units[u]
        near, cols = near_count(tb), slice(tb * TB, (tb + 1) * TB)
        gp_ref[u % 2, :near, :] = nn(v_ref[:near, :], do_ref[h, :, cols])
        gp_ref[u % 2, near : near + BANK, :] = nn(v_ref[FAR, :], df_ref[h, :, cols])

    def rows_part(u):
        tb, h = units[u]
        near, cols = near_count(tb), slice(tb * TB, (tb + 1) * TB)
        head_rows = slice(h * HD, (h + 1) * HD)
        for row in range(0, seen_count(tb), TB):
            some, which = slice(row, row + TB), h if row < near else 2 + h
            gp = gp_ref[u % 2, some, :] - dot_ref[which : which + 1, cols]
            ds_refs[tb][h, some, :] = (e_refs[tb][h, some, :].astype(F32) * gp).astype(BF16)
        dq = nn(kt_ref[head_rows, :near], ds_refs[tb][h, :near, :])
        dq = dq + nn(kt_ref[head_rows, FAR], ds_refs[tb][h, near:, :])
        dqt_ref[head_rows, cols] = dq * (1.0 / math.sqrt(HD))

    def keys_part(h, tb):
        near, cols = near_count(tb), slice(tb * TB, (tb + 1) * TB)
        q_head = head_lanes(q_ref[cols, :], h)
        pieces = (
            (slice(0, near), slice(0, near), do_ref[h, :, cols]),
            (FAR, slice(near, near + BANK), df_ref[h, :, cols]),
        )
        for keys, some, grad_out in pieces:
            dv = nt(e_refs[tb][h, some, :], grad_out)
            dk = nn(ds_refs[tb][h, some, :], q_head)
            if h == 0 and tb == NT - 1:
                dv_acc[keys, :] = dv
                dk_acc[keys, :] = dk
            else:
                dv_acc[keys, :] += dv
                dk_acc[keys, :] += dk

    start(0)
    for u, (tb, h) in enumerate(units):
        if u + 1 < len(units):
            start(u + 1)
        rows_part(u)
        if h == 1:
            keys_part(0, NT - 1 - tb)
    for tb in range(NT):
        keys_part(1, tb)
    dv_ref[...] = dv_acc[...].astype(BF16)
    dk_ref[...] = (dk_acc[...] * (1.0 / LOG2E)).astype(BF16)
    dq_ref[...] = dqt_ref[...].T.astype(BF16)


def unattend_kernel(q, kt, v, e, grad_local, grad_fetched, dots, first, count, after=(), alias=()):
    spec_cols = lambda rows: pl.BlockSpec((rows, PAIR), lambda p: (0, p + first))
    spec_rows = lambda cols: pl.BlockSpec((PAIR, cols), lambda p: (p + first, 0))
    return call(
        unattend_body,
        (count,),
        [
            spec_cols(LEN),
            spec_rows(ROWS),
            spec_cols(ROWS),
            *[pl.BlockSpec((2, seen_count(tb), TB), lambda p: (p + first, 0, 0)) for tb in range(NT)],
            spec_rows(LEN),
            spec_rows(LEN),
            pl.BlockSpec((1, 8, LEN), lambda p: (p + first, 0, 0)),
        ],
        [
            spec_cols(LEN),
            spec_cols(ROWS),
            spec_cols(ROWS),
        ],
        [
            sds((LEN, D), BF16),
            sds((ROWS, D), BF16),
            sds((ROWS, D), BF16),
        ],
        count * 10e9,
        count * 14e6,
        "unattend",
        scratch=[
            *[pltpu.VMEM((2, seen_count(tb), TB), BF16) for tb in range(NT)],
            pltpu.VMEM((2, PAIR, LEN), BF16),
            pltpu.VMEM((2, PAIR, LEN), BF16),
            pltpu.VMEM((PAIR, LEN), F32),
            pltpu.VMEM((ROWS, PAIR), F32),
            pltpu.VMEM((ROWS, PAIR), F32),
            pltpu.VMEM((2, ROWS, TB), F32),
        ],
        after=after,
        alias=alias,
        vmem=36 * 1024 * 1024,
    )(q, kt, v, *e, grad_local, grad_fetched, dots)


def all_heads(gl_ref):
    return jnp.concatenate([gl_ref[p] for p in range(NPAIR)], axis=0).astype(BF16)


def proj_grads_body(xt_ref, dq_ref, dk_ref, dv_ref, gl_ref, g_ref, gate_ref):
    g_ref[0] = nn(xt_ref[:, MEM:CTX], dq_ref[...]).astype(BF16)
    g_ref[1] = nn(xt_ref[...], dk_ref[...]).astype(BF16)
    g_ref[2] = nn(xt_ref[...], dv_ref[...]).astype(BF16)

    @pl.when(pl.program_id(0) == 0)
    def _():
        gate_ref[...] = nt(all_heads(gl_ref), xt_ref[:, MEM:CTX])


def proj_grads_kernel(xt, dq, dk, dv, gl, place=None, chips=0, planes=0, after=()):
    steps = 2
    fast = place is not None
    wide = lambda rows: pl.BlockSpec((rows, D // steps), lambda i, *_: (0, i))
    in_specs = [whole((D, ROWS)), wide(LEN), wide(ROWS), wide(ROWS), whole((NPAIR, 2, LEN))]
    gate_spec, gate_shape = whole((H, D)), sds((H, D), F32)
    flops, nbytes = 8e9, 10e6
    if not fast:
        return call(
            proj_grads_body,
            (steps,),
            in_specs,
            [pl.BlockSpec((3, D, D // steps), lambda i: (0, 0, i)), gate_spec],
            [sds((3, D, D), BF16), gate_shape],
            flops,
            nbytes,
            "proj_grads",
        )(xt, dq, dk, dv, gl)
    own_rows, own_cols, group = D // (2 * chips), D // planes, planes // steps

    def body(place_ref, xt_ref, dq_ref, dk_ref, dv_ref, gl_ref, keep_ref, send_ref, gate_ref, all_ref):
        proj_grads_body(xt_ref, dq_ref, dk_ref, dv_ref, gl_ref, all_ref, gate_ref)
        for b in range(group):
            col = b ^ (place_ref[2] % group)
            cols = slice(b * own_cols, (b + 1) * own_cols)
            for chip in range(chips):
                slot = place_ref[0] ^ chip
                for j in range(3):
                    here = slice(j * own_rows, (j + 1) * own_rows)
                    keep_ref[slot, col, here, :] = all_ref[j, part(chip * 2 + place_ref[1], own_rows), cols]
                    send_ref[slot, col, here, :] = all_ref[j, part(chip * 2 + 1 - place_ref[1], own_rows), cols]

    out = pl.BlockSpec(
        (chips, group, 3 * own_rows, own_cols), lambda i, place_ref: (0, i ^ (place_ref[2] // group), 0, 0)
    )
    shape = sds((chips, planes, 3 * own_rows, own_cols), BF16)
    return call(
        body,
        (steps,),
        in_specs,
        [out, out, gate_spec],
        [shape, shape, gate_shape],
        flops,
        nbytes,
        "proj_grads",
        scratch=[pltpu.VMEM((3, D, D // steps), BF16)],
        prefetch=1,
        after=after,
        vmem=24 * 1024 * 1024,
    )(place, xt, dq, dk, dv, gl)


def input_body(dq_ref, dk_ref, dv_ref, gl_ref, w_ref, tok_ref, mem_ref, vec_ref, gres_ref, gin_ref, gain_ref):
    i = pl.program_id(0)
    gn = nt(dk_ref[...], w_ref[1]) + nt(dv_ref[...], w_ref[2])

    @pl.when(i < MC)
    def _():
        wide = mem_ref[...].astype(F32)
        part = jnp.sum(gn * (wide * rms_factor(wide)), axis=0, keepdims=True)

        @pl.when(i == 0)
        def _():
            gain_ref[...] = part

        @pl.when(i > 0)
        def _():
            gain_ref[...] += part

    @pl.when(i >= MC)
    def _():
        wide = tok_ref[...].astype(F32)
        factor = rms_factor(wide)
        hat = wide * factor
        full = gn + nt(dq_ref[...], w_ref[0]) + tn(all_heads(gl_ref), vec_ref[2:10, :].astype(BF16))
        gain_ref[...] += jnp.sum(full * hat, axis=0, keepdims=True)
        scaled = full * vec_ref[0:1, :]
        gin_ref[...] = (
            gres_ref[...] + factor * (scaled - hat * jnp.mean(scaled * hat, axis=-1, keepdims=True))
        ).astype(BF16)


def input_kernel(dq, dk, dv, gl, w, tokens, memory, vectors, gres, after=()):
    tok = lambda i: jnp.clip(i - MC, 0, NT - 1)
    rows = pl.BlockSpec((TB, D), lambda i: (tok(i), 0))
    return call(
        input_body,
        (MC + NT,),
        [
            rows,
            pl.BlockSpec((TB, D), lambda i: (i, 0)),
            pl.BlockSpec((TB, D), lambda i: (i, 0)),
            pl.BlockSpec((NPAIR, 2, TB), lambda i: (0, 0, tok(i))),
            whole((3, D, D)),
            rows,
            pl.BlockSpec((TB, D), lambda i: (jnp.minimum(i, MC - 1), 0)),
            whole((2 + H, D)),
            rows,
        ],
        [rows, whole((1, D))],
        [sds((LEN, D), BF16), sds((1, D), F32)],
        9e9,
        10e6,
        "input",
        after=after,
        vmem=SMALL,
    )(dq, dk, dv, gl, w, tokens, memory, vectors, gres)


def exchange(slots, axis):
    size = len(slots)
    return [slots[0]] + [
        lax.ppermute(slots[r], axis, [(i, i ^ r) for i in range(size)]) for r in range(1, size)
    ]


def added(parts):
    total = parts[0].astype(F32)
    for other in parts[1:]:
        total = total + other.astype(F32)
    return total


PLANES = (("up",), ("q", "k"), ("v", "o"), ("down",))
EXTRA = 16


def alone(body, operands, out_shape, name, scratch=(), place=None, after=(), flops=2e9, vmem=SMALL, resident=0):
    specs = [RESIDENT if j < resident else whole(x.shape) for j, x in enumerate(operands)]
    if place is not None:
        specs, operands = [SMEM] + specs, (place, *operands)
    return call(
        body,
        (1,),
        specs,
        [whole(x.shape) for x in out_shape],
        out_shape,
        flops,
        2e6,
        name,
        scratch=scratch,
        after=after,
        vmem=vmem,
    )(*operands)


def first_payload(attn_weights):
    rows, cols = attn_weights.shape[1:]

    def body(aw_ref, out_ref):
        for j in range(3):
            out_ref[j * rows : (j + 1) * rows, :] = aw_ref[j].astype(BF16)

    return alone(body, (attn_weights,), [vmem((3 * rows, cols), BF16)], "first_payload", vmem=VMEM_LIMIT)[0]


def second_payloads(place, attn_weights, up_weights, down_weights, attn_moment, up_moment, down_moment, after):
    rows, cols = attn_weights.shape[1:]
    wide = up_weights.shape[1]
    planes = len(PLANES)
    width = cols + 3 * wide

    def body(place_ref, aw_ref, uw_ref, dw_ref, am_ref, um_ref, dm_ref, *rest):
        outs, all_ref = rest[:planes], rest[planes]
        all_ref[...] = jnp.zeros(all_ref.shape, BF16)
        all_ref[0] = um_ref[...].astype(BF16)
        all_ref[3] = dm_ref[...].astype(BF16)
        for j in range(4):
            all_ref[1 + j // 2, :, (j % 2) * cols : (j % 2 + 1) * cols] = am_ref[j].astype(BF16)
        for r in range(planes):
            outs[r][:, :cols] = aw_ref[3].astype(BF16)
            outs[r][:, cols : cols + wide] = uw_ref[...].astype(BF16)
            outs[r][:, cols + wide : cols + 2 * wide] = dw_ref[...].astype(BF16)
            outs[r][:, cols + 2 * wide :] = all_ref[place_ref[2] ^ r]

    return alone(
        body,
        (attn_weights, up_weights, down_weights, attn_moment, up_moment, down_moment),
        [vmem((rows, width), BF16)] * planes,
        "second_payloads",
        scratch=[pltpu.VMEM((planes, rows, wide), BF16)],
        place=place,
        after=after,
        vmem=VMEM_LIMIT,
    )


def stacked_pair(parts, width):
    rows = parts[0].shape[0]
    other = parts[0].shape[1] - width

    def body(*refs):
        for r in range(len(parts)):
            refs[-2][r] = refs[r][:, :width]
            refs[-1][r] = refs[r][:, width:]

    shapes = [sds((len(parts), rows, width), BF16), sds((len(parts), rows, other), BF16)]
    return alone(body, parts, shapes, "stacked_pair", resident=len(parts))


def stacked(parts, after=()):
    def body(*refs):
        for r in range(len(parts)):
            refs[-1][r] = refs[r][...]

    return alone(body, parts, [sds((len(parts),) + parts[0].shape, parts[0].dtype)], "stacked", after=after, resident=len(parts))[0]


def core_blocks(plane):
    return plane + [exchange([b, b], "core")[1] for b in plane]


def fold_cores(keep, other):
    chips, planes, rows, width = keep.shape

    def body(keep_ref, other_ref, *outs):
        for chip in range(chips):
            outs[chip][...] = added([keep_ref[chip], other_ref[chip]]).astype(BF16)

    spec = pl.BlockSpec((chips, 1, rows, width), lambda i: (0, i, 0, 0))
    return call(
        body,
        (planes,),
        [spec, spec],
        [pl.BlockSpec((1, rows, width), lambda i: (i, 0, 0))] * chips,
        [sds((planes, rows, width), BF16)] * chips,
        4e9,
        7e6,
        "fold_cores",
        vmem=SMALL,
    )(keep, other)


def fold_chips(parts):
    planes, rows, width = parts[0].shape

    def body(*refs):
        for plane in range(planes):
            refs[len(parts) + plane][...] = added([r[plane] for r in refs[: len(parts)]]).astype(BF16)

    return alone(body, parts, [sds((rows, width), BF16)] * planes, "fold_chips", resident=len(parts))


VEC = 2 + H
VEC_ROWS = 128


def put_vectors(ref, first, values):
    high = values.astype(BF16)
    low = (values - high.astype(F32)).astype(BF16)
    ref[first : first + VEC_ROWS, :] = jnp.zeros((VEC_ROWS, 128), BF16)
    for j in range(4):
        lanes = slice(j * 128, (j + 1) * 128)
        ref[first + j * 16 : first + j * 16 + VEC, :] = high[:, lanes]
        ref[first + 64 + j * 16 : first + 64 + j * 16 + VEC, :] = low[:, lanes]


def get_vectors(refs, first):
    pieces = []
    for j in range(4):
        rows = lambda offset: slice(first + offset + j * 16, first + offset + j * 16 + VEC)
        pieces.append(added([r[rows(offset), :] for r in refs for offset in (0, 64)]))
    return jnp.concatenate(pieces, axis=1)


def fold_cores_first(keep, other):
    chips = keep.shape[0]

    def body(keep_ref, other_ref, *outs):
        for chip in range(chips):
            outs[chip][...] = added([keep_ref[chip], other_ref[chip]]).astype(BF16)

    return alone(body, (keep, other), [sds(keep.shape[1:], BF16)] * chips, "fold_cores_first")


def fold_chips_first(parts, gain_attn, gain_ffn, grad_gate):
    planes, rows, width = parts[0].shape
    count = len(parts)

    def body(*refs):
        ins, (ga_ref, gf_ref, gg_ref) = refs[:count], refs[count : count + 3]
        outs, vec_ref = refs[count + 3 : -1], refs[-1]
        vec_ref[0:1, :] = ga_ref[...]
        vec_ref[1:2, :] = gf_ref[...]
        vec_ref[2:VEC, :] = gg_ref[...]
        for plane in range(planes):
            outs[plane][:rows, :] = added([r[plane] for r in ins]).astype(BF16)
            put_vectors(outs[plane], rows, vec_ref[...])

    return alone(
        body,
        (*parts, gain_attn, gain_ffn, grad_gate),
        [sds((rows + VEC_ROWS, width), BF16)] * planes,
        "fold_chips_first",
        resident=count,
        scratch=[pltpu.VMEM((VEC, D), F32)],
    )


def stack_with_vectors(parts, vec, after):
    count, width = len(parts), parts[0].shape[1]
    rows = parts[0].shape[0] - EXTRA

    def body(*refs):
        vec_ref, out_ref = refs[count], refs[count + 1]
        for r in range(count):
            out_ref[r * rows : (r + 1) * rows, :] = refs[r][:rows, :]
        squares = added([r[rows:, :] for r in refs[:count]])
        squares = jnp.sum(squares, axis=0, keepdims=True) + jnp.zeros((EXTRA, width), F32)
        high = squares.astype(BF16).astype(F32)
        middle = (squares - high).astype(BF16).astype(F32)
        row = lax.broadcasted_iota(jnp.int32, (EXTRA, width), 0)
        extra = jnp.where(row == VEC, high, jnp.where(row == VEC + 1, middle, squares - high - middle))
        values = jnp.concatenate([vec_ref[...], jnp.zeros((EXTRA - VEC, width), F32)], axis=0)
        first = values.astype(BF16).astype(F32)
        here = count * rows
        out_ref[here : here + EXTRA, :] = jnp.where(row < VEC, first, extra).astype(BF16)
        out_ref[here + EXTRA :, :] = (values - first).astype(BF16)

    return alone(
        body, (*parts, vec), [sds((count * rows + 2 * EXTRA, width), BF16)], "stack_with_vectors", after=after, resident=count + 1
    )[0]


def owned_kernel(place, parts_a, parts_b):
    planes = len(parts_a)
    size, cols = parts_a[0].shape[0] - VEC_ROWS, parts_a[0].shape[1]
    rows, width = parts_b[0].shape
    wide = (width - cols) // 2

    def body(place_ref, *refs):
        a_refs, b_refs = refs[:planes], refs[planes : 2 * planes]
        ga_ref, gb_ref, vec_ref, *rest = refs[2 * planes :]
        slots, all_ref = rest[:planes], rest[planes]
        ga = added([r[:size, :] for r in a_refs])
        gb = added([r[...] for r in b_refs])
        ga_ref[...] = ga
        gb_ref[...] = gb
        vec_ref[...] = get_vectors(a_refs, size)
        squares = jnp.sum(ga * ga, keepdims=True) + jnp.sum(gb * gb, keepdims=True)
        all_ref[...] = jnp.zeros(all_ref.shape, BF16)
        for j in range(4):
            grad = ga[j * rows : (j + 1) * rows, :] if j < 3 else gb[:, :cols]
            all_ref[1 + j // 2, :, (j % 2) * cols : (j % 2 + 1) * cols] = grad.astype(BF16)
        all_ref[0] = gb[:, cols : cols + wide].astype(BF16)
        all_ref[3] = gb[:, cols + wide :].astype(BF16)
        wide_squares = squares + jnp.zeros((EXTRA, wide), F32)
        row = lax.broadcasted_iota(jnp.int32, (EXTRA, wide), 0)
        high = wide_squares.astype(BF16).astype(F32)
        middle = (wide_squares - high).astype(BF16).astype(F32)
        low = wide_squares - high - middle
        extra = jnp.where(row == 0, high, jnp.where(row == 1, middle, jnp.where(row == 2, low, 0.0))).astype(BF16)
        for r in range(planes):
            slots[r][:rows, :] = all_ref[place_ref[2] ^ r]
            slots[r][rows:, :] = extra

    return alone(
        body,
        (*parts_a, *parts_b),
        [hbm((size, cols), F32), hbm((rows, width), F32), sds((VEC, D), F32)]
        + [sds((rows + EXTRA, wide), BF16)] * planes,
        "owned",
        resident=2 * planes,
        scratch=[pltpu.VMEM((planes, rows, wide), BF16)],
        place=place,
    )


def orthogonal_kernel(place, grads, moments, vectors, vec_moment, after):
    count = len(grads)
    chips = count // 2
    planes, rows, wide = moments[0].shape[1:]
    cols = D // planes
    limit = clip_fraction * math.sqrt(PARAMS)

    def body(place_ref, *refs):
        grad_refs, moment_refs, refs = refs[:count], refs[count : count + 2], refs[count + 2 :]
        vec_ref, vm_ref, norm_ref, vn_ref, vmn_ref = refs[:5]
        outs = refs[5 : 5 + planes]
        low_ref, x_ref, mix_ref, diag_ref, all_ref = refs[5 + planes :]
        pair = (place_ref[2] == 1) | (place_ref[2] == 2)
        own = part(place_ref[0] * 2 + place_ref[1], rows)
        after = planes * rows
        extra = added([r[after : after + EXTRA, :] for r in grad_refs])
        grad_vec = extra[:VEC, :] + added([r[after + EXTRA : after + EXTRA + VEC, :] for r in grad_refs])
        total = jnp.sum(extra[VEC : VEC + 3, 0:1], axis=0, keepdims=True) + jnp.sum(grad_vec * grad_vec, keepdims=True)
        norm = jnp.sqrt(total)
        norm_ref[...] = norm
        clip = limit / jnp.maximum(norm, limit)
        vec_mom = vector_decay * vm_ref[...] + clip * grad_vec
        vmn_ref[...] = vec_mom
        vn_ref[...] = vec_ref[...] - vector_rate * vec_mom

        def momentum(core, chip, plane, lanes):
            b = core * chips + chip
            moment = moment_refs[core][chip, plane, :, lanes].astype(F32)
            grad = grad_refs[b][plane * rows : (plane + 1) * rows, lanes].astype(F32)
            return muon_decay * moment + clip * grad

        def gram_of(start, width):
            half = D // 2
            upper, lower = low_ref[:half, start : start + width], low_ref[half:, start : start + width]
            corner = nt(lower, upper)
            first = jnp.concatenate([nt(upper, upper), corner.T], axis=1)
            return jnp.concatenate([first, jnp.concatenate([corner, nt(lower, lower)], axis=1)], axis=0)

        def mixing(gram):
            eye = lax.broadcasted_iota(jnp.int32, (D, D), 0) == lax.broadcasted_iota(jnp.int32, (D, D), 1)
            low = gram.astype(BF16)
            mix = coef_second * low.astype(F32) + coef_third * nn(low, low)
            diag_ref[...] = coef_first + jnp.sum(jnp.where(eye, mix, 0.0), axis=1, keepdims=True)
            mix_ref[...] = jnp.where(eye, 0.0, mix).astype(BF16)

        def advance(start, width, scale):
            for c in range(start, start + width, D):
                lanes = slice(c, c + D)
                new = diag_ref[...] * x_ref[:, lanes] + nn(mix_ref[...], low_ref[:, lanes])
                if scale is not None:
                    new = new * scale
                x_ref[:, lanes] = new
                low_ref[:, lanes] = new.astype(BF16)

        def first_step(start, width):
            gram = gram_of(start, width)
            eye = lax.broadcasted_iota(jnp.int32, (D, D), 0) == lax.broadcasted_iota(jnp.int32, (D, D), 1)
            scale = 1.0 / (jnp.sqrt(jnp.sum(jnp.where(eye, gram, 0.0), keepdims=True)) + 1e-07)
            mixing(gram * (scale * scale))
            advance(start, width, scale)

        def step(start, width):
            mixing(gram_of(start, width))
            advance(start, width, None)

        def last_step(start, width):
            mix_ref[...] = gram_of(start, width).astype(BF16)
            low = mix_ref[own, :]
            mix = coef_second * low.astype(F32) + coef_third * nn(low, mix_ref[...])
            row = lax.broadcasted_iota(jnp.int32, (rows, D), 0) + (place_ref[0] * 2 + place_ref[1]) * rows
            eye = row == lax.broadcasted_iota(jnp.int32, (rows, D), 1)
            diag = coef_first + jnp.sum(jnp.where(eye, mix, 0.0), axis=1, keepdims=True)
            mix = jnp.where(eye, 0.0, mix).astype(BF16)
            for c in range(start, start + width, D):
                lanes = slice(c, c + D)
                x_ref[own, lanes] = diag * x_ref[own, lanes] + nn(mix, low_ref[:, lanes])

        def iterations(ranges):
            for start, width in ranges:
                first_step(start, width)

            def middle(_, carry):
                for start, width in ranges:
                    step(start, width)
                return carry

            lax.fori_loop(1, NS_ITERS - 1, middle, 0)
            for start, width in ranges:
                last_step(start, width)

        @pl.when(pair)
        def _():
            for core, chip, plane, row, col in each_block(place_ref, chips, planes):
                for j in range(2):
                    new = momentum(core, chip, plane, slice(j * cols, (j + 1) * cols))
                    x_ref[part(row, rows), part(col + j * planes, cols)] = new
                    low_ref[part(row, rows), part(col + j * planes, cols)] = new.astype(BF16)
            iterations([(0, D), (D, D)])
            for plane in range(planes):
                for j in range(2):
                    first = j * D + plane * cols
                    all_ref[plane, :, j * cols : (j + 1) * cols] = x_ref[own, first : first + cols].astype(BF16)

        @pl.when(jnp.logical_not(pair))
        def _():
            for core, chip, plane, row, col in each_block(place_ref, chips, planes):
                new = momentum(core, chip, plane, slice(0, wide))
                x_ref[part(row, rows), part(col, wide)] = new
                low_ref[part(row, rows), part(col, wide)] = new.astype(BF16)
            iterations([(0, FF)])
            for plane in range(planes):
                all_ref[plane] = x_ref[own, plane * wide : (plane + 1) * wide].astype(BF16)

        for r in range(planes):
            outs[r][...] = all_ref[place_ref[2] ^ r]

    return alone(
        body,
        (*grads, *moments, vectors, vec_moment),
        [sds((1, 1), F32), sds((VEC, D), F32), sds((VEC, D), F32)] + [sds((rows, wide), BF16)] * planes,
        "orthogonal",
        scratch=[
            pltpu.VMEM((D, FF), BF16),
            pltpu.VMEM((D, FF), F32),
            pltpu.VMEM((D, D), BF16),
            pltpu.VMEM((D, 1), F32),
            pltpu.VMEM((planes, rows, wide), BF16),
        ],
        place=place,
        after=after,
        flops=18e9,
        vmem=24 * 1024 * 1024,
        resident=count + 2,
    )


def outside(arrays):
    return [pltpu.with_memory_space_constraint(x, pltpu.HBM) for x in arrays]


def moments_kernel(norm, ga, gb, attn_moment, up_moment, down_moment, after):
    rows, cols = attn_moment.shape[1:]
    wide = up_moment.shape[1]
    limit = clip_fraction * math.sqrt(PARAMS)

    def body(norm_ref, ga_ref, gb_ref, am_ref, um_ref, dm_ref, amn_ref, umn_ref, dmn_ref):
        clip = limit / jnp.maximum(norm_ref[...], limit)
        for j in range(4):
            grad = ga_ref[j * rows : (j + 1) * rows, :] if j < 3 else gb_ref[:, :cols]
            amn_ref[j] = muon_decay * am_ref[j] + clip * grad
        umn_ref[...] = muon_decay * um_ref[...] + clip * gb_ref[:, cols : cols + wide]
        dmn_ref[...] = muon_decay * dm_ref[...] + clip * gb_ref[:, cols + wide :]

    moments = (attn_moment, up_moment, down_moment)
    return alone(
        body,
        (norm, *outside((ga, gb, *moments))),
        [sds(x.shape, F32) for x in moments],
        "moments",
        after=after,
    )


def update_kernel(place, slots, attn_weights, up_weights, down_weights):
    planes = len(slots)
    cols = attn_weights.shape[2]
    shape_factor = math.sqrt(max(1.0, FF / D))

    def body(place_ref, *refs):
        slot_refs, (aw_ref, uw_ref, dw_ref, an_ref, un_ref, dn_ref, all_ref) = refs[:planes], refs[planes:]
        for r in range(planes):
            all_ref[place_ref[2] ^ r] = slot_refs[r][...]
        for j in range(4):
            ortho = all_ref[1 + j // 2, :, (j % 2) * cols : (j % 2 + 1) * cols].astype(F32)
            an_ref[j] = aw_ref[j] - muon_rate * ortho
        un_ref[...] = uw_ref[...] - muon_rate * all_ref[0].astype(F32)
        dn_ref[...] = dw_ref[...] - muon_rate * shape_factor * all_ref[3].astype(F32)

    weights = (attn_weights, up_weights, down_weights)
    return alone(
        body,
        (*slots, *outside(weights)),
        [sds(x.shape, F32) for x in weights],
        "update",
        resident=planes,
        scratch=[pltpu.VMEM((planes,) + slots[0].shape, BF16)],
        place=place,
    )


def documents(starts):
    doc = jnp.cumsum(starts).astype(F32)
    return doc.reshape(1, LEN), doc.reshape(LEN, 1)


def plain_tail(sizes, grads, attn_weights, up_weights, down_weights, vectors, attn_moment, up_moment, down_moment, vec_moment):
    dp = ("chip", "core")
    grad_attn, grad_up, grad_down, grad_vectors = grads

    def owned(grad, narrow_dim, dp_dim):
        part_sum = lax.psum_scatter(grad.astype(BF16), "narrow", scatter_dimension=narrow_dim, tiled=True)
        return lax.psum_scatter(part_sum, dp, scatter_dimension=dp_dim, tiled=True).astype(F32)

    owned_attn, owned_up, owned_down = owned(grad_attn, 2, 1), owned(grad_up, 1, 0), owned(grad_down, 0, 1)
    own_squares = jnp.sum(owned_attn * owned_attn) + jnp.sum(owned_up * owned_up) + jnp.sum(owned_down * owned_down)
    vector_sum, square_sum = lax.psum((grad_vectors, own_squares), ("chip", "core", "narrow"))
    grad_norm = jnp.sqrt(square_sum + jnp.sum(vector_sum * vector_sum))
    clip_limit = clip_fraction * math.sqrt(PARAMS)
    clip_factor = clip_limit / jnp.maximum(grad_norm, clip_limit)
    attn_mom_new = muon_decay * attn_moment + clip_factor * owned_attn
    up_mom_new = muon_decay * up_moment + clip_factor * owned_up
    down_mom_new = muon_decay * down_moment + clip_factor * owned_down
    gather = lambda x, dim: lax.all_gather(x.astype(BF16), dp, axis=dim, tiled=True).astype(F32)
    ortho = (gather(attn_mom_new, 1), gather(up_mom_new, 0), gather(down_mom_new, 1))
    ortho_attn, ortho_up, ortho_down = ortho
    for iteration in range(NS_ITERS):
        gram_attn = jnp.einsum("imc,inc->imn", ortho_attn, ortho_attn, precision=highest)
        gram_up = lax.dot_general(ortho_up, ortho_up, (((1,), (1,)), ((), ())), precision=highest)
        gram_down = lax.dot_general(ortho_down, ortho_down, (((0,), (0,)), ((), ())), precision=highest)
        partial_grams = jnp.concatenate([gram_attn, gram_up[None], gram_down[None]], axis=0)
        gram_total = lax.psum(partial_grams.astype(BF16), "narrow").astype(F32)
        if iteration == 0:
            norm_scales = 1.0 / (jnp.sqrt(jnp.trace(gram_total, axis1=1, axis2=2)) + 1e-07)
            ortho_attn = ortho_attn * norm_scales[:4, None, None]
            ortho_up = ortho_up * norm_scales[4]
            ortho_down = ortho_down * norm_scales[5]
            gram_total = gram_total * (norm_scales * norm_scales)[:, None, None]
        once = jnp.einsum("imn,inc->imc", gram_total[:4], ortho_attn, precision=highest)
        twice = jnp.einsum("imn,inc->imc", gram_total[:4], once, precision=highest)
        ortho_attn = coef_first * ortho_attn + coef_second * once + coef_third * twice
        once = jnp.dot(gram_total[4], ortho_up, precision=highest)
        twice = jnp.dot(gram_total[4], once, precision=highest)
        ortho_up = coef_first * ortho_up + coef_second * once + coef_third * twice
        once = jnp.dot(ortho_down, gram_total[5], precision=highest)
        twice = jnp.dot(once, gram_total[5], precision=highest)
        ortho_down = coef_first * ortho_down + coef_second * once + coef_third * twice
    row_share = D // sizes["dp"]
    row_start = lax.axis_index(dp) * row_share
    final_attn = lax.dynamic_slice_in_dim(ortho_attn, row_start, row_share, 1)
    final_up = lax.dynamic_slice_in_dim(ortho_up, row_start, row_share, 0)
    final_down = lax.dynamic_slice_in_dim(ortho_down, row_start, row_share, 1)
    shape_factor = math.sqrt(max(1.0, FF / D))
    vector_mom_new = vector_decay * vec_moment + clip_factor * vector_sum
    return (
        attn_weights - muon_rate * final_attn,
        up_weights - muon_rate * final_up,
        down_weights - muon_rate * shape_factor * final_down,
        attn_mom_new,
        up_mom_new,
        down_mom_new,
        vectors - vector_rate * vector_mom_new,
        vector_mom_new,
        grad_norm,
    )


def per_device(
    sizes,
    tokens, memory, neighbour_bank, starts, neighbours, cotangent,
    attn_weights, up_weights, down_weights, vectors,
    attn_moment, up_moment, down_moment, vector_moment,
):
    memory = memory.reshape(MEM, D)
    bank = neighbour_bank.reshape(BANK, D)
    own = (attn_weights, up_weights, down_weights)
    moments = (attn_moment, up_moment, down_moment)
    chips, planes = sizes["dp"] // 2, sizes["narrow"]
    if planes == len(PLANES) and chips == 4:
        return fast_device(
            chips, planes, tokens, memory, bank, starts, neighbours, cotangent, own, vectors, moments, vector_moment
        )
    full = lambda x, narrow_dim, dp_dim: lax.all_gather(
        lax.all_gather(x.astype(BF16), ("chip", "core"), axis=dp_dim, tiled=True), "narrow", axis=narrow_dim, tiled=True
    )
    attn_full = full(attn_weights, 2, 1)
    second = [attn_full[3], full(up_weights, 1, 0), full(down_weights, 0, 1).T]
    x, xt, cot_t, gate = context_kernel(tokens, memory, bank, cotangent, vectors)
    doc_row, doc_col = documents(starts)
    bias_tok, bias_bank = mask_kernel(doc_row, doc_col, neighbours.T)
    w, q, k, v, qt, kt, vt, qn, kn = project_kernel(x, attn_full[:3])
    e, local, fetched, stat, mixed, mixed_t = attend_kernel(qt, k, vt, qn, kn, bias_tok, bias_bank, doc_row, gate, 0, NPAIR)
    out, act, gh, ffn_t, branch, gres, gmt, gain_ffn = feed_kernel(mixed, tokens, cotangent, vectors, second)
    grad_down_t, grad_up, grad_o = feed_grads_kernel(cot_t, act, ffn_t, gh, mixed_t, branch)
    *back, gl = prepare_kernel(gmt, local, fetched, stat, gate)
    dq, dk, dv = unattend_kernel(q, kt, v, e, *back, 0, NPAIR)
    grad_qkv, grad_gate = proj_grads_kernel(xt, dq, dk, dv, gl)
    grad_in, gain_attn = input_kernel(dq, dk, dv, gl, w, tokens, memory, vectors, gres)
    grad_vectors = jnp.concatenate([gain_attn, gain_ffn, grad_gate], axis=0)
    grads = (jnp.concatenate([grad_qkv, grad_o[None]], axis=0), grad_up, grad_down_t.T, grad_vectors)
    return (out, grad_in) + plain_tail(sizes, grads, *own, vectors, *moments, vector_moment)


def ordered(first, second):
    return lax.optimization_barrier((first, second))[0]


def fast_device(
    chips, planes, tokens, memory, bank, starts, neighbours, cotangent, own, vectors, moments, vector_moment
):
    own, moments = own[:2] + (own[2].T,), moments[:2] + (moments[2].T,)
    place = jnp.stack([lax.axis_index("chip"), lax.axis_index("core"), lax.axis_index("narrow")]).astype(jnp.int32)
    payload = first_payload(own[0])
    payloads = second_payloads(place, *own, *moments, after=[payload])
    near_a = exchange([payload] * planes, "narrow")
    doc_row, doc_col = documents(starts)
    near_t = ordered(neighbours.T, payload)
    near_b = exchange(ordered(payloads, near_a), "narrow")
    column_a = stacked(near_a)
    plane_a = exchange([column_a] * chips, "chip")
    x, xt, cot_t, gate = context_kernel(tokens, memory, bank, cotangent, vectors, after=[column_a])
    bias_tok, bias_bank = mask_kernel(doc_row, doc_col, near_t, after=[x])
    first = core_blocks(ordered(plane_a, bias_tok))
    column_b, column_m = stacked_pair(ordered(near_b, first), payloads[0].shape[1] - own[1].shape[1])
    w, q, k, v, qt, kt, vt, qn, kn = project_kernel(x, first, place, after=[column_b])
    plane_b = exchange([column_b] * chips, "chip")
    e, local, fetched, stat, mixed, mixed_t = attend_kernel(qt, k, vt, qn, kn, bias_tok, bias_bank, doc_row, gate, 0, NPAIR)
    own_b = exchange([column_b, column_b], "core")[1]
    late_b = ordered(plane_b[1:], mixed)
    second = [column_b, *late_b, own_b] + [exchange([b, b], "core")[1] for b in late_b]
    gres, gmt, gain_ffn, keep_b, send_b, residual, act, down_t = feed_blocks(
        mixed, mixed_t, tokens, cotangent, cot_t, vectors, second, place
    )
    q, kt, xt = outside((q, kt, xt))
    *back, gl = prepare_kernel(gmt, local, fetched, stat, gate)
    other_b = ordered(exchange([send_b, send_b], "core")[1], back[0])
    slots_b = fold_cores(keep_b, other_b)
    dq, dk, dv = unattend_kernel(q, kt, v, e, *back, 0, NPAIR, after=[slots_b[0]])
    slots_b = fold_chips(ordered(exchange(slots_b, "chip"), dq))
    keep_a, send_a, grad_gate = proj_grads_kernel(xt, dq, dk, dv, gl, place, chips, planes, after=[slots_b[0]])
    slots_a = fold_cores_first(keep_a, exchange([send_a, send_a], "core")[1])
    grad_in, gain_attn = input_kernel(dq, dk, dv, gl, w, tokens, memory, vectors, gres, after=[slots_a[0]])
    parts_a = exchange(slots_a, "chip")
    parts_b = exchange([slots_b[0], ordered(slots_b[1], grad_in), *slots_b[2:]], "narrow")
    parts_a = ordered(parts_a, grad_in)
    slots_a = fold_chips_first(parts_a, gain_attn, gain_ffn, grad_gate)
    parts_a = exchange(slots_a, "narrow")
    early_m = ordered(column_m, slots_a[0])
    ga, gb, vec, *slots = owned_kernel(place, parts_a, parts_b)
    plane_m = exchange([early_m, ordered(early_m, vec), *[early_m] * (chips - 2)], "chip")
    whole_m = stacked(plane_m)
    all_m = exchange([whole_m, whole_m], "core")
    column_g = stack_with_vectors(exchange(slots, "narrow"), vec, after=[])
    plane_g = exchange([column_g] * chips, "chip")
    out = output_kernel(*outside((residual, act, down_t)), after=[column_g, whole_m])
    grads = core_blocks(ordered(plane_g, out))
    norm, vec_new, vec_mom, *slots = orthogonal_kernel(place, grads, all_m, vectors, vector_moment, [])
    final = exchange(slots, "narrow")
    attn_mom, up_mom, down_mom = moments_kernel(norm, ga, gb, *moments, after=[slots[0]])
    attn_new, up_new, down_new = update_kernel(place, ordered(final, attn_mom), *own)
    new = (attn_new, up_new, down_new.T, attn_mom, up_mom, down_mom.T)
    return (out, grad_in, *new, vec_new, vec_mom, norm.reshape(()))


def solution(mesh):
    sizes = dict(mesh.shape)
    split = Mesh(
        mesh.devices.reshape(sizes["dp"] // 2, 2, sizes["narrow"]), ("chip", "core", "narrow")
    )
    dp = ("chip", "core")
    rows = ("chip", "core", "narrow")
    weights = (P(None, dp, "narrow"), P(dp, "narrow"), P("narrow", dp))
    return jax.shard_map(
        lambda *operands: per_device(sizes, *operands),
        mesh=split,
        in_specs=(P(rows, None), P(rows, None, None), P(rows, None, None), P(rows), P(rows, None), P(rows, None))
        + weights + (P(),) + weights + (P(),),
        out_specs=(P(rows, None), P(rows, None)) + weights + weights + (P(), P(), P()),
        check_vma=False,
    )
```
